32 devices in a mesh: dp: 8 (over z, y), head: 4 (over x, core).
Axes of the slice: x: 2, y: 2, z: 4, core: 2. Of those that a mesh axis runs over, the one named last changes fastest.
Arguments:
- patches: bfloat16 [18432, 768], P('dp'), may hold values from -6 to 6
- cotangent: bfloat16 [18432, 768], P('dp'), may hold values from -6 to 6
- expert_ids: int32 [18432, 2], P('dp'), may hold values from 0 to 7, as said below
- slot_pos: int32 [18432, 2], P('dp'), may hold values from 0 to 288, as said below
- owners: int32 [4, 96], P('head'), may hold values from 0 to 7, as said below
- tile_master: float32 [768, 8, 768], P(('dp', 'head'))
- tile_first: float32 [768, 8, 768], P(('dp', 'head'))
- tile_second: float32 [768, 8, 768], P(('dp', 'head'))
- expert_up: float32 [8, 768, 3072], P('dp', None, 'head'), may hold values from -0.21875 to 0.21875
- up_first: float32 [8, 768, 3072], P('dp', None, 'head')
- up_second: float32 [8, 768, 3072], P('dp', None, 'head')
- expert_down: float32 [8, 3072, 768], P('dp', 'head'), may hold values from -0.875 to 0.875
- down_first: float32 [8, 3072, 768], P('dp', 'head')
- down_second: float32 [8, 3072, 768], P('dp', 'head')
- router: float32 [8, 768], replicated, may hold values from -0.15625 to 0.15625
- router_first: float32 [8, 768], replicated
- router_second: float32 [8, 768], replicated
- norm_params: float32 [4, 768], replicated
- norm_first: float32 [4, 768], replicated
- norm_second: float32 [4, 768], replicated
Outputs:
- block_out: bfloat16 [18432, 768], P('dp')
- input_grad: float32 [18432, 768], P('dp')
- tile_new: float32 [768, 8, 768], P(('dp', 'head'))
- tile_first_new: float32 [768, 8, 768], P(('dp', 'head'))
- tile_second_new: float32 [768, 8, 768], P(('dp', 'head'))
- tile_copy: bfloat16 [768, 8, 768], P(('dp', 'head'))
- up_new: float32 [8, 768, 3072], P('dp', None, 'head')
- up_first_new: float32 [8, 768, 3072], P('dp', None, 'head')
- up_second_new: float32 [8, 768, 3072], P('dp', None, 'head')
- up_copy: bfloat16 [8, 768, 3072], P('dp', None, 'head')
- down_new: float32 [8, 3072, 768], P('dp', 'head')
- down_first_new: float32 [8, 3072, 768], P('dp', 'head')
- down_second_new: float32 [8, 3072, 768], P('dp', 'head')
- down_copy: bfloat16 [8, 3072, 768], P('dp', 'head')
- router_new: float32 [8, 768], replicated
- router_first_new: float32 [8, 768], replicated
- router_second_new: float32 [8, 768], replicated
- norm_new: float32 [4, 768], replicated
- norm_first_new: float32 [4, 768], replicated
- norm_second_new: float32 [2, 768], replicated
- later_second_new: float32 [2, 768], replicated
The draws below stay inside these ranges and needn't reach their ends.
Inputs may be any that keep to these rules, and one draw needn't show every extreme that they name: `expert_ids`: A token's two experts differ. `slot_pos`: the value 288 marks a dropped pair. Among the tokens of one dp index (rows s * 2304 to s * 2304 + 2303), the kept pairs that name one expert hold the distinct slots 0 to n - 1 for some n; in each such block some expert has all 288 slots taken. `owners`: row h names, for each of the 96 tiles of head group h, the dp index that owns it; no dp index owns more than 24 tiles of one group, and in every group one dp index owns exactly 24.
All inputs are finite; a program needn't handle non-finite values.
Results may differ from the reference program's by a relative error of at most 0.025.
Values may be sent and summed in bfloat16 or wider, within the bound.
A program may use at most 256 MiB of HBM per device.

```python
import math
import jax
import jax.numpy as jnp
from jax import lax

D = 768
FF = 3072
HEADS = 12
HD = 64
PATCH = 576
TILE = 8
STEP = 10
HEAD_SPLIT = 4
EXPERTS = 8
TOK_DEV = 2304
TOKENS = 18432
CAP = 288
NTILE = 96
SLOTS = 24


def route_table(key):
    key = jax.random.fold_in(key, 71)
    pick_key, offset_key, order_key, favour_key = jax.random.split(key, 4)
    blocks = TOKENS // TOK_DEV
    first_pick = jax.random.randint(pick_key, (blocks, TOK_DEV), 0, EXPERTS)
    offset = jax.random.randint(offset_key, (blocks, TOK_DEV), 1, EXPERTS)
    token_order = jax.vmap(lambda subkey: jax.random.permutation(subkey, TOK_DEV))(jax.random.split(order_key, blocks))
    priority = jnp.argsort(token_order, axis=1)
    favoured = jax.random.randint(favour_key, (blocks, 1), 0, EXPERTS)
    first_pick = jnp.where(priority <= CAP, favoured, first_pick)
    second_pick = (first_pick + offset) % EXPERTS
    pair_ids = jnp.stack([first_pick, second_pick], axis=2)
    pair_rank = jnp.stack([priority, priority + TOK_DEV], axis=2).reshape(blocks, 2 * TOK_DEV)
    pair_expert = pair_ids.reshape(blocks, 2 * TOK_DEV)

    def slot_block(operands):
        rank_row, expert_row = operands
        same_expert = expert_row[:, None] == expert_row[None, :]
        ranked_ahead = rank_row[None, :] < rank_row[:, None]
        return jnp.sum(jnp.where(same_expert & ranked_ahead, 1, 0), axis=1)
    ahead_count = lax.map(slot_block, (pair_rank, pair_expert))
    slot_table = jnp.minimum(ahead_count, CAP).reshape(TOKENS, 2)
    return (pair_ids.reshape(TOKENS, 2).astype(jnp.int32), slot_table.astype(jnp.int32))


def owner_table(key):
    key = jax.random.fold_in(key, 83)
    cell_count = EXPERTS * SLOTS

    def one_group(subkey):
        pick_key, favour_key = jax.random.split(subkey)
        favoured = jax.random.randint(favour_key, (), 0, EXPERTS)
        score = jax.random.permutation(pick_key, cell_count)
        cell_owner = jnp.arange(cell_count) // SLOTS
        score = jnp.where(cell_owner == favoured, score - cell_count, score)
        chosen = jnp.argsort(score)[:NTILE]
        return (chosen // SLOTS).astype(jnp.int32)
    return jax.vmap(one_group)(jax.random.split(key, HEAD_SPLIT))


def slot_kinds(key):
    owner_grid = owner_table(key)
    order_index = jnp.arange(NTILE, dtype=jnp.int32)
    same_owner = owner_grid[:, :, None] == owner_grid[:, None, :]
    earlier = (order_index[None, :] < order_index[:, None])[None]
    tile_rank = jnp.sum(jnp.where(same_owner & earlier, 1, 0), axis=2)
    group_index = jnp.arange(HEAD_SPLIT, dtype=jnp.int32)[:, None]
    slot_place = (owner_grid * HEAD_SPLIT + group_index) * SLOTS + tile_rank
    tile_kind = jnp.broadcast_to(order_index * 4 // NTILE, (HEAD_SPLIT, NTILE))
    empty_kind = jnp.full((EXPERTS * HEAD_SPLIT * SLOTS,), 4, jnp.int32)
    return empty_kind.at[slot_place.reshape(-1)].set(tile_kind.reshape(-1))


def out_scale():
    return max(FF // (EXPERTS * EXPERTS), 1) ** (-0.5)


def first_moment(key, shape, grad_size):
    return jax.random.normal(key, shape, jnp.float32) * (grad_size / 9.0)


def second_moment(key, shape, grad_size):
    factor = jnp.exp(jax.random.uniform(key, shape, jnp.float32, 0.0, math.log(4.0)))
    return factor * (grad_size * grad_size * 0.001)


def tile_sizes(key):
    kinds = slot_kinds(key)
    table = jnp.array([0.5, 0.5, 0.6, 0.08, 0.5], jnp.float32) * TOKENS ** 0.5
    return table[kinds][:, None, None]


def up_size():
    return (TOKENS / EXPERTS) ** 0.5 * 0.6 * D ** 0.5 * out_scale() / EXPERTS


def down_size():
    return 0.65 * (TOKENS / EXPERTS) ** 0.5 / EXPERTS


def router_size():
    return TOKENS ** 0.5 * EXPERTS ** (-1.5) * D ** 0.5 * FF ** 0.5 * 0.65 * out_scale()


def norm_sizes():
    root = TOKENS ** 0.5
    return jnp.array([root, root, 0.3 * root, 0.3 * root], jnp.float32)[:, None]


def draw_expert_ids(key, part):
    routed = route_table(key)
    return routed[0]


def draw_slot_pos(key, part):
    routed = route_table(key)
    return routed[1]


def draw_owners(key, part):
    owner_grid = owner_table(key)
    return owner_grid


def draw_tile_master(key, part):
    kinds = slot_kinds(key)
    key = jax.random.fold_in(key, 6)
    spread = D ** (-0.5)
    table = jnp.array([spread, spread, spread, 0.25, spread], jnp.float32)
    shape = (EXPERTS * HEAD_SPLIT * SLOTS, TILE, D)
    return jax.random.normal(key, shape, jnp.float32) * table[kinds][:, None, None]


def draw_tile_first(key, part):
    grad_size = tile_sizes(key)
    key = jax.random.fold_in(key, 7)
    return first_moment(key, (EXPERTS * HEAD_SPLIT * SLOTS, TILE, D), grad_size)


def draw_tile_second(key, part):
    grad_size = tile_sizes(key)
    key = jax.random.fold_in(key, 8)
    return second_moment(key, (EXPERTS * HEAD_SPLIT * SLOTS, TILE, D), grad_size)


def draw_up_first(key, part):
    key = jax.random.fold_in(key, 9)
    return first_moment(key, (EXPERTS, D, FF), up_size())


def draw_up_second(key, part):
    key = jax.random.fold_in(key, 10)
    return second_moment(key, (EXPERTS, D, FF), up_size())


def draw_down_first(key, part):
    key = jax.random.fold_in(key, 11)
    return first_moment(key, (EXPERTS, FF, D), down_size())


def draw_down_second(key, part):
    key = jax.random.fold_in(key, 12)
    return second_moment(key, (EXPERTS, FF, D), down_size())


def draw_router_first(key, part):
    key = jax.random.fold_in(key, 13)
    return first_moment(key, (EXPERTS, D), router_size())


def draw_router_second(key, part):
    key = jax.random.fold_in(key, 14)
    return second_moment(key, (EXPERTS, D), router_size())


def draw_norm_params(key, part):
    key = jax.random.fold_in(key, 15)
    gain_key, shift_key = jax.random.split(key)
    gains = jax.random.uniform(gain_key, (2, D), jnp.float32, 0.5, 1.5)
    shifts = jax.random.uniform(shift_key, (2, D), jnp.float32, -0.3, 0.3)
    return jnp.stack([gains[0], shifts[0], gains[1], shifts[1]])


def draw_norm_first(key, part):
    key = jax.random.fold_in(key, 16)
    return first_moment(key, (4, D), norm_sizes())


def draw_norm_second(key, part):
    key = jax.random.fold_in(key, 17)
    return second_moment(key, (4, D), norm_sizes())


def block_levels(own_key, dims, cuts, smallest, high):
    def one(position, parts):
        draws = jax.random.uniform(jax.random.fold_in(jax.random.fold_in(own_key, 6), position), (parts,), jnp.float32, smallest / len(cuts), high / len(cuts))
        return jnp.repeat(jnp.exp(draws), dims[position] // parts).reshape((-1,) + (1,) * (len(dims) - position - 1))

    loudness = one(*cuts[0])
    for cut in cuts[1:]:
        loudness = loudness * one(*cut)
    return loudness


def gaussian(stream_key, dims, width, limit, cuts=(), kind=jnp.bfloat16):
    values = width * jax.random.normal(stream_key, dims, jnp.float32)
    if cuts:
        values = values * block_levels(stream_key, dims, cuts, -0.22, 0.18)
    return jnp.clip(values, -limit, limit).astype(kind)


def setup_inputs(seed: int = 0) -> dict:
    streams_of = jax.random.split(jax.random.key(seed), 21)
    return {
        "patches": gaussian(streams_of[0], (TOKENS, D), 1.0, 6.0, ((0, 8),)),
        "cotangent": gaussian(streams_of[1], (TOKENS, D), 1.0, 6.0, ((0, 8),)),
        "expert_ids": draw_expert_ids(jax.random.fold_in(streams_of[20], 71), 0),
        "slot_pos": draw_slot_pos(jax.random.fold_in(streams_of[20], 71), 0),
        "owners": draw_owners(jax.random.fold_in(streams_of[20], 71), 0),
        "tile_master": draw_tile_master(jax.random.fold_in(streams_of[20], 71), 0),
        "tile_first": draw_tile_first(jax.random.fold_in(streams_of[20], 71), 0),
        "tile_second": draw_tile_second(jax.random.fold_in(streams_of[20], 71), 0),
        "expert_up": gaussian(streams_of[8], (EXPERTS, D, FF), D ** -0.5, 0.21875, ((0, 8), (2, 4)), jnp.float32),
        "up_first": draw_up_first(jax.random.fold_in(streams_of[20], 71), 0),
        "up_second": draw_up_second(jax.random.fold_in(streams_of[20], 71), 0),
        "expert_down": gaussian(streams_of[11], (EXPERTS, FF, D), (max(FF // (EXPERTS * EXPERTS), 1)) ** -0.5, 0.875, ((0, 8), (1, 4)), jnp.float32),
        "down_first": draw_down_first(jax.random.fold_in(streams_of[20], 71), 0),
        "down_second": draw_down_second(jax.random.fold_in(streams_of[20], 71), 0),
        "router": gaussian(streams_of[14], (EXPERTS, D), (2 * D) ** -0.5, 0.15625, (), jnp.float32),
        "router_first": draw_router_first(jax.random.fold_in(streams_of[20], 71), 0),
        "router_second": draw_router_second(jax.random.fold_in(streams_of[20], 71), 0),
        "norm_params": draw_norm_params(jax.random.fold_in(streams_of[20], 71), 0),
        "norm_first": draw_norm_first(jax.random.fold_in(streams_of[20], 71), 0),
        "norm_second": draw_norm_second(jax.random.fold_in(streams_of[20], 71), 0),
    }


@jax.custom_vjp
def low(v):
    return lax.optimization_barrier(v.astype(jnp.bfloat16)).astype(jnp.float32)

@jax.custom_vjp
def low_back(v):
    return v

def low_keep(v):
    return (low(v), None)

def low_pass(kept, grad):
    return (grad,)

def back_keep(v):
    return (v, None)

def back_low(kept, grad):
    return (low(grad),)
low.defvjp(low_keep, low_pass)
low_back.defvjp(back_keep, back_low)
highest = lax.Precision.HIGHEST
eps_norm = 1e-06
beta_one = 0.9
beta_two = 0.999
adam_eps = 1e-08
rate_attention = 0.12
rate_up = 0.08
rate_down = 0.3
rate_router = 0.05
rate_norm = 0.4
decay_factor = 0.1

def layer_norm(values, gain_row, shift_row):
    average = lax.optimization_barrier(jnp.mean(values, axis=-1, keepdims=True))
    centred = values - average
    variance = lax.optimization_barrier(jnp.mean(centred * centred, axis=-1, keepdims=True))
    return centred * lax.rsqrt(variance + eps_norm) * gain_row + shift_row

def smooth_gelu(values):
    return jax.nn.gelu(values, approximate=True)

def adam_update(weight, moment_one, moment_two, gradient, step_rate, weight_decay):
    moment_one = beta_one * moment_one + (1.0 - beta_one) * gradient
    moment_two = beta_two * moment_two + (1.0 - beta_two) * gradient * gradient
    fixed_one = moment_one / (1.0 - beta_one ** STEP)
    fixed_two = moment_two / (1.0 - beta_two ** STEP)
    weight = weight - step_rate * (fixed_one / (jnp.sqrt(fixed_two) + adam_eps) + weight_decay * weight)
    return (weight, moment_one, moment_two)

def owner_rows(owners):
    order_index = jnp.arange(NTILE, dtype=jnp.int32)
    same_owner = owners[:, :, None] == owners[:, None, :]
    earlier = (order_index[None, :] < order_index[:, None])[None]
    tile_rank = lax.optimization_barrier(jnp.sum(jnp.where(same_owner & earlier, 1, 0), axis=2)).astype(jnp.int32)
    group_index = jnp.arange(HEAD_SPLIT, dtype=jnp.int32)[:, None]
    return (owners * HEAD_SPLIT + group_index) * SLOTS + tile_rank

def image_attention(block_rows):
    query_rows, key_rows, value_rows = block_rows
    scores = low_back(jnp.einsum('qhd,khd->hqk', query_rows, key_rows, precision=highest) * HD ** (-0.5))
    weights = low(jax.nn.softmax(scores, axis=-1))
    return jnp.einsum('hqk,khd->qhd', weights, value_rows, precision=highest)

def forward(inputs, tile_master, expert_up, expert_down, router, norm_params, owners, expert_ids, slot_pos):
    slot_place = owner_rows(owners)
    tile_rows = low(tile_master[slot_place]).reshape(HEAD_SPLIT, 4, NTILE * TILE // 4, D)
    w_query = tile_rows[:, 0].reshape(HEADS * HD, D)
    w_key = tile_rows[:, 1].reshape(HEADS * HD, D)
    w_value = tile_rows[:, 2].reshape(HEADS * HD, D)
    w_proj = tile_rows[:, 3].reshape(HEADS * HD, D)
    normed_low = low(layer_norm(inputs, norm_params[0], norm_params[1]))
    image_count = TOKENS // PATCH

    def project(weight):
        projected = low(low_back(jnp.dot(normed_low, weight.T, precision=highest)))
        return projected.reshape(image_count, PATCH, HEADS, HD)
    mixed_rows = lax.map(jax.checkpoint(image_attention), (project(w_query), project(w_key), project(w_value)))
    mixed_rows = low(low_back(mixed_rows.reshape(TOKENS, HEADS * HD)))
    residual_one = inputs + low_back(jnp.dot(mixed_rows, w_proj, precision=highest))
    normed_two = low(layer_norm(residual_one, norm_params[2], norm_params[3]))
    logits = low_back(jnp.dot(normed_two, low(router).T, precision=highest))
    gate_probs = jax.nn.softmax(logits, axis=-1)
    gate_pair = jnp.take_along_axis(gate_probs, expert_ids, axis=1).reshape(EXPERTS, TOK_DEV, 2)
    ids_block = expert_ids.reshape(EXPERTS, TOK_DEV, 2)
    slot_block = slot_pos.reshape(EXPERTS, TOK_DEV, 2)
    source = jnp.broadcast_to(jnp.arange(EXPERTS, dtype=jnp.int32)[:, None, None], (EXPERTS, TOK_DEV, 2))
    rows_block = jnp.broadcast_to(normed_two.reshape(EXPERTS, TOK_DEV, 1, D), (EXPERTS, TOK_DEV, 2, D))
    buffer_rows = jnp.zeros((EXPERTS, EXPERTS, CAP + 1, D), jnp.float32).at[source, ids_block, slot_block].add(rows_block)
    dispatched = low_back(buffer_rows[:, :, :CAP])
    hidden = low_back(jnp.einsum('secd,edf->secf', dispatched, low(expert_up), precision=highest))
    activated = low(smooth_gelu(hidden))
    expert_out = low(low_back(jnp.einsum('secf,efd->secd', activated, low(expert_down), precision=highest)))
    padded = jnp.concatenate([expert_out, jnp.zeros((EXPERTS, EXPERTS, 1, D), jnp.float32)], axis=2)
    picked = padded[source, ids_block, slot_block]
    expert_mix = lax.optimization_barrier(jnp.sum(gate_pair[..., None] * picked, axis=2)).reshape(TOKENS, D)
    return residual_one + expert_mix

def reference(patches, cotangent, expert_ids, slot_pos, owners, tile_master, tile_first, tile_second, expert_up, up_first, up_second, expert_down, down_first, down_second, router, router_first, router_second, norm_params, norm_first, norm_second):

    def whole_block(inputs, masters, up_weight, down_weight, router_weight, norm_weight):
        return forward(inputs, masters, up_weight, down_weight, router_weight, norm_weight, owners, expert_ids, slot_pos)
    result, pull_back = jax.vjp(whole_block, patches.astype(jnp.float32), tile_master, expert_up, expert_down, router, norm_params)
    input_grad, tile_grad, up_grad, down_grad, router_grad, norm_grad = pull_back(cotangent.astype(jnp.float32))
    tile_new, tile_first_new, tile_second_new = adam_update(tile_master, tile_first, tile_second, tile_grad, rate_attention, decay_factor)
    up_new, up_first_new, up_second_new = adam_update(expert_up, up_first, up_second, up_grad, rate_up, decay_factor)
    down_new, down_first_new, down_second_new = adam_update(expert_down, down_first, down_second, down_grad, rate_down, decay_factor)
    router_new, router_first_new, router_second_new = adam_update(router, router_first, router_second, router_grad, rate_router, decay_factor)
    norm_new, norm_first_new, norm_second_all = adam_update(norm_params, norm_first, norm_second, norm_grad, rate_norm, 0.0)
    return (result.astype(jnp.bfloat16), input_grad, tile_new, tile_first_new, tile_second_new, tile_new.astype(jnp.bfloat16), up_new, up_first_new, up_second_new, up_new.astype(jnp.bfloat16), down_new, down_first_new, down_second_new, down_new.astype(jnp.bfloat16), router_new, router_first_new, router_second_new, norm_new, norm_first_new, norm_second_all[:2], norm_second_all[2:])
```

```python
import functools

import jax
import jax.numpy as jnp
from jax import lax
from jax.experimental import pallas as pl
from jax.experimental.pallas import tpu as pltpu
from jax.sharding import PartitionSpec as P

HD = 64
PATCH = 576
TILE = 8
STEP = 10

eps_norm = 1e-06
beta_one = 0.9
beta_two = 0.999
adam_eps = 1e-08
rate_attention = 0.12
rate_up = 0.08
rate_down = 0.3
rate_router = 0.05
rate_norm = 0.4
decay_factor = 0.1

LOW = jnp.bfloat16
FULL = jnp.float32
MESH = pl.DeviceIdType.MESH
VMEM_BYTES = 56 * 1024 * 1024


def adam_update(weight, moment_one, moment_two, gradient, step_rate, weight_decay):
    moment_one = beta_one * moment_one + (1.0 - beta_one) * gradient
    moment_two = beta_two * moment_two + (1.0 - beta_two) * gradient * gradient
    fixed_one = moment_one / (1.0 - beta_one**STEP)
    fixed_two = moment_two / (1.0 - beta_two**STEP)
    weight = weight - step_rate * (
        fixed_one / (jnp.sqrt(fixed_two) + adam_eps) + weight_decay * weight
    )
    return (weight, moment_one, moment_two)


def nn(left, right):
    return lax.dot_general(left, right, (((1,), (0,)), ((), ())), preferred_element_type=FULL)


def nt(left, right):
    return lax.dot_general(left, right, (((1,), (1,)), ((), ())), preferred_element_type=FULL)


def tn(left, right):
    return lax.dot_general(left, right, (((0,), (0,)), ((), ())), preferred_element_type=FULL)


def params(**more):
    return pltpu.CompilerParams(vmem_limit_bytes=VMEM_BYTES, **more)


def whole(shape):
    return pl.BlockSpec(shape, lambda *_: (0,) * len(shape))


def lead(shape):
    return pl.BlockSpec(shape, lambda i: (i,) + (0,) * (len(shape) - 1))


def normalise(values):
    average = jnp.mean(values, axis=-1, keepdims=True)
    centred = values - average
    variance = jnp.mean(centred * centred, axis=-1, keepdims=True)
    scale = lax.rsqrt(variance + eps_norm)
    return centred * scale, scale


def norm_back(normal, scale, gain, upstream):
    inner = upstream * gain
    mean_inner = jnp.mean(inner, axis=-1, keepdims=True)
    mean_cross = jnp.mean(inner * normal, axis=-1, keepdims=True)
    result = scale * (inner - mean_inner - normal * mean_cross)
    gain_sum = jnp.sum(upstream * normal, axis=0, keepdims=True)
    shift_sum = jnp.sum(upstream, axis=0, keepdims=True)
    return result, gain_sum, shift_sum


def one_hot(condition):
    return jnp.where(condition, 1.0, 0.0).astype(LOW)


def head_mask(shape, axis, head):
    return lax.broadcasted_iota(jnp.int32, shape, axis) // HD == head


def attention_front(
    x_ref, norm_ref, held_ref, src_ref,
    w_ref, xn_ref, q_ref, qt_ref, k_ref, kt_ref, v_ref, lse_ref, ot_ref, part_ref,
):
    rows = w_ref.shape[0] // 4
    heads = rows // HD

    @pl.when(pl.program_id(0) == 0)
    def _():
        total = held_ref.shape[0]
        for part in range(4):
            block = pl.ds(part * rows, rows)
            lanes = lax.broadcasted_iota(jnp.int32, (rows, total), 1)
            pick = one_hot(lanes == src_ref[block, :])
            w_ref[block, :] = nn(pick, held_ref[...]).astype(LOW)

    normal, _ = normalise(x_ref[...].astype(FULL))
    xn = (normal * norm_ref[0:1, :] + norm_ref[1:2, :]).astype(LOW)
    xn_ref[...] = xn
    wq, wk, wv = (w_ref[pl.ds(part * rows, rows), :] for part in range(3))
    shrink = HD ** (-0.5)
    q_ref[...] = (nt(xn, wq) * shrink).astype(LOW)
    qt = (nt(wq, xn) * shrink).astype(LOW)
    qt_ref[0] = qt
    k = nt(xn, wk).astype(LOW)
    k_ref[...] = k
    kt_ref[0] = nt(wk, xn).astype(LOW)
    v_ref[...] = nt(xn, wv).astype(LOW)
    vt = nt(wv, xn).astype(LOW)
    mixed = []
    for head in range(heads):
        span = slice(head * HD, (head + 1) * HD)
        only = jnp.where(head_mask(qt.shape, 0, head), qt, jnp.zeros_like(qt))
        scores = nn(k, only)
        top = jnp.max(scores, axis=0, keepdims=True)
        weights = jnp.exp(scores - top)
        total = jnp.sum(weights, axis=0, keepdims=True)
        mixed.append(nn(vt[span], weights.astype(LOW)) / total)
        lse_ref[0, head:head + 1, :] = top + jnp.log(total)
    ot = jnp.concatenate(mixed, axis=0).astype(LOW)
    ot_ref[0] = ot
    part_ref[...] = tn(ot, w_ref[pl.ds(3 * rows, rows), :]).astype(LOW)


def attention_forward(patches, norm_params, held, src_col):
    tokens, width = patches.shape
    images = tokens // PATCH
    all_rows = src_col.shape[0]
    rows = all_rows // 4
    flat = jax.ShapeDtypeStruct((tokens, rows), LOW)
    turned = jax.ShapeDtypeStruct((images, rows, PATCH), LOW)
    wide = jax.ShapeDtypeStruct((tokens, width), LOW)
    flat_spec, turned_spec, wide_spec = (
        lead((PATCH, rows)), lead((1, rows, PATCH)), lead((PATCH, width))
    )
    return pl.pallas_call(
        attention_front,
        grid=(images,),
        in_specs=[wide_spec, whole(norm_params.shape), whole(held.shape), whole(src_col.shape)],
        out_specs=[
            whole((all_rows, width)), wide_spec, flat_spec, turned_spec, flat_spec, turned_spec,
            flat_spec, lead((1, 8, PATCH)), turned_spec, wide_spec,
        ],
        out_shape=[
            jax.ShapeDtypeStruct((all_rows, width), LOW), wide, flat, turned, flat, turned,
            flat, jax.ShapeDtypeStruct((images, 8, PATCH), FULL), turned, wide,
        ],
        compiler_params=params(),
        name="attention_forward",
    )(patches, norm_params, held, src_col)


def attention_rear(
    x1g_ref, w_ref, xn_ref, q_ref, qt_ref, k_ref, kt_ref, v_ref, lse_ref, ot_ref, src_ref,
    part_ref, padded_ref, grad_ref,
):
    rows = w_ref.shape[0] // 4
    heads = rows // HD
    step = pl.program_id(0)
    wq, wk, wv, wo = (w_ref[pl.ds(part * rows, rows), :] for part in range(4))
    x1g, xn = x1g_ref[...], xn_ref[...]
    q, qt, k, kt, v, ot = q_ref[...], qt_ref[0], k_ref[...], kt_ref[0], v_ref[...], ot_ref[0]
    do = nt(x1g, wo).astype(LOW)
    dot = nt(wo, x1g).astype(LOW)
    product = dot.astype(FULL) * ot.astype(FULL)
    shrink = HD ** (-0.5)
    dqt, dk, dv = [], None, None
    for head in range(heads):
        span = slice(head * HD, (head + 1) * HD)
        zero_t = jnp.zeros_like(qt)
        mask_t = head_mask(qt.shape, 0, head)
        mask = head_mask(q.shape, 1, head)
        scores = nn(k, jnp.where(mask_t, qt, zero_t))
        weights = jnp.exp(scores - lse_ref[0, head:head + 1, :])
        back = nn(v, jnp.where(mask_t, dot, zero_t))
        delta = jnp.sum(product[span], axis=0, keepdims=True)
        score_grad = (weights * (back - delta)).astype(LOW)
        dqt.append(nn(kt[span], score_grad) * shrink)
        dk_one = nn(score_grad, jnp.where(mask, q, jnp.zeros_like(q)))
        dv_one = nn(weights.astype(LOW), jnp.where(mask, do, jnp.zeros_like(do)))
        dk = dk_one if dk is None else dk + dk_one
        dv = dv_one if dv is None else dv + dv_one
    dqt = jnp.concatenate(dqt, axis=0).astype(LOW)
    dk, dv = dk.astype(LOW), dv.astype(LOW)
    part_ref[...] = (tn(dqt, wq) + nn(dk, wk) + nn(dv, wv)).astype(LOW)
    pieces = (nn(dqt, xn), tn(dk, xn), tn(dv, xn), nn(ot, x1g))

    @pl.when(step == 0)
    def _():
        for part, piece in enumerate(pieces):
            grad_ref[pl.ds(part * rows, rows), :] = piece

    @pl.when(step > 0)
    def _():
        for part, piece in enumerate(pieces):
            grad_ref[pl.ds(part * rows, rows), :] += piece

    @pl.when(step == pl.num_programs(0) - 1)
    def _():
        low = grad_ref[...].astype(LOW)
        total = padded_ref.shape[0]
        cut = total // 4
        for part in range(4):
            row = lax.broadcasted_iota(jnp.int32, (cut, low.shape[0]), 0) + part * cut
            pick = one_hot(row == src_ref[...])
            padded_ref[pl.ds(part * cut, cut), :] = nn(pick, low).astype(LOW)


def attention_backward(x1_grad, saved, src_row, padded_rows):
    w, xn, q, qt, k, kt, v, lse, ot = saved
    tokens, width = x1_grad.shape
    images = tokens // PATCH
    rows = q.shape[1]
    flat_spec, turned_spec, wide_spec = (
        lead((PATCH, rows)), lead((1, rows, PATCH)), lead((PATCH, width))
    )
    return pl.pallas_call(
        attention_rear,
        grid=(images,),
        in_specs=[
            wide_spec, whole(w.shape), wide_spec, flat_spec, turned_spec, flat_spec, turned_spec,
            flat_spec, lead((1, 8, PATCH)), turned_spec, whole(src_row.shape),
        ],
        out_specs=[wide_spec, whole((padded_rows, width))],
        out_shape=[
            jax.ShapeDtypeStruct((tokens, width), LOW),
            jax.ShapeDtypeStruct((padded_rows, width), LOW),
        ],
        scratch_shapes=[pltpu.VMEM(w.shape, FULL)],
        compiler_params=params(),
        name="attention_backward",
    )(x1_grad, *saved, src_row)


def dispatch_plain(rows_ref, col_ref, out_ref, sum_ref):
    place_rows(rows_ref[...], col_ref, out_ref, sum_ref)


def dispatch_normed(rows_ref, norm_ref, col_ref, out_ref, sum_ref):
    normal, _ = normalise(rows_ref[...].astype(FULL))
    low = (normal * norm_ref[2:3, :] + norm_ref[3:4, :]).astype(LOW)
    place_rows(low, col_ref, out_ref, sum_ref)


def place_rows(rows, col_ref, out_ref, sum_ref):
    step = pl.program_id(0)
    shape = (out_ref.shape[0], rows.shape[0])
    slots = lax.broadcasted_iota(jnp.int32, shape, 0)
    col = col_ref[0]
    pick = one_hot((slots == col[0:1, :]) | (slots == col[1:2, :]))
    part = nn(pick, rows)

    @pl.when(step == 0)
    def _():
        sum_ref[...] = part

    @pl.when(step > 0)
    def _():
        sum_ref[...] += part

    @pl.when(step == pl.num_programs(0) - 1)
    def _():
        out_ref[...] = sum_ref[...].astype(LOW)


def dispatch(rows, norm_params, col_rows, slots):
    width = rows.shape[1]
    wide_spec = lead((PATCH, width))
    operands, specs, kernel = [rows], [wide_spec], dispatch_plain
    if norm_params is not None:
        operands, specs, kernel = (
            [rows, norm_params], [wide_spec, whole(norm_params.shape)], dispatch_normed
        )
    return pl.pallas_call(
        kernel,
        grid=(rows.shape[0] // PATCH,),
        in_specs=specs + [lead((1,) + col_rows.shape[1:])],
        out_specs=whole((slots, width)),
        out_shape=jax.ShapeDtypeStruct((slots, width), LOW),
        scratch_shapes=[pltpu.VMEM((slots, width), FULL)],
        compiler_params=params(),
        name="dispatch_rows",
    )(*operands, col_rows)


def picked_rows(col_ref, held_ref):
    tokens = col_ref.shape[0]
    slots, width = held_ref.shape
    cut = slots // 4
    total = jnp.zeros((tokens, width), FULL)
    for part in range(4):
        lanes = lax.broadcasted_iota(jnp.int32, (tokens, cut), 1) + part * cut
        pick = one_hot((lanes == col_ref[:, 0:1]) | (lanes == col_ref[:, 1:2]))
        total = total + nn(pick, held_ref[pl.ds(part * cut, cut), :])
    return total


def combine_front(col_ref, held_ref, x1_ref, out_ref):
    mix = picked_rows(col_ref, held_ref)
    out_ref[...] = (x1_ref[...].astype(FULL) + mix).astype(LOW)


def combine_rear(col_ref, held_ref, x1_ref, g_ref, norm_ref, out_ref, sums_ref):
    step = pl.program_id(0)
    upstream = picked_rows(col_ref, held_ref)
    normal, scale = normalise(x1_ref[...].astype(FULL))
    back, gain_sum, shift_sum = norm_back(normal, scale, norm_ref[2:3, :], upstream)
    out_ref[...] = (g_ref[...].astype(FULL) + back).astype(LOW)

    @pl.when(step == 0)
    def _():
        sums_ref[...] = jnp.zeros_like(sums_ref)

    sums_ref[0:1, :] += gain_sum
    sums_ref[1:2, :] += shift_sum


def combine_forward(col, held, x1):
    tokens, width = x1.shape
    wide_spec = lead((PATCH, width))
    return pl.pallas_call(
        combine_front,
        grid=(tokens // PATCH,),
        in_specs=[lead((PATCH, 2)), whole(held.shape), wide_spec],
        out_specs=wide_spec,
        out_shape=jax.ShapeDtypeStruct((tokens, width), LOW),
        compiler_params=params(),
        name="combine_forward",
    )(col, held, x1)


def combine_backward(col, held, x1, cotangent, norm_params):
    tokens, width = x1.shape
    wide_spec = lead((PATCH, width))
    return pl.pallas_call(
        combine_rear,
        grid=(tokens // PATCH,),
        in_specs=[
            lead((PATCH, 2)), whole(held.shape), wide_spec, wide_spec, whole(norm_params.shape)
        ],
        out_specs=[wide_spec, whole((8, width))],
        out_shape=[
            jax.ShapeDtypeStruct((tokens, width), LOW), jax.ShapeDtypeStruct((8, width), FULL)
        ],
        compiler_params=params(),
        name="combine_backward",
    )(col, held, x1, cotangent, norm_params)


def expert_kernel(
    rows_ref, g_ref, up_ref, down_ref, router_ref, own_ref, count_ref,
    back_ref, out_ref, upg_ref, downg_ref, router_grad_ref,
    out_sum, back_sum, og_ref, gate_ref, probs_ref,
):
    step = pl.program_id(0)
    rows = rows_ref[...]

    @pl.when(step == 0)
    def _():
        logits = nt(rows, router_ref[...]) + count_ref[...]
        top = jnp.max(logits, axis=-1, keepdims=True)
        weights = jnp.exp(logits - top)
        probs = weights / jnp.sum(weights, axis=-1, keepdims=True)
        gate = jnp.sum(probs * own_ref[...], axis=-1, keepdims=True)
        probs_ref[...] = probs
        gate_ref[...] = gate
        og_ref[...] = (gate * g_ref[...].astype(FULL)).astype(LOW)
        out_sum[...] = jnp.zeros_like(out_sum)
        back_sum[...] = jnp.zeros_like(back_sum)

    og = og_ref[...]
    up, down = up_ref[0], down_ref[0]
    hidden = nn(rows, up)
    slope = (2.0 / jnp.pi) ** 0.5
    square = hidden * hidden
    bend = jnp.tanh(slope * (hidden + 0.044715 * (square * hidden)))
    act = (0.5 * hidden * (1.0 + bend)).astype(LOW)
    out_sum[...] += nn(act, down)
    act_grad = nt(og, down)
    inner = slope * (1.0 + (3.0 * 0.044715) * square)
    curve = 0.5 * (1.0 + bend) + 0.5 * hidden * (1.0 - bend * bend) * inner
    hidden_grad = (curve * act_grad).astype(LOW)
    back_sum[...] += nt(hidden_grad, up)
    upg_ref[0] = tn(rows, hidden_grad).astype(LOW)
    downg_ref[0] = tn(act, og).astype(LOW)

    @pl.when(step == pl.num_programs(0) - 1)
    def _():
        out = out_sum[...].astype(LOW).astype(FULL)
        gate, probs = gate_ref[...], probs_ref[...]
        out_ref[...] = (gate * out).astype(LOW)
        gate_grad = jnp.sum(g_ref[...].astype(FULL) * out, axis=-1, keepdims=True)
        logit_grad = (gate_grad * (probs * (own_ref[...] - gate))).astype(LOW)
        back = back_sum[...].astype(LOW).astype(FULL) + nn(logit_grad, router_ref[...])
        back_ref[...] = back.astype(LOW)
        router_grad_ref[...] = tn(logit_grad, rows)


def experts_both_ways(rows, g_rows, up, down, router_low, own):
    slots, width = rows.shape
    parts, _, units = up.shape
    experts = router_low.shape[0]
    lanes = 128
    router_wide = jnp.zeros((lanes, width), LOW).at[:experts].set(router_low)
    lane = jnp.arange(lanes, dtype=jnp.int32)[None, :]
    own_row = jnp.where(lane == own, 1.0, 0.0).astype(FULL)
    closed = jnp.where(lane < experts, 0.0, -1e30).astype(FULL)
    wide_spec = whole((slots, width))
    return pl.pallas_call(
        expert_kernel,
        grid=(parts,),
        in_specs=[
            wide_spec, wide_spec, lead((1, width, units)), lead((1, units, width)),
            whole((lanes, width)), whole((1, lanes)), whole((1, lanes)),
        ],
        out_specs=[
            wide_spec, wide_spec, lead((1, width, units)), lead((1, units, width)),
            whole((lanes, width)),
        ],
        out_shape=[
            jax.ShapeDtypeStruct((slots, width), LOW),
            jax.ShapeDtypeStruct((slots, width), LOW),
            jax.ShapeDtypeStruct(up.shape, LOW),
            jax.ShapeDtypeStruct(down.shape, LOW),
            jax.ShapeDtypeStruct((lanes, width), FULL),
        ],
        scratch_shapes=[
            pltpu.VMEM((slots, width), FULL), pltpu.VMEM((slots, width), FULL),
            pltpu.VMEM((slots, width), LOW), pltpu.VMEM((slots, 1), FULL),
            pltpu.VMEM((slots, lanes), FULL),
        ],
        compiler_params=params(),
        name="experts_both_ways",
    )(rows, g_rows, up, down, router_wide, own_row, closed)


def partners():
    me = lax.axis_index("head")
    near = me + 1 - 2 * lax.rem(me, 2)
    far = lax.rem(me + 2, 4)
    corner = near + 2 - 4 * (near // 2)
    return me, near, far, corner


def greet(near, far):
    barrier = pltpu.get_barrier_semaphore()
    for other in (near, far):
        pl.semaphore_signal(barrier, inc=1, device_id={"head": other}, device_id_type=MESH)
    pl.semaphore_wait(barrier, 2)


def gather_kernel(cuts, x_ref, out_ref, local_sem, send_sem, recv_sem):
    me, near, far, corner = partners()
    greet(near, far)
    size = x_ref.shape[0] // cuts

    def remote(src, dst, lane, index, other):
        return pltpu.make_async_remote_copy(
            src_ref=src, dst_ref=dst, send_sem=send_sem.at[lane, index],
            recv_sem=recv_sem.at[lane, index], device_id={"head": other}, device_id_type=MESH,
        )

    local = pltpu.make_async_copy(x_ref, out_ref.at[me], local_sem)
    local.start()
    across, beside, onward = [], [], []
    for cut in range(cuts):
        span = pl.ds(cut * size, size)
        across.append(remote(x_ref.at[span], out_ref.at[me, span], 0, cut, far))
        across[-1].start()
    for cut in range(cuts):
        span = pl.ds(cut * size, size)
        beside.append(remote(x_ref.at[span], out_ref.at[me, span], 1, cut, near))
        beside[-1].start()
    for cut in range(cuts):
        span = pl.ds(cut * size, size)
        across[cut].wait_recv()
        onward.append(remote(out_ref.at[far, span], out_ref.at[far, span], 2, cut, near))
        onward[-1].start()
    for cut in range(cuts):
        across[cut].wait_send()
        beside[cut].wait()
        onward[cut].wait()
    local.wait()


def head_gather(x, collective_id, cuts=4):
    return pl.pallas_call(
        functools.partial(gather_kernel, cuts),
        in_specs=[pl.BlockSpec(memory_space=pl.ANY)],
        out_specs=pl.BlockSpec(memory_space=pl.ANY),
        out_shape=jax.ShapeDtypeStruct((4,) + x.shape, x.dtype),
        scratch_shapes=[
            pltpu.SemaphoreType.DMA, pltpu.SemaphoreType.DMA((3, cuts)),
            pltpu.SemaphoreType.DMA((3, cuts)),
        ],
        compiler_params=params(collective_id=collective_id, has_side_effects=True),
        name="head_gather",
    )(x)


def scatter_kernel(
    cuts, x_ref, out_ref, mine, passed, corner_in, near_in, far_in,
    local_sem, send_sem, recv_sem,
):
    me, near, far, corner = partners()
    greet(near, far)
    size = out_ref.shape[0] // cuts

    def remote(src, dst, lane, index, other):
        return pltpu.make_async_remote_copy(
            src_ref=src, dst_ref=dst, send_sem=send_sem.at[lane, index],
            recv_sem=recv_sem.at[lane, index], device_id={"head": other}, device_id_type=MESH,
        )

    locals_, first, second, third = [], [], [], []
    for cut in range(cuts):
        span = pl.ds(cut * size, size)
        first.append(remote(x_ref.at[corner, span], corner_in.at[span], 0, cut, near))
        first[-1].start()
        locals_.append(
            pltpu.make_async_copy(x_ref.at[far, span], passed.at[span], local_sem.at[0, cut])
        )
        locals_[-1].start()
    own = []
    for cut in range(cuts):
        span = pl.ds(cut * size, size)
        second.append(remote(x_ref.at[near, span], near_in.at[span], 1, cut, near))
        second[-1].start()
        own.append(pltpu.make_async_copy(x_ref.at[me, span], mine.at[span], local_sem.at[1, cut]))
        own[-1].start()
    for cut in range(cuts):
        span = pl.ds(cut * size, size)
        first[cut].wait_recv()
        locals_[cut].wait()
        both = passed[span, :].astype(FULL) + corner_in[span, :].astype(FULL)
        passed[span, :] = both.astype(LOW)
        third.append(remote(passed.at[span], far_in.at[span], 2, cut, far))
        third[-1].start()
    for cut in range(cuts):
        span = pl.ds(cut * size, size)
        second[cut].wait_recv()
        own[cut].wait()
        third[cut].wait_recv()
        total = mine[span, :].astype(FULL) + near_in[span, :].astype(FULL)
        out_ref[span, :] = (total + far_in[span, :].astype(FULL)).astype(LOW)
    for cut in range(cuts):
        first[cut].wait_send()
        second[cut].wait_send()
        third[cut].wait_send()


def head_scatter(x, collective_id, cuts=4):
    shape = x.shape[1:]
    return pl.pallas_call(
        functools.partial(scatter_kernel, cuts),
        in_specs=[pl.BlockSpec(memory_space=pl.ANY)],
        out_specs=pl.BlockSpec(memory_space=pltpu.VMEM),
        out_shape=jax.ShapeDtypeStruct(shape, LOW),
        scratch_shapes=[pltpu.VMEM(shape, LOW)] * 5
        + [
            pltpu.SemaphoreType.DMA((2, cuts)), pltpu.SemaphoreType.DMA((3, cuts)),
            pltpu.SemaphoreType.DMA((3, cuts)),
        ],
        compiler_params=params(collective_id=collective_id, has_side_effects=True),
        name="head_scatter",
    )(x)


def first_norm_kernel(x_ref, n1g_ref, x1g_ref, norm_ref, out_ref, sums_ref):
    normal, scale = normalise(x_ref[...].astype(FULL))
    upstream = n1g_ref[...].astype(FULL)
    back, gain_sum, shift_sum = norm_back(normal, scale, norm_ref[0:1, :], upstream)
    out_ref[...] = (x1g_ref[...].astype(FULL) + back).astype(LOW)
    sums_ref[...] = jnp.zeros_like(sums_ref)
    sums_ref[0:1, :] = gain_sum
    sums_ref[1:2, :] = shift_sum


def first_norm_backward(x, normed_grad, x1_grad, norm_params):
    rows, width = x.shape
    return pl.pallas_call(
        first_norm_kernel,
        out_shape=[
            jax.ShapeDtypeStruct((rows, width), LOW), jax.ShapeDtypeStruct((8, width), FULL)
        ],
        compiler_params=params(),
        name="first_norm_backward",
    )(x, normed_grad, x1_grad, norm_params)


def body(
    patches, cotangent, expert_ids, slot_pos, owners,
    tile_master, tile_first, tile_second,
    expert_up, up_first, up_second,
    expert_down, down_first, down_second,
    router, router_first, router_second,
    norm_params, norm_first, norm_second,
):
    tok_rows, width = patches.shape
    experts = router.shape[0]
    capacity = tok_rows // experts
    dp_count = lax.axis_size("dp")
    head_count = lax.axis_size("head")
    me_head = lax.axis_index("head")
    me_dp = lax.axis_index("dp")
    images = tok_rows // PATCH
    share = capacity // head_count
    own_slots = experts * share
    own_rows = tok_rows // head_count
    slot_count = tile_master.shape[0]

    gathered = lax.all_gather(tile_master.astype(LOW), "dp", axis=0, tiled=True)
    owner_row = owners[0]
    tile_count = owner_row.shape[0]
    order_index = jnp.arange(tile_count, dtype=jnp.int32)
    same_owner = owner_row[:, None] == owner_row[None, :]
    earlier = order_index[None, :] < order_index[:, None]
    tile_rank = jnp.sum(jnp.where(same_owner & earlier, 1, 0), axis=1).astype(jnp.int32)
    tile_place = owner_row * slot_count + tile_rank
    src = (tile_place[:, None] * TILE + jnp.arange(TILE, dtype=jnp.int32)[None, :]).reshape(-1)
    held = gathered.reshape(dp_count * slot_count * TILE, width)

    up_low = expert_up[0].astype(LOW)
    down_low = expert_down[0].astype(LOW)
    up_all = lax.all_gather(up_low, "head", axis=0)
    down_all = lax.all_gather(down_low, "head", axis=0)

    kept = slot_pos < capacity
    col = (slot_pos // share) * own_slots + expert_ids * share + lax.rem(slot_pos, share)
    col = jnp.where(kept, col, tok_rows)
    col_rows = (col - me_head * own_slots).reshape(images, PATCH, 2).transpose(0, 2, 1)

    def to_experts(rows):
        rows = rows.reshape(experts, share, width)
        return lax.all_to_all(rows, "dp", 0, 0, tiled=True).reshape(own_slots, width)

    g_rows = to_experts(dispatch(cotangent, None, col_rows, own_slots))

    *saved, partial = attention_forward(patches, norm_params, held, src[:, None])
    own_patches = lax.dynamic_slice_in_dim(patches, me_head * own_rows, own_rows, 0)
    attended = head_scatter(partial.reshape(head_count, own_rows, width), 0)
    x1_own = (own_patches.astype(FULL) + attended.astype(FULL)).astype(LOW)
    x1 = head_gather(x1_own, 1).reshape(tok_rows, width)

    rows = to_experts(dispatch(x1, norm_params, col_rows, own_slots))
    back, out, up_part, down_part, router_part = experts_both_ways(
        rows, g_rows, up_all, down_all, router.astype(LOW), me_dp
    )
    back_all = head_gather(to_experts(back), 2).reshape(tok_rows, width)
    x1_grad, second_sums = combine_backward(col, back_all, x1, cotangent, norm_params)

    partial_grad, padded = attention_backward(
        x1_grad, saved, src[None, :], dp_count * slot_count * TILE
    )
    normed_grad = head_scatter(partial_grad.reshape(head_count, own_rows, width), 3)
    own_grad = lax.dynamic_slice_in_dim(x1_grad, me_head * own_rows, own_rows, 0)
    input_own, first_sums = first_norm_backward(own_patches, normed_grad, own_grad, norm_params)
    input_grad = head_gather(input_own, 4).reshape(tok_rows, width).astype(FULL)

    out_all = lax.all_gather(to_experts(out), "head", axis=0, tiled=True)
    block_out = combine_forward(col, out_all, x1)

    up_grad = lax.psum_scatter(up_part, "head", scatter_dimension=0).astype(FULL)
    down_grad = lax.psum_scatter(down_part, "head", scatter_dimension=0).astype(FULL)
    owned_grad = lax.psum_scatter(
        padded.reshape(dp_count * slot_count, TILE, width), "dp", scatter_dimension=0, tiled=True
    ).astype(FULL)

    small = jnp.concatenate(
        [router_part[:experts], first_sums[:2], second_sums[:2] * (1.0 / head_count)], axis=0
    )
    small = lax.psum(small, ("dp", "head"))
    router_total, norm_total = small[:experts], small[experts:]

    tile_new, tile_first_new, tile_second_new = adam_update(
        tile_master, tile_first, tile_second, owned_grad, rate_attention, decay_factor
    )
    up_new, up_first_new, up_second_new = adam_update(
        expert_up, up_first, up_second, up_grad[None], rate_up, decay_factor
    )
    down_new, down_first_new, down_second_new = adam_update(
        expert_down, down_first, down_second, down_grad[None], rate_down, decay_factor
    )
    router_new, router_first_new, router_second_new = adam_update(
        router, router_first, router_second, router_total, rate_router, decay_factor
    )
    norm_new, norm_first_new, norm_second_all = adam_update(
        norm_params, norm_first, norm_second, norm_total, rate_norm, 0.0
    )
    return (
        block_out,
        input_grad,
        tile_new,
        tile_first_new,
        tile_second_new,
        tile_new.astype(LOW),
        up_new,
        up_first_new,
        up_second_new,
        up_new.astype(LOW),
        down_new,
        down_first_new,
        down_second_new,
        down_new.astype(LOW),
        router_new,
        router_first_new,
        router_second_new,
        norm_new,
        norm_first_new,
        norm_second_all[:2],
        norm_second_all[2:],
    )


def solution(mesh):
    row = P("dp", None)
    tiles = P(("dp", "head"), None, None)
    up = P("dp", None, "head")
    down = P("dp", "head", None)
    in_specs = (
        row, row, row, row, P("head", None), tiles, tiles, tiles,
        up, up, up, down, down, down, P(), P(), P(), P(), P(), P(),
    )
    out_specs = (
        row, row, tiles, tiles, tiles, tiles, up, up, up, up, down, down, down, down,
        P(), P(), P(), P(), P(), P(), P(),
    )
    return jax.shard_map(body, mesh=mesh, in_specs=in_specs, out_specs=out_specs, check_vma=False)
```

```python
import functools

import jax
import jax.numpy as jnp
from jax import lax
from jax.experimental import pallas as pl
from jax.experimental.pallas import tpu as pltpu
from jax.sharding import PartitionSpec as P

HD = 64
PATCH = 576
TILE = 8
STEP = 10

eps_norm = 1e-06
beta_one = 0.9
beta_two = 0.999
adam_eps = 1e-08
rate_attention = 0.12
rate_up = 0.08
rate_down = 0.3
rate_router = 0.05
rate_norm = 0.4
decay_factor = 0.1

LOW = jnp.bfloat16
FULL = jnp.float32
MESH = pl.DeviceIdType.MESH
VMEM_BYTES = 56 * 1024 * 1024


def adam_update(weight, moment_one, moment_two, gradient, step_rate, weight_decay):
    moment_one = beta_one * moment_one + (1.0 - beta_one) * gradient
    moment_two = beta_two * moment_two + (1.0 - beta_two) * gradient * gradient
    fixed_one = moment_one / (1.0 - beta_one**STEP)
    fixed_two = moment_two / (1.0 - beta_two**STEP)
    weight = weight - step_rate * (
        fixed_one / (jnp.sqrt(fixed_two) + adam_eps) + weight_decay * weight
    )
    return (weight, moment_one, moment_two)


def nn(left, right):
    return lax.dot_general(left, right, (((1,), (0,)), ((), ())), preferred_element_type=FULL)


def nt(left, right):
    return lax.dot_general(left, right, (((1,), (1,)), ((), ())), preferred_element_type=FULL)


def tn(left, right):
    return lax.dot_general(left, right, (((0,), (0,)), ((), ())), preferred_element_type=FULL)


def params(**more):
    return pltpu.CompilerParams(vmem_limit_bytes=VMEM_BYTES, **more)


def whole(shape):
    return pl.BlockSpec(shape, lambda *_: (0,) * len(shape))


def lead(shape):
    return pl.BlockSpec(shape, lambda i: (i,) + (0,) * (len(shape) - 1))


def normalise(values):
    average = jnp.mean(values, axis=-1, keepdims=True)
    centred = values - average
    variance = jnp.mean(centred * centred, axis=-1, keepdims=True)
    scale = lax.rsqrt(variance + eps_norm)
    return centred * scale, scale


def norm_back(normal, scale, gain, upstream):
    inner = upstream * gain
    mean_inner = jnp.mean(inner, axis=-1, keepdims=True)
    mean_cross = jnp.mean(inner * normal, axis=-1, keepdims=True)
    result = scale * (inner - mean_inner - normal * mean_cross)
    gain_sum = jnp.sum(upstream * normal, axis=0, keepdims=True)
    shift_sum = jnp.sum(upstream, axis=0, keepdims=True)
    return result, gain_sum, shift_sum


def one_hot(condition):
    return jnp.where(condition, 1.0, 0.0).astype(LOW)


def remote(src, dst, sends, recvs, index, axis, other):
    return pltpu.make_async_remote_copy(
        src_ref=src, dst_ref=dst, send_sem=sends.at[index], recv_sem=recvs.at[index],
        device_id={axis: other}, device_id_type=MESH,
    )


def greet(*others):
    barrier = pltpu.get_barrier_semaphore()
    for axis, other in others:
        pl.semaphore_signal(barrier, inc=1, device_id={axis: other}, device_id_type=MESH)
    pl.semaphore_wait(barrier, len(others))


def partners():
    me = lax.axis_index("head")
    near = me + 1 - 2 * lax.rem(me, 2)
    far = lax.rem(me + 2, 4)
    corner = lax.rem(near + 2, 4)
    return me, near, far, corner


class LineGather:
    def __init__(self, held, up_send, up_recv, down_send, down_recv, pair_send, pair_recv):
        self.held = held
        self.length = held.shape[0] // 2
        self.sems = ((up_send, up_recv), (down_send, down_recv), (pair_send, pair_recv))
        me = lax.axis_index("dp")
        self.place, self.side = me // 2, lax.rem(me, 2)
        self.above = lax.rem(self.place + 1, self.length) * 2 + self.side
        self.below = lax.rem(self.place + self.length - 1, self.length) * 2 + self.side
        self.other = self.place * 2 + 1 - self.side

    def neighbours(self):
        return ("dp", self.above), ("dp", self.below), ("dp", self.other)

    def copy(self, way, origin, side=None):
        index = origin * 2 + (self.side if side is None else side)
        target = (self.above, self.below, self.other)[way]
        block = self.held.at[index]
        return remote(block, block, *self.sems[way], origin, "dp", target)

    def pass_on(self, origin, up, down):
        @pl.when(up & (self.place < self.length - 1))
        def _():
            self.copy(0, origin).start()

        @pl.when(down & (self.place > 0))
        def _():
            self.copy(1, origin).start()

        self.copy(2, origin).start()

    def start(self):
        self.pass_on(self.place, True, True)

    def step(self, k):
        low, high = self.place - k, self.place + k

        @pl.when(low >= 0)
        def _():
            self.copy(0, low).wait_recv()
            self.pass_on(low, True, False)

        @pl.when(high < self.length)
        def _():
            self.copy(1, high).wait_recv()
            self.pass_on(high, False, True)

    def finish(self):
        @pl.loop(0, self.length)
        def _(origin):
            self.copy(2, origin).wait_recv()
            self.copy(2, origin).wait_send()

            @pl.when((origin <= self.place) & (self.place < self.length - 1))
            def _():
                self.copy(0, origin).wait_send()

            @pl.when((origin >= self.place) & (self.place > 0))
            def _():
                self.copy(1, origin).wait_send()


class ImageSum:
    def __init__(self, stage, corner_in, near_in, passed, mine, far_in, sends, recvs):
        self.stage, self.corner_in, self.near_in = stage, corner_in, near_in
        self.passed, self.mine, self.far_in = passed, mine, far_in
        self.sends, self.recvs = sends, recvs
        self.me, self.near, self.far, self.corner = partners()
        self.core = lax.rem(self.me, 2)

    def image(self, turn):
        base = self.me - self.core
        other = lax.rem(base + 2, 4)
        return jnp.where(turn < 2, other, base - 2) + turn

    def to_corner(self):
        return remote(
            self.stage.at[0], self.corner_in, self.sends, self.recvs, 0, "head", self.near
        )

    def to_near(self):
        return remote(
            self.stage.at[1], self.near_in, self.sends, self.recvs, 1, "head", self.near
        )

    def to_far(self):
        return remote(self.passed, self.far_in, self.sends, self.recvs, 2, "head", self.far)

    def give(self, turn, part):
        theirs = lax.rem(turn, 2) != self.core

        @pl.when((turn < 2) & theirs)
        def _():
            self.stage[0] = part.astype(LOW)
            self.to_corner().start()

        @pl.when((turn >= 2) & theirs)
        def _():
            self.stage[1] = part.astype(LOW)
            self.to_near().start()

        @pl.when((turn < 2) & ~theirs)
        def _():
            self.to_corner().wait_recv()
            self.passed[...] = (part + self.corner_in[...].astype(FULL)).astype(LOW)
            self.to_far().start()

        @pl.when((turn >= 2) & ~theirs)
        def _():
            self.mine[...] = part

    def result(self):
        self.to_near().wait_recv()
        self.to_far().wait_recv()
        return self.mine[...] + self.near_in[...].astype(FULL) + self.far_in[...].astype(FULL)

    def finish(self):
        self.to_corner().wait_send()
        self.to_near().wait_send()
        self.to_far().wait_send()


def image_sum_scratch(width):
    block = pltpu.VMEM((PATCH, width), LOW)
    return [
        pltpu.VMEM((2, PATCH, width), LOW), block, block, block,
        pltpu.VMEM((PATCH, width), FULL), block,
        pltpu.SemaphoreType.DMA((3,)), pltpu.SemaphoreType.DMA((3,)),
    ]


GATHER_CUTS = 4


class ImageGather:
    def __init__(self, held, sends, recvs):
        self.held, self.sends, self.recvs = held, sends, recvs
        self.me, self.near, self.far, self.corner = partners()
        self.size = held.shape[1] // GATHER_CUTS

    def piece(self, image, cut, lane, other):
        span = pl.ds(cut * self.size, self.size)
        block = self.held.at[image, span]
        return remote(block, block, self.sends, self.recvs, lane * GATHER_CUTS + cut, "head", other)

    def start(self):
        for cut in range(GATHER_CUTS):
            self.piece(self.me, cut, 0, self.far).start()
        for cut in range(GATHER_CUTS):
            self.piece(self.me, cut, 1, self.near).start()

    def wait_near(self):
        for cut in range(GATHER_CUTS):
            self.piece(self.me, cut, 1, self.near).wait_recv()

    def wait_far(self):
        for cut in range(GATHER_CUTS):
            self.piece(self.me, cut, 0, self.far).wait_recv()
            self.piece(self.far, cut, 2, self.near).start()

    def wait_corner(self):
        for cut in range(GATHER_CUTS):
            self.piece(self.far, cut, 2, self.near).wait_recv()

    def finish(self):
        for cut in range(GATHER_CUTS):
            self.piece(self.me, cut, 0, self.far).wait_send()
            self.piece(self.me, cut, 1, self.near).wait_send()
            self.piece(self.far, cut, 2, self.near).wait_send()


def image_gather_sems():
    return [pltpu.SemaphoreType.DMA((3 * GATHER_CUTS,)), pltpu.SemaphoreType.DMA((3 * GATHER_CUTS,))]


ANYWHERE = pl.BlockSpec(memory_space=pl.ANY)
INSIDE = pl.BlockSpec(memory_space=pltpu.VMEM)


def prepare_kernel(
    tile_ref, x_ref, g_ref, norm_ref, src_ref, col_ref,
    w_ref, xn_ref, sent_ref,
    held, sent_sum, *sems,
):
    images = x_ref.shape[0]
    gather = LineGather(held, *sems)
    greet(*gather.neighbours())
    me = lax.axis_index("dp")
    held[me] = tile_ref[...].astype(LOW)
    gather.start()

    def image_step(image):
        normal, _ = normalise(x_ref[image].astype(FULL))
        xn_ref[image] = (normal * norm_ref[0:1, :] + norm_ref[1:2, :]).astype(LOW)
        shape = (sent_ref.shape[0], PATCH)
        slots = lax.broadcasted_iota(jnp.int32, shape, 0)
        col = col_ref[image]
        pick = one_hot((slots == col[0:1, :]) | (slots == col[1:2, :]))
        sent_sum[...] += nn(pick, g_ref[image])

    sent_sum[...] = jnp.zeros_like(sent_sum)
    steps = gather.length - 1

    @pl.loop(0, max(steps, images))
    def _(turn):
        @pl.when(turn < images)
        def _():
            image_step(turn)

        @pl.when(turn < steps)
        def _():
            gather.step(turn + 1)

    sent_ref[...] = sent_sum[...].astype(LOW)
    gather.finish()
    rows = w_ref.shape[0] // 4
    blocks, depth, width = held.shape
    for part in range(4):
        block = pl.ds(part * rows, rows)
        lanes = lax.broadcasted_iota(jnp.int32, (rows, blocks * depth), 1)
        pick = one_hot(lanes == src_ref[block, :])
        w_ref[block, :] = nn(pick, held[...].reshape(blocks * depth, width)).astype(LOW)


def prepare(tiles, patches, cotangent, norm_params, src_col, col_rows, slots, dp_count):
    images, _, width = patches.shape
    line = dp_count // 2
    return pl.pallas_call(
        prepare_kernel,
        in_specs=[INSIDE] * 6,
        out_specs=[INSIDE] * 3,
        out_shape=[
            jax.ShapeDtypeStruct((src_col.shape[0], width), LOW),
            jax.ShapeDtypeStruct(patches.shape, LOW),
            jax.ShapeDtypeStruct((slots, width), LOW),
        ],
        scratch_shapes=[
            pltpu.VMEM((dp_count,) + tiles.shape, LOW), pltpu.VMEM((slots, width), FULL),
        ] + [pltpu.SemaphoreType.DMA((line,))] * 6,
        compiler_params=params(collective_id=0, has_side_effects=True),
        name="prepare",
    )(tiles, patches, cotangent, norm_params, src_col, col_rows)


def head_mask(shape, axis, head):
    return lax.broadcasted_iota(jnp.int32, shape, axis) // HD == head


def forward_kernel(
    xn_ref, w_ref, x_ref, norm_ref, col_ref,
    lse_ref, sent_ref, q_out, qt_out, k_out, kt_out, v_out, ot_out, x1_out,
    q_ref, qt_ref, k_ref, kt_ref, v_ref, ot_ref, x1_ref, own_ref, sent_sum,
    save_sems, own_sem, *exchange,
):
    images = xn_ref.shape[0]
    rows = w_ref.shape[0] // 4
    heads = rows // HD
    total_of = ImageSum(*exchange[:8])
    spread = ImageGather(x1_ref, *exchange[8:])
    me, near, far, corner = partners()
    greet(("head", near), ("head", far))
    own = pltpu.make_async_copy(x_ref.at[me], own_ref, own_sem)
    own.start()
    kept = ((q_ref, q_out), (qt_ref, qt_out), (k_ref, k_out), (kt_ref, kt_out), (v_ref, v_out), (ot_ref, ot_out))
    shrink = HD ** (-0.5)

    def save(image):
        return [
            pltpu.make_async_copy(ref.at[image], out.at[image], save_sems.at[index, image])
            for index, (ref, out) in enumerate(kept)
        ]

    @pl.loop(0, images)
    def _(turn):
        image = total_of.image(turn)
        xn = xn_ref[image]
        wq, wk, wv, wo = (w_ref[pl.ds(part * rows, rows), :] for part in range(4))
        q_ref[image] = (nt(xn, wq) * shrink).astype(LOW)
        qt = (nt(wq, xn) * shrink).astype(LOW)
        qt_ref[image] = qt
        k = nt(xn, wk).astype(LOW)
        k_ref[image] = k
        kt_ref[image] = nt(wk, xn).astype(LOW)
        v_ref[image] = nt(xn, wv).astype(LOW)
        vt = nt(wv, xn).astype(LOW)
        mixed = []
        for head in range(heads):
            span = slice(head * HD, (head + 1) * HD)
            only = jnp.where(head_mask(qt.shape, 0, head), qt, jnp.zeros_like(qt))
            scores = nn(k, only)
            top = jnp.max(scores, axis=0, keepdims=True)
            weights = jnp.exp(scores - top)
            total = jnp.sum(weights, axis=0, keepdims=True)
            mixed.append(nn(vt[span], weights.astype(LOW)) / total)
            lse_ref[image, head:head + 1, :] = top + jnp.log(total)
        ot = jnp.concatenate(mixed, axis=0).astype(LOW)
        ot_ref[image] = ot
        total_of.give(turn, tn(ot, wo))
        for copy in save(image):
            copy.start()

    own.wait()
    x1_ref[me] = (own_ref[...].astype(FULL) + total_of.result()).astype(LOW)
    spread.start()
    sent_sum[...] = jnp.zeros_like(sent_sum)

    def place(image):
        normal, _ = normalise(x1_ref[image].astype(FULL))
        low = (normal * norm_ref[2:3, :] + norm_ref[3:4, :]).astype(LOW)
        slots = lax.broadcasted_iota(jnp.int32, (sent_ref.shape[0], PATCH), 0)
        col = col_ref[image]
        pick = one_hot((slots == col[0:1, :]) | (slots == col[1:2, :]))
        sent_sum[...] += nn(pick, low)

    place(me)
    spread.wait_near()
    place(near)
    spread.wait_far()
    place(far)
    spread.wait_corner()
    keep = pltpu.make_async_copy(x1_ref, x1_out, own_sem)
    keep.start()
    place(corner)
    sent_ref[...] = sent_sum[...].astype(LOW)
    spread.finish()
    total_of.finish()
    keep.wait()

    @pl.loop(0, images)
    def _(image):
        for copy in save(image):
            copy.wait()


def attention_forward(xn, w, patches, norm_params, col_rows, slots):
    images, _, width = patches.shape
    rows = w.shape[0] // 4
    flat, turned = (images, PATCH, rows), (images, rows, PATCH)
    saved = [flat, turned, flat, turned, flat, turned, patches.shape]
    return pl.pallas_call(
        forward_kernel,
        in_specs=[INSIDE, INSIDE, ANYWHERE, INSIDE, INSIDE],
        out_specs=[INSIDE, INSIDE] + [ANYWHERE] * 7,
        out_shape=[
            jax.ShapeDtypeStruct((images, 8, PATCH), FULL), jax.ShapeDtypeStruct((slots, width), LOW),
        ] + [jax.ShapeDtypeStruct(shape, LOW) for shape in saved],
        scratch_shapes=[pltpu.VMEM(shape, LOW) for shape in saved]
        + [
            pltpu.VMEM((PATCH, width), LOW), pltpu.VMEM((slots, width), FULL),
            pltpu.SemaphoreType.DMA((6, images)), pltpu.SemaphoreType.DMA,
        ]
        + image_sum_scratch(width) + image_gather_sems(),
        compiler_params=params(collective_id=1, has_side_effects=True),
        name="attention_forward",
    )(xn, w, patches, norm_params, col_rows)


def backward_kernel(
    x1g_ref, w_ref, xn_ref, q_ref, qt_ref, k_ref, kt_ref, v_ref, lse_ref, ot_ref, src_ref,
    x_ref, norm_ref,
    padded_ref, sums_ref, input_out,
    grad_ref, own_ref, input_ref, own_sem, *exchange,
):
    images = x1g_ref.shape[0]
    rows = w_ref.shape[0] // 4
    heads = rows // HD
    total_of = ImageSum(*exchange[:8])
    spread = ImageGather(input_ref, *exchange[8:])
    me, near, far, corner = partners()
    greet(("head", near), ("head", far))
    own = pltpu.make_async_copy(x_ref.at[me], own_ref, own_sem)
    own.start()
    shrink = HD ** (-0.5)
    grad_ref[...] = jnp.zeros_like(grad_ref)

    @pl.loop(0, images)
    def _(turn):
        image = total_of.image(turn)
        wq, wk, wv, wo = (w_ref[pl.ds(part * rows, rows), :] for part in range(4))
        x1g, xn = x1g_ref[image], xn_ref[image]
        q, qt, k, kt = q_ref[image], qt_ref[image], k_ref[image], kt_ref[image]
        v, ot = v_ref[image], ot_ref[image]
        do = nt(x1g, wo).astype(LOW)
        dot = nt(wo, x1g).astype(LOW)
        product = dot.astype(FULL) * ot.astype(FULL)
        dqt, dk, dv = [], None, None
        for head in range(heads):
            span = slice(head * HD, (head + 1) * HD)
            zero_t = jnp.zeros_like(qt)
            mask_t = head_mask(qt.shape, 0, head)
            mask = head_mask(q.shape, 1, head)
            scores = nn(k, jnp.where(mask_t, qt, zero_t))
            weights = jnp.exp(scores - lse_ref[image, head:head + 1, :])
            back = nn(v, jnp.where(mask_t, dot, zero_t))
            delta = jnp.sum(product[span], axis=0, keepdims=True)
            score_grad = (weights * (back - delta)).astype(LOW)
            dqt.append(nn(kt[span], score_grad) * shrink)
            dk_one = nn(score_grad, jnp.where(mask, q, jnp.zeros_like(q)))
            dv_one = nn(weights.astype(LOW), jnp.where(mask, do, jnp.zeros_like(do)))
            dk = dk_one if dk is None else dk + dk_one
            dv = dv_one if dv is None else dv + dv_one
        dqt = jnp.concatenate(dqt, axis=0).astype(LOW)
        dk, dv = dk.astype(LOW), dv.astype(LOW)
        total_of.give(turn, tn(dqt, wq) + nn(dk, wk) + nn(dv, wv))
        pieces = (nn(dqt, xn), tn(dk, xn), tn(dv, xn), nn(ot, x1g))
        for part, piece in enumerate(pieces):
            grad_ref[pl.ds(part * rows, rows), :] += piece

    own.wait()
    normal, scale = normalise(own_ref[...].astype(FULL))
    back, gain_sum, shift_sum = norm_back(normal, scale, norm_ref[0:1, :], total_of.result())
    sums_ref[...] = jnp.zeros_like(sums_ref)
    sums_ref[0:1, :] = gain_sum
    sums_ref[1:2, :] = shift_sum
    input_ref[me] = (x1g_ref[me].astype(FULL) + back).astype(LOW)
    spread.start()
    low = grad_ref[...].astype(LOW)
    cut = padded_ref.shape[0] // 4
    for part in range(4):
        row = lax.broadcasted_iota(jnp.int32, (cut, low.shape[0]), 0) + part * cut
        pick = one_hot(row == src_ref[...])
        padded_ref[pl.ds(part * cut, cut), :] = nn(pick, low).astype(LOW)
    spread.wait_near()
    spread.wait_far()
    spread.wait_corner()
    keep = pltpu.make_async_copy(input_ref, input_out, own_sem)
    keep.start()
    spread.finish()
    total_of.finish()
    keep.wait()


def attention_backward(x1_grad, w, xn, saved, lse, src_row, patches, norm_params, padded_rows):
    q, qt, k, kt, v, ot = saved
    images, _, width = patches.shape
    return pl.pallas_call(
        backward_kernel,
        in_specs=[INSIDE] * 11 + [ANYWHERE, INSIDE],
        out_specs=[INSIDE, INSIDE, ANYWHERE],
        out_shape=[
            jax.ShapeDtypeStruct((padded_rows, width), LOW), jax.ShapeDtypeStruct((8, width), FULL),
            jax.ShapeDtypeStruct(patches.shape, LOW),
        ],
        scratch_shapes=[
            pltpu.VMEM(w.shape, FULL), pltpu.VMEM((PATCH, width), LOW),
            pltpu.VMEM(patches.shape, LOW), pltpu.SemaphoreType.DMA,
        ]
        + image_sum_scratch(width) + image_gather_sems(),
        compiler_params=params(collective_id=2, has_side_effects=True),
        name="attention_backward",
    )(x1_grad, w, xn, q, qt, k, kt, v, lse, ot, src_row, patches, norm_params)


def picked_rows(col_ref, held_ref):
    tokens = col_ref.shape[0]
    slots, width = held_ref.shape
    cut = slots // 4
    total = jnp.zeros((tokens, width), FULL)
    for part in range(4):
        lanes = lax.broadcasted_iota(jnp.int32, (tokens, cut), 1) + part * cut
        pick = one_hot((lanes == col_ref[:, 0:1]) | (lanes == col_ref[:, 1:2]))
        total = total + nn(pick, held_ref[pl.ds(part * cut, cut), :])
    return total


def combine_front(col_ref, held_ref, x1_ref, out_ref):
    mix = picked_rows(col_ref, held_ref)
    out_ref[...] = (x1_ref[...].astype(FULL) + mix).astype(LOW)


def combine_rear(col_ref, held_ref, x1_ref, g_ref, norm_ref, out_ref, sums_ref):
    step = pl.program_id(0)
    upstream = picked_rows(col_ref, held_ref)
    normal, scale = normalise(x1_ref[...].astype(FULL))
    back, gain_sum, shift_sum = norm_back(normal, scale, norm_ref[2:3, :], upstream)
    out_ref[...] = (g_ref[...].astype(FULL) + back).astype(LOW)

    @pl.when(step == 0)
    def _():
        sums_ref[...] = jnp.zeros_like(sums_ref)

    sums_ref[0:1, :] += gain_sum
    sums_ref[1:2, :] += shift_sum


def combine_forward(col, held, x1):
    tokens, width = x1.shape
    wide_spec = lead((PATCH, width))
    return pl.pallas_call(
        combine_front,
        grid=(tokens // PATCH,),
        in_specs=[lead((PATCH, 2)), whole(held.shape), wide_spec],
        out_specs=wide_spec,
        out_shape=jax.ShapeDtypeStruct((tokens, width), LOW),
        compiler_params=params(),
        name="combine_forward",
    )(col, held, x1)


def combine_backward(col, held, x1, cotangent, norm_params):
    tokens, width = x1.shape
    wide_spec = lead((PATCH, width))
    return pl.pallas_call(
        combine_rear,
        grid=(tokens // PATCH,),
        in_specs=[
            lead((PATCH, 2)), whole(held.shape), wide_spec, wide_spec, whole(norm_params.shape)
        ],
        out_specs=[wide_spec, whole((8, width))],
        out_shape=[
            jax.ShapeDtypeStruct((tokens, width), LOW), jax.ShapeDtypeStruct((8, width), FULL)
        ],
        compiler_params=params(),
        name="combine_backward",
    )(col, held, x1, cotangent, norm_params)


def expert_kernel(
    rows_ref, g_ref, up_ref, down_ref, router_ref, own_ref, count_ref,
    back_ref, out_ref, upg_ref, downg_ref, router_grad_ref,
    out_sum, back_sum, og_ref, gate_ref, probs_ref,
):
    step = pl.program_id(0)
    rows = rows_ref[...]

    @pl.when(step == 0)
    def _():
        logits = nt(rows, router_ref[...]) + count_ref[...]
        top = jnp.max(logits, axis=-1, keepdims=True)
        weights = jnp.exp(logits - top)
        probs = weights / jnp.sum(weights, axis=-1, keepdims=True)
        gate = jnp.sum(probs * own_ref[...], axis=-1, keepdims=True)
        probs_ref[...] = probs
        gate_ref[...] = gate
        og_ref[...] = (gate * g_ref[...].astype(FULL)).astype(LOW)
        out_sum[...] = jnp.zeros_like(out_sum)
        back_sum[...] = jnp.zeros_like(back_sum)

    og = og_ref[...]
    up, down = up_ref[0], down_ref[0]
    hidden = nn(rows, up)
    slope = (2.0 / jnp.pi) ** 0.5
    square = hidden * hidden
    bend = jnp.tanh(slope * (hidden + 0.044715 * (square * hidden)))
    act = (0.5 * hidden * (1.0 + bend)).astype(LOW)
    out_sum[...] += nn(act, down)
    act_grad = nt(og, down)
    inner = slope * (1.0 + (3.0 * 0.044715) * square)
    curve = 0.5 * (1.0 + bend) + 0.5 * hidden * (1.0 - bend * bend) * inner
    hidden_grad = (curve * act_grad).astype(LOW)
    back_sum[...] += nt(hidden_grad, up)
    upg_ref[0] = tn(rows, hidden_grad).astype(LOW)
    downg_ref[0] = tn(act, og).astype(LOW)

    @pl.when(step == pl.num_programs(0) - 1)
    def _():
        out = out_sum[...].astype(LOW).astype(FULL)
        gate, probs = gate_ref[...], probs_ref[...]
        out_ref[...] = (gate * out).astype(LOW)
        gate_grad = jnp.sum(g_ref[...].astype(FULL) * out, axis=-1, keepdims=True)
        logit_grad = (gate_grad * (probs * (own_ref[...] - gate))).astype(LOW)
        back = back_sum[...].astype(LOW).astype(FULL) + nn(logit_grad, router_ref[...])
        back_ref[...] = back.astype(LOW)
        router_grad_ref[...] = tn(logit_grad, rows)


def experts_both_ways(rows, g_rows, up, down, router_low, own):
    slots, width = rows.shape
    parts, _, units = up.shape
    experts = router_low.shape[0]
    lanes = 128
    router_wide = jnp.zeros((lanes, width), LOW).at[:experts].set(router_low)
    lane = jnp.arange(lanes, dtype=jnp.int32)[None, :]
    own_row = jnp.where(lane == own, 1.0, 0.0).astype(FULL)
    closed = jnp.where(lane < experts, 0.0, -1e30).astype(FULL)
    wide_spec = whole((slots, width))
    return pl.pallas_call(
        expert_kernel,
        grid=(parts,),
        in_specs=[
            wide_spec, wide_spec, lead((1, width, units)), lead((1, units, width)),
            whole((lanes, width)), whole((1, lanes)), whole((1, lanes)),
        ],
        out_specs=[
            wide_spec, wide_spec, lead((1, width, units)), lead((1, units, width)),
            whole((lanes, width)),
        ],
        out_shape=[
            jax.ShapeDtypeStruct((slots, width), LOW),
            jax.ShapeDtypeStruct((slots, width), LOW),
            jax.ShapeDtypeStruct(up.shape, LOW),
            jax.ShapeDtypeStruct(down.shape, LOW),
            jax.ShapeDtypeStruct((lanes, width), FULL),
        ],
        scratch_shapes=[
            pltpu.VMEM((slots, width), FULL), pltpu.VMEM((slots, width), FULL),
            pltpu.VMEM((slots, width), LOW), pltpu.VMEM((slots, 1), FULL),
            pltpu.VMEM((slots, lanes), FULL),
        ],
        compiler_params=params(),
        name="experts_both_ways",
    )(rows, g_rows, up, down, router_wide, own_row, closed)


def gather_kernel(cuts, x_ref, out_ref, local_sem, send_sem, recv_sem):
    me, near, far, corner = partners()
    greet(("head", near), ("head", far))
    size = x_ref.shape[0] // cuts

    def remote(src, dst, lane, index, other):
        return pltpu.make_async_remote_copy(
            src_ref=src, dst_ref=dst, send_sem=send_sem.at[lane, index],
            recv_sem=recv_sem.at[lane, index], device_id={"head": other}, device_id_type=MESH,
        )

    local = pltpu.make_async_copy(x_ref, out_ref.at[me], local_sem)
    local.start()
    across, beside, onward = [], [], []
    for cut in range(cuts):
        span = pl.ds(cut * size, size)
        across.append(remote(x_ref.at[span], out_ref.at[me, span], 0, cut, far))
        across[-1].start()
    for cut in range(cuts):
        span = pl.ds(cut * size, size)
        beside.append(remote(x_ref.at[span], out_ref.at[me, span], 1, cut, near))
        beside[-1].start()
    for cut in range(cuts):
        span = pl.ds(cut * size, size)
        across[cut].wait_recv()
        onward.append(remote(out_ref.at[far, span], out_ref.at[far, span], 2, cut, near))
        onward[-1].start()
    for cut in range(cuts):
        across[cut].wait_send()
        beside[cut].wait()
        onward[cut].wait()
    local.wait()


def head_gather(x, collective_id, cuts=4):
    return pl.pallas_call(
        functools.partial(gather_kernel, cuts),
        in_specs=[pl.BlockSpec(memory_space=pl.ANY)],
        out_specs=pl.BlockSpec(memory_space=pl.ANY),
        out_shape=jax.ShapeDtypeStruct((4,) + x.shape, x.dtype),
        scratch_shapes=[
            pltpu.SemaphoreType.DMA, pltpu.SemaphoreType.DMA((3, cuts)),
            pltpu.SemaphoreType.DMA((3, cuts)),
        ],
        compiler_params=params(collective_id=collective_id, has_side_effects=True),
        name="head_gather",
    )(x)


def body(
    patches, cotangent, expert_ids, slot_pos, owners,
    tile_master, tile_first, tile_second,
    expert_up, up_first, up_second,
    expert_down, down_first, down_second,
    router, router_first, router_second,
    norm_params, norm_first, norm_second,
):
    tok_rows, width = patches.shape
    experts = router.shape[0]
    capacity = tok_rows // experts
    dp_count = lax.axis_size("dp")
    head_count = lax.axis_size("head")
    me_head = lax.axis_index("head")
    me_dp = lax.axis_index("dp")
    images = tok_rows // PATCH
    share = capacity // head_count
    own_slots = experts * share
    slot_count = tile_master.shape[0]

    owner_row = owners[0]
    tile_count = owner_row.shape[0]
    order_index = jnp.arange(tile_count, dtype=jnp.int32)
    same_owner = owner_row[:, None] == owner_row[None, :]
    earlier = order_index[None, :] < order_index[:, None]
    tile_rank = jnp.sum(jnp.where(same_owner & earlier, 1, 0), axis=1).astype(jnp.int32)
    tile_place = owner_row * slot_count + tile_rank
    src = (tile_place[:, None] * TILE + jnp.arange(TILE, dtype=jnp.int32)[None, :]).reshape(-1)

    up_low = expert_up[0].astype(LOW)
    down_low = expert_down[0].astype(LOW)
    up_all = lax.all_gather(up_low, "head", axis=0)
    down_all = lax.all_gather(down_low, "head", axis=0)

    ids, pos = expert_ids.T, slot_pos.T
    col = (pos // share) * own_slots + ids * share + lax.rem(pos, share)
    col = jnp.where(pos < capacity, col, tok_rows)
    col_rows = (col - me_head * own_slots).reshape(2, images, PATCH).transpose(1, 0, 2)
    col = col.T

    def to_experts(rows):
        rows = rows.reshape(experts, share, width)
        return lax.all_to_all(rows, "dp", 0, 0, tiled=True).reshape(own_slots, width)

    by_image = (images, PATCH, width)
    x_images = patches.reshape(by_image)
    w, xn, g_sent = prepare(
        tile_master.reshape(slot_count * TILE, width), x_images, cotangent.reshape(by_image),
        norm_params, src[:, None], col_rows, own_slots, dp_count,
    )
    g_rows = to_experts(g_sent)
    lse, sent, *saved, x1 = attention_forward(xn, w, x_images, norm_params, col_rows, own_slots)
    x1 = x1.reshape(tok_rows, width)
    rows = to_experts(sent)
    back, out, up_part, down_part, router_part = experts_both_ways(
        rows, g_rows, up_all, down_all, router.astype(LOW), me_dp
    )
    back_all = head_gather(to_experts(back), 3).reshape(tok_rows, width)
    x1_grad, second_sums = combine_backward(col, back_all, x1, cotangent, norm_params)
    padded, first_sums, input_low = attention_backward(
        x1_grad.reshape(by_image), w, xn, saved, lse, src[None, :], x_images, norm_params,
        dp_count * slot_count * TILE,
    )
    input_grad = input_low.reshape(tok_rows, width).astype(FULL)

    out_all = lax.all_gather(to_experts(out), "head", axis=0, tiled=True)
    block_out = combine_forward(col, out_all, x1)

    up_grad = lax.psum_scatter(up_part, "head", scatter_dimension=0).astype(FULL)
    down_grad = lax.psum_scatter(down_part, "head", scatter_dimension=0).astype(FULL)
    owned_grad = lax.psum_scatter(
        padded.reshape(dp_count * slot_count, TILE, width), "dp", scatter_dimension=0, tiled=True
    ).astype(FULL)

    small = jnp.concatenate(
        [router_part[:experts], first_sums[:2], second_sums[:2] * (1.0 / head_count)], axis=0
    )
    small = lax.psum(small, ("dp", "head"))
    router_total, norm_total = small[:experts], small[experts:]

    tile_new, tile_first_new, tile_second_new = adam_update(
        tile_master, tile_first, tile_second, owned_grad, rate_attention, decay_factor
    )
    up_new, up_first_new, up_second_new = adam_update(
        expert_up, up_first, up_second, up_grad[None], rate_up, decay_factor
    )
    down_new, down_first_new, down_second_new = adam_update(
        expert_down, down_first, down_second, down_grad[None], rate_down, decay_factor
    )
    router_new, router_first_new, router_second_new = adam_update(
        router, router_first, router_second, router_total, rate_router, decay_factor
    )
    norm_new, norm_first_new, norm_second_all = adam_update(
        norm_params, norm_first, norm_second, norm_total, rate_norm, 0.0
    )
    return (
        block_out,
        input_grad,
        tile_new,
        tile_first_new,
        tile_second_new,
        tile_new.astype(LOW),
        up_new,
        up_first_new,
        up_second_new,
        up_new.astype(LOW),
        down_new,
        down_first_new,
        down_second_new,
        down_new.astype(LOW),
        router_new,
        router_first_new,
        router_second_new,
        norm_new,
        norm_first_new,
        norm_second_all[:2],
        norm_second_all[2:],
    )


def solution(mesh):
    row = P("dp", None)
    tiles = P(("dp", "head"), None, None)
    up = P("dp", None, "head")
    down = P("dp", "head", None)
    in_specs = (
        row, row, row, row, P("head", None), tiles, tiles, tiles,
        up, up, up, down, down, down, P(), P(), P(), P(), P(), P(),
    )
    out_specs = (
        row, row, tiles, tiles, tiles, tiles, up, up, up, up, down, down, down, down,
        P(), P(), P(), P(), P(), P(), P(),
    )
    return jax.shard_map(body, mesh=mesh, in_specs=in_specs, out_specs=out_specs, check_vma=False)
```

```python
import functools

import jax
import jax.numpy as jnp
from jax import lax
from jax.experimental import pallas as pl
from jax.experimental.pallas import tpu as pltpu
from jax.sharding import PartitionSpec as P

HD = 64
PATCH = 576
TILE = 8
STEP = 10

eps_norm = 1e-06
beta_one = 0.9
beta_two = 0.999
adam_eps = 1e-08
rate_attention = 0.12
rate_up = 0.08
rate_down = 0.3
rate_router = 0.05
rate_norm = 0.4
decay_factor = 0.1

LOW = jnp.bfloat16
FULL = jnp.float32
MESH = pl.DeviceIdType.MESH
VMEM_BYTES = 56 * 1024 * 1024


def adam_update(weight, moment_one, moment_two, gradient, step_rate, weight_decay):
    moment_one = beta_one * moment_one + (1.0 - beta_one) * gradient
    moment_two = beta_two * moment_two + (1.0 - beta_two) * gradient * gradient
    fixed_one = moment_one / (1.0 - beta_one**STEP)
    fixed_two = moment_two / (1.0 - beta_two**STEP)
    weight = weight - step_rate * (
        fixed_one / (jnp.sqrt(fixed_two) + adam_eps) + weight_decay * weight
    )
    return (weight, moment_one, moment_two)


def nn(left, right):
    return lax.dot_general(left, right, (((1,), (0,)), ((), ())), preferred_element_type=FULL)


def nt(left, right):
    return lax.dot_general(left, right, (((1,), (1,)), ((), ())), preferred_element_type=FULL)


def tn(left, right):
    return lax.dot_general(left, right, (((0,), (0,)), ((), ())), preferred_element_type=FULL)


def params(**more):
    return pltpu.CompilerParams(vmem_limit_bytes=VMEM_BYTES, **more)


def whole(shape):
    return pl.BlockSpec(shape, lambda *_: (0,) * len(shape))


def lead(shape):
    return pl.BlockSpec(shape, lambda i: (i,) + (0,) * (len(shape) - 1))


def normalise(values):
    average = jnp.mean(values, axis=-1, keepdims=True)
    centred = values - average
    variance = jnp.mean(centred * centred, axis=-1, keepdims=True)
    scale = lax.rsqrt(variance + eps_norm)
    return centred * scale, scale


def norm_back(normal, scale, gain, upstream):
    inner = upstream * gain
    mean_inner = jnp.mean(inner, axis=-1, keepdims=True)
    mean_cross = jnp.mean(inner * normal, axis=-1, keepdims=True)
    result = scale * (inner - mean_inner - normal * mean_cross)
    gain_sum = jnp.sum(upstream * normal, axis=0, keepdims=True)
    shift_sum = jnp.sum(upstream, axis=0, keepdims=True)
    return result, gain_sum, shift_sum


def one_hot(condition):
    return jnp.where(condition, 1.0, 0.0).astype(LOW)


def remote(src, dst, sends, recvs, index, axis, other):
    return pltpu.make_async_remote_copy(
        src_ref=src, dst_ref=dst, send_sem=sends.at[index], recv_sem=recvs.at[index],
        device_id={axis: other}, device_id_type=MESH,
    )


def greet(*others):
    barrier = pltpu.get_barrier_semaphore()
    for axis, other in others:
        pl.semaphore_signal(barrier, inc=1, device_id={axis: other}, device_id_type=MESH)
    pl.semaphore_wait(barrier, len(others))


def partners():
    me = lax.axis_index("head")
    near = me + 1 - 2 * lax.rem(me, 2)
    far = lax.rem(me + 2, 4)
    corner = lax.rem(near + 2, 4)
    return me, near, far, corner


class LineGather:
    def __init__(self, held, up_send, up_recv, down_send, down_recv, pair_send, pair_recv):
        self.held = held
        self.length = held.shape[0] // 2
        self.sems = ((up_send, up_recv), (down_send, down_recv), (pair_send, pair_recv))
        me = lax.axis_index("dp")
        self.place, self.side = me // 2, lax.rem(me, 2)
        self.above = lax.rem(self.place + 1, self.length) * 2 + self.side
        self.below = lax.rem(self.place + self.length - 1, self.length) * 2 + self.side
        self.other = self.place * 2 + 1 - self.side

    def neighbours(self):
        return ("dp", self.above), ("dp", self.below), ("dp", self.other)

    def copy(self, way, origin, side=None):
        index = origin * 2 + (self.side if side is None else side)
        target = (self.above, self.below, self.other)[way]
        block = self.held.at[index]
        return remote(block, block, *self.sems[way], origin, "dp", target)

    def pass_on(self, origin, up, down):
        @pl.when(up & (self.place < self.length - 1))
        def _():
            self.copy(0, origin).start()

        @pl.when(down & (self.place > 0))
        def _():
            self.copy(1, origin).start()

        self.copy(2, origin).start()

    def start(self):
        self.pass_on(self.place, True, True)

    def step(self, k):
        low, high = self.place - k, self.place + k

        @pl.when(low >= 0)
        def _():
            self.copy(0, low).wait_recv()
            self.pass_on(low, True, False)

        @pl.when(high < self.length)
        def _():
            self.copy(1, high).wait_recv()
            self.pass_on(high, False, True)

    def finish(self):
        @pl.loop(0, self.length)
        def _(origin):
            self.copy(2, origin).wait_recv()
            self.copy(2, origin).wait_send()

            @pl.when((origin <= self.place) & (self.place < self.length - 1))
            def _():
                self.copy(0, origin).wait_send()

            @pl.when((origin >= self.place) & (self.place > 0))
            def _():
                self.copy(1, origin).wait_send()


class ImageSum:
    def __init__(self, stage, corner_in, near_in, passed, mine, far_in, sends, recvs):
        self.stage, self.corner_in, self.near_in = stage, corner_in, near_in
        self.passed, self.mine, self.far_in = passed, mine, far_in
        self.sends, self.recvs = sends, recvs
        self.me, self.near, self.far, self.corner = partners()
        self.core = lax.rem(self.me, 2)

    def image(self, turn):
        base = self.me - self.core
        other = lax.rem(base + 2, 4)
        return jnp.where(turn < 2, other, base - 2) + turn

    def to_corner(self):
        return remote(
            self.stage.at[0], self.corner_in, self.sends, self.recvs, 0, "head", self.near
        )

    def to_near(self):
        return remote(
            self.stage.at[1], self.near_in, self.sends, self.recvs, 1, "head", self.near
        )

    def to_far(self):
        return remote(self.passed, self.far_in, self.sends, self.recvs, 2, "head", self.far)

    def give(self, turn, part):
        theirs = lax.rem(turn, 2) != self.core

        @pl.when((turn < 2) & theirs)
        def _():
            self.stage[0] = part.astype(LOW)
            self.to_corner().start()

        @pl.when((turn >= 2) & theirs)
        def _():
            self.stage[1] = part.astype(LOW)
            self.to_near().start()

        @pl.when((turn < 2) & ~theirs)
        def _():
            self.to_corner().wait_recv()
            self.passed[...] = (part + self.corner_in[...].astype(FULL)).astype(LOW)
            self.to_far().start()

        @pl.when((turn >= 2) & ~theirs)
        def _():
            self.mine[...] = part

    def result(self):
        self.to_near().wait_recv()
        self.to_far().wait_recv()
        return self.mine[...] + self.near_in[...].astype(FULL) + self.far_in[...].astype(FULL)

    def finish(self):
        self.to_corner().wait_send()
        self.to_near().wait_send()
        self.to_far().wait_send()


def image_sum_scratch(width):
    block = pltpu.VMEM((PATCH, width), LOW)
    return [
        pltpu.VMEM((2, PATCH, width), LOW), block, block, block,
        pltpu.VMEM((PATCH, width), FULL), block,
        pltpu.SemaphoreType.DMA((3,)), pltpu.SemaphoreType.DMA((3,)),
    ]


class LineScatter:
    def __init__(
        self, blocks, out, pair_in, up_in, down_in, total,
        up_send, up_recv, down_send, down_recv, pair_send, pair_recv,
    ):
        self.blocks, self.out, self.total = blocks, out, total
        self.arrived = (up_in, down_in, pair_in)
        self.sems = ((up_send, up_recv), (down_send, down_recv), (pair_send, pair_recv))
        self.length = blocks.shape[0] // 2
        me = lax.axis_index("dp")
        self.place, self.side = me // 2, lax.rem(me, 2)
        self.targets = (
            lax.rem(self.place + 1, self.length) * 2 + self.side,
            lax.rem(self.place + self.length - 1, self.length) * 2 + self.side,
            self.place * 2 + 1 - self.side,
        )

    def copy(self, way, block):
        source = (
            self.blocks.at[block * 2 + 1 - self.side] if way == 2 else self.total.at[block]
        )
        return remote(
            source, self.arrived[way].at[block], *self.sems[way], block, "dp", self.targets[way]
        )

    def start(self):
        @pl.loop(0, self.length)
        def _(turn):
            distance = self.length - 1 - turn

            @pl.when(self.place + distance < self.length)
            def _():
                self.copy(2, self.place + distance).start()

            @pl.when((self.place >= distance) & (distance > 0))
            def _():
                self.copy(2, self.place - distance).start()

    def pair_sum(self, block):
        self.copy(2, block).wait_recv()
        own = self.blocks[block * 2 + self.side].astype(FULL)
        return own + self.arrived[2][block].astype(FULL)

    def forward(self, way, block, first):
        both = self.pair_sum(block)

        @pl.when(first)
        def _():
            self.total[block] = both.astype(LOW)

        @pl.when(~first)
        def _():
            self.copy(way, block).wait_recv()
            self.total[block] = (both + self.arrived[way][block].astype(FULL)).astype(LOW)

        self.copy(way, block).start()

    def step(self, distance):
        @pl.when(self.place + distance < self.length)
        def _():
            self.forward(0, self.place + distance, self.place == 0)

        @pl.when(self.place >= distance)
        def _():
            self.forward(1, self.place - distance, self.place == self.length - 1)

    def result(self):
        self.out[...] = self.pair_sum(self.place)

        @pl.when(self.place > 0)
        def _():
            self.copy(0, self.place).wait_recv()
            self.out[...] += self.arrived[0][self.place].astype(FULL)

        @pl.when(self.place < self.length - 1)
        def _():
            self.copy(1, self.place).wait_recv()
            self.out[...] += self.arrived[1][self.place].astype(FULL)

    def finish(self):
        @pl.loop(0, self.length)
        def _(block):
            self.copy(2, block).wait_send()

            @pl.when(block > self.place)
            def _():
                self.copy(0, block).wait_send()

            @pl.when(block < self.place)
            def _():
                self.copy(1, block).wait_send()


def line_scatter_scratch(dp_count, rows, width):
    line = dp_count // 2
    return [pltpu.VMEM((line, rows, width), LOW)] * 4 + [pltpu.SemaphoreType.DMA((line,))] * 6


class SmallSum:
    def __init__(self, flat, head_in, dp_in, done, head_send, head_recv, dp_send, dp_recv):
        self.flat, self.head_in, self.dp_in, self.done = flat, head_in, dp_in, done
        self.head_sems, self.dp_sems = (head_send, head_recv), (dp_send, dp_recv)
        self.me, *self.others = partners()
        self.place, self.count = lax.axis_index("dp"), dp_in.shape[0]

    def to_head(self, lane):
        other = self.others[lane]
        return remote(
            self.flat.at[other], self.head_in.at[self.me], *self.head_sems, lane, "head", other
        )

    def back_head(self, lane):
        block = self.done.at[self.me]
        return remote(block, block, *self.head_sems, 3 + lane, "head", self.others[lane])

    def to_dp(self, shift):
        block = self.dp_in.at[self.place]
        other = lax.rem(self.place + shift, self.count)
        return remote(block, block, *self.dp_sems, shift, "dp", other)

    def start(self, value):
        groups, rows, lanes = self.flat.shape
        flat = jnp.concatenate(
            [value[:, at:at + lanes] for at in range(0, value.shape[1], lanes)], axis=0
        )
        for group in range(groups):
            self.flat[group] = flat[group * rows:(group + 1) * rows]
        for lane in range(3):
            self.to_head(lane).start()
        self.head_in[self.me] = self.flat[self.me]

    def across(self):
        for lane in range(3):
            self.to_head(lane).wait_recv()
        total = self.head_in[0]
        for head in range(1, self.head_in.shape[0]):
            total = total + self.head_in[head]
        self.dp_in[self.place] = total

        @pl.loop(1, self.count)
        def _(shift):
            self.to_dp(shift).start()

    def back(self):
        @pl.loop(1, self.count)
        def _(shift):
            self.to_dp(shift).wait_recv()

        total = lax.fori_loop(
            1, self.count, lambda at, so_far: so_far + self.dp_in[at], self.dp_in[0]
        )
        self.done[self.me] = total
        for lane in range(3):
            self.back_head(lane).start()

    def result(self, out):
        for lane in range(3):
            self.back_head(lane).wait_recv()
        flat = jnp.concatenate([self.done[group] for group in range(self.done.shape[0])], axis=0)
        rows, width = out.shape
        lanes = flat.shape[1]
        for at in range(width // lanes):
            out[:, at * lanes:(at + 1) * lanes] = flat[at * rows:(at + 1) * rows]

    def finish(self):
        for lane in range(3):
            self.to_head(lane).wait_send()
            self.back_head(lane).wait_send()

        @pl.loop(1, self.count)
        def _(shift):
            self.to_dp(shift).wait_send()


def small_sum_scratch(rows, width, dp_count):
    block = (rows * width // 128 // 4, 128)
    return [
        pltpu.VMEM((4,) + block, FULL), pltpu.VMEM((4,) + block, FULL),
        pltpu.VMEM((dp_count,) + block, FULL), pltpu.VMEM((4,) + block, FULL),
        pltpu.SemaphoreType.DMA((6,)), pltpu.SemaphoreType.DMA((6,)),
        pltpu.SemaphoreType.DMA((dp_count,)), pltpu.SemaphoreType.DMA((dp_count,)),
    ]


GATHER_CUTS = 4


class ImageGather:
    def __init__(self, held, sends, recvs):
        self.held, self.sends, self.recvs = held, sends, recvs
        self.me, self.near, self.far, self.corner = partners()
        self.size = held.shape[1] // GATHER_CUTS

    def piece(self, image, cut, lane, other):
        span = pl.ds(cut * self.size, self.size)
        block = self.held.at[image, span]
        return remote(block, block, self.sends, self.recvs, lane * GATHER_CUTS + cut, "head", other)

    def start(self):
        for cut in range(GATHER_CUTS):
            self.piece(self.me, cut, 0, self.far).start()
        for cut in range(GATHER_CUTS):
            self.piece(self.me, cut, 1, self.near).start()

    def wait_near(self):
        for cut in range(GATHER_CUTS):
            self.piece(self.me, cut, 1, self.near).wait_recv()

    def wait_far(self):
        for cut in range(GATHER_CUTS):
            self.piece(self.me, cut, 0, self.far).wait_recv()
            self.piece(self.far, cut, 2, self.near).start()

    def wait_corner(self):
        for cut in range(GATHER_CUTS):
            self.piece(self.far, cut, 2, self.near).wait_recv()

    def finish(self):
        for cut in range(GATHER_CUTS):
            self.piece(self.me, cut, 0, self.far).wait_send()
            self.piece(self.me, cut, 1, self.near).wait_send()
            self.piece(self.far, cut, 2, self.near).wait_send()


def image_gather_sems():
    return [pltpu.SemaphoreType.DMA((3 * GATHER_CUTS,)), pltpu.SemaphoreType.DMA((3 * GATHER_CUTS,))]


ANYWHERE = pl.BlockSpec(memory_space=pl.ANY)
INSIDE = pl.BlockSpec(memory_space=pltpu.VMEM)


def prepare_kernel(
    tile_ref, x_ref, g_ref, norm_ref, src_ref, col_ref,
    w_ref, xn_ref, sent_ref,
    held, sent_sum, *sems,
):
    images = x_ref.shape[0]
    gather = LineGather(held, *sems)
    greet(*gather.neighbours())
    me = lax.axis_index("dp")
    held[me] = tile_ref[...].astype(LOW)
    gather.start()

    def image_step(image):
        normal, _ = normalise(x_ref[image].astype(FULL))
        xn_ref[image] = (normal * norm_ref[0:1, :] + norm_ref[1:2, :]).astype(LOW)
        shape = (sent_ref.shape[0], PATCH)
        slots = lax.broadcasted_iota(jnp.int32, shape, 0)
        col = col_ref[image]
        pick = one_hot((slots == col[0:1, :]) | (slots == col[1:2, :]))
        sent_sum[...] += nn(pick, g_ref[image])

    sent_sum[...] = jnp.zeros_like(sent_sum)
    steps = gather.length - 1

    @pl.loop(0, max(steps, images))
    def _(turn):
        @pl.when(turn < images)
        def _():
            image_step(turn)

        @pl.when(turn < steps)
        def _():
            gather.step(turn + 1)

    sent_ref[...] = sent_sum[...].astype(LOW)
    gather.finish()
    rows = w_ref.shape[0] // 4
    blocks, depth, width = held.shape
    for part in range(4):
        block = pl.ds(part * rows, rows)
        lanes = lax.broadcasted_iota(jnp.int32, (rows, blocks * depth), 1)
        pick = one_hot(lanes == src_ref[block, :])
        w_ref[block, :] = nn(pick, held[...].reshape(blocks * depth, width)).astype(LOW)


def prepare(tiles, patches, cotangent, norm_params, src_col, col_rows, slots, dp_count):
    images, _, width = patches.shape
    line = dp_count // 2
    return pl.pallas_call(
        prepare_kernel,
        in_specs=[INSIDE] * 6,
        out_specs=[INSIDE] * 3,
        out_shape=[
            jax.ShapeDtypeStruct((src_col.shape[0], width), LOW),
            jax.ShapeDtypeStruct(patches.shape, LOW),
            jax.ShapeDtypeStruct((slots, width), LOW),
        ],
        scratch_shapes=[
            pltpu.VMEM((dp_count,) + tiles.shape, LOW), pltpu.VMEM((slots, width), FULL),
        ] + [pltpu.SemaphoreType.DMA((line,))] * 6,
        compiler_params=params(collective_id=0, has_side_effects=True),
        name="prepare",
    )(tiles, patches, cotangent, norm_params, src_col, col_rows)


def head_mask(shape, axis, head):
    return lax.broadcasted_iota(jnp.int32, shape, axis) // HD == head


def forward_kernel(
    xn_ref, w_ref, x_ref, norm_ref, col_ref,
    lse_ref, sent_ref, q_out, qt_out, k_out, kt_out, v_out, ot_out, x1_out,
    q_ref, qt_ref, k_ref, kt_ref, v_ref, ot_ref, x1_ref, own_ref, sent_sum,
    save_sems, own_sem, *exchange,
):
    images = xn_ref.shape[0]
    rows = w_ref.shape[0] // 4
    heads = rows // HD
    total_of = ImageSum(*exchange[:8])
    spread = ImageGather(x1_ref, *exchange[8:])
    me, near, far, corner = partners()
    greet(("head", near), ("head", far))
    own = pltpu.make_async_copy(x_ref.at[me], own_ref, own_sem)
    own.start()
    kept = ((q_ref, q_out), (qt_ref, qt_out), (k_ref, k_out), (kt_ref, kt_out), (v_ref, v_out), (ot_ref, ot_out))
    shrink = HD ** (-0.5)

    def save(image):
        return [
            pltpu.make_async_copy(ref.at[image], out.at[image], save_sems.at[index, image])
            for index, (ref, out) in enumerate(kept)
        ]

    @pl.loop(0, images)
    def _(turn):
        image = total_of.image(turn)
        xn = xn_ref[image]
        wq, wk, wv, wo = (w_ref[pl.ds(part * rows, rows), :] for part in range(4))
        q_ref[image] = (nt(xn, wq) * shrink).astype(LOW)
        qt = (nt(wq, xn) * shrink).astype(LOW)
        qt_ref[image] = qt
        k = nt(xn, wk).astype(LOW)
        k_ref[image] = k
        kt_ref[image] = nt(wk, xn).astype(LOW)
        v_ref[image] = nt(xn, wv).astype(LOW)
        vt = nt(wv, xn).astype(LOW)
        mixed = []
        for head in range(heads):
            span = slice(head * HD, (head + 1) * HD)
            only = jnp.where(head_mask(qt.shape, 0, head), qt, jnp.zeros_like(qt))
            scores = nn(k, only)
            top = jnp.max(scores, axis=0, keepdims=True)
            weights = jnp.exp(scores - top)
            total = jnp.sum(weights, axis=0, keepdims=True)
            mixed.append(nn(vt[span], weights.astype(LOW)) / total)
            lse_ref[image, head:head + 1, :] = top + jnp.log(total)
        ot = jnp.concatenate(mixed, axis=0).astype(LOW)
        ot_ref[image] = ot
        total_of.give(turn, tn(ot, wo))
        for copy in save(image):
            copy.start()

    own.wait()
    x1_ref[me] = (own_ref[...].astype(FULL) + total_of.result()).astype(LOW)
    spread.start()
    sent_sum[...] = jnp.zeros_like(sent_sum)

    def place(image):
        normal, _ = normalise(x1_ref[image].astype(FULL))
        low = (normal * norm_ref[2:3, :] + norm_ref[3:4, :]).astype(LOW)
        slots = lax.broadcasted_iota(jnp.int32, (sent_ref.shape[0], PATCH), 0)
        col = col_ref[image]
        pick = one_hot((slots == col[0:1, :]) | (slots == col[1:2, :]))
        sent_sum[...] += nn(pick, low)

    place(me)
    spread.wait_near()
    place(near)
    spread.wait_far()
    place(far)
    spread.wait_corner()
    keep = pltpu.make_async_copy(x1_ref, x1_out, own_sem)
    keep.start()
    place(corner)
    sent_ref[...] = sent_sum[...].astype(LOW)
    spread.finish()
    total_of.finish()
    keep.wait()

    @pl.loop(0, images)
    def _(image):
        for copy in save(image):
            copy.wait()


def attention_forward(xn, w, patches, norm_params, col_rows, slots):
    images, _, width = patches.shape
    rows = w.shape[0] // 4
    flat, turned = (images, PATCH, rows), (images, rows, PATCH)
    saved = [flat, turned, flat, turned, flat, turned, patches.shape]
    return pl.pallas_call(
        forward_kernel,
        in_specs=[INSIDE, INSIDE, ANYWHERE, INSIDE, INSIDE],
        out_specs=[INSIDE, INSIDE] + [ANYWHERE] * 7,
        out_shape=[
            jax.ShapeDtypeStruct((images, 8, PATCH), FULL), jax.ShapeDtypeStruct((slots, width), LOW),
        ] + [jax.ShapeDtypeStruct(shape, LOW) for shape in saved],
        scratch_shapes=[pltpu.VMEM(shape, LOW) for shape in saved]
        + [
            pltpu.VMEM((PATCH, width), LOW), pltpu.VMEM((slots, width), FULL),
            pltpu.SemaphoreType.DMA((6, images)), pltpu.SemaphoreType.DMA,
        ]
        + image_sum_scratch(width) + image_gather_sems(),
        compiler_params=params(collective_id=1, has_side_effects=True),
        name="attention_forward",
    )(xn, w, patches, norm_params, col_rows)


def backward_kernel(
    experts,
    x1g_ref, w_ref, xn_ref, q_ref, qt_ref, k_ref, kt_ref, v_ref, lse_ref, ot_ref, src_ref,
    norm_ref, small_ref, col_ref, x_ref, out_rows_ref, x1_ref,
    owned_ref, small_out, block_ref, input_out,
    grad_ref, own_ref, input_ref, padded_ref, out_ref, own_sem, *exchange,
):
    images = x1g_ref.shape[0]
    rows = w_ref.shape[0] // 4
    heads = rows // HD
    total_of = ImageSum(*exchange[:8])
    spread = ImageGather(input_ref, *exchange[8:10])
    spread_out = ImageGather(out_ref, *exchange[10:12])
    weights_sum = LineScatter(padded_ref, owned_ref, *exchange[12:22])
    small_sum = SmallSum(*exchange[22:])
    me, near, far, corner = partners()
    dp_count = padded_ref.shape[0]
    place = lax.axis_index("dp")
    barrier = pltpu.get_barrier_semaphore()
    for other in (near, far, corner):
        pl.semaphore_signal(barrier, inc=1, device_id={"head": other}, device_id_type=MESH)

    @pl.loop(1, dp_count)
    def _(shift):
        other = lax.rem(place + shift, dp_count)
        pl.semaphore_signal(barrier, inc=1, device_id={"dp": other}, device_id_type=MESH)

    own = pltpu.make_async_copy(x_ref.at[me], own_ref, own_sem.at[0])
    own.start()
    own_out = pltpu.make_async_copy(out_rows_ref, out_ref.at[me], own_sem.at[1])
    own_out.start()
    x1_copy = pltpu.make_async_copy(x1_ref, block_ref, own_sem.at[2])
    x1_copy.start()
    pl.semaphore_wait(barrier, dp_count + 2)
    own_out.wait()
    spread_out.start()
    shrink = HD ** (-0.5)
    grad_ref[...] = jnp.zeros_like(grad_ref)

    @pl.loop(0, images)
    def _(turn):
        image = total_of.image(turn)
        wq, wk, wv, wo = (w_ref[pl.ds(part * rows, rows), :] for part in range(4))
        x1g, xn = x1g_ref[image], xn_ref[image]
        q, qt, k, kt = q_ref[image], qt_ref[image], k_ref[image], kt_ref[image]
        v, ot = v_ref[image], ot_ref[image]
        do = nt(x1g, wo).astype(LOW)
        dot = nt(wo, x1g).astype(LOW)
        product = dot.astype(FULL) * ot.astype(FULL)
        dqt, dk, dv = [], None, None
        for head in range(heads):
            span = slice(head * HD, (head + 1) * HD)
            zero_t = jnp.zeros_like(qt)
            mask_t = head_mask(qt.shape, 0, head)
            mask = head_mask(q.shape, 1, head)
            scores = nn(k, jnp.where(mask_t, qt, zero_t))
            weights = jnp.exp(scores - lse_ref[image, head:head + 1, :])
            back = nn(v, jnp.where(mask_t, dot, zero_t))
            delta = jnp.sum(product[span], axis=0, keepdims=True)
            score_grad = (weights * (back - delta)).astype(LOW)
            dqt.append(nn(kt[span], score_grad) * shrink)
            dk_one = nn(score_grad, jnp.where(mask, q, jnp.zeros_like(q)))
            dv_one = nn(weights.astype(LOW), jnp.where(mask, do, jnp.zeros_like(do)))
            dk = dk_one if dk is None else dk + dk_one
            dv = dv_one if dv is None else dv + dv_one
        dqt = jnp.concatenate(dqt, axis=0).astype(LOW)
        dk, dv = dk.astype(LOW), dv.astype(LOW)
        total_of.give(turn, tn(dqt, wq) + nn(dk, wk) + nn(dv, wv))
        pieces = (nn(dqt, xn), tn(dk, xn), tn(dv, xn), nn(ot, x1g))
        for part, piece in enumerate(pieces):
            grad_ref[pl.ds(part * rows, rows), :] += piece

        @pl.when(turn == 2)
        def _():
            spread_out.wait_far()

    own.wait()
    normal, scale = normalise(own_ref[...].astype(FULL))
    back, gain_sum, shift_sum = norm_back(normal, scale, norm_ref[0:1, :], total_of.result())
    input_ref[me] = (x1g_ref[me].astype(FULL) + back).astype(LOW)
    spread.start()
    low = grad_ref[...].astype(LOW)
    depth = padded_ref.shape[1]
    parts = min(dp_count, 8)
    cut = dp_count // parts * depth
    for part in range(parts):
        row = lax.broadcasted_iota(jnp.int32, (cut, low.shape[0]), 0) + part * cut
        pick = one_hot(row == src_ref[...])
        block = nn(pick, low).astype(LOW)
        padded_ref[pl.ds(part * (dp_count // parts), dp_count // parts)] = block.reshape(
            dp_count // parts, depth, block.shape[1]
        )
    weights_sum.start()
    small = small_ref[...]
    row = lax.broadcasted_iota(jnp.int32, small.shape, 0)
    small = small + jnp.where(row == experts, gain_sum, 0.0)
    small_sum.start(small + jnp.where(row == experts + 1, shift_sum, 0.0))
    spread_out.wait_near()
    spread_out.wait_corner()
    x1_copy.wait()
    steps = weights_sum.length

    @pl.loop(0, max(steps, images))
    def _(turn):
        @pl.when(turn < images)
        def _():
            mix = picked_rows(col_ref[turn], out_ref)
            block_ref[turn] = (block_ref[turn].astype(FULL) + mix).astype(LOW)

        @pl.when(turn < steps - 1)
        def _():
            weights_sum.step(steps - 1 - turn)

        @pl.when(turn == 0)
        def _():
            small_sum.across()

        @pl.when(turn == 1)
        def _():
            spread.wait_far()

        @pl.when(turn == 2)
        def _():
            small_sum.back()

    weights_sum.result()
    small_sum.result(small_out)
    spread.wait_near()
    spread.wait_corner()
    keep = pltpu.make_async_copy(input_ref, input_out, own_sem.at[0])
    keep.start()
    spread.finish()
    spread_out.finish()
    total_of.finish()
    weights_sum.finish()
    small_sum.finish()
    keep.wait()


def attention_backward(
    experts, dp_count, depth,
    x1_grad, w, xn, saved, lse, src_row, norm_params, small, col, patches, out_rows, x1,
):
    q, qt, k, kt, v, ot = saved
    images, _, width = patches.shape
    return pl.pallas_call(
        functools.partial(backward_kernel, experts),
        in_specs=[INSIDE] * 14 + [ANYWHERE] * 3,
        out_specs=[INSIDE, INSIDE, INSIDE, ANYWHERE],
        out_shape=[
            jax.ShapeDtypeStruct((depth, width), FULL), jax.ShapeDtypeStruct(small.shape, FULL),
            jax.ShapeDtypeStruct(patches.shape, LOW), jax.ShapeDtypeStruct(patches.shape, LOW),
        ],
        scratch_shapes=[
            pltpu.VMEM(w.shape, FULL), pltpu.VMEM((PATCH, width), LOW),
            pltpu.VMEM(patches.shape, LOW), pltpu.VMEM((dp_count, depth, width), LOW),
            pltpu.VMEM((4,) + out_rows.shape, LOW), pltpu.SemaphoreType.DMA((3,)),
        ]
        + image_sum_scratch(width) + image_gather_sems() + image_gather_sems()
        + line_scatter_scratch(dp_count, depth, width)
        + small_sum_scratch(small.shape[0], width, dp_count),
        compiler_params=params(collective_id=2, has_side_effects=True),
        name="attention_backward",
    )(
        x1_grad, w, xn, q, qt, k, kt, v, lse, ot, src_row, norm_params, small, col,
        patches, out_rows, x1,
    )


def picked_rows(col, held_ref):
    groups, cut, width = held_ref.shape
    tokens = col.shape[0]
    total = jnp.zeros((tokens, width), FULL)
    for part in range(groups):
        lanes = lax.broadcasted_iota(jnp.int32, (tokens, cut), 1) + part * cut
        pick = one_hot((lanes == col[:, 0:1]) | (lanes == col[:, 1:2]))
        total = total + nn(pick, held_ref[part])
    return total


def combine_rear(col_ref, held_ref, x1_ref, g_ref, norm_ref, out_ref, sums_ref):
    step = pl.program_id(0)
    upstream = picked_rows(col_ref[...], held_ref)
    normal, scale = normalise(x1_ref[...].astype(FULL))
    back, gain_sum, shift_sum = norm_back(normal, scale, norm_ref[2:3, :], upstream)
    out_ref[...] = (g_ref[...].astype(FULL) + back).astype(LOW)

    @pl.when(step == 0)
    def _():
        sums_ref[...] = jnp.zeros_like(sums_ref)

    sums_ref[0:1, :] += gain_sum
    sums_ref[1:2, :] += shift_sum


def combine_backward(col, held, x1, cotangent, norm_params):
    tokens, width = x1.shape
    wide_spec = lead((PATCH, width))
    return pl.pallas_call(
        combine_rear,
        grid=(tokens // PATCH,),
        in_specs=[
            lead((PATCH, 2)), whole(held.shape), wide_spec, wide_spec, whole(norm_params.shape)
        ],
        out_specs=[wide_spec, whole((8, width))],
        out_shape=[
            jax.ShapeDtypeStruct((tokens, width), LOW), jax.ShapeDtypeStruct((8, width), FULL)
        ],
        compiler_params=params(),
        name="combine_backward",
    )(col, held, x1, cotangent, norm_params)


def expert_kernel(
    rows_ref, g_ref, up_ref, down_ref, router_ref, own_ref, count_ref,
    back_ref, out_ref, upg_ref, downg_ref, router_grad_ref,
    out_sum, back_sum, og_ref, gate_ref, probs_ref,
):
    step = pl.program_id(0)
    rows = rows_ref[...]

    @pl.when(step == 0)
    def _():
        logits = nt(rows, router_ref[...]) + count_ref[...]
        top = jnp.max(logits, axis=-1, keepdims=True)
        weights = jnp.exp(logits - top)
        probs = weights / jnp.sum(weights, axis=-1, keepdims=True)
        gate = jnp.sum(probs * own_ref[...], axis=-1, keepdims=True)
        probs_ref[...] = probs
        gate_ref[...] = gate
        og_ref[...] = (gate * g_ref[...].astype(FULL)).astype(LOW)
        out_sum[...] = jnp.zeros_like(out_sum)
        back_sum[...] = jnp.zeros_like(back_sum)

    og = og_ref[...]
    up, down = up_ref[0], down_ref[0]
    hidden = nn(rows, up)
    slope = (2.0 / jnp.pi) ** 0.5
    square = hidden * hidden
    bend = jnp.tanh(slope * (hidden + 0.044715 * (square * hidden)))
    act = (0.5 * hidden * (1.0 + bend)).astype(LOW)
    out_sum[...] += nn(act, down)
    act_grad = nt(og, down)
    inner = slope * (1.0 + (3.0 * 0.044715) * square)
    curve = 0.5 * (1.0 + bend) + 0.5 * hidden * (1.0 - bend * bend) * inner
    hidden_grad = (curve * act_grad).astype(LOW)
    back_sum[...] += nt(hidden_grad, up)
    upg_ref[0] = tn(rows, hidden_grad).astype(LOW)
    downg_ref[0] = tn(act, og).astype(LOW)

    @pl.when(step == pl.num_programs(0) - 1)
    def _():
        out = out_sum[...].astype(LOW).astype(FULL)
        gate, probs = gate_ref[...], probs_ref[...]
        out_ref[...] = (gate * out).astype(LOW)
        gate_grad = jnp.sum(g_ref[...].astype(FULL) * out, axis=-1, keepdims=True)
        logit_grad = (gate_grad * (probs * (own_ref[...] - gate))).astype(LOW)
        back = back_sum[...].astype(LOW).astype(FULL) + nn(logit_grad, router_ref[...])
        back_ref[...] = back.astype(LOW)
        router_grad_ref[...] = tn(logit_grad, rows)


def experts_both_ways(rows, g_rows, up, down, router_low, own):
    slots, width = rows.shape
    parts, _, units = up.shape
    experts = router_low.shape[0]
    lanes = 128
    router_wide = jnp.zeros((lanes, width), LOW).at[:experts].set(router_low)
    lane = jnp.arange(lanes, dtype=jnp.int32)[None, :]
    own_row = jnp.where(lane == own, 1.0, 0.0).astype(FULL)
    closed = jnp.where(lane < experts, 0.0, -1e30).astype(FULL)
    wide_spec = whole((slots, width))
    return pl.pallas_call(
        expert_kernel,
        grid=(parts,),
        in_specs=[
            wide_spec, wide_spec, lead((1, width, units)), lead((1, units, width)),
            whole((lanes, width)), whole((1, lanes)), whole((1, lanes)),
        ],
        out_specs=[
            wide_spec, wide_spec, lead((1, width, units)), lead((1, units, width)),
            whole((lanes, width)),
        ],
        out_shape=[
            jax.ShapeDtypeStruct((slots, width), LOW),
            jax.ShapeDtypeStruct((slots, width), LOW),
            jax.ShapeDtypeStruct(up.shape, LOW),
            jax.ShapeDtypeStruct(down.shape, LOW),
            jax.ShapeDtypeStruct((lanes, width), FULL),
        ],
        scratch_shapes=[
            pltpu.VMEM((slots, width), FULL), pltpu.VMEM((slots, width), FULL),
            pltpu.VMEM((slots, width), LOW), pltpu.VMEM((slots, 1), FULL),
            pltpu.VMEM((slots, lanes), FULL),
        ],
        compiler_params=params(),
        name="experts_both_ways",
    )(rows, g_rows, up, down, router_wide, own_row, closed)


def gather_kernel(cuts, x_ref, out_ref, local_sem, send_sem, recv_sem):
    me, near, far, corner = partners()
    greet(("head", near), ("head", far))
    size = x_ref.shape[0] // cuts

    def remote(src, dst, lane, index, other):
        return pltpu.make_async_remote_copy(
            src_ref=src, dst_ref=dst, send_sem=send_sem.at[lane, index],
            recv_sem=recv_sem.at[lane, index], device_id={"head": other}, device_id_type=MESH,
        )

    local = pltpu.make_async_copy(x_ref, out_ref.at[me], local_sem)
    local.start()
    across, beside, onward = [], [], []
    for cut in range(cuts):
        span = pl.ds(cut * size, size)
        across.append(remote(x_ref.at[span], out_ref.at[me, span], 0, cut, far))
        across[-1].start()
    for cut in range(cuts):
        span = pl.ds(cut * size, size)
        beside.append(remote(x_ref.at[span], out_ref.at[me, span], 1, cut, near))
        beside[-1].start()
    for cut in range(cuts):
        span = pl.ds(cut * size, size)
        across[cut].wait_recv()
        onward.append(remote(out_ref.at[far, span], out_ref.at[far, span], 2, cut, near))
        onward[-1].start()
    for cut in range(cuts):
        across[cut].wait_send()
        beside[cut].wait()
        onward[cut].wait()
    local.wait()


def head_gather(x, collective_id, cuts=4):
    return pl.pallas_call(
        functools.partial(gather_kernel, cuts),
        in_specs=[pl.BlockSpec(memory_space=pl.ANY)],
        out_specs=pl.BlockSpec(memory_space=pl.ANY),
        out_shape=jax.ShapeDtypeStruct((4,) + x.shape, x.dtype),
        scratch_shapes=[
            pltpu.SemaphoreType.DMA, pltpu.SemaphoreType.DMA((3, cuts)),
            pltpu.SemaphoreType.DMA((3, cuts)),
        ],
        compiler_params=params(collective_id=collective_id, has_side_effects=True),
        name="head_gather",
    )(x)


def body(
    patches, cotangent, expert_ids, slot_pos, owners,
    tile_master, tile_first, tile_second,
    expert_up, up_first, up_second,
    expert_down, down_first, down_second,
    router, router_first, router_second,
    norm_params, norm_first, norm_second,
):
    tok_rows, width = patches.shape
    experts = router.shape[0]
    capacity = tok_rows // experts
    dp_count = lax.axis_size("dp")
    head_count = lax.axis_size("head")
    me_head = lax.axis_index("head")
    me_dp = lax.axis_index("dp")
    images = tok_rows // PATCH
    share = capacity // head_count
    own_slots = experts * share
    slot_count = tile_master.shape[0]

    owner_row = owners[0]
    tile_count = owner_row.shape[0]
    order_index = jnp.arange(tile_count, dtype=jnp.int32)
    same_owner = owner_row[:, None] == owner_row[None, :]
    earlier = order_index[None, :] < order_index[:, None]
    tile_rank = jnp.sum(jnp.where(same_owner & earlier, 1, 0), axis=1).astype(jnp.int32)
    tile_place = owner_row * slot_count + tile_rank
    src = (tile_place[:, None] * TILE + jnp.arange(TILE, dtype=jnp.int32)[None, :]).reshape(-1)

    up_low = expert_up[0].astype(LOW)
    down_low = expert_down[0].astype(LOW)
    up_all = lax.all_gather(up_low, "head", axis=0)
    down_all = lax.all_gather(down_low, "head", axis=0)

    ids, pos = expert_ids.T, slot_pos.T
    holder = lax.div(pos, share)
    col = holder * (own_slots - share) + ids * share + pos
    col = jnp.where(pos < capacity, col, tok_rows)
    col_rows = (col - me_head * own_slots).reshape(2, images, PATCH).transpose(1, 0, 2)
    col = col.T

    def to_experts(rows):
        rows = rows.reshape(experts, share, width)
        return lax.all_to_all(rows, "dp", 0, 0, tiled=True).reshape(own_slots, width)

    by_image = (images, PATCH, width)
    x_images = patches.reshape(by_image)
    w, xn, g_sent = prepare(
        tile_master.reshape(slot_count * TILE, width), x_images, cotangent.reshape(by_image),
        norm_params, src[:, None], col_rows, own_slots, dp_count,
    )
    g_rows = to_experts(g_sent)
    lse, sent, *saved, x1 = attention_forward(xn, w, x_images, norm_params, col_rows, own_slots)
    x1 = x1.reshape(tok_rows, width)
    rows = to_experts(sent)
    back, out, up_part, down_part, router_part = experts_both_ways(
        rows, g_rows, up_all, down_all, router.astype(LOW), me_dp
    )
    back_all = head_gather(to_experts(back), 3)
    x1_grad, second_sums = combine_backward(col, back_all, x1, cotangent, norm_params)
    small_rows = -(-(experts + 4) // 16) * 16
    small = jnp.concatenate(
        [
            router_part[:experts], jnp.zeros((2, width), FULL),
            second_sums[:2] * (1.0 / head_count),
            jnp.zeros((small_rows - experts - 4, width), FULL),
        ]
    )
    owned_grad, small, block_out, input_low = attention_backward(
        experts, dp_count, slot_count * TILE,
        x1_grad.reshape(by_image), w, xn, saved, lse, src[None, :], norm_params, small,
        col.reshape(images, PATCH, 2), x_images, to_experts(out), x1.reshape(by_image),
    )
    block_out = block_out.reshape(tok_rows, width)
    owned_grad = owned_grad.reshape(slot_count, TILE, width)
    input_grad = input_low.reshape(tok_rows, width).astype(FULL)

    up_grad = lax.psum_scatter(up_part, "head", scatter_dimension=0).astype(FULL)
    down_grad = lax.psum_scatter(down_part, "head", scatter_dimension=0).astype(FULL)
    router_total, norm_total = small[:experts], small[experts:experts + 4]

    tile_new, tile_first_new, tile_second_new = adam_update(
        tile_master, tile_first, tile_second, owned_grad, rate_attention, decay_factor
    )
    up_new, up_first_new, up_second_new = adam_update(
        expert_up, up_first, up_second, up_grad[None], rate_up, decay_factor
    )
    down_new, down_first_new, down_second_new = adam_update(
        expert_down, down_first, down_second, down_grad[None], rate_down, decay_factor
    )
    router_new, router_first_new, router_second_new = adam_update(
        router, router_first, router_second, router_total, rate_router, decay_factor
    )
    norm_new, norm_first_new, norm_second_all = adam_update(
        norm_params, norm_first, norm_second, norm_total, rate_norm, 0.0
    )
    return (
        block_out,
        input_grad,
        tile_new,
        tile_first_new,
        tile_second_new,
        tile_new.astype(LOW),
        up_new,
        up_first_new,
        up_second_new,
        up_new.astype(LOW),
        down_new,
        down_first_new,
        down_second_new,
        down_new.astype(LOW),
        router_new,
        router_first_new,
        router_second_new,
        norm_new,
        norm_first_new,
        norm_second_all[:2],
        norm_second_all[2:],
    )


def solution(mesh):
    row = P("dp", None)
    tiles = P(("dp", "head"), None, None)
    up = P("dp", None, "head")
    down = P("dp", "head", None)
    in_specs = (
        row, row, row, row, P("head", None), tiles, tiles, tiles,
        up, up, up, down, down, down, P(), P(), P(), P(), P(), P(),
    )
    out_specs = (
        row, row, tiles, tiles, tiles, tiles, up, up, up, up, down, down, down, down,
        P(), P(), P(), P(), P(), P(), P(),
    )
    return jax.shard_map(body, mesh=mesh, in_specs=in_specs, out_specs=out_specs, check_vma=False)
```

```python
import functools

import jax
import jax.numpy as jnp
from jax import lax
from jax.experimental import pallas as pl
from jax.experimental.pallas import tpu as pltpu
from jax.sharding import PartitionSpec as P

HD = 64
PATCH = 576
TILE = 8
STEP = 10

eps_norm = 1e-06
beta_one = 0.9
beta_two = 0.999
adam_eps = 1e-08
rate_attention = 0.12
rate_up = 0.08
rate_down = 0.3
rate_router = 0.05
rate_norm = 0.4
decay_factor = 0.1

LOW = jnp.bfloat16
FULL = jnp.float32
MESH = pl.DeviceIdType.MESH
VMEM_BYTES = 60 * 1024 * 1024


def adam_update(weight, moment_one, moment_two, gradient, step_rate, weight_decay):
    moment_one = beta_one * moment_one + (1.0 - beta_one) * gradient
    moment_two = beta_two * moment_two + (1.0 - beta_two) * gradient * gradient
    fixed_one = moment_one / (1.0 - beta_one**STEP)
    fixed_two = moment_two / (1.0 - beta_two**STEP)
    weight = weight - step_rate * (
        fixed_one / (jnp.sqrt(fixed_two) + adam_eps) + weight_decay * weight
    )
    return (weight, moment_one, moment_two)


def nn(left, right):
    return lax.dot_general(left, right, (((1,), (0,)), ((), ())), preferred_element_type=FULL)


def nt(left, right):
    return lax.dot_general(left, right, (((1,), (1,)), ((), ())), preferred_element_type=FULL)


def tn(left, right):
    return lax.dot_general(left, right, (((0,), (0,)), ((), ())), preferred_element_type=FULL)


def params(**more):
    return pltpu.CompilerParams(vmem_limit_bytes=VMEM_BYTES, **more)


def whole(shape):
    return pl.BlockSpec(shape, lambda *_: (0,) * len(shape))


def lead(shape):
    return pl.BlockSpec(shape, lambda i: (i,) + (0,) * (len(shape) - 1))


def normalise(values):
    average = jnp.mean(values, axis=-1, keepdims=True)
    centred = values - average
    variance = jnp.mean(centred * centred, axis=-1, keepdims=True)
    scale = lax.rsqrt(variance + eps_norm)
    return centred * scale, scale


def norm_back(normal, scale, gain, upstream):
    inner = upstream * gain
    mean_inner = jnp.mean(inner, axis=-1, keepdims=True)
    mean_cross = jnp.mean(inner * normal, axis=-1, keepdims=True)
    result = scale * (inner - mean_inner - normal * mean_cross)
    gain_sum = jnp.sum(upstream * normal, axis=0, keepdims=True)
    shift_sum = jnp.sum(upstream, axis=0, keepdims=True)
    return result, gain_sum, shift_sum


def one_hot(condition):
    return jnp.where(condition, 1.0, 0.0).astype(LOW)


def remote(src, dst, sends, recvs, index, axis, other):
    return pltpu.make_async_remote_copy(
        src_ref=src, dst_ref=dst, send_sem=sends.at[index], recv_sem=recvs.at[index],
        device_id={axis: other}, device_id_type=MESH,
    )


def greet(*others):
    barrier = pltpu.get_barrier_semaphore()
    for axis, other in others:
        pl.semaphore_signal(barrier, inc=1, device_id={axis: other}, device_id_type=MESH)
    pl.semaphore_wait(barrier, len(others))


def partners():
    me = lax.axis_index("head")
    near = me + 1 - 2 * lax.rem(me, 2)
    far = lax.rem(me + 2, 4)
    corner = lax.rem(near + 2, 4)
    return me, near, far, corner


class LineGather:
    def __init__(self, held, up_send, up_recv, down_send, down_recv, pair_send, pair_recv):
        self.held = held
        self.length = held.shape[0] // 2
        self.sems = ((up_send, up_recv), (down_send, down_recv), (pair_send, pair_recv))
        me = lax.axis_index("dp")
        self.place, self.side = me // 2, lax.rem(me, 2)
        self.above = lax.rem(self.place + 1, self.length) * 2 + self.side
        self.below = lax.rem(self.place + self.length - 1, self.length) * 2 + self.side
        self.other = self.place * 2 + 1 - self.side

    def neighbours(self):
        return ("dp", self.above), ("dp", self.below), ("dp", self.other)

    def copy(self, way, origin, side=None):
        index = origin * 2 + (self.side if side is None else side)
        target = (self.above, self.below, self.other)[way]
        block = self.held.at[index]
        return remote(block, block, *self.sems[way], origin, "dp", target)

    def pass_on(self, origin, up, down):
        @pl.when(up & (self.place < self.length - 1))
        def _():
            self.copy(0, origin).start()

        @pl.when(down & (self.place > 0))
        def _():
            self.copy(1, origin).start()

        self.copy(2, origin).start()

    def start(self):
        self.pass_on(self.place, True, True)

    def step(self, k):
        low, high = self.place - k, self.place + k

        @pl.when(low >= 0)
        def _():
            self.copy(0, low).wait_recv()
            self.pass_on(low, True, False)

        @pl.when(high < self.length)
        def _():
            self.copy(1, high).wait_recv()
            self.pass_on(high, False, True)

    def finish(self):
        @pl.loop(0, self.length)
        def _(origin):
            self.copy(2, origin).wait_recv()
            self.copy(2, origin).wait_send()

            @pl.when((origin <= self.place) & (self.place < self.length - 1))
            def _():
                self.copy(0, origin).wait_send()

            @pl.when((origin >= self.place) & (self.place > 0))
            def _():
                self.copy(1, origin).wait_send()


class ImageSum:
    def __init__(self, stage, corner_in, near_in, passed, mine, far_in, sends, recvs):
        self.stage, self.corner_in, self.near_in = stage, corner_in, near_in
        self.passed, self.mine, self.far_in = passed, mine, far_in
        self.sends, self.recvs = sends, recvs
        self.me, self.near, self.far, self.corner = partners()
        self.core = lax.rem(self.me, 2)

    def image(self, turn):
        base = self.me - self.core
        other = lax.rem(base + 2, 4)
        return jnp.where(turn < 2, other, base - 2) + turn

    def to_corner(self):
        return remote(
            self.stage.at[0], self.corner_in, self.sends, self.recvs, 0, "head", self.near
        )

    def to_near(self):
        return remote(
            self.stage.at[1], self.near_in, self.sends, self.recvs, 1, "head", self.near
        )

    def to_far(self):
        return remote(self.passed, self.far_in, self.sends, self.recvs, 2, "head", self.far)

    def give(self, turn, part):
        theirs = lax.rem(turn, 2) != self.core

        @pl.when((turn < 2) & theirs)
        def _():
            self.stage[0] = part.astype(LOW)
            self.to_corner().start()

        @pl.when((turn >= 2) & theirs)
        def _():
            self.stage[1] = part.astype(LOW)
            self.to_near().start()

        @pl.when((turn < 2) & ~theirs)
        def _():
            self.to_corner().wait_recv()
            self.passed[...] = (part + self.corner_in[...].astype(FULL)).astype(LOW)
            self.to_far().start()

        @pl.when((turn >= 2) & ~theirs)
        def _():
            self.mine[...] = part

    def result(self):
        self.to_near().wait_recv()
        self.to_far().wait_recv()
        return self.mine[...] + self.near_in[...].astype(FULL) + self.far_in[...].astype(FULL)

    def finish(self):
        self.to_corner().wait_send()
        self.to_near().wait_send()
        self.to_far().wait_send()


def image_sum_scratch(width):
    block = pltpu.VMEM((PATCH, width), LOW)
    return [
        pltpu.VMEM((2, PATCH, width), LOW), block, block, block,
        pltpu.VMEM((PATCH, width), FULL), block,
        pltpu.SemaphoreType.DMA((3,)), pltpu.SemaphoreType.DMA((3,)),
    ]


class LineScatter:
    def __init__(
        self, blocks, out, pair_in, up_in, down_in, total,
        up_send, up_recv, down_send, down_recv, pair_send, pair_recv,
    ):
        self.blocks, self.out, self.total = blocks, out, total
        self.arrived = (up_in, down_in, pair_in)
        self.sems = ((up_send, up_recv), (down_send, down_recv), (pair_send, pair_recv))
        self.length = blocks.shape[0] // 2
        me = lax.axis_index("dp")
        self.place, self.side = me // 2, lax.rem(me, 2)
        self.targets = (
            lax.rem(self.place + 1, self.length) * 2 + self.side,
            lax.rem(self.place + self.length - 1, self.length) * 2 + self.side,
            self.place * 2 + 1 - self.side,
        )

    def copy(self, way, block):
        source = (
            self.blocks.at[block * 2 + 1 - self.side] if way == 2 else self.total.at[block]
        )
        return remote(
            source, self.arrived[way].at[block], *self.sems[way], block, "dp", self.targets[way]
        )

    def start(self):
        @pl.loop(0, self.length)
        def _(turn):
            distance = self.length - 1 - turn

            @pl.when(self.place + distance < self.length)
            def _():
                self.copy(2, self.place + distance).start()

            @pl.when((self.place >= distance) & (distance > 0))
            def _():
                self.copy(2, self.place - distance).start()

    def pair_sum(self, block):
        self.copy(2, block).wait_recv()
        own = self.blocks[block * 2 + self.side].astype(FULL)
        return own + self.arrived[2][block].astype(FULL)

    def forward(self, way, block, first):
        both = self.pair_sum(block)

        @pl.when(first)
        def _():
            self.total[block] = both.astype(LOW)

        @pl.when(~first)
        def _():
            self.copy(way, block).wait_recv()
            self.total[block] = (both + self.arrived[way][block].astype(FULL)).astype(LOW)

        self.copy(way, block).start()

    def step(self, distance):
        @pl.when(self.place + distance < self.length)
        def _():
            self.forward(0, self.place + distance, self.place == 0)

        @pl.when(self.place >= distance)
        def _():
            self.forward(1, self.place - distance, self.place == self.length - 1)

    def result(self):
        self.out[...] = self.pair_sum(self.place)

        @pl.when(self.place > 0)
        def _():
            self.copy(0, self.place).wait_recv()
            self.out[...] += self.arrived[0][self.place].astype(FULL)

        @pl.when(self.place < self.length - 1)
        def _():
            self.copy(1, self.place).wait_recv()
            self.out[...] += self.arrived[1][self.place].astype(FULL)

    def finish(self):
        @pl.loop(0, self.length)
        def _(block):
            self.copy(2, block).wait_send()

            @pl.when(block > self.place)
            def _():
                self.copy(0, block).wait_send()

            @pl.when(block < self.place)
            def _():
                self.copy(1, block).wait_send()


def line_scatter_scratch(dp_count, rows, width):
    line = dp_count // 2
    return [pltpu.VMEM((line, rows, width), LOW)] * 4 + [pltpu.SemaphoreType.DMA((line,))] * 6


class SmallSum:
    def __init__(self, flat, head_in, dp_in, done, head_send, head_recv, dp_send, dp_recv):
        self.flat, self.head_in, self.dp_in, self.done = flat, head_in, dp_in, done
        self.head_sems, self.dp_sems = (head_send, head_recv), (dp_send, dp_recv)
        self.me, *self.others = partners()
        self.place, self.count = lax.axis_index("dp"), dp_in.shape[0]

    def to_head(self, lane):
        other = self.others[lane]
        return remote(
            self.flat.at[other], self.head_in.at[self.me], *self.head_sems, lane, "head", other
        )

    def back_head(self, lane):
        block = self.done.at[self.me]
        return remote(block, block, *self.head_sems, 3 + lane, "head", self.others[lane])

    def to_dp(self, shift):
        block = self.dp_in.at[self.place]
        other = lax.rem(self.place + shift, self.count)
        return remote(block, block, *self.dp_sems, shift, "dp", other)

    def start(self, value):
        groups, rows, lanes = self.flat.shape
        flat = jnp.concatenate(
            [value[:, at:at + lanes] for at in range(0, value.shape[1], lanes)], axis=0
        )
        for group in range(groups):
            self.flat[group] = flat[group * rows:(group + 1) * rows]
        for lane in range(3):
            self.to_head(lane).start()
        self.head_in[self.me] = self.flat[self.me]

    def across(self):
        for lane in range(3):
            self.to_head(lane).wait_recv()
        total = self.head_in[0]
        for head in range(1, self.head_in.shape[0]):
            total = total + self.head_in[head]
        self.dp_in[self.place] = total

        @pl.loop(1, self.count)
        def _(shift):
            self.to_dp(shift).start()

    def back(self):
        @pl.loop(1, self.count)
        def _(shift):
            self.to_dp(shift).wait_recv()

        total = lax.fori_loop(
            1, self.count, lambda at, so_far: so_far + self.dp_in[at], self.dp_in[0]
        )
        self.done[self.me] = total
        for lane in range(3):
            self.back_head(lane).start()

    def result(self, out):
        for lane in range(3):
            self.back_head(lane).wait_recv()
        flat = jnp.concatenate([self.done[group] for group in range(self.done.shape[0])], axis=0)
        rows, width = out.shape
        lanes = flat.shape[1]
        for at in range(width // lanes):
            out[:, at * lanes:(at + 1) * lanes] = flat[at * rows:(at + 1) * rows]

    def finish(self):
        for lane in range(3):
            self.to_head(lane).wait_send()
            self.back_head(lane).wait_send()

        @pl.loop(1, self.count)
        def _(shift):
            self.to_dp(shift).wait_send()


def small_sum_scratch(rows, width, dp_count):
    block = (rows * width // 128 // 4, 128)
    return [
        pltpu.VMEM((4,) + block, FULL), pltpu.VMEM((4,) + block, FULL),
        pltpu.VMEM((dp_count,) + block, FULL), pltpu.VMEM((4,) + block, FULL),
        pltpu.SemaphoreType.DMA((6,)), pltpu.SemaphoreType.DMA((6,)),
        pltpu.SemaphoreType.DMA((dp_count,)), pltpu.SemaphoreType.DMA((dp_count,)),
    ]


GATHER_CUTS = 4


class ImageGather:
    def __init__(self, held, sends, recvs):
        self.held, self.sends, self.recvs = held, sends, recvs
        self.me, self.near, self.far, self.corner = partners()
        self.size = held.shape[1] // GATHER_CUTS

    def piece(self, image, cut, lane, other):
        span = pl.ds(cut * self.size, self.size)
        block = self.held.at[image, span]
        return remote(block, block, self.sends, self.recvs, lane * GATHER_CUTS + cut, "head", other)

    def start(self):
        for cut in range(GATHER_CUTS):
            self.piece(self.me, cut, 0, self.far).start()
        for cut in range(GATHER_CUTS):
            self.piece(self.me, cut, 1, self.near).start()

    def wait_near(self):
        for cut in range(GATHER_CUTS):
            self.piece(self.me, cut, 1, self.near).wait_recv()

    def wait_far(self):
        for cut in range(GATHER_CUTS):
            self.piece(self.me, cut, 0, self.far).wait_recv()
            self.piece(self.far, cut, 2, self.near).start()

    def wait_corner(self):
        for cut in range(GATHER_CUTS):
            self.piece(self.far, cut, 2, self.near).wait_recv()

    def finish(self):
        for cut in range(GATHER_CUTS):
            self.piece(self.me, cut, 0, self.far).wait_send()
            self.piece(self.me, cut, 1, self.near).wait_send()
            self.piece(self.far, cut, 2, self.near).wait_send()


def image_gather_sems():
    return [pltpu.SemaphoreType.DMA((3 * GATHER_CUTS,)), pltpu.SemaphoreType.DMA((3 * GATHER_CUTS,))]


class Slots:
    def __init__(self, count, share):
        self.count, self.share = count, share
        self.big = -(-share // 16) * 16
        rest = 2 * share - self.big
        self.small = rest if rest > 0 and rest % 16 == 0 else self.big
        self.more = self.big - self.small
        self.both = self.big + self.small
        self.rows = count // 2 * self.both
        self.turns = count // 4
        self.phase_rows = self.turns * 2 * self.both

    def size(self, source, head):
        return self.small + self.more * ((head + source + 1) % 2)

    def packed(self, source, head):
        return (source // 2) * self.both + (source % 2) * self.size(0, head)

    def row(self, source, head, shift):
        first = self.size(source, 0) * (head % 2)
        group = (head // 2) * self.turns * self.both + self.turns * first
        return (
            (shift // self.turns) * self.phase_rows + group
            + (shift % self.turns) * self.size(source, head)
        )

    def holder(self, source, slot):
        pair, within = slot // self.both, slot % self.both
        first = self.size(source, 0)
        second = jnp.where(within >= first, 1, 0)
        return 2 * pair + second, within - second * first

    def span(self, start, extra):
        if extra:
            return pl.ds(pl.multiple_of(start + self.small, 16), self.more)
        return pl.ds(pl.multiple_of(start, 16), self.small)

    def each(self, is_big, make, action):
        getattr(make(False), action)()
        if self.more:
            @pl.when(is_big)
            def _():
                getattr(make(True), action)()


class SlotExchange:
    def __init__(self, slots, sent, rows, sends, recvs, local_sems):
        self.slots, self.sent, self.rows = slots, sent, rows
        self.sems, self.local_sems = (sends, recvs), local_sems
        self.place, self.head = lax.axis_index("dp"), lax.axis_index("head")

    def out(self, shift, action):
        slots = self.slots
        expert = lax.rem(self.place + shift, slots.count)
        mine = slots.size(self.place, self.head)
        at, to = expert * mine, slots.packed(self.place, self.head)
        slots.each(mine > slots.small, lambda extra: remote(
            self.sent.at[slots.span(at, extra)], self.rows.at[slots.span(to, extra)],
            *self.sems, 2 * shift + int(extra), "dp", expert,
        ), action)

    def into(self, shift):
        slots = self.slots
        source = lax.rem(self.place + slots.count - shift, slots.count)
        size = slots.size(source, self.head)
        to = slots.packed(source, self.head)
        slots.each(size > slots.small, lambda extra: remote(
            self.sent.at[slots.span(0, extra)], self.rows.at[slots.span(to, extra)],
            *self.sems, 2 * shift + int(extra), "dp", source,
        ), "wait_recv")

    def own(self, action):
        slots = self.slots
        mine = slots.size(self.place, self.head)
        at, to = self.place * mine, slots.packed(self.place, self.head)
        slots.each(mine > slots.small, lambda extra: pltpu.make_async_copy(
            self.sent.at[slots.span(at, extra)], self.rows.at[slots.span(to, extra)],
            self.local_sems.at[int(extra)],
        ), action)

    def start(self):
        @pl.loop(1, self.slots.count)
        def _(shift):
            self.out(shift, "start")

        self.own("start")

    def finish(self):
        @pl.loop(1, self.slots.count)
        def _(shift):
            self.into(shift)
            self.out(shift, "wait_send")

        self.own("wait")


def slot_exchange_sems(count):
    return [
        pltpu.SemaphoreType.DMA((2 * count,)), pltpu.SemaphoreType.DMA((2 * count,)),
        pltpu.SemaphoreType.DMA((2,)),
    ]


class ReturnGather:
    def __init__(self, slots, rows, held, sends, recvs, local_sems):
        self.slots, self.rows, self.held = slots, rows, held
        self.sems, self.local_sems = (sends, recvs), local_sems
        self.place = lax.axis_index("dp")
        self.me, self.near, self.far, self.corner = partners()

    def out(self, shift, action):
        slots = self.slots
        source = lax.rem(self.place + shift, slots.count)
        size = slots.size(source, self.me)
        at, to = slots.packed(source, self.me), slots.row(source, self.me, shift)
        slots.each(size > slots.small, lambda extra: remote(
            self.rows.at[slots.span(at, extra)], self.held.at[slots.span(to, extra)],
            *self.sems, 2 * shift + int(extra), "dp", source,
        ), action)

    def own(self, action):
        slots = self.slots
        size = slots.size(self.place, self.me)
        at, to = slots.packed(self.place, self.me), slots.row(self.place, self.me, 0)
        slots.each(size > slots.small, lambda extra: pltpu.make_async_copy(
            self.rows.at[slots.span(at, extra)], self.held.at[slots.span(to, extra)],
            self.local_sems.at[int(extra)],
        ), action)

    def block(self, lane, head, shift, axis, other, action):
        slots = self.slots
        size = slots.size(self.place, head)
        to = slots.row(self.place, head, shift)

        def make(extra):
            block = self.held.at[slots.span(to, extra)]
            index = 2 * (lane * slots.count + shift) + int(extra)
            return remote(block, block, *self.sems, index, axis, other)

        slots.each(size > slots.small, make, action)

    def start(self):
        @pl.loop(1, self.slots.count)
        def _(shift):
            self.out(shift, "start")

        self.own("start")

    def relay(self, shift):
        @pl.when(shift == 0)
        def _():
            self.own("wait")

        @pl.when(shift > 0)
        def _():
            expert = lax.rem(self.place + self.slots.count - shift, self.slots.count)
            self.block(0, self.me, shift, "dp", expert, "wait_recv")

        self.block(1, self.me, shift, "head", self.far, "start")
        self.block(2, self.me, shift, "head", self.near, "start")

    def forward(self, shift):
        self.block(1, self.far, shift, "head", self.far, "wait_recv")
        self.block(3, self.far, shift, "head", self.near, "start")

    def rest(self, shift):
        self.block(2, self.near, shift, "head", self.near, "wait_recv")
        self.block(3, self.corner, shift, "head", self.near, "wait_recv")

    def of_phase(self, phase, action):
        @pl.loop(0, self.slots.turns)
        def _(turn):
            action(phase * self.slots.turns + turn)

    def finish(self):
        @pl.loop(0, self.slots.count)
        def _(shift):
            @pl.when(shift > 0)
            def _():
                self.out(shift, "wait_send")

            self.block(1, self.me, shift, "head", self.far, "wait_send")
            self.block(2, self.me, shift, "head", self.near, "wait_send")
            self.block(3, self.far, shift, "head", self.near, "wait_send")


def return_gather_sems(count):
    return [
        pltpu.SemaphoreType.DMA((8 * count,)), pltpu.SemaphoreType.DMA((8 * count,)),
        pltpu.SemaphoreType.DMA((2,)),
    ]


def greet_all(heads, dp_count):
    barrier = pltpu.get_barrier_semaphore()
    place = lax.axis_index("dp")
    for other in heads:
        pl.semaphore_signal(barrier, inc=1, device_id={"head": other}, device_id_type=MESH)

    @pl.loop(1, dp_count)
    def _(shift):
        other = lax.rem(place + shift, dp_count)
        pl.semaphore_signal(barrier, inc=1, device_id={"dp": other}, device_id_type=MESH)

    pl.semaphore_wait(barrier, len(heads) + dp_count - 1)


ANYWHERE = pl.BlockSpec(memory_space=pl.ANY)
INSIDE = pl.BlockSpec(memory_space=pltpu.VMEM)


def prepare_kernel(
    tile_ref, x_ref, g_ref, norm_ref, src_ref, col_ref, up_ref,
    w_ref, xn_ref, sent_ref, up_out,
    held, sent_sum, local_sem, *sems,
):
    images = x_ref.shape[0]
    gather = LineGather(held, *sems[:6])
    spread = ImageGather(up_out, *sems[6:])
    own = pltpu.make_async_copy(up_ref, up_out.at[spread.me], local_sem)
    own.start()
    me = lax.axis_index("dp")
    held[me] = tile_ref[...].astype(LOW)
    greet(*gather.neighbours(), ("head", spread.near), ("head", spread.far))
    gather.start()
    own.wait()
    spread.start()

    def image_step(image):
        normal, _ = normalise(x_ref[image].astype(FULL))
        xn_ref[image] = (normal * norm_ref[0:1, :] + norm_ref[1:2, :]).astype(LOW)
        shape = (sent_ref.shape[0], PATCH)
        slots = lax.broadcasted_iota(jnp.int32, shape, 0)
        col = col_ref[image]
        pick = one_hot((slots == col[0:1, :]) | (slots == col[1:2, :]))
        sent_sum[...] += nn(pick, g_ref[image])

    sent_sum[...] = jnp.zeros_like(sent_sum)
    steps = gather.length - 1

    @pl.loop(0, max(steps, (images + 1) // 2))
    def _(turn):
        @pl.loop(2 * turn, jnp.minimum(2 * turn + 2, images))
        def _(image):
            image_step(image)

        @pl.when(turn < steps)
        def _():
            gather.step(turn + 1)

    sent_ref[...] = sent_sum[...].astype(LOW)
    gather.finish()
    rows = w_ref.shape[0] // 4
    blocks, depth, width = held.shape
    for part in range(4):
        block = pl.ds(part * rows, rows)
        lanes = lax.broadcasted_iota(jnp.int32, (rows, blocks * depth), 1)
        pick = one_hot(lanes == src_ref[block, :])
        w_ref[block, :] = nn(pick, held[...].reshape(blocks * depth, width)).astype(LOW)
    spread.wait_far()
    spread.wait_near()
    spread.wait_corner()
    spread.finish()


def prepare(tiles, patches, cotangent, norm_params, src_col, col_rows, up_low, slots, dp_count):
    images, _, width = patches.shape
    line = dp_count // 2
    return pl.pallas_call(
        prepare_kernel,
        in_specs=[INSIDE] * 6 + [ANYWHERE],
        out_specs=[INSIDE] * 3 + [ANYWHERE],
        out_shape=[
            jax.ShapeDtypeStruct((src_col.shape[0], width), LOW),
            jax.ShapeDtypeStruct(patches.shape, LOW),
            jax.ShapeDtypeStruct((slots, width), LOW),
            jax.ShapeDtypeStruct((4,) + up_low.shape, LOW),
        ],
        scratch_shapes=[
            pltpu.VMEM((dp_count,) + tiles.shape, LOW), pltpu.VMEM((slots, width), FULL),
            pltpu.SemaphoreType.DMA,
        ] + [pltpu.SemaphoreType.DMA((line,))] * 6 + image_gather_sems(),
        compiler_params=params(collective_id=0, has_side_effects=True),
        name="prepare",
    )(tiles, patches, cotangent, norm_params, src_col, col_rows, up_low)


def head_mask(shape, axis, head):
    return lax.broadcasted_iota(jnp.int32, shape, axis) // HD == head


def forward_kernel(
    slots,
    xn_ref, w_ref, norm_ref, col_ref, x_ref, g_sent_ref, down_ref,
    lse_ref, q_out, qt_out, k_out, kt_out, v_out, ot_out, x1_out, rows_out, g_rows_out, down_out,
    q_ref, qt_ref, k_ref, kt_ref, v_ref, ot_ref, x1_ref, own_ref, sent_ref, sent_sum,
    save_sems, own_sem, *exchange,
):
    images = xn_ref.shape[0]
    rows = w_ref.shape[0] // 4
    heads = rows // HD
    total_of = ImageSum(*exchange[:8])
    spread = ImageGather(x1_ref, *exchange[8:10])
    spread_down = ImageGather(down_out, *exchange[10:12])
    send_g = SlotExchange(slots, g_sent_ref, g_rows_out, *exchange[12:15])
    send_rows = SlotExchange(slots, sent_ref, rows_out, *exchange[15:])
    me, near, far, corner = partners()
    own = pltpu.make_async_copy(x_ref.at[me], own_ref, own_sem.at[0])
    own.start()
    own_down = pltpu.make_async_copy(down_ref, down_out.at[me], own_sem.at[1])
    own_down.start()
    greet_all((near, far), slots.count)
    send_g.start()
    kept = ((q_ref, q_out), (qt_ref, qt_out), (k_ref, k_out), (kt_ref, kt_out), (v_ref, v_out), (ot_ref, ot_out))
    shrink = HD ** (-0.5)

    def save(image):
        return [
            pltpu.make_async_copy(ref.at[image], out.at[image], save_sems.at[index, image])
            for index, (ref, out) in enumerate(kept)
        ]

    @pl.loop(0, images)
    def _(turn):
        image = total_of.image(turn)
        xn = xn_ref[image]
        wq, wk, wv, wo = (w_ref[pl.ds(part * rows, rows), :] for part in range(4))
        q_ref[image] = (nt(xn, wq) * shrink).astype(LOW)
        qt = (nt(wq, xn) * shrink).astype(LOW)
        qt_ref[image] = qt
        k = nt(xn, wk).astype(LOW)
        k_ref[image] = k
        kt_ref[image] = nt(wk, xn).astype(LOW)
        v_ref[image] = nt(xn, wv).astype(LOW)
        vt = nt(wv, xn).astype(LOW)
        mixed = []
        for head in range(heads):
            span = slice(head * HD, (head + 1) * HD)
            only = jnp.where(head_mask(qt.shape, 0, head), qt, jnp.zeros_like(qt))
            scores = nn(k, only)
            top = jnp.max(scores, axis=0, keepdims=True)
            weights = jnp.exp(scores - top)
            total = jnp.sum(weights, axis=0, keepdims=True)
            mixed.append(nn(vt[span], weights.astype(LOW)) / total)
            lse_ref[image, head:head + 1, :] = top + jnp.log(total)
        ot = jnp.concatenate(mixed, axis=0).astype(LOW)
        ot_ref[image] = ot
        total_of.give(turn, tn(ot, wo))
        for copy in save(image):
            copy.start()

    own.wait()
    x1_ref[me] = (own_ref[...].astype(FULL) + total_of.result()).astype(LOW)
    spread.start()
    sent_sum[...] = jnp.zeros_like(sent_sum)

    def place(image):
        normal, _ = normalise(x1_ref[image].astype(FULL))
        low = (normal * norm_ref[2:3, :] + norm_ref[3:4, :]).astype(LOW)
        slots = lax.broadcasted_iota(jnp.int32, (sent_ref.shape[0], PATCH), 0)
        col = col_ref[image]
        pick = one_hot((slots == col[0:1, :]) | (slots == col[1:2, :]))
        sent_sum[...] += nn(pick, low)

    place(me)
    spread.wait_near()
    place(near)
    spread.wait_far()
    place(far)
    spread.wait_corner()
    keep = pltpu.make_async_copy(x1_ref, x1_out, own_sem.at[0])
    keep.start()
    own_down.wait()
    spread_down.start()
    place(corner)
    sent_ref[...] = sent_sum[...].astype(LOW)
    send_rows.start()
    spread.finish()
    total_of.finish()
    keep.wait()
    send_g.finish()
    spread_down.wait_far()
    spread_down.wait_near()
    spread_down.wait_corner()
    spread_down.finish()
    send_rows.finish()

    @pl.loop(0, images)
    def _(image):
        for copy in save(image):
            copy.wait()


def attention_forward(slots, xn, w, norm_params, col_rows, patches, g_sent, down_low):
    images, _, width = patches.shape
    rows = w.shape[0] // 4
    flat, turned = (images, PATCH, rows), (images, rows, PATCH)
    saved = [flat, turned, flat, turned, flat, turned, patches.shape]
    outs = saved + [(slots.rows, width), (slots.rows, width), (4,) + down_low.shape]
    most = slots.count * slots.big
    return pl.pallas_call(
        functools.partial(forward_kernel, slots),
        in_specs=[INSIDE] * 4 + [ANYWHERE] * 3,
        out_specs=[INSIDE] + [ANYWHERE] * 10,
        out_shape=[jax.ShapeDtypeStruct((images, 8, PATCH), FULL)]
        + [jax.ShapeDtypeStruct(shape, LOW) for shape in outs],
        scratch_shapes=[pltpu.VMEM(shape, LOW) for shape in saved]
        + [
            pltpu.VMEM((PATCH, width), LOW), pltpu.VMEM((most, width), LOW),
            pltpu.VMEM((most, width), FULL),
            pltpu.SemaphoreType.DMA((6, images)), pltpu.SemaphoreType.DMA((2,)),
        ]
        + image_sum_scratch(width) + image_gather_sems() + image_gather_sems()
        + slot_exchange_sems(slots.count) + slot_exchange_sems(slots.count),
        compiler_params=params(collective_id=1, has_side_effects=True),
        name="attention_forward",
    )(xn, w, norm_params, col_rows, patches, g_sent, down_low)


def backward_kernel(
    experts, slots,
    x1g_ref, w_ref, xn_ref, q_ref, qt_ref, k_ref, kt_ref, v_ref, lse_ref, ot_ref, src_ref,
    norm_ref, small_ref, col_ref, x_ref, out_rows_ref, x1_ref,
    owned_ref, small_out, block_ref, input_out,
    grad_ref, own_ref, input_ref, padded_ref, out_ref, own_sem, *exchange,
):
    images = x1g_ref.shape[0]
    rows = w_ref.shape[0] // 4
    heads = rows // HD
    total_of = ImageSum(*exchange[:8])
    spread = ImageGather(input_ref, *exchange[8:10])
    back_out = ReturnGather(slots, out_rows_ref, out_ref, *exchange[10:13])
    weights_sum = LineScatter(padded_ref, owned_ref, *exchange[13:23])
    small_sum = SmallSum(*exchange[23:])
    me, near, far, corner = partners()
    dp_count = slots.count
    own = pltpu.make_async_copy(x_ref.at[me], own_ref, own_sem.at[0])
    own.start()
    x1_copy = pltpu.make_async_copy(x1_ref, block_ref, own_sem.at[1])
    x1_copy.start()
    greet_all((near, far, corner), dp_count)
    back_out.start()
    shrink = HD ** (-0.5)
    grad_ref[...] = jnp.zeros_like(grad_ref)

    @pl.loop(0, images)
    def _(turn):
        image = total_of.image(turn)
        wq, wk, wv, wo = (w_ref[pl.ds(part * rows, rows), :] for part in range(4))
        x1g, xn = x1g_ref[image], xn_ref[image]
        q, qt, k, kt = q_ref[image], qt_ref[image], k_ref[image], kt_ref[image]
        v, ot = v_ref[image], ot_ref[image]
        do = nt(x1g, wo).astype(LOW)
        dot = nt(wo, x1g).astype(LOW)
        product = dot.astype(FULL) * ot.astype(FULL)
        dqt, dk, dv = [], None, None
        for head in range(heads):
            span = slice(head * HD, (head + 1) * HD)
            zero_t = jnp.zeros_like(qt)
            mask_t = head_mask(qt.shape, 0, head)
            mask = head_mask(q.shape, 1, head)
            scores = nn(k, jnp.where(mask_t, qt, zero_t))
            weights = jnp.exp(scores - lse_ref[image, head:head + 1, :])
            back = nn(v, jnp.where(mask_t, dot, zero_t))
            delta = jnp.sum(product[span], axis=0, keepdims=True)
            score_grad = (weights * (back - delta)).astype(LOW)
            dqt.append(nn(kt[span], score_grad) * shrink)
            dk_one = nn(score_grad, jnp.where(mask, q, jnp.zeros_like(q)))
            dv_one = nn(weights.astype(LOW), jnp.where(mask, do, jnp.zeros_like(do)))
            dk = dk_one if dk is None else dk + dk_one
            dv = dv_one if dv is None else dv + dv_one
        dqt = jnp.concatenate(dqt, axis=0).astype(LOW)
        dk, dv = dk.astype(LOW), dv.astype(LOW)
        total_of.give(turn, tn(dqt, wq) + nn(dk, wk) + nn(dv, wv))
        pieces = (nn(dqt, xn), tn(dk, xn), tn(dv, xn), nn(ot, x1g))
        for part, piece in enumerate(pieces):
            grad_ref[pl.ds(part * rows, rows), :] += piece

        @pl.when((turn == 1) | (turn == 2))
        def _():
            back_out.of_phase(2 * turn - 2, back_out.relay)
            back_out.of_phase(2 * turn - 1, back_out.relay)

    own.wait()
    normal, scale = normalise(own_ref[...].astype(FULL))
    back, gain_sum, shift_sum = norm_back(normal, scale, norm_ref[0:1, :], total_of.result())
    input_ref[me] = (x1g_ref[me].astype(FULL) + back).astype(LOW)
    spread.start()
    low = grad_ref[...].astype(LOW)
    depth = padded_ref.shape[1]
    parts = min(dp_count, 8)
    cut = dp_count // parts * depth
    for part in range(parts):
        row = lax.broadcasted_iota(jnp.int32, (cut, low.shape[0]), 0) + part * cut
        pick = one_hot(row == src_ref[...])
        block = nn(pick, low).astype(LOW)
        padded_ref[pl.ds(part * (dp_count // parts), dp_count // parts)] = block.reshape(
            dp_count // parts, depth, block.shape[1]
        )
    weights_sum.start()
    small = small_ref[...]
    row = lax.broadcasted_iota(jnp.int32, small.shape, 0)
    small = small + jnp.where(row == experts, gain_sum, 0.0)
    small_sum.start(small + jnp.where(row == experts + 1, shift_sum, 0.0))
    @pl.loop(0, slots.count)
    def _(shift):
        back_out.forward(shift)

    @pl.loop(0, slots.count)
    def _(shift):
        back_out.rest(shift)

    x1_copy.wait()
    steps = weights_sum.length

    @pl.loop(0, max(steps, images))
    def _(turn):
        @pl.when(turn < images)
        def _():
            mix = block_ref[turn].astype(FULL)
            for phase in range(4):
                mix = mix + picked_rows(slots, col_ref[turn], out_ref, phase)
            block_ref[turn] = mix.astype(LOW)

        @pl.when(turn < steps - 1)
        def _():
            weights_sum.step(steps - 1 - turn)

        @pl.when(turn == 0)
        def _():
            small_sum.across()

        @pl.when(turn == 1)
        def _():
            spread.wait_far()

        @pl.when(turn == 2)
        def _():
            small_sum.back()

    weights_sum.result()
    small_sum.result(small_out)
    spread.wait_near()
    spread.wait_corner()
    keep = pltpu.make_async_copy(input_ref, input_out, own_sem.at[0])
    keep.start()
    spread.finish()
    back_out.finish()
    total_of.finish()
    weights_sum.finish()
    small_sum.finish()
    keep.wait()


def attention_backward(
    experts, slots, depth,
    x1_grad, w, xn, saved, lse, src_row, norm_params, small, col, patches, out_rows, x1,
):
    q, qt, k, kt, v, ot = saved
    images, _, width = patches.shape
    dp_count = slots.count
    return pl.pallas_call(
        functools.partial(backward_kernel, experts, slots),
        in_specs=[INSIDE] * 14 + [ANYWHERE] * 3,
        out_specs=[INSIDE, INSIDE, INSIDE, ANYWHERE],
        out_shape=[
            jax.ShapeDtypeStruct((depth, width), FULL), jax.ShapeDtypeStruct(small.shape, FULL),
            jax.ShapeDtypeStruct(patches.shape, LOW), jax.ShapeDtypeStruct(patches.shape, LOW),
        ],
        scratch_shapes=[
            pltpu.VMEM(w.shape, FULL), pltpu.VMEM((PATCH, width), LOW),
            pltpu.VMEM(patches.shape, LOW), pltpu.VMEM((dp_count, depth, width), LOW),
            pltpu.VMEM((4 * slots.phase_rows, width), LOW), pltpu.SemaphoreType.DMA((2,)),
        ]
        + image_sum_scratch(width) + image_gather_sems() + return_gather_sems(dp_count)
        + line_scatter_scratch(dp_count, depth, width)
        + small_sum_scratch(small.shape[0], width, dp_count),
        compiler_params=params(collective_id=2, has_side_effects=True),
        name="attention_backward",
    )(
        x1_grad, w, xn, q, qt, k, kt, v, lse, ot, src_row, norm_params, small, col,
        patches, out_rows, x1,
    )


def picked_rows(slots, col, held_ref, phase):
    start = phase * slots.phase_rows
    lanes = lax.broadcasted_iota(jnp.int32, (col.shape[0], slots.phase_rows), 1) + start
    pick = one_hot((lanes == col[:, 0:1]) | (lanes == col[:, 1:2]))
    return nn(pick, held_ref[pl.ds(start, slots.phase_rows), :])


def combine_kernel(
    slots,
    col_ref, x1_ref, g_ref, norm_ref, rows_ref,
    out_ref, sums_ref,
    held, total, *sems,
):
    images = x1_ref.shape[0]
    back = ReturnGather(slots, rows_ref, held, *sems)
    greet_all((back.near, back.far), slots.count)
    back.start()
    back.of_phase(0, back.relay)

    @pl.loop(0, 4)
    def _(phase):
        back.of_phase(phase, back.forward)

        @pl.when(phase < 3)
        def _():
            back.of_phase(phase + 1, back.relay)

        back.of_phase(phase, back.rest)

        @pl.loop(0, images)
        def _(image):
            part = picked_rows(slots, col_ref[image], held, phase)

            @pl.when(phase == 0)
            def _():
                total[image] = part

            @pl.when(phase > 0)
            def _():
                total[image] += part

    sums_ref[...] = jnp.zeros_like(sums_ref)

    @pl.loop(0, images)
    def _(image):
        normal, scale = normalise(x1_ref[image].astype(FULL))
        result, gain_sum, shift_sum = norm_back(normal, scale, norm_ref[2:3, :], total[image])
        out_ref[image] = (g_ref[image].astype(FULL) + result).astype(LOW)
        sums_ref[0:1, :] += gain_sum
        sums_ref[1:2, :] += shift_sum

    back.finish()


def combine_backward(slots, col, x1, cotangent, norm_params, rows):
    images, _, width = x1.shape
    return pl.pallas_call(
        functools.partial(combine_kernel, slots),
        in_specs=[INSIDE] * 4 + [ANYWHERE],
        out_specs=[INSIDE] * 2,
        out_shape=[
            jax.ShapeDtypeStruct(x1.shape, LOW), jax.ShapeDtypeStruct((8, width), FULL)
        ],
        scratch_shapes=[
            pltpu.VMEM((4 * slots.phase_rows, width), LOW), pltpu.VMEM(x1.shape, FULL),
        ] + return_gather_sems(slots.count),
        compiler_params=params(collective_id=3, has_side_effects=True),
        name="combine_backward",
    )(col, x1, cotangent, norm_params, rows)


def expert_kernel(
    rows_ref, g_ref, up_ref, down_ref, router_ref, own_ref, count_ref,
    back_ref, out_ref, upg_ref, downg_ref, router_grad_ref,
    out_sum, back_sum, og_ref, gate_ref, probs_ref,
):
    step = pl.program_id(0)
    rows = rows_ref[...]

    @pl.when(step == 0)
    def _():
        logits = nt(rows, router_ref[...]) + count_ref[...]
        top = jnp.max(logits, axis=-1, keepdims=True)
        weights = jnp.exp(logits - top)
        probs = weights / jnp.sum(weights, axis=-1, keepdims=True)
        gate = jnp.sum(probs * own_ref[...], axis=-1, keepdims=True)
        probs_ref[...] = probs
        gate_ref[...] = gate
        og_ref[...] = (gate * g_ref[...].astype(FULL)).astype(LOW)
        out_sum[...] = jnp.zeros_like(out_sum)
        back_sum[...] = jnp.zeros_like(back_sum)

    og = og_ref[...]
    up, down = up_ref[0], down_ref[0]
    hidden = nn(rows, up)
    slope = (2.0 / jnp.pi) ** 0.5
    square = hidden * hidden
    bend = jnp.tanh(slope * (hidden + 0.044715 * (square * hidden)))
    act = (0.5 * hidden * (1.0 + bend)).astype(LOW)
    out_sum[...] += nn(act, down)
    act_grad = nt(og, down)
    inner = slope * (1.0 + (3.0 * 0.044715) * square)
    curve = 0.5 * (1.0 + bend) + 0.5 * hidden * (1.0 - bend * bend) * inner
    hidden_grad = (curve * act_grad).astype(LOW)
    back_sum[...] += nt(hidden_grad, up)
    upg_ref[0] = tn(rows, hidden_grad).astype(LOW)
    downg_ref[0] = tn(act, og).astype(LOW)

    @pl.when(step == pl.num_programs(0) - 1)
    def _():
        out = out_sum[...].astype(LOW).astype(FULL)
        gate, probs = gate_ref[...], probs_ref[...]
        out_ref[...] = (gate * out).astype(LOW)
        gate_grad = jnp.sum(g_ref[...].astype(FULL) * out, axis=-1, keepdims=True)
        logit_grad = (gate_grad * (probs * (own_ref[...] - gate))).astype(LOW)
        back = back_sum[...].astype(LOW).astype(FULL) + nn(logit_grad, router_ref[...])
        back_ref[...] = back.astype(LOW)
        router_grad_ref[...] = tn(logit_grad, rows)


def experts_both_ways(rows, g_rows, up, down, router_low, own):
    slots, width = rows.shape
    parts, _, units = up.shape
    experts = router_low.shape[0]
    lanes = 128
    router_wide = jnp.zeros((lanes, width), LOW).at[:experts].set(router_low)
    lane = jnp.arange(lanes, dtype=jnp.int32)[None, :]
    own_row = jnp.where(lane == own, 1.0, 0.0).astype(FULL)
    closed = jnp.where(lane < experts, 0.0, -1e30).astype(FULL)
    wide_spec = whole((slots, width))
    return pl.pallas_call(
        expert_kernel,
        grid=(parts,),
        in_specs=[
            wide_spec, wide_spec, lead((1, width, units)), lead((1, units, width)),
            whole((lanes, width)), whole((1, lanes)), whole((1, lanes)),
        ],
        out_specs=[
            wide_spec, wide_spec, lead((1, width, units)), lead((1, units, width)),
            whole((lanes, width)),
        ],
        out_shape=[
            jax.ShapeDtypeStruct((slots, width), LOW),
            jax.ShapeDtypeStruct((slots, width), LOW),
            jax.ShapeDtypeStruct(up.shape, LOW),
            jax.ShapeDtypeStruct(down.shape, LOW),
            jax.ShapeDtypeStruct((lanes, width), FULL),
        ],
        scratch_shapes=[
            pltpu.VMEM((slots, width), FULL), pltpu.VMEM((slots, width), FULL),
            pltpu.VMEM((slots, width), LOW), pltpu.VMEM((slots, 1), FULL),
            pltpu.VMEM((slots, lanes), FULL),
        ],
        compiler_params=params(),
        name="experts_both_ways",
    )(rows, g_rows, up, down, router_wide, own_row, closed)


def body(
    patches, cotangent, expert_ids, slot_pos, owners,
    tile_master, tile_first, tile_second,
    expert_up, up_first, up_second,
    expert_down, down_first, down_second,
    router, router_first, router_second,
    norm_params, norm_first, norm_second,
):
    tok_rows, width = patches.shape
    experts = router.shape[0]
    capacity = tok_rows // experts
    dp_count = lax.axis_size("dp")
    head_count = lax.axis_size("head")
    me_head = lax.axis_index("head")
    me_dp = lax.axis_index("dp")
    images = tok_rows // PATCH
    slots = Slots(dp_count, capacity // head_count)
    slot_count = tile_master.shape[0]

    owner_row = owners[0]
    tile_count = owner_row.shape[0]
    order_index = jnp.arange(tile_count, dtype=jnp.int32)
    same_owner = owner_row[:, None] == owner_row[None, :]
    earlier = order_index[None, :] < order_index[:, None]
    tile_rank = jnp.sum(jnp.where(same_owner & earlier, 1, 0), axis=1).astype(jnp.int32)
    tile_place = owner_row * slot_count + tile_rank
    src = (tile_place[:, None] * TILE + jnp.arange(TILE, dtype=jnp.int32)[None, :]).reshape(-1)

    ids, pos = expert_ids.T, slot_pos.T
    kept = pos < capacity
    holder, within = slots.holder(me_dp, jnp.minimum(pos, capacity - 1))
    size = slots.size(me_dp, me_head)
    col_rows = jnp.where(kept & (holder == me_head), ids * size + within, -1)
    col_rows = col_rows.reshape(2, images, PATCH).transpose(1, 0, 2)
    shift = (me_dp + dp_count - ids) % dp_count
    col = jnp.where(kept, slots.row(me_dp, holder, shift) + within, -1)
    col = col.T.reshape(images, PATCH, 2)

    by_image = (images, PATCH, width)
    x_images, g_images = patches.reshape(by_image), cotangent.reshape(by_image)
    w, xn, g_sent, up_all = prepare(
        tile_master.reshape(slot_count * TILE, width), x_images, g_images, norm_params,
        src[:, None], col_rows, expert_up[0].astype(LOW), slots.count * slots.big, dp_count,
    )
    lse, *saved, x1, rows, g_rows, down_all = attention_forward(
        slots, xn, w, norm_params, col_rows, x_images, g_sent, expert_down[0].astype(LOW)
    )
    back, out, up_part, down_part, router_part = experts_both_ways(
        rows, g_rows, up_all, down_all, router.astype(LOW), me_dp
    )
    x1_grad, second_sums = combine_backward(slots, col, x1, g_images, norm_params, back)

    small_rows = -(-(experts + 4) // 16) * 16
    small = jnp.concatenate(
        [
            router_part[:experts], jnp.zeros((2, width), FULL),
            second_sums[:2] * (1.0 / head_count),
            jnp.zeros((small_rows - experts - 4, width), FULL),
        ]
    )
    owned_grad, small, block_out, input_low = attention_backward(
        experts, slots, slot_count * TILE,
        x1_grad, w, xn, saved, lse, src[None, :], norm_params, small, col, x_images, out, x1,
    )
    block_out = block_out.reshape(tok_rows, width)
    owned_grad = owned_grad.reshape(slot_count, TILE, width)
    input_grad = input_low.reshape(tok_rows, width).astype(FULL)

    up_grad = lax.psum_scatter(up_part, "head", scatter_dimension=0).astype(FULL)
    down_grad = lax.psum_scatter(down_part, "head", scatter_dimension=0).astype(FULL)
    router_total, norm_total = small[:experts], small[experts:experts + 4]

    tile_new, tile_first_new, tile_second_new = adam_update(
        tile_master, tile_first, tile_second, owned_grad, rate_attention, decay_factor
    )
    up_new, up_first_new, up_second_new = adam_update(
        expert_up, up_first, up_second, up_grad[None], rate_up, decay_factor
    )
    down_new, down_first_new, down_second_new = adam_update(
        expert_down, down_first, down_second, down_grad[None], rate_down, decay_factor
    )
    router_new, router_first_new, router_second_new = adam_update(
        router, router_first, router_second, router_total, rate_router, decay_factor
    )
    norm_new, norm_first_new, norm_second_all = adam_update(
        norm_params, norm_first, norm_second, norm_total, rate_norm, 0.0
    )
    return (
        block_out,
        input_grad,
        tile_new,
        tile_first_new,
        tile_second_new,
        tile_new.astype(LOW),
        up_new,
        up_first_new,
        up_second_new,
        up_new.astype(LOW),
        down_new,
        down_first_new,
        down_second_new,
        down_new.astype(LOW),
        router_new,
        router_first_new,
        router_second_new,
        norm_new,
        norm_first_new,
        norm_second_all[:2],
        norm_second_all[2:],
    )


def solution(mesh):
    row = P("dp", None)
    tiles = P(("dp", "head"), None, None)
    up = P("dp", None, "head")
    down = P("dp", "head", None)
    in_specs = (
        row, row, row, row, P("head", None), tiles, tiles, tiles,
        up, up, up, down, down, down, P(), P(), P(), P(), P(), P(),
    )
    out_specs = (
        row, row, tiles, tiles, tiles, tiles, up, up, up, up, down, down, down, down,
        P(), P(), P(), P(), P(), P(), P(),
    )
    return jax.shard_map(body, mesh=mesh, in_specs=in_specs, out_specs=out_specs, check_vma=False)
```

```python
import functools

import jax
import jax.numpy as jnp
from jax import lax
from jax.experimental import pallas as pl
from jax.experimental.pallas import tpu as pltpu
from jax.sharding import PartitionSpec as P

HD = 64
PATCH = 576
TILE = 8
STEP = 10

eps_norm = 1e-06
beta_one = 0.9
beta_two = 0.999
adam_eps = 1e-08
rate_attention = 0.12
rate_up = 0.08
rate_down = 0.3
rate_router = 0.05
rate_norm = 0.4
decay_factor = 0.1

LOW = jnp.bfloat16
FULL = jnp.float32
MESH = pl.DeviceIdType.MESH
VMEM_BYTES = 60 * 1024 * 1024


def adam_update(weight, moment_one, moment_two, gradient, step_rate, weight_decay):
    moment_one = beta_one * moment_one + (1.0 - beta_one) * gradient
    moment_two = beta_two * moment_two + (1.0 - beta_two) * gradient * gradient
    fixed_one = moment_one / (1.0 - beta_one**STEP)
    fixed_two = moment_two / (1.0 - beta_two**STEP)
    weight = weight - step_rate * (
        fixed_one / (jnp.sqrt(fixed_two) + adam_eps) + weight_decay * weight
    )
    return (weight, moment_one, moment_two)


def nn(left, right):
    return lax.dot_general(left, right, (((1,), (0,)), ((), ())), preferred_element_type=FULL)


def nt(left, right):
    return lax.dot_general(left, right, (((1,), (1,)), ((), ())), preferred_element_type=FULL)


def tn(left, right):
    return lax.dot_general(left, right, (((0,), (0,)), ((), ())), preferred_element_type=FULL)


def params(**more):
    return pltpu.CompilerParams(vmem_limit_bytes=VMEM_BYTES, **more)


def whole(shape):
    return pl.BlockSpec(shape, lambda *_: (0,) * len(shape))


def lead(shape):
    return pl.BlockSpec(shape, lambda i: (i,) + (0,) * (len(shape) - 1))


def normalise(values):
    average = jnp.mean(values, axis=-1, keepdims=True)
    centred = values - average
    variance = jnp.mean(centred * centred, axis=-1, keepdims=True)
    scale = lax.rsqrt(variance + eps_norm)
    return centred * scale, scale


def norm_back(normal, scale, gain, upstream):
    inner = upstream * gain
    mean_inner = jnp.mean(inner, axis=-1, keepdims=True)
    mean_cross = jnp.mean(inner * normal, axis=-1, keepdims=True)
    result = scale * (inner - mean_inner - normal * mean_cross)
    gain_sum = jnp.sum(upstream * normal, axis=0, keepdims=True)
    shift_sum = jnp.sum(upstream, axis=0, keepdims=True)
    return result, gain_sum, shift_sum


def one_hot(condition):
    return jnp.where(condition, 1.0, 0.0).astype(LOW)


def remote(src, dst, sends, recvs, index, axis, other):
    return pltpu.make_async_remote_copy(
        src_ref=src, dst_ref=dst, send_sem=sends.at[index], recv_sem=recvs.at[index],
        device_id={axis: other}, device_id_type=MESH,
    )


def greet(*others):
    barrier = pltpu.get_barrier_semaphore()
    for axis, other in others:
        pl.semaphore_signal(barrier, inc=1, device_id={axis: other}, device_id_type=MESH)
    pl.semaphore_wait(barrier, len(others))


def partners():
    me = lax.axis_index("head")
    near = me + 1 - 2 * lax.rem(me, 2)
    far = lax.rem(me + 2, 4)
    corner = lax.rem(near + 2, 4)
    return me, near, far, corner


class LineGather:
    def __init__(self, held, up_send, up_recv, down_send, down_recv, pair_send, pair_recv):
        self.held = held
        self.length = held.shape[0] // 2
        self.sems = ((up_send, up_recv), (down_send, down_recv), (pair_send, pair_recv))
        me = lax.axis_index("dp")
        self.place, self.side = me // 2, lax.rem(me, 2)
        self.above = lax.rem(self.place + 1, self.length) * 2 + self.side
        self.below = lax.rem(self.place + self.length - 1, self.length) * 2 + self.side
        self.other = self.place * 2 + 1 - self.side

    def neighbours(self):
        return ("dp", self.above), ("dp", self.below), ("dp", self.other)

    def copy(self, way, origin, side=None):
        index = origin * 2 + (self.side if side is None else side)
        target = (self.above, self.below, self.other)[way]
        block = self.held.at[index]
        return remote(block, block, *self.sems[way], origin, "dp", target)

    def pass_on(self, origin, up, down):
        @pl.when(up & (self.place < self.length - 1))
        def _():
            self.copy(0, origin).start()

        @pl.when(down & (self.place > 0))
        def _():
            self.copy(1, origin).start()

        self.copy(2, origin).start()

    def start(self):
        self.pass_on(self.place, True, True)

    def step(self, k):
        low, high = self.place - k, self.place + k

        @pl.when(low >= 0)
        def _():
            self.copy(0, low).wait_recv()
            self.pass_on(low, True, False)

        @pl.when(high < self.length)
        def _():
            self.copy(1, high).wait_recv()
            self.pass_on(high, False, True)

    def finish(self):
        @pl.loop(0, self.length)
        def _(origin):
            self.copy(2, origin).wait_recv()
            self.copy(2, origin).wait_send()

            @pl.when((origin <= self.place) & (self.place < self.length - 1))
            def _():
                self.copy(0, origin).wait_send()

            @pl.when((origin >= self.place) & (self.place > 0))
            def _():
                self.copy(1, origin).wait_send()


class ImageSum:
    def __init__(self, stage, corner_in, near_in, passed, mine, far_in, sends, recvs):
        self.stage, self.corner_in, self.near_in = stage, corner_in, near_in
        self.passed, self.mine, self.far_in = passed, mine, far_in
        self.sends, self.recvs = sends, recvs
        self.me, self.near, self.far, self.corner = partners()
        self.core = lax.rem(self.me, 2)

    def image(self, turn):
        base = self.me - self.core
        other = lax.rem(base + 2, 4)
        return jnp.where(turn < 2, other, base - 2) + turn

    def to_corner(self):
        return remote(
            self.stage.at[0], self.corner_in, self.sends, self.recvs, 0, "head", self.near
        )

    def to_near(self):
        return remote(
            self.stage.at[1], self.near_in, self.sends, self.recvs, 1, "head", self.near
        )

    def to_far(self):
        return remote(self.passed, self.far_in, self.sends, self.recvs, 2, "head", self.far)

    def give(self, turn, part):
        theirs = lax.rem(turn, 2) != self.core

        @pl.when((turn < 2) & theirs)
        def _():
            self.stage[0] = part.astype(LOW)
            self.to_corner().start()

        @pl.when((turn >= 2) & theirs)
        def _():
            self.stage[1] = part.astype(LOW)
            self.to_near().start()

        @pl.when((turn < 2) & ~theirs)
        def _():
            self.to_corner().wait_recv()
            self.passed[...] = (part + self.corner_in[...].astype(FULL)).astype(LOW)
            self.to_far().start()

        @pl.when((turn >= 2) & ~theirs)
        def _():
            self.mine[...] = part

    def result(self):
        self.to_near().wait_recv()
        self.to_far().wait_recv()
        return self.mine[...] + self.near_in[...].astype(FULL) + self.far_in[...].astype(FULL)

    def finish(self):
        self.to_corner().wait_send()
        self.to_near().wait_send()
        self.to_far().wait_send()


def image_sum_scratch(rows, width):
    block = pltpu.VMEM((rows, width), LOW)
    return [
        pltpu.VMEM((2, rows, width), LOW), block, block, block,
        pltpu.VMEM((rows, width), FULL), block,
        pltpu.SemaphoreType.DMA((3,)), pltpu.SemaphoreType.DMA((3,)),
    ]


class LineScatter:
    def __init__(
        self, blocks, out, pair_in, up_in, down_in, total,
        up_send, up_recv, down_send, down_recv, pair_send, pair_recv,
    ):
        self.blocks, self.out, self.total = blocks, out, total
        self.arrived = (up_in, down_in, pair_in)
        self.sems = ((up_send, up_recv), (down_send, down_recv), (pair_send, pair_recv))
        self.length = blocks.shape[0] // 2
        me = lax.axis_index("dp")
        self.place, self.side = me // 2, lax.rem(me, 2)
        self.targets = (
            lax.rem(self.place + 1, self.length) * 2 + self.side,
            lax.rem(self.place + self.length - 1, self.length) * 2 + self.side,
            self.place * 2 + 1 - self.side,
        )

    def copy(self, way, block):
        source = (
            self.blocks.at[block * 2 + 1 - self.side] if way == 2 else self.total.at[block]
        )
        return remote(
            source, self.arrived[way].at[block], *self.sems[way], block, "dp", self.targets[way]
        )

    def start(self):
        @pl.loop(0, self.length)
        def _(turn):
            distance = self.length - 1 - turn

            @pl.when(self.place + distance < self.length)
            def _():
                self.copy(2, self.place + distance).start()

            @pl.when((self.place >= distance) & (distance > 0))
            def _():
                self.copy(2, self.place - distance).start()

    def pair_sum(self, block):
        self.copy(2, block).wait_recv()
        own = self.blocks[block * 2 + self.side].astype(FULL)
        return own + self.arrived[2][block].astype(FULL)

    def forward(self, way, block, first):
        both = self.pair_sum(block)

        @pl.when(first)
        def _():
            self.total[block] = both.astype(LOW)

        @pl.when(~first)
        def _():
            self.copy(way, block).wait_recv()
            self.total[block] = (both + self.arrived[way][block].astype(FULL)).astype(LOW)

        self.copy(way, block).start()

    def step(self, distance):
        @pl.when(self.place + distance < self.length)
        def _():
            self.forward(0, self.place + distance, self.place == 0)

        @pl.when(self.place >= distance)
        def _():
            self.forward(1, self.place - distance, self.place == self.length - 1)

    def result(self):
        self.out[...] = self.pair_sum(self.place)

        @pl.when(self.place > 0)
        def _():
            self.copy(0, self.place).wait_recv()
            self.out[...] += self.arrived[0][self.place].astype(FULL)

        @pl.when(self.place < self.length - 1)
        def _():
            self.copy(1, self.place).wait_recv()
            self.out[...] += self.arrived[1][self.place].astype(FULL)

    def finish(self):
        @pl.loop(0, self.length)
        def _(block):
            self.copy(2, block).wait_send()

            @pl.when(block > self.place)
            def _():
                self.copy(0, block).wait_send()

            @pl.when(block < self.place)
            def _():
                self.copy(1, block).wait_send()


def line_scatter_scratch(dp_count, rows, width):
    line = dp_count // 2
    return [pltpu.VMEM((line, rows, width), LOW)] * 4 + [pltpu.SemaphoreType.DMA((line,))] * 6


class SmallSum:
    def __init__(self, flat, head_in, dp_in, done, head_send, head_recv, dp_send, dp_recv):
        self.flat, self.head_in, self.dp_in, self.done = flat, head_in, dp_in, done
        self.head_sems, self.dp_sems = (head_send, head_recv), (dp_send, dp_recv)
        self.me, *self.others = partners()
        self.place, self.count = lax.axis_index("dp"), dp_in.shape[0]

    def to_head(self, lane):
        other = self.others[lane]
        return remote(
            self.flat.at[other], self.head_in.at[self.me], *self.head_sems, lane, "head", other
        )

    def back_head(self, lane):
        block = self.done.at[self.me]
        return remote(block, block, *self.head_sems, 3 + lane, "head", self.others[lane])

    def to_dp(self, shift):
        block = self.dp_in.at[self.place]
        other = lax.rem(self.place + shift, self.count)
        return remote(block, block, *self.dp_sems, shift, "dp", other)

    def start(self, value):
        groups, rows, lanes = self.flat.shape
        flat = jnp.concatenate(
            [value[:, at:at + lanes] for at in range(0, value.shape[1], lanes)], axis=0
        )
        for group in range(groups):
            self.flat[group] = flat[group * rows:(group + 1) * rows]
        for lane in range(3):
            self.to_head(lane).start()
        self.head_in[self.me] = self.flat[self.me]

    def across(self):
        for lane in range(3):
            self.to_head(lane).wait_recv()
        total = self.head_in[0]
        for head in range(1, self.head_in.shape[0]):
            total = total + self.head_in[head]
        self.dp_in[self.place] = total

        @pl.loop(1, self.count)
        def _(shift):
            self.to_dp(shift).start()

    def back(self):
        @pl.loop(1, self.count)
        def _(shift):
            self.to_dp(shift).wait_recv()

        total = lax.fori_loop(
            1, self.count, lambda at, so_far: so_far + self.dp_in[at], self.dp_in[0]
        )
        self.done[self.me] = total
        for lane in range(3):
            self.back_head(lane).start()

    def result(self, out):
        for lane in range(3):
            self.back_head(lane).wait_recv()
        flat = jnp.concatenate([self.done[group] for group in range(self.done.shape[0])], axis=0)
        rows, width = out.shape
        lanes = flat.shape[1]
        for at in range(width // lanes):
            out[:, at * lanes:(at + 1) * lanes] = flat[at * rows:(at + 1) * rows]

    def finish(self):
        for lane in range(3):
            self.to_head(lane).wait_send()
            self.back_head(lane).wait_send()

        @pl.loop(1, self.count)
        def _(shift):
            self.to_dp(shift).wait_send()


def small_sum_scratch(rows, width, dp_count):
    block = (rows * width // 128 // 4, 128)
    return [
        pltpu.VMEM((4,) + block, FULL), pltpu.VMEM((4,) + block, FULL),
        pltpu.VMEM((dp_count,) + block, FULL), pltpu.VMEM((4,) + block, FULL),
        pltpu.SemaphoreType.DMA((6,)), pltpu.SemaphoreType.DMA((6,)),
        pltpu.SemaphoreType.DMA((dp_count,)), pltpu.SemaphoreType.DMA((dp_count,)),
    ]


GATHER_CUTS = 4


class ImageGather:
    def __init__(self, held, sends, recvs, own=None, local_sem=None):
        self.held, self.sends, self.recvs = held, sends, recvs
        self.me, self.near, self.far, self.corner = partners()
        self.own = held.at[self.me] if own is None else own
        self.local = None if own is None else pltpu.make_async_copy(own, held.at[self.me], local_sem)
        self.size = held.shape[1] // GATHER_CUTS

    def piece(self, lane, cut):
        span = pl.ds(cut * self.size, self.size)
        image = self.far if lane == 2 else self.me
        block = self.held.at[image, span]
        source = block if lane == 2 else self.own.at[span]
        other = self.far if lane == 0 else self.near
        index = lane * GATHER_CUTS + cut
        return remote(source, block, self.sends, self.recvs, index, "head", other)

    def start_far(self, first=0, last=GATHER_CUTS):
        for cut in range(first, last):
            self.piece(0, cut).start()

    def start_near(self):
        for cut in range(GATHER_CUTS):
            self.piece(1, cut).start()
        if self.local is not None:
            self.local.start()

    def start(self):
        self.start_far()
        self.start_near()

    def wait_near(self):
        for cut in range(GATHER_CUTS):
            self.piece(1, cut).wait_recv()

    def wait_far(self):
        for cut in range(GATHER_CUTS):
            self.piece(0, cut).wait_recv()
            self.piece(2, cut).start()

    def wait_corner(self):
        for cut in range(GATHER_CUTS):
            self.piece(2, cut).wait_recv()

    def finish(self):
        for cut in range(GATHER_CUTS):
            for lane in range(3):
                self.piece(lane, cut).wait_send()
        if self.local is not None:
            self.local.wait()


def image_gather_sems():
    return [pltpu.SemaphoreType.DMA((3 * GATHER_CUTS,)), pltpu.SemaphoreType.DMA((3 * GATHER_CUTS,))]


class BlockSum:
    def __init__(self, parts, mine, passed, corner_in, near_in, far_in, local_sems, sends, recvs):
        self.mine, self.passed, self.corner_in = mine, passed, corner_in
        self.near_in, self.far_in = near_in, far_in
        me, near, far, corner = partners()
        self.to_corner = remote(parts.at[corner], corner_in, sends, recvs, 0, "head", near)
        self.to_near = remote(parts.at[near], near_in, sends, recvs, 1, "head", near)
        self.to_far = remote(passed, far_in, sends, recvs, 2, "head", far)
        self.load_far = pltpu.make_async_copy(parts.at[far], passed, local_sems.at[0])
        self.load_mine = pltpu.make_async_copy(parts.at[me], mine, local_sems.at[1])

    def start(self):
        for copy in (self.to_corner, self.load_far, self.to_near, self.load_mine):
            copy.start()

    def across(self):
        self.load_far.wait()
        self.to_corner.wait_recv()
        both = self.passed[...].astype(FULL) + self.corner_in[...].astype(FULL)
        self.passed[...] = both.astype(LOW)
        self.to_far.start()

    def result(self):
        self.load_mine.wait()
        self.to_near.wait_recv()
        self.to_far.wait_recv()
        total = self.mine[...].astype(FULL) + self.near_in[...].astype(FULL)
        return total + self.far_in[...].astype(FULL)

    def finish(self):
        for copy in (self.to_corner, self.to_near, self.to_far):
            copy.wait_send()


def block_sum_scratch(rows, width):
    return [pltpu.VMEM((rows, width), LOW)] * 5 + [
        pltpu.SemaphoreType.DMA((2,)), pltpu.SemaphoreType.DMA((3,)), pltpu.SemaphoreType.DMA((3,)),
    ]


class Slots:
    def __init__(self, count, share):
        self.count, self.share = count, share
        self.big = -(-share // 16) * 16
        rest = 2 * share - self.big
        self.small = rest if rest > 0 and rest % 16 == 0 else self.big
        self.more = self.big - self.small
        self.both = self.big + self.small
        self.rows = count // 2 * self.both
        self.turns = count // 4
        self.phase_rows = self.turns * 2 * self.both

    def size(self, source, head):
        return self.small + self.more * ((head + source + 1) % 2)

    def packed(self, source, head):
        return (source // 2) * self.both + (source % 2) * self.size(0, head)

    def row(self, source, head, shift):
        first = self.size(source, 0) * (head % 2)
        group = (head // 2) * self.turns * self.both + self.turns * first
        return (
            (shift // self.turns) * self.phase_rows + group
            + (shift % self.turns) * self.size(source, head)
        )

    def holder(self, source, slot):
        pair, within = slot // self.both, slot % self.both
        first = self.size(source, 0)
        second = jnp.where(within >= first, 1, 0)
        return 2 * pair + second, within - second * first

    def span(self, start, extra):
        if extra:
            return pl.ds(pl.multiple_of(start + self.small, 16), self.more)
        return pl.ds(pl.multiple_of(start, 16), self.small)

    def each(self, is_big, make, action):
        getattr(make(False), action)()
        if self.more:
            @pl.when(is_big)
            def _():
                getattr(make(True), action)()


class SlotExchange:
    def __init__(self, slots, sent, rows, sends, recvs, local_sems):
        self.slots, self.sent, self.rows = slots, sent, rows
        self.sems, self.local_sems = (sends, recvs), local_sems
        self.place, self.head = lax.axis_index("dp"), lax.axis_index("head")

    def out(self, shift, action):
        slots = self.slots
        expert = lax.rem(self.place + shift, slots.count)
        mine = slots.size(self.place, self.head)
        at, to = expert * mine, slots.packed(self.place, self.head)
        slots.each(mine > slots.small, lambda extra: remote(
            self.sent.at[slots.span(at, extra)], self.rows.at[slots.span(to, extra)],
            *self.sems, 2 * shift + int(extra), "dp", expert,
        ), action)

    def into(self, shift):
        slots = self.slots
        source = lax.rem(self.place + slots.count - shift, slots.count)
        size = slots.size(source, self.head)
        to = slots.packed(source, self.head)
        slots.each(size > slots.small, lambda extra: remote(
            self.sent.at[slots.span(0, extra)], self.rows.at[slots.span(to, extra)],
            *self.sems, 2 * shift + int(extra), "dp", source,
        ), "wait_recv")

    def own(self, action):
        slots = self.slots
        mine = slots.size(self.place, self.head)
        at, to = self.place * mine, slots.packed(self.place, self.head)
        slots.each(mine > slots.small, lambda extra: pltpu.make_async_copy(
            self.sent.at[slots.span(at, extra)], self.rows.at[slots.span(to, extra)],
            self.local_sems.at[int(extra)],
        ), action)

    def start(self):
        @pl.loop(1, self.slots.count)
        def _(shift):
            self.out(shift, "start")

        self.own("start")

    def finish(self):
        @pl.loop(1, self.slots.count)
        def _(shift):
            self.into(shift)
            self.out(shift, "wait_send")

        self.own("wait")


class SlotReturn:
    def __init__(self, slots, rows, back, zeros, sends, recvs, local_sems):
        self.slots, self.rows, self.back, self.zeros = slots, rows, back, zeros
        self.sems, self.local_sems = (sends, recvs), local_sems
        self.place, self.head = lax.axis_index("dp"), lax.axis_index("head")
        self.mine = slots.size(self.place, self.head)

    def out(self, shift, action):
        slots = self.slots
        source = lax.rem(self.place + shift, slots.count)
        size = slots.size(source, self.head)
        at, to = slots.packed(source, self.head), shift * size
        slots.each(size > slots.small, lambda extra: remote(
            self.rows.at[slots.span(at, extra)], self.back.at[slots.span(to, extra)],
            *self.sems, 2 * shift + int(extra), "dp", source,
        ), action)

    def into(self, shift):
        slots = self.slots
        expert = lax.rem(self.place + slots.count - shift, slots.count)
        slots.each(self.mine > slots.small, lambda extra: remote(
            self.rows.at[slots.span(0, extra)], self.back.at[slots.span(shift * self.mine, extra)],
            *self.sems, 2 * shift + int(extra), "dp", expert,
        ), "wait_recv")

    def own(self, action):
        slots = self.slots
        at = slots.packed(self.place, self.head)
        slots.each(self.mine > slots.small, lambda extra: pltpu.make_async_copy(
            self.rows.at[slots.span(at, extra)], self.back.at[slots.span(0, extra)],
            self.local_sems.at[int(extra)],
        ), action)

    def blank(self, action):
        slots = self.slots
        if slots.more:
            @pl.when(self.mine == slots.small)
            def _():
                tail = self.back.at[pl.ds(slots.count * slots.small, slots.count * slots.more)]
                copy = pltpu.make_async_copy(self.zeros, tail, self.local_sems.at[2])
                getattr(copy, action)()

    def start(self):
        if self.slots.more:
            self.zeros[...] = jnp.zeros_like(self.zeros)
        self.blank("start")

        @pl.loop(1, self.slots.count)
        def _(shift):
            self.out(shift, "start")

        self.own("start")

    def finish(self):
        @pl.loop(1, self.slots.count)
        def _(shift):
            self.into(shift)
            self.out(shift, "wait_send")

        self.own("wait")
        self.blank("wait")


def slot_return_scratch(slots, width):
    return [pltpu.VMEM((max(slots.count * slots.more, 16), width), LOW)] + [
        pltpu.SemaphoreType.DMA((2 * slots.count,)), pltpu.SemaphoreType.DMA((2 * slots.count,)),
        pltpu.SemaphoreType.DMA((3,)),
    ]


def slot_exchange_sems(count):
    return [
        pltpu.SemaphoreType.DMA((2 * count,)), pltpu.SemaphoreType.DMA((2 * count,)),
        pltpu.SemaphoreType.DMA((2,)),
    ]


class ReturnGather:
    def __init__(self, slots, rows, held, sends, recvs, local_sems):
        self.slots, self.rows, self.held = slots, rows, held
        self.sems, self.local_sems = (sends, recvs), local_sems
        self.place = lax.axis_index("dp")
        self.me, self.near, self.far, self.corner = partners()

    def out(self, shift, action):
        slots = self.slots
        source = lax.rem(self.place + shift, slots.count)
        size = slots.size(source, self.me)
        at, to = slots.packed(source, self.me), slots.row(source, self.me, shift)
        slots.each(size > slots.small, lambda extra: remote(
            self.rows.at[slots.span(at, extra)], self.held.at[slots.span(to, extra)],
            *self.sems, 2 * shift + int(extra), "dp", source,
        ), action)

    def own(self, action):
        slots = self.slots
        size = slots.size(self.place, self.me)
        at, to = slots.packed(self.place, self.me), slots.row(self.place, self.me, 0)
        slots.each(size > slots.small, lambda extra: pltpu.make_async_copy(
            self.rows.at[slots.span(at, extra)], self.held.at[slots.span(to, extra)],
            self.local_sems.at[int(extra)],
        ), action)

    def block(self, lane, head, shift, axis, other, action):
        slots = self.slots
        size = slots.size(self.place, head)
        to = slots.row(self.place, head, shift)

        def make(extra):
            block = self.held.at[slots.span(to, extra)]
            index = 2 * (lane * slots.count + shift) + int(extra)
            return remote(block, block, *self.sems, index, axis, other)

        slots.each(size > slots.small, make, action)

    def start(self):
        @pl.loop(1, self.slots.count)
        def _(shift):
            self.out(shift, "start")

        self.own("start")

    def relay(self, shift):
        @pl.when(shift == 0)
        def _():
            self.own("wait")

        @pl.when(shift > 0)
        def _():
            expert = lax.rem(self.place + self.slots.count - shift, self.slots.count)
            self.block(0, self.me, shift, "dp", expert, "wait_recv")

        self.block(1, self.me, shift, "head", self.far, "start")
        self.block(2, self.me, shift, "head", self.near, "start")

    def forward(self, shift):
        self.block(1, self.far, shift, "head", self.far, "wait_recv")
        self.block(3, self.far, shift, "head", self.near, "start")

    def rest(self, shift):
        self.block(2, self.near, shift, "head", self.near, "wait_recv")
        self.block(3, self.corner, shift, "head", self.near, "wait_recv")

    def of_phase(self, phase, action):
        @pl.loop(0, self.slots.turns)
        def _(turn):
            action(phase * self.slots.turns + turn)

    def finish(self):
        @pl.loop(0, self.slots.count)
        def _(shift):
            @pl.when(shift > 0)
            def _():
                self.out(shift, "wait_send")

            self.block(1, self.me, shift, "head", self.far, "wait_send")
            self.block(2, self.me, shift, "head", self.near, "wait_send")
            self.block(3, self.far, shift, "head", self.near, "wait_send")


def return_gather_sems(count):
    return [
        pltpu.SemaphoreType.DMA((8 * count,)), pltpu.SemaphoreType.DMA((8 * count,)),
        pltpu.SemaphoreType.DMA((2,)),
    ]


def greet_all(heads, dp_count):
    barrier = pltpu.get_barrier_semaphore()
    place = lax.axis_index("dp")
    for other in heads:
        pl.semaphore_signal(barrier, inc=1, device_id={"head": other}, device_id_type=MESH)

    @pl.loop(1, dp_count)
    def _(shift):
        other = lax.rem(place + shift, dp_count)
        pl.semaphore_signal(barrier, inc=1, device_id={"dp": other}, device_id_type=MESH)

    pl.semaphore_wait(barrier, len(heads) + dp_count - 1)


ANYWHERE = pl.BlockSpec(memory_space=pl.ANY)
INSIDE = pl.BlockSpec(memory_space=pltpu.VMEM)


def prepare_kernel(
    tile_ref, norm_ref, src_ref, col_ref, up_ref, x_in, g_in,
    w_ref, xn_out, sent_out, up_out,
    x_ref, g_ref, xn_ref, up_full, up_low, held, sent_sum, sent_ref,
    load_sems, save_sems, *sems,
):
    images = x_ref.shape[0]
    gather = LineGather(held, *sems[:6])
    spread = ImageGather(up_out, *sems[6:8], own=up_low, local_sem=sems[8])
    load_up = pltpu.make_async_copy(up_ref, up_full, load_sems.at[2, 0])
    load_up.start()

    def load(image):
        return (
            pltpu.make_async_copy(x_in.at[image], x_ref.at[image], load_sems.at[0, image]),
            pltpu.make_async_copy(g_in.at[image], g_ref.at[image], load_sems.at[1, image]),
        )

    def save(image):
        return pltpu.make_async_copy(xn_ref.at[image], xn_out.at[image], save_sems.at[image])

    for image in range(images):
        for copy in load(image):
            copy.start()
    me = lax.axis_index("dp")
    held[me] = tile_ref[...].astype(LOW)
    greet(*gather.neighbours(), ("head", spread.near), ("head", spread.far))
    gather.start()
    load_up.wait()
    up_low[...] = up_full[...].astype(LOW)
    spread.start()
    shape = (sent_ref.shape[0], PATCH)
    sent_sum[...] = jnp.zeros_like(sent_sum)
    steps = gather.length - 1

    def image_step(image):
        for copy in load(image):
            copy.wait()
        normal, _ = normalise(x_ref[image].astype(FULL))
        xn_ref[image] = (normal * norm_ref[0:1, :] + norm_ref[1:2, :]).astype(LOW)
        save(image).start()
        slots = lax.broadcasted_iota(jnp.int32, shape, 0)
        col = col_ref[image]
        pick = one_hot((slots == col[0:1, :]) | (slots == col[1:2, :]))
        sent_sum[...] += nn(pick, g_ref[image])

    @pl.loop(0, max(steps, (images + 1) // 2))
    def _(turn):
        @pl.loop(2 * turn, jnp.minimum(2 * turn + 2, images))
        def _(image):
            image_step(image)

        @pl.when(turn < steps)
        def _():
            gather.step(turn + 1)

    sent_ref[...] = sent_sum[...].astype(LOW)
    save_sent = pltpu.make_async_copy(sent_ref, sent_out, load_sems.at[2, 1])
    save_sent.start()
    gather.finish()
    rows = w_ref.shape[0] // 4
    blocks, depth, width = held.shape
    for part in range(4):
        block = pl.ds(part * rows, rows)
        lanes = lax.broadcasted_iota(jnp.int32, (rows, blocks * depth), 1)
        pick = one_hot(lanes == src_ref[block, :])
        w_ref[block, :] = nn(pick, held[...].reshape(blocks * depth, width)).astype(LOW)
    spread.wait_far()
    spread.wait_near()
    spread.wait_corner()
    spread.finish()
    save_sent.wait()

    @pl.loop(0, images)
    def _(image):
        save(image).wait()


def prepare(tiles, patches, cotangent, norm_params, src_col, col_rows, up, slots, dp_count):
    images, _, width = patches.shape
    line = dp_count // 2
    return pl.pallas_call(
        prepare_kernel,
        in_specs=[INSIDE] * 4 + [ANYWHERE] * 3,
        out_specs=[INSIDE] + [ANYWHERE] * 3,
        out_shape=[
            jax.ShapeDtypeStruct((src_col.shape[0], width), LOW),
            jax.ShapeDtypeStruct(patches.shape, LOW),
            jax.ShapeDtypeStruct((slots, width), LOW),
            jax.ShapeDtypeStruct((4,) + up.shape, LOW),
        ],
        scratch_shapes=[pltpu.VMEM(patches.shape, LOW)] * 3
        + [
            pltpu.VMEM(up.shape, FULL), pltpu.VMEM(up.shape, LOW),
            pltpu.VMEM((dp_count,) + tiles.shape, LOW), pltpu.VMEM((slots, width), FULL),
            pltpu.VMEM((slots, width), LOW),
            pltpu.SemaphoreType.DMA((3, images)), pltpu.SemaphoreType.DMA((images,)),
        ]
        + [pltpu.SemaphoreType.DMA((line,))] * 6 + image_gather_sems() + [pltpu.SemaphoreType.DMA],
        compiler_params=params(collective_id=0, has_side_effects=True),
        name="prepare",
    )(tiles, norm_params, src_col, col_rows, up, patches, cotangent)


def head_mask(shape, axis, head):
    return lax.broadcasted_iota(jnp.int32, shape, axis) // HD == head


def forward_kernel(
    slots,
    w_ref, norm_ref, col_ref, xn_in, x_ref, g_sent_ref, down_ref,
    lse_ref, q_out, qt_out, k_out, kt_out, v_out, ot_out, x1_out, rows_out, g_rows_out, down_out,
    q_ref, qt_ref, k_ref, kt_ref, v_ref, ot_ref, x1_ref, xn_ref, own_ref, sent_ref, sent_sum,
    down_full, down_low, save_sems, own_sem, *exchange,
):
    images = xn_ref.shape[0]
    rows = w_ref.shape[0] // 4
    heads = rows // HD
    total_of = ImageSum(*exchange[:8])
    spread = ImageGather(x1_ref, *exchange[8:10])
    spread_down = ImageGather(down_out, *exchange[10:12], own=down_low, local_sem=exchange[12])
    send_g = SlotExchange(slots, g_sent_ref, g_rows_out, *exchange[13:16])
    send_rows = SlotExchange(slots, sent_ref, rows_out, *exchange[16:])
    me, near, far, corner = partners()

    def load(turn):
        image = total_of.image(turn)
        return pltpu.make_async_copy(xn_in.at[image], xn_ref.at[image], save_sems.at[6, turn])

    for turn in range(images):
        load(turn).start()
    load_down = pltpu.make_async_copy(down_ref, down_full, own_sem.at[1])
    load_down.start()
    own = pltpu.make_async_copy(x_ref.at[me], own_ref, own_sem.at[0])
    own.start()
    greet_all((near, far), slots.count)
    load_down.wait()
    down_low[...] = down_full[...].astype(LOW)
    spread_down.start_far(0, 1)
    spread_down.start_near()
    send_g.start()
    kept = ((q_ref, q_out), (qt_ref, qt_out), (k_ref, k_out), (kt_ref, kt_out), (v_ref, v_out), (ot_ref, ot_out))
    shrink = HD ** (-0.5)

    def save(image):
        return [
            pltpu.make_async_copy(ref.at[image], out.at[image], save_sems.at[index, image])
            for index, (ref, out) in enumerate(kept)
        ]

    @pl.loop(0, images)
    def _(turn):
        image = total_of.image(turn)
        load(turn).wait()
        xn = xn_ref[image]
        wq, wk, wv, wo = (w_ref[pl.ds(part * rows, rows), :] for part in range(4))
        q_ref[image] = (nt(xn, wq) * shrink).astype(LOW)
        qt = (nt(wq, xn) * shrink).astype(LOW)
        qt_ref[image] = qt
        k = nt(xn, wk).astype(LOW)
        k_ref[image] = k
        kt_ref[image] = nt(wk, xn).astype(LOW)
        v_ref[image] = nt(xn, wv).astype(LOW)
        vt = nt(wv, xn).astype(LOW)
        mixed = []
        for head in range(heads):
            span = slice(head * HD, (head + 1) * HD)
            only = jnp.where(head_mask(qt.shape, 0, head), qt, jnp.zeros_like(qt))
            scores = nn(k, only)
            top = jnp.max(scores, axis=0, keepdims=True)
            weights = jnp.exp(scores - top)
            total = jnp.sum(weights, axis=0, keepdims=True)
            mixed.append(nn(vt[span], weights.astype(LOW)) / total)
            lse_ref[image, head:head + 1, :] = top + jnp.log(total)
        ot = jnp.concatenate(mixed, axis=0).astype(LOW)
        ot_ref[image] = ot
        total_of.give(turn, tn(ot, wo))
        for copy in save(image):
            copy.start()

    own.wait()
    x1_ref[me] = (own_ref[...].astype(FULL) + total_of.result()).astype(LOW)
    spread.start()
    sent_sum[...] = jnp.zeros_like(sent_sum)

    def place(image):
        normal, _ = normalise(x1_ref[image].astype(FULL))
        low = (normal * norm_ref[2:3, :] + norm_ref[3:4, :]).astype(LOW)
        slots = lax.broadcasted_iota(jnp.int32, (sent_ref.shape[0], PATCH), 0)
        col = col_ref[image]
        pick = one_hot((slots == col[0:1, :]) | (slots == col[1:2, :]))
        sent_sum[...] += nn(pick, low)

    place(me)
    spread.wait_near()
    place(near)
    spread.wait_far()
    place(far)
    spread.wait_corner()
    keep = pltpu.make_async_copy(x1_ref, x1_out, own_sem.at[0])
    keep.start()
    spread_down.start_far(1)
    place(corner)
    sent_ref[...] = sent_sum[...].astype(LOW)
    send_rows.start()
    spread.finish()
    total_of.finish()
    keep.wait()
    send_g.finish()
    spread_down.wait_far()
    spread_down.wait_near()
    spread_down.wait_corner()
    spread_down.finish()
    send_rows.finish()

    @pl.loop(0, images)
    def _(image):
        for copy in save(image):
            copy.wait()


def attention_forward(slots, xn, w, norm_params, col_rows, patches, g_sent, down):
    images, _, width = patches.shape
    rows = w.shape[0] // 4
    flat, turned = (images, PATCH, rows), (images, rows, PATCH)
    saved = [flat, turned, flat, turned, flat, turned, patches.shape]
    outs = saved + [(slots.rows, width), (slots.rows, width), (4,) + down.shape]
    most = slots.count * slots.big
    return pl.pallas_call(
        functools.partial(forward_kernel, slots),
        in_specs=[INSIDE] * 3 + [ANYWHERE] * 4,
        out_specs=[INSIDE] + [ANYWHERE] * 10,
        out_shape=[jax.ShapeDtypeStruct((images, 8, PATCH), FULL)]
        + [jax.ShapeDtypeStruct(shape, LOW) for shape in outs],
        scratch_shapes=[pltpu.VMEM(shape, LOW) for shape in saved]
        + [
            pltpu.VMEM(patches.shape, LOW),
            pltpu.VMEM((PATCH, width), LOW), pltpu.VMEM((most, width), LOW),
            pltpu.VMEM((most, width), FULL),
            pltpu.VMEM(down.shape, FULL), pltpu.VMEM(down.shape, LOW),
            pltpu.SemaphoreType.DMA((7, images)), pltpu.SemaphoreType.DMA((2,)),
        ]
        + image_sum_scratch(PATCH, width) + image_gather_sems() + image_gather_sems()
        + [pltpu.SemaphoreType.DMA]
        + slot_exchange_sems(slots.count) + slot_exchange_sems(slots.count),
        compiler_params=params(collective_id=1, has_side_effects=True),
        name="attention_forward",
    )(w, norm_params, col_rows, xn, patches, g_sent, down)


def backward_kernel(
    experts, slots,
    w_ref, lse_ref, src_ref, norm_ref, small_ref,
    x1g_in, xn_in, q_in, qt_in, k_in, kt_in, v_in, ot_in, x_ref, out_rows_ref, down_part,
    owned_ref, small_out, down_grad_ref, input_out, out_back,
    x1g_ref, xn_ref, q_ref, qt_ref, k_ref, kt_ref, v_ref, ot_ref,
    grad_ref, own_ref, input_ref, padded_ref, load_sems, own_sem, *exchange,
):
    images = x1g_ref.shape[0]
    rows = w_ref.shape[0] // 4
    heads = rows // HD
    total_of = ImageSum(*exchange[:8])
    spread = ImageGather(input_ref, *exchange[8:10])
    back_out = SlotReturn(slots, out_rows_ref, out_back, *exchange[10:14])
    weights_sum = LineScatter(padded_ref, owned_ref, *exchange[14:24])
    down_sum = BlockSum(down_part, *exchange[24:32])
    small_sum = SmallSum(*exchange[32:])
    me, near, far, corner = partners()
    dp_count = slots.count
    streamed = (
        (xn_in, xn_ref), (q_in, q_ref), (qt_in, qt_ref), (k_in, k_ref), (kt_in, kt_ref),
        (v_in, v_ref), (ot_in, ot_ref),
    )

    def load(turn):
        image, slot = total_of.image(turn), lax.rem(turn, 2)
        copies = [
            pltpu.make_async_copy(source.at[image], target.at[slot], load_sems.at[index, slot])
            for index, (source, target) in enumerate(streamed)
        ]
        copies.append(
            pltpu.make_async_copy(x1g_in.at[image], x1g_ref.at[image], load_sems.at[7, slot])
        )
        return copies

    for turn in range(2):
        for copy in load(turn):
            copy.start()
    own = pltpu.make_async_copy(x_ref.at[me], own_ref, own_sem.at[0])
    own.start()
    greet_all((near, far, corner), dp_count)
    down_sum.start()
    back_out.start()
    down_sum.across()
    shrink = HD ** (-0.5)
    grad_ref[...] = jnp.zeros_like(grad_ref)

    @pl.loop(0, images)
    def _(turn):
        image, slot = total_of.image(turn), lax.rem(turn, 2)
        for copy in load(turn):
            copy.wait()
        wq, wk, wv, wo = (w_ref[pl.ds(part * rows, rows), :] for part in range(4))
        x1g, xn = x1g_ref[image], xn_ref[slot]
        q, qt, k, kt = q_ref[slot], qt_ref[slot], k_ref[slot], kt_ref[slot]
        v, ot = v_ref[slot], ot_ref[slot]
        do = nt(x1g, wo).astype(LOW)
        dot = nt(wo, x1g).astype(LOW)
        product = dot.astype(FULL) * ot.astype(FULL)
        dqt, dk, dv = [], None, None
        for head in range(heads):
            span = slice(head * HD, (head + 1) * HD)
            zero_t = jnp.zeros_like(qt)
            mask_t = head_mask(qt.shape, 0, head)
            mask = head_mask(q.shape, 1, head)
            scores = nn(k, jnp.where(mask_t, qt, zero_t))
            weights = jnp.exp(scores - lse_ref[image, head:head + 1, :])
            back = nn(v, jnp.where(mask_t, dot, zero_t))
            delta = jnp.sum(product[span], axis=0, keepdims=True)
            score_grad = (weights * (back - delta)).astype(LOW)
            dqt.append(nn(kt[span], score_grad) * shrink)
            dk_one = nn(score_grad, jnp.where(mask, q, jnp.zeros_like(q)))
            dv_one = nn(weights.astype(LOW), jnp.where(mask, do, jnp.zeros_like(do)))
            dk = dk_one if dk is None else dk + dk_one
            dv = dv_one if dv is None else dv + dv_one
        dqt = jnp.concatenate(dqt, axis=0).astype(LOW)
        dk, dv = dk.astype(LOW), dv.astype(LOW)
        total_of.give(turn, tn(dqt, wq) + nn(dk, wk) + nn(dv, wv))
        pieces = (nn(dqt, xn), tn(dk, xn), tn(dv, xn), nn(ot, x1g))
        for part, piece in enumerate(pieces):
            grad_ref[pl.ds(part * rows, rows), :] += piece

        @pl.when(turn + 2 < images)
        def _():
            for copy in load(turn + 2):
                copy.start()

    own.wait()
    normal, scale = normalise(own_ref[...].astype(FULL))
    back, gain_sum, shift_sum = norm_back(normal, scale, norm_ref[0:1, :], total_of.result())
    input_ref[me] = (x1g_ref[me].astype(FULL) + back).astype(LOW)
    spread.start()
    small = small_ref[...]
    row = lax.broadcasted_iota(jnp.int32, small.shape, 0)
    small = small + jnp.where(row == experts, gain_sum, 0.0)
    small_sum.start(small + jnp.where(row == experts + 1, shift_sum, 0.0))
    low = grad_ref[...].astype(LOW)
    depth = padded_ref.shape[1]
    parts = min(dp_count, 8)
    cut = dp_count // parts * depth
    for part in range(parts):
        row = lax.broadcasted_iota(jnp.int32, (cut, low.shape[0]), 0) + part * cut
        pick = one_hot(row == src_ref[...])
        block = nn(pick, low).astype(LOW)
        padded_ref[pl.ds(part * (dp_count // parts), dp_count // parts)] = block.reshape(
            dp_count // parts, depth, block.shape[1]
        )
    weights_sum.start()
    small_sum.across()
    steps = weights_sum.length

    @pl.loop(0, steps - 1)
    def _(turn):
        weights_sum.step(steps - 1 - turn)

        @pl.when(turn == 0)
        def _():
            small_sum.back()

        @pl.when(turn == steps - 2)
        def _():
            spread.wait_far()

    weights_sum.result()
    small_sum.result(small_out)
    down_grad_ref[...] = down_sum.result()
    spread.wait_near()
    spread.wait_corner()
    keep = pltpu.make_async_copy(input_ref, input_out, own_sem.at[0])
    keep.start()
    back_out.finish()
    spread.finish()
    total_of.finish()
    weights_sum.finish()
    small_sum.finish()
    down_sum.finish()
    keep.wait()


def attention_backward(
    experts, slots, depth,
    x1_grad, w, xn, saved, lse, src_row, norm_params, small, patches, out_rows, down_part,
):
    images, _, width = patches.shape
    rows = w.shape[0] // 4
    dp_count = slots.count
    flat, turned = (2, PATCH, rows), (2, rows, PATCH)
    units = down_part.shape[1]
    return pl.pallas_call(
        functools.partial(backward_kernel, experts, slots),
        in_specs=[INSIDE] * 5 + [ANYWHERE] * 11,
        out_specs=[INSIDE] * 3 + [ANYWHERE] * 2,
        out_shape=[
            jax.ShapeDtypeStruct((depth, width), FULL), jax.ShapeDtypeStruct(small.shape, FULL),
            jax.ShapeDtypeStruct((units, width), FULL),
            jax.ShapeDtypeStruct(patches.shape, LOW),
            jax.ShapeDtypeStruct((dp_count * slots.big, width), LOW),
        ],
        scratch_shapes=[pltpu.VMEM(patches.shape, LOW), pltpu.VMEM((2, PATCH, width), LOW)]
        + [pltpu.VMEM(shape, LOW) for shape in (flat, turned, flat, turned, flat, turned)]
        + [
            pltpu.VMEM(w.shape, FULL), pltpu.VMEM((PATCH, width), LOW),
            pltpu.VMEM(patches.shape, LOW), pltpu.VMEM((dp_count, depth, width), LOW),
            pltpu.SemaphoreType.DMA((8, 2)), pltpu.SemaphoreType.DMA((2,)),
        ]
        + image_sum_scratch(PATCH, width) + image_gather_sems()
        + slot_return_scratch(slots, width)
        + line_scatter_scratch(dp_count, depth, width)
        + block_sum_scratch(units, width)
        + small_sum_scratch(small.shape[0], width, dp_count),
        compiler_params=params(collective_id=2, has_side_effects=True),
        name="attention_backward",
    )(
        w, lse, src_row, norm_params, small, x1_grad, xn, *saved, patches, out_rows, down_part,
    )


def picked_rows(slots, col, held_ref, phase):
    start = phase * slots.phase_rows
    lanes = lax.broadcasted_iota(jnp.int32, (col.shape[0], slots.phase_rows), 1) + start
    pick = one_hot((lanes == col[:, 0:1]) | (lanes == col[:, 1:2]))
    return nn(pick, held_ref[pl.ds(start, slots.phase_rows), :])


def combine_kernel(col_ref, x1_ref, *refs):
    *held, out_ref = refs
    total = x1_ref[0].astype(FULL)
    col = col_ref[0]
    for part, rows_ref in enumerate(held):
        count = rows_ref.shape[0]
        lanes = lax.broadcasted_iota(jnp.int32, (col.shape[0], count), 1) + part * count
        pick = one_hot((lanes == col[:, 0:1]) | (lanes == col[:, 1:2]))
        total = total + nn(pick, rows_ref[...])
    out_ref[0] = total.astype(LOW)


def combine_forward(col, x1, held):
    images, _, width = x1.shape
    wide = lead((1, PATCH, width))
    return pl.pallas_call(
        combine_kernel,
        grid=(images,),
        in_specs=[lead((1, PATCH, 2)), wide] + [whole(rows.shape) for rows in held],
        out_specs=wide,
        out_shape=jax.ShapeDtypeStruct(x1.shape, LOW),
        compiler_params=params(),
        cost_estimate=pl.CostEstimate(
            flops=2 * images * PATCH * sum(rows.size for rows in held),
            bytes_accessed=4 * x1.size + 2 * sum(rows.size for rows in held), transcendentals=0,
        ),
        name="combine_forward",
    )(col, x1, *held)


def expert_kernel(
    slots,
    rows_ref, g_ref, router_ref, own_ref, closed_ref, col_ref, norm_ref,
    up_in, down_in, x1_in, cot_in,
    up_grad_ref, router_grad_ref, sums_ref, down_out, out_out, x1g_out,
    up_ref, down_ref, og_ref, gate_ref, probs_ref, down_stage, out_ref, back_ref,
    held, total, x1_ref, cot_ref, x1g_ref,
    load_sems, save_sems, image_sems, out_sem, *exchange,
):
    images, count = x1_in.shape[0], rows_ref.shape[0]
    out_sum, back_sum = total.at[pl.ds(0, count)], total.at[pl.ds(count, count)]
    up_sum = ImageSum(*exchange[:8])
    back = ReturnGather(slots, back_ref, held, *exchange[8:])
    parts = up_in.shape[0]

    def load(turn):
        part, slot = up_sum.image(turn), lax.rem(turn, 2)
        return (
            pltpu.make_async_copy(up_in.at[part], up_ref.at[slot], load_sems.at[0, slot]),
            pltpu.make_async_copy(down_in.at[part], down_ref.at[slot], load_sems.at[1, slot]),
        )

    def save(turn):
        slot = lax.rem(turn, 2)
        return pltpu.make_async_copy(
            down_stage.at[slot], down_out.at[up_sum.image(turn)], save_sems.at[slot]
        )

    for turn in range(2):
        for copy in load(turn):
            copy.start()
    rows = rows_ref[...]
    logits = nt(rows, router_ref[...]) + closed_ref[...]
    top = jnp.max(logits, axis=-1, keepdims=True)
    weights = jnp.exp(logits - top)
    probs = weights / jnp.sum(weights, axis=-1, keepdims=True)
    gate = jnp.sum(probs * own_ref[...], axis=-1, keepdims=True)
    probs_ref[...] = probs
    gate_ref[...] = gate
    og_ref[...] = (gate * g_ref[...].astype(FULL)).astype(LOW)
    out_sum[...] = jnp.zeros_like(out_sum)
    back_sum[...] = jnp.zeros_like(back_sum)
    greet_all((back.near, back.far), slots.count)

    @pl.loop(0, parts)
    def _(turn):
        slot = lax.rem(turn, 2)
        for copy in load(turn):
            copy.wait()
        rows, og = rows_ref[...], og_ref[...]
        up, down = up_ref[slot], down_ref[slot]
        hidden = nn(rows, up)
        slope = (2.0 / jnp.pi) ** 0.5
        square = hidden * hidden
        bend = jnp.tanh(slope * (hidden + 0.044715 * (square * hidden)))
        act = (0.5 * hidden * (1.0 + bend)).astype(LOW)
        out_sum[...] += nn(act, down)
        act_grad = nt(og, down)
        inner = slope * (1.0 + (3.0 * 0.044715) * square)
        curve = 0.5 * (1.0 + bend) + 0.5 * hidden * (1.0 - bend * bend) * inner
        hidden_grad = (curve * act_grad).astype(LOW)
        back_sum[...] += nt(hidden_grad, up)
        up_sum.give(turn, tn(rows, hidden_grad))

        @pl.when(turn >= 2)
        def _():
            save(turn - 2).wait()

        down_stage[lax.rem(turn, 2)] = tn(act, og).astype(LOW)
        save(turn).start()

        @pl.when(turn + 2 < parts)
        def _():
            for copy in load(turn + 2):
                copy.start()

    out = out_sum[...].astype(LOW).astype(FULL)
    gate, probs = gate_ref[...], probs_ref[...]
    gate_grad = jnp.sum(g_ref[...].astype(FULL) * out, axis=-1, keepdims=True)
    logit_grad = (gate_grad * (probs * (own_ref[...] - gate))).astype(LOW)
    plain = back_sum[...].astype(LOW).astype(FULL)
    back_ref[...] = (plain + nn(logit_grad, router_ref[...])).astype(LOW)
    back.start()
    out_ref[...] = (gate * out).astype(LOW)
    save_out = pltpu.make_async_copy(out_ref, out_out, out_sem)
    save_out.start()
    router_grad_ref[...] = tn(logit_grad, rows_ref[...])

    def image_load(image):
        slot = lax.rem(image, 2)
        return (
            pltpu.make_async_copy(x1_in.at[image], x1_ref.at[slot], image_sems.at[0, slot]),
            pltpu.make_async_copy(cot_in.at[image], cot_ref.at[slot], image_sems.at[1, slot]),
        )

    def image_save(image):
        slot = lax.rem(image, 2)
        return pltpu.make_async_copy(x1g_ref.at[slot], x1g_out.at[image], image_sems.at[2, slot])

    for image in range(2):
        for copy in image_load(image):
            copy.start()
    back.of_phase(0, back.relay)

    @pl.loop(0, 4)
    def _(phase):
        back.of_phase(phase, back.forward)

        @pl.when(phase < 3)
        def _():
            back.of_phase(phase + 1, back.relay)

        back.of_phase(phase, back.rest)

        @pl.loop(0, images)
        def _(image):
            part = picked_rows(slots, col_ref[image], held, phase)

            @pl.when(phase == 0)
            def _():
                total[pl.ds(image * PATCH, PATCH)] = part

            @pl.when(phase > 0)
            def _():
                total[pl.ds(image * PATCH, PATCH)] += part

    sums_ref[...] = jnp.zeros_like(sums_ref)

    @pl.loop(0, images)
    def _(image):
        slot = lax.rem(image, 2)
        for copy in image_load(image):
            copy.wait()

        @pl.when(image >= 2)
        def _():
            image_save(image - 2).wait()

        normal, scale = normalise(x1_ref[slot].astype(FULL))
        upstream = total[pl.ds(image * PATCH, PATCH)]
        result, gain_sum, shift_sum = norm_back(normal, scale, norm_ref[2:3, :], upstream)
        x1g_ref[slot] = (cot_ref[slot].astype(FULL) + result).astype(LOW)
        sums_ref[0:1, :] += gain_sum
        sums_ref[1:2, :] += shift_sum
        image_save(image).start()

        @pl.when(image + 2 < images)
        def _():
            for copy in image_load(image + 2):
                copy.start()

    up_grad_ref[...] = up_sum.result()
    back.finish()
    up_sum.finish()
    save_out.wait()
    for turn in range(parts - 2, parts):
        save(turn).wait()
    for image in range(images - 2, images):
        image_save(image).wait()


def expert_stage(slots, rows, g_rows, up, down, router_low, own, col, x1, cotangent, norm_params):
    count, width = rows.shape
    parts, _, units = up.shape
    images = x1.shape[0]
    experts = router_low.shape[0]
    lanes = 128
    router_wide = jnp.zeros((lanes, width), LOW).at[:experts].set(router_low)
    lane = jnp.arange(lanes, dtype=jnp.int32)[None, :]
    own_row = jnp.where(lane == own, 1.0, 0.0).astype(FULL)
    closed = jnp.where(lane < experts, 0.0, -1e30).astype(FULL)
    flat = pltpu.VMEM((count, width), LOW)
    pair = pltpu.VMEM((2, PATCH, width), LOW)
    return pl.pallas_call(
        functools.partial(expert_kernel, slots),
        in_specs=[INSIDE] * 7 + [ANYWHERE] * 4,
        out_specs=[INSIDE] * 3 + [ANYWHERE] * 3,
        out_shape=[
            jax.ShapeDtypeStruct((width, units), FULL),
            jax.ShapeDtypeStruct((lanes, width), FULL),
            jax.ShapeDtypeStruct((8, width), FULL),
            jax.ShapeDtypeStruct(down.shape, LOW),
            jax.ShapeDtypeStruct((count, width), LOW),
            jax.ShapeDtypeStruct(x1.shape, LOW),
        ],
        scratch_shapes=[
            pltpu.VMEM((2,) + up.shape[1:], LOW), pltpu.VMEM((2,) + down.shape[1:], LOW), flat,
            pltpu.VMEM((count, 1), FULL), pltpu.VMEM((count, lanes), FULL),
            pltpu.VMEM((2, units, width), LOW), flat, flat,
            pltpu.VMEM((4 * slots.phase_rows, width), LOW),
            pltpu.VMEM((max(images * PATCH, 2 * count), width), FULL), pair, pair, pair,
            pltpu.SemaphoreType.DMA((2, 2)), pltpu.SemaphoreType.DMA((2,)),
            pltpu.SemaphoreType.DMA((3, 2)), pltpu.SemaphoreType.DMA,
        ]
        + image_sum_scratch(width, units) + return_gather_sems(slots.count),
        compiler_params=params(collective_id=3, has_side_effects=True),
        name="expert_stage",
    )(
        rows, g_rows, router_wide, own_row, closed, col, norm_params, up, down, x1, cotangent,
    )


def body(
    patches, cotangent, expert_ids, slot_pos, owners,
    tile_master, tile_first, tile_second,
    expert_up, up_first, up_second,
    expert_down, down_first, down_second,
    router, router_first, router_second,
    norm_params, norm_first, norm_second,
):
    tok_rows, width = patches.shape
    experts = router.shape[0]
    capacity = tok_rows // experts
    dp_count = lax.axis_size("dp")
    head_count = lax.axis_size("head")
    me_head = lax.axis_index("head")
    me_dp = lax.axis_index("dp")
    images = tok_rows // PATCH
    slots = Slots(dp_count, capacity // head_count)
    slot_count = tile_master.shape[0]

    owner_row = owners[0]
    tile_count = owner_row.shape[0]
    order_index = jnp.arange(tile_count, dtype=jnp.int32)
    same_owner = owner_row[:, None] == owner_row[None, :]
    earlier = order_index[None, :] < order_index[:, None]
    tile_rank = jnp.sum(jnp.where(same_owner & earlier, 1, 0), axis=1).astype(jnp.int32)
    tile_place = owner_row * slot_count + tile_rank
    src = (tile_place[:, None] * TILE + jnp.arange(TILE, dtype=jnp.int32)[None, :]).reshape(-1)

    ids, pos = expert_ids.T, slot_pos.T
    kept = pos < capacity
    holder, within = slots.holder(me_dp, jnp.minimum(pos, capacity - 1))
    size = slots.size(me_dp, me_head)
    col_rows = jnp.where(kept & (holder == me_head), ids * size + within, -1)
    col_rows = col_rows.reshape(2, images, PATCH).transpose(1, 0, 2)
    shift = (me_dp + dp_count - ids) % dp_count
    col = jnp.where(kept, slots.row(me_dp, holder, shift) + within, -1)
    col = col.T.reshape(images, PATCH, 2)
    seen = lax.bitwise_xor(holder, me_head) * (dp_count * slots.big)
    col_out = jnp.where(kept, seen + shift * slots.size(me_dp, holder) + within, -1)
    col_out = col_out.T.reshape(images, PATCH, 2)

    by_image = (images, PATCH, width)
    x_images, g_images = patches.reshape(by_image), cotangent.reshape(by_image)
    w, xn, g_sent, up_all = prepare(
        tile_master.reshape(slot_count * TILE, width), x_images, g_images, norm_params,
        src[:, None], col_rows, expert_up[0], slots.count * slots.big, dp_count,
    )
    lse, *saved, x1, rows, g_rows, down_all = attention_forward(
        slots, xn, w, norm_params, col_rows, x_images, g_sent, expert_down[0]
    )
    up_grad, router_part, second_sums, down_part, out, x1_grad = expert_stage(
        slots, rows, g_rows, up_all, down_all, router.astype(LOW), me_dp, col, x1, g_images,
        norm_params,
    )

    small_rows = -(-(experts + 4) // 16) * 16
    small = jnp.concatenate(
        [
            router_part[:experts], jnp.zeros((2, width), FULL),
            second_sums[:2] * (1.0 / head_count),
            jnp.zeros((small_rows - experts - 4, width), FULL),
        ]
    )
    owned_grad, small, down_grad, input_low, out_back = attention_backward(
        experts, slots, slot_count * TILE,
        x1_grad, w, xn, saved, lse, src[None, :], norm_params, small, x_images, out, down_part,
    )
    owned_grad = owned_grad.reshape(slot_count, TILE, width)
    input_grad = input_low.reshape(tok_rows, width).astype(FULL)

    def from_head(rows, apart):
        return lax.ppermute(rows, "head", [(at, at ^ apart) for at in range(head_count)])

    out_far = from_head(out_back, 2)
    held = [out_back, from_head(out_back, 1), out_far, from_head(out_far, 1)]
    block_out = combine_forward(col_out, x1, held).reshape(tok_rows, width)

    router_total, norm_total = small[:experts], small[experts:experts + 4]

    tile_new, tile_first_new, tile_second_new = adam_update(
        tile_master, tile_first, tile_second, owned_grad, rate_attention, decay_factor
    )
    up_new, up_first_new, up_second_new = adam_update(
        expert_up, up_first, up_second, up_grad[None], rate_up, decay_factor
    )
    down_new, down_first_new, down_second_new = adam_update(
        expert_down, down_first, down_second, down_grad[None], rate_down, decay_factor
    )
    router_new, router_first_new, router_second_new = adam_update(
        router, router_first, router_second, router_total, rate_router, decay_factor
    )
    norm_new, norm_first_new, norm_second_all = adam_update(
        norm_params, norm_first, norm_second, norm_total, rate_norm, 0.0
    )
    return (
        block_out,
        input_grad,
        tile_new,
        tile_first_new,
        tile_second_new,
        tile_new.astype(LOW),
        up_new,
        up_first_new,
        up_second_new,
        up_new.astype(LOW),
        down_new,
        down_first_new,
        down_second_new,
        down_new.astype(LOW),
        router_new,
        router_first_new,
        router_second_new,
        norm_new,
        norm_first_new,
        norm_second_all[:2],
        norm_second_all[2:],
    )


def solution(mesh):
    row = P("dp", None)
    tiles = P(("dp", "head"), None, None)
    up = P("dp", None, "head")
    down = P("dp", "head", None)
    in_specs = (
        row, row, row, row, P("head", None), tiles, tiles, tiles,
        up, up, up, down, down, down, P(), P(), P(), P(), P(), P(),
    )
    out_specs = (
        row, row, tiles, tiles, tiles, tiles, up, up, up, up, down, down, down, down,
        P(), P(), P(), P(), P(), P(), P(),
    )
    return jax.shard_map(body, mesh=mesh, in_specs=in_specs, out_specs=out_specs, check_vma=False)
```

```python
import functools

import jax
import jax.numpy as jnp
from jax import lax
from jax.experimental import pallas as pl
from jax.experimental.pallas import tpu as pltpu
from jax.sharding import PartitionSpec as P

HD = 64
PATCH = 576
TILE = 8
STEP = 10

eps_norm = 1e-06
beta_one = 0.9
beta_two = 0.999
adam_eps = 1e-08
rate_attention = 0.12
rate_up = 0.08
rate_down = 0.3
rate_router = 0.05
rate_norm = 0.4
decay_factor = 0.1

LOW = jnp.bfloat16
FULL = jnp.float32
MESH = pl.DeviceIdType.MESH
VMEM_BYTES = 60 * 1024 * 1024


def adam_update(weight, moment_one, moment_two, gradient, step_rate, weight_decay):
    moment_one = beta_one * moment_one + (1.0 - beta_one) * gradient
    moment_two = beta_two * moment_two + (1.0 - beta_two) * gradient * gradient
    fixed_one = moment_one / (1.0 - beta_one**STEP)
    fixed_two = moment_two / (1.0 - beta_two**STEP)
    weight = weight - step_rate * (
        fixed_one / (jnp.sqrt(fixed_two) + adam_eps) + weight_decay * weight
    )
    return (weight, moment_one, moment_two)


def nn(left, right):
    return lax.dot_general(left, right, (((1,), (0,)), ((), ())), preferred_element_type=FULL)


def nt(left, right):
    return lax.dot_general(left, right, (((1,), (1,)), ((), ())), preferred_element_type=FULL)


def tn(left, right):
    return lax.dot_general(left, right, (((0,), (0,)), ((), ())), preferred_element_type=FULL)


def params(**more):
    return pltpu.CompilerParams(vmem_limit_bytes=VMEM_BYTES, **more)


def whole(shape):
    return pl.BlockSpec(shape, lambda *_: (0,) * len(shape))


def lead(shape):
    return pl.BlockSpec(shape, lambda i: (i,) + (0,) * (len(shape) - 1))


def normalise(values):
    average = jnp.mean(values, axis=-1, keepdims=True)
    centred = values - average
    variance = jnp.mean(centred * centred, axis=-1, keepdims=True)
    scale = lax.rsqrt(variance + eps_norm)
    return centred * scale, scale


def norm_back(normal, scale, gain, upstream):
    inner = upstream * gain
    mean_inner = jnp.mean(inner, axis=-1, keepdims=True)
    mean_cross = jnp.mean(inner * normal, axis=-1, keepdims=True)
    result = scale * (inner - mean_inner - normal * mean_cross)
    gain_sum = jnp.sum(upstream * normal, axis=0, keepdims=True)
    shift_sum = jnp.sum(upstream, axis=0, keepdims=True)
    return result, gain_sum, shift_sum


def one_hot(condition):
    return jnp.where(condition, 1.0, 0.0).astype(LOW)


def remote(src, dst, sends, recvs, index, axis, other):
    return pltpu.make_async_remote_copy(
        src_ref=src, dst_ref=dst, send_sem=sends.at[index], recv_sem=recvs.at[index],
        device_id={axis: other}, device_id_type=MESH,
    )


def greet(*others):
    barrier = pltpu.get_barrier_semaphore()
    for axis, other in others:
        pl.semaphore_signal(barrier, inc=1, device_id={axis: other}, device_id_type=MESH)
    pl.semaphore_wait(barrier, len(others))


def partners():
    me = lax.axis_index("head")
    near = me + 1 - 2 * lax.rem(me, 2)
    far = lax.rem(me + 2, 4)
    corner = lax.rem(near + 2, 4)
    return me, near, far, corner


class LineGather:
    def __init__(self, held, up_send, up_recv, down_send, down_recv, pair_send, pair_recv):
        self.held = held
        self.length = held.shape[0] // 2
        self.sems = ((up_send, up_recv), (down_send, down_recv), (pair_send, pair_recv))
        me = lax.axis_index("dp")
        self.place, self.side = me // 2, lax.rem(me, 2)
        self.above = lax.rem(self.place + 1, self.length) * 2 + self.side
        self.below = lax.rem(self.place + self.length - 1, self.length) * 2 + self.side
        self.other = self.place * 2 + 1 - self.side

    def neighbours(self):
        return ("dp", self.above), ("dp", self.below), ("dp", self.other)

    def copy(self, way, origin, side=None):
        index = origin * 2 + (self.side if side is None else side)
        target = (self.above, self.below, self.other)[way]
        block = self.held.at[index]
        return remote(block, block, *self.sems[way], origin, "dp", target)

    def pass_on(self, origin, up, down):
        @pl.when(up & (self.place < self.length - 1))
        def _():
            self.copy(0, origin).start()

        @pl.when(down & (self.place > 0))
        def _():
            self.copy(1, origin).start()

        self.copy(2, origin).start()

    def start(self):
        self.pass_on(self.place, True, True)

    def step(self, k):
        low, high = self.place - k, self.place + k

        @pl.when(low >= 0)
        def _():
            self.copy(0, low).wait_recv()
            self.pass_on(low, True, False)

        @pl.when(high < self.length)
        def _():
            self.copy(1, high).wait_recv()
            self.pass_on(high, False, True)

    def finish(self):
        @pl.loop(0, self.length)
        def _(origin):
            self.copy(2, origin).wait_recv()
            self.copy(2, origin).wait_send()

            @pl.when((origin <= self.place) & (self.place < self.length - 1))
            def _():
                self.copy(0, origin).wait_send()

            @pl.when((origin >= self.place) & (self.place > 0))
            def _():
                self.copy(1, origin).wait_send()


class ImageSum:
    def __init__(self, stage, corner_in, near_in, passed, mine, far_in, sends, recvs):
        self.stage, self.corner_in, self.near_in = stage, corner_in, near_in
        self.passed, self.mine, self.far_in = passed, mine, far_in
        self.sends, self.recvs = sends, recvs
        self.me, self.near, self.far, self.corner = partners()
        self.core = lax.rem(self.me, 2)

    def image(self, turn):
        base = self.me - self.core
        other = lax.rem(base + 2, 4)
        return jnp.where(turn < 2, other, base - 2) + turn

    def to_corner(self):
        return remote(
            self.stage.at[0], self.corner_in, self.sends, self.recvs, 0, "head", self.near
        )

    def to_near(self):
        return remote(
            self.stage.at[1], self.near_in, self.sends, self.recvs, 1, "head", self.near
        )

    def to_far(self):
        return remote(self.passed, self.far_in, self.sends, self.recvs, 2, "head", self.far)

    def give(self, turn, part):
        theirs = lax.rem(turn, 2) != self.core

        @pl.when((turn < 2) & theirs)
        def _():
            self.stage[0] = part.astype(LOW)
            self.to_corner().start()

        @pl.when((turn >= 2) & theirs)
        def _():
            self.stage[1] = part.astype(LOW)
            self.to_near().start()

        @pl.when((turn < 2) & ~theirs)
        def _():
            self.to_corner().wait_recv()
            self.passed[...] = (part + self.corner_in[...].astype(FULL)).astype(LOW)
            self.to_far().start()

        @pl.when((turn >= 2) & ~theirs)
        def _():
            self.mine[...] = part

    def result(self):
        self.to_near().wait_recv()
        self.to_far().wait_recv()
        return self.mine[...] + self.near_in[...].astype(FULL) + self.far_in[...].astype(FULL)

    def finish(self):
        self.to_corner().wait_send()
        self.to_near().wait_send()
        self.to_far().wait_send()


def image_sum_scratch(rows, width):
    block = pltpu.VMEM((rows, width), LOW)
    return [
        pltpu.VMEM((2, rows, width), LOW), block, block, block,
        pltpu.VMEM((rows, width), FULL), block,
        pltpu.SemaphoreType.DMA((3,)), pltpu.SemaphoreType.DMA((3,)),
    ]


class LineScatter:
    def __init__(
        self, blocks, out, pair_in, up_in, down_in, total,
        up_send, up_recv, down_send, down_recv, pair_send, pair_recv,
    ):
        self.blocks, self.out, self.total = blocks, out, total
        self.arrived = (up_in, down_in, pair_in)
        self.sems = ((up_send, up_recv), (down_send, down_recv), (pair_send, pair_recv))
        self.length = blocks.shape[0] // 2
        me = lax.axis_index("dp")
        self.place, self.side = me // 2, lax.rem(me, 2)
        self.targets = (
            lax.rem(self.place + 1, self.length) * 2 + self.side,
            lax.rem(self.place + self.length - 1, self.length) * 2 + self.side,
            self.place * 2 + 1 - self.side,
        )

    def copy(self, way, block):
        source = (
            self.blocks.at[block * 2 + 1 - self.side] if way == 2 else self.total.at[block]
        )
        return remote(
            source, self.arrived[way].at[block], *self.sems[way], block, "dp", self.targets[way]
        )

    def start(self):
        @pl.loop(0, self.length)
        def _(turn):
            distance = self.length - 1 - turn

            @pl.when(self.place + distance < self.length)
            def _():
                self.copy(2, self.place + distance).start()

            @pl.when((self.place >= distance) & (distance > 0))
            def _():
                self.copy(2, self.place - distance).start()

    def pair_sum(self, block):
        self.copy(2, block).wait_recv()
        own = self.blocks[block * 2 + self.side].astype(FULL)
        return own + self.arrived[2][block].astype(FULL)

    def forward(self, way, block, first):
        both = self.pair_sum(block)

        @pl.when(first)
        def _():
            self.total[block] = both.astype(LOW)

        @pl.when(~first)
        def _():
            self.copy(way, block).wait_recv()
            self.total[block] = (both + self.arrived[way][block].astype(FULL)).astype(LOW)

        self.copy(way, block).start()

    def step(self, distance):
        @pl.when(self.place + distance < self.length)
        def _():
            self.forward(0, self.place + distance, self.place == 0)

        @pl.when(self.place >= distance)
        def _():
            self.forward(1, self.place - distance, self.place == self.length - 1)

    def result(self):
        self.out[...] = self.pair_sum(self.place)

        @pl.when(self.place > 0)
        def _():
            self.copy(0, self.place).wait_recv()
            self.out[...] += self.arrived[0][self.place].astype(FULL)

        @pl.when(self.place < self.length - 1)
        def _():
            self.copy(1, self.place).wait_recv()
            self.out[...] += self.arrived[1][self.place].astype(FULL)

    def finish(self):
        @pl.loop(0, self.length)
        def _(block):
            self.copy(2, block).wait_send()

            @pl.when(block > self.place)
            def _():
                self.copy(0, block).wait_send()

            @pl.when(block < self.place)
            def _():
                self.copy(1, block).wait_send()


def line_scatter_scratch(dp_count, rows, width):
    line = dp_count // 2
    return [pltpu.VMEM((line, rows, width), LOW)] * 4 + [pltpu.SemaphoreType.DMA((line,))] * 6


class SmallSum:
    def __init__(self, flat, head_in, dp_in, done, head_send, head_recv, dp_send, dp_recv):
        self.flat, self.head_in, self.dp_in, self.done = flat, head_in, dp_in, done
        self.head_sems, self.dp_sems = (head_send, head_recv), (dp_send, dp_recv)
        self.me, *self.others = partners()
        self.place, self.count = lax.axis_index("dp"), dp_in.shape[0]

    def to_head(self, lane):
        other = self.others[lane]
        return remote(
            self.flat.at[other], self.head_in.at[self.me], *self.head_sems, lane, "head", other
        )

    def back_head(self, lane):
        block = self.done.at[self.me]
        return remote(block, block, *self.head_sems, 3 + lane, "head", self.others[lane])

    def to_dp(self, shift):
        block = self.dp_in.at[self.place]
        other = lax.rem(self.place + shift, self.count)
        return remote(block, block, *self.dp_sems, shift, "dp", other)

    def start(self, value):
        groups, rows, lanes = self.flat.shape
        flat = jnp.concatenate(
            [value[:, at:at + lanes] for at in range(0, value.shape[1], lanes)], axis=0
        )
        for group in range(groups):
            self.flat[group] = flat[group * rows:(group + 1) * rows]
        for lane in range(3):
            self.to_head(lane).start()
        self.head_in[self.me] = self.flat[self.me]

    def across(self):
        for lane in range(3):
            self.to_head(lane).wait_recv()
        total = self.head_in[0]
        for head in range(1, self.head_in.shape[0]):
            total = total + self.head_in[head]
        self.dp_in[self.place] = total

        @pl.loop(1, self.count)
        def _(shift):
            self.to_dp(shift).start()

    def back(self):
        @pl.loop(1, self.count)
        def _(shift):
            self.to_dp(shift).wait_recv()

        total = lax.fori_loop(
            1, self.count, lambda at, so_far: so_far + self.dp_in[at], self.dp_in[0]
        )
        self.done[self.me] = total
        for lane in range(3):
            self.back_head(lane).start()

    def result(self, out):
        for lane in range(3):
            self.back_head(lane).wait_recv()
        flat = jnp.concatenate([self.done[group] for group in range(self.done.shape[0])], axis=0)
        rows, width = out.shape
        lanes = flat.shape[1]
        for at in range(width // lanes):
            out[:, at * lanes:(at + 1) * lanes] = flat[at * rows:(at + 1) * rows]

    def finish(self):
        for lane in range(3):
            self.to_head(lane).wait_send()
            self.back_head(lane).wait_send()

        @pl.loop(1, self.count)
        def _(shift):
            self.to_dp(shift).wait_send()


def small_sum_scratch(rows, width, dp_count):
    block = (rows * width // 128 // 4, 128)
    return [
        pltpu.VMEM((4,) + block, FULL), pltpu.VMEM((4,) + block, FULL),
        pltpu.VMEM((dp_count,) + block, FULL), pltpu.VMEM((4,) + block, FULL),
        pltpu.SemaphoreType.DMA((6,)), pltpu.SemaphoreType.DMA((6,)),
        pltpu.SemaphoreType.DMA((dp_count,)), pltpu.SemaphoreType.DMA((dp_count,)),
    ]


class LateSum:
    def __init__(self, dp_in, head_in, dp_send, dp_recv, head_send, head_recv):
        self.dp_in, self.head_in = dp_in, head_in
        self.dp_sems, self.head_sems = (dp_send, dp_recv), (head_send, head_recv)
        self.me, *self.others = partners()
        self.place, self.count = lax.axis_index("dp"), dp_in.shape[0]

    def to_dp(self, shift):
        block = self.dp_in.at[self.place]
        other = lax.rem(self.place + shift, self.count)
        return remote(block, block, *self.dp_sems, shift, "dp", other)

    def to_head(self, lane):
        block = self.head_in.at[self.me]
        return remote(block, block, *self.head_sems, lane, "head", self.others[lane])

    def start(self, rows):
        lanes = self.dp_in.shape[2]
        cuts = [
            row[:, at:at + lanes] for row in rows for at in range(0, row.shape[1], lanes)
        ]
        cuts += [jnp.zeros_like(cuts[0])] * (self.dp_in.shape[1] - len(cuts))
        self.dp_in[self.place] = jnp.concatenate(cuts, axis=0)

        @pl.loop(1, self.count)
        def _(shift):
            self.to_dp(shift).start()

    def across(self):
        @pl.loop(1, self.count)
        def _(shift):
            self.to_dp(shift).wait_recv()

        self.head_in[self.me] = lax.fori_loop(
            1, self.count, lambda at, so_far: so_far + self.dp_in[at], self.dp_in[0]
        )
        for lane in range(3):
            self.to_head(lane).start()

    def result(self, out, first):
        for lane in range(3):
            self.to_head(lane).wait_recv()
        total = self.head_in[0]
        for head in range(1, self.head_in.shape[0]):
            total = total + self.head_in[head]
        lanes = total.shape[1]
        cuts = out.shape[1] // lanes
        for row in range(2):
            for at in range(cuts):
                piece = total[row * cuts + at:row * cuts + at + 1]
                out[first + row:first + row + 1, at * lanes:(at + 1) * lanes] = piece

    def finish(self):
        for lane in range(3):
            self.to_head(lane).wait_send()

        @pl.loop(1, self.count)
        def _(shift):
            self.to_dp(shift).wait_send()


def late_sum_scratch(width, dp_count):
    block = (-(-2 * width // 128 // 8) * 8, 128)
    return [
        pltpu.VMEM((dp_count,) + block, FULL), pltpu.VMEM((4,) + block, FULL),
        pltpu.SemaphoreType.DMA((dp_count,)), pltpu.SemaphoreType.DMA((dp_count,)),
        pltpu.SemaphoreType.DMA((3,)), pltpu.SemaphoreType.DMA((3,)),
    ]


GATHER_CUTS = 4


class ImageGather:
    def __init__(self, held, sends, recvs, own=None, local_sem=None):
        self.held, self.sends, self.recvs = held, sends, recvs
        self.me, self.near, self.far, self.corner = partners()
        self.own = held.at[self.me] if own is None else own
        self.local = None if own is None else pltpu.make_async_copy(own, held.at[self.me], local_sem)
        self.size = held.shape[1] // GATHER_CUTS

    def piece(self, lane, cut):
        span = pl.ds(cut * self.size, self.size)
        image = self.far if lane == 2 else self.me
        block = self.held.at[image, span]
        source = block if lane == 2 else self.own.at[span]
        other = self.far if lane == 0 else self.near
        index = lane * GATHER_CUTS + cut
        return remote(source, block, self.sends, self.recvs, index, "head", other)

    def start_far(self, first=0, last=GATHER_CUTS):
        for cut in range(first, last):
            self.piece(0, cut).start()

    def start_near(self):
        for cut in range(GATHER_CUTS):
            self.piece(1, cut).start()
        if self.local is not None:
            self.local.start()

    def start(self):
        self.start_far()
        self.start_near()

    def wait_near(self):
        for cut in range(GATHER_CUTS):
            self.piece(1, cut).wait_recv()

    def wait_far(self, first=0, last=GATHER_CUTS):
        for cut in range(first, last):
            self.piece(0, cut).wait_recv()
            self.piece(2, cut).start()

    def wait_corner(self):
        for cut in range(GATHER_CUTS):
            self.piece(2, cut).wait_recv()

    def finish(self):
        for cut in range(GATHER_CUTS):
            for lane in range(3):
                self.piece(lane, cut).wait_send()
        if self.local is not None:
            self.local.wait()


def image_gather_sems():
    return [pltpu.SemaphoreType.DMA((3 * GATHER_CUTS,)), pltpu.SemaphoreType.DMA((3 * GATHER_CUTS,))]


class BlockSum:
    def __init__(self, parts, mine, passed, corner_in, near_in, far_in, local_sems, sends, recvs):
        self.mine, self.passed, self.corner_in = mine, passed, corner_in
        self.near_in, self.far_in = near_in, far_in
        me, near, far, corner = partners()
        self.to_corner = remote(parts.at[corner], corner_in, sends, recvs, 0, "head", near)
        self.to_near = remote(parts.at[near], near_in, sends, recvs, 1, "head", near)
        self.to_far = remote(passed, far_in, sends, recvs, 2, "head", far)
        self.load_far = pltpu.make_async_copy(parts.at[far], passed, local_sems.at[0])
        self.load_mine = pltpu.make_async_copy(parts.at[me], mine, local_sems.at[1])

    def start(self):
        for copy in (self.to_corner, self.load_far, self.to_near, self.load_mine):
            copy.start()

    def across(self):
        self.load_far.wait()
        self.to_corner.wait_recv()
        both = self.passed[...].astype(FULL) + self.corner_in[...].astype(FULL)
        self.passed[...] = both.astype(LOW)
        self.to_far.start()

    def result(self):
        self.load_mine.wait()
        self.to_near.wait_recv()
        self.to_far.wait_recv()
        total = self.mine[...].astype(FULL) + self.near_in[...].astype(FULL)
        return total + self.far_in[...].astype(FULL)

    def finish(self):
        for copy in (self.to_corner, self.to_near, self.to_far):
            copy.wait_send()


def block_sum_scratch(rows, width):
    return [pltpu.VMEM((rows, width), LOW)] * 5 + [
        pltpu.SemaphoreType.DMA((2,)), pltpu.SemaphoreType.DMA((3,)), pltpu.SemaphoreType.DMA((3,)),
    ]


class Slots:
    def __init__(self, count, share):
        self.count, self.share = count, share
        self.big = -(-share // 16) * 16
        rest = 2 * share - self.big
        self.small = rest if rest > 0 and rest % 16 == 0 else self.big
        self.more = self.big - self.small
        self.both = self.big + self.small
        self.rows = count // 2 * self.both
        self.turns = count // 4
        self.phase_rows = self.turns * 2 * self.both

    def size(self, source, head):
        return self.small + self.more * ((head + source + 1) % 2)

    def packed(self, source, head):
        return (source // 2) * self.both + (source % 2) * self.size(0, head)

    def row(self, source, head, shift):
        first = self.size(source, 0) * (head % 2)
        group = (head // 2) * self.turns * self.both + self.turns * first
        return (
            (shift // self.turns) * self.phase_rows + group
            + (shift % self.turns) * self.size(source, head)
        )

    def holder(self, source, slot):
        pair, within = slot // self.both, slot % self.both
        first = self.size(source, 0)
        second = jnp.where(within >= first, 1, 0)
        return 2 * pair + second, within - second * first

    def span(self, start, extra):
        if extra:
            return pl.ds(pl.multiple_of(start + self.small, 16), self.more)
        return pl.ds(pl.multiple_of(start, 16), self.small)

    def each(self, is_big, make, action):
        getattr(make(False), action)()
        if self.more:
            @pl.when(is_big)
            def _():
                getattr(make(True), action)()


class SlotExchange:
    def __init__(self, slots, sent, rows, sends, recvs, local_sems):
        self.slots, self.sent, self.rows = slots, sent, rows
        self.sems, self.local_sems = (sends, recvs), local_sems
        self.place, self.head = lax.axis_index("dp"), lax.axis_index("head")

    def out(self, shift, action):
        slots = self.slots
        expert = lax.rem(self.place + shift, slots.count)
        mine = slots.size(self.place, self.head)
        at, to = expert * mine, slots.packed(self.place, self.head)
        slots.each(mine > slots.small, lambda extra: remote(
            self.sent.at[slots.span(at, extra)], self.rows.at[slots.span(to, extra)],
            *self.sems, 2 * shift + int(extra), "dp", expert,
        ), action)

    def into(self, shift):
        slots = self.slots
        source = lax.rem(self.place + slots.count - shift, slots.count)
        size = slots.size(source, self.head)
        to = slots.packed(source, self.head)
        slots.each(size > slots.small, lambda extra: remote(
            self.sent.at[slots.span(0, extra)], self.rows.at[slots.span(to, extra)],
            *self.sems, 2 * shift + int(extra), "dp", source,
        ), "wait_recv")

    def own(self, action):
        slots = self.slots
        mine = slots.size(self.place, self.head)
        at, to = self.place * mine, slots.packed(self.place, self.head)
        slots.each(mine > slots.small, lambda extra: pltpu.make_async_copy(
            self.sent.at[slots.span(at, extra)], self.rows.at[slots.span(to, extra)],
            self.local_sems.at[int(extra)],
        ), action)

    def start(self):
        @pl.loop(1, self.slots.count)
        def _(shift):
            self.out(shift, "start")

        self.own("start")

    def finish(self):
        @pl.loop(1, self.slots.count)
        def _(shift):
            self.into(shift)
            self.out(shift, "wait_send")

        self.own("wait")


class SlotReturn:
    def __init__(self, slots, rows, back, zeros, sends, recvs, local_sems):
        self.slots, self.rows, self.back, self.zeros = slots, rows, back, zeros
        self.sems, self.local_sems = (sends, recvs), local_sems
        self.place, self.head = lax.axis_index("dp"), lax.axis_index("head")
        self.mine = slots.size(self.place, self.head)

    def out(self, shift, action):
        slots = self.slots
        source = lax.rem(self.place + shift, slots.count)
        size = slots.size(source, self.head)
        at, to = slots.packed(source, self.head), shift * size
        slots.each(size > slots.small, lambda extra: remote(
            self.rows.at[slots.span(at, extra)], self.back.at[slots.span(to, extra)],
            *self.sems, 2 * shift + int(extra), "dp", source,
        ), action)

    def into(self, shift):
        slots = self.slots
        expert = lax.rem(self.place + slots.count - shift, slots.count)
        slots.each(self.mine > slots.small, lambda extra: remote(
            self.rows.at[slots.span(0, extra)], self.back.at[slots.span(shift * self.mine, extra)],
            *self.sems, 2 * shift + int(extra), "dp", expert,
        ), "wait_recv")

    def own(self, action):
        slots = self.slots
        at = slots.packed(self.place, self.head)
        slots.each(self.mine > slots.small, lambda extra: pltpu.make_async_copy(
            self.rows.at[slots.span(at, extra)], self.back.at[slots.span(0, extra)],
            self.local_sems.at[int(extra)],
        ), action)

    def blank(self, action):
        slots = self.slots
        if slots.more:
            @pl.when(self.mine == slots.small)
            def _():
                tail = self.back.at[pl.ds(slots.count * slots.small, slots.count * slots.more)]
                copy = pltpu.make_async_copy(self.zeros, tail, self.local_sems.at[2])
                getattr(copy, action)()

    def start(self):
        if self.slots.more:
            self.zeros[...] = jnp.zeros_like(self.zeros)
        self.blank("start")

        @pl.loop(1, self.slots.count)
        def _(shift):
            self.out(shift, "start")

        self.own("start")

    def finish(self):
        @pl.loop(1, self.slots.count)
        def _(shift):
            self.into(shift)
            self.out(shift, "wait_send")

        self.own("wait")
        self.blank("wait")


def slot_return_scratch(slots, width):
    return [pltpu.VMEM((max(slots.count * slots.more, 16), width), LOW)] + [
        pltpu.SemaphoreType.DMA((2 * slots.count,)), pltpu.SemaphoreType.DMA((2 * slots.count,)),
        pltpu.SemaphoreType.DMA((3,)),
    ]


def slot_exchange_sems(count):
    return [
        pltpu.SemaphoreType.DMA((2 * count,)), pltpu.SemaphoreType.DMA((2 * count,)),
        pltpu.SemaphoreType.DMA((2,)),
    ]


class ReturnGather:
    def __init__(self, slots, rows, held, sends, recvs, local_sems):
        self.slots, self.rows, self.held = slots, rows, held
        self.sems, self.local_sems = (sends, recvs), local_sems
        self.place = lax.axis_index("dp")
        self.me, self.near, self.far, self.corner = partners()

    def out(self, shift, action):
        slots = self.slots
        source = lax.rem(self.place + shift, slots.count)
        size = slots.size(source, self.me)
        at, to = slots.packed(source, self.me), slots.row(source, self.me, shift)
        slots.each(size > slots.small, lambda extra: remote(
            self.rows.at[slots.span(at, extra)], self.held.at[slots.span(to, extra)],
            *self.sems, 2 * shift + int(extra), "dp", source,
        ), action)

    def own(self, action):
        slots = self.slots
        size = slots.size(self.place, self.me)
        at, to = slots.packed(self.place, self.me), slots.row(self.place, self.me, 0)
        slots.each(size > slots.small, lambda extra: pltpu.make_async_copy(
            self.rows.at[slots.span(at, extra)], self.held.at[slots.span(to, extra)],
            self.local_sems.at[int(extra)],
        ), action)

    def block(self, lane, head, shift, axis, other, action):
        slots = self.slots
        size = slots.size(self.place, head)
        to = slots.row(self.place, head, shift)

        def make(extra):
            block = self.held.at[slots.span(to, extra)]
            index = 2 * (lane * slots.count + shift) + int(extra)
            return remote(block, block, *self.sems, index, axis, other)

        slots.each(size > slots.small, make, action)

    def start(self):
        @pl.loop(1, self.slots.count)
        def _(shift):
            self.out(shift, "start")

        self.own("start")

    def relay(self, shift):
        @pl.when(shift == 0)
        def _():
            self.own("wait")

        @pl.when(shift > 0)
        def _():
            expert = lax.rem(self.place + self.slots.count - shift, self.slots.count)
            self.block(0, self.me, shift, "dp", expert, "wait_recv")

        self.block(1, self.me, shift, "head", self.far, "start")
        self.block(2, self.me, shift, "head", self.near, "start")

    def forward(self, shift):
        self.block(1, self.far, shift, "head", self.far, "wait_recv")
        self.block(3, self.far, shift, "head", self.near, "start")

    def rest(self, shift):
        self.block(2, self.near, shift, "head", self.near, "wait_recv")
        self.block(3, self.corner, shift, "head", self.near, "wait_recv")

    def of_phase(self, phase, action):
        @pl.loop(0, self.slots.turns)
        def _(turn):
            action(phase * self.slots.turns + turn)

    def finish(self):
        @pl.loop(0, self.slots.count)
        def _(shift):
            @pl.when(shift > 0)
            def _():
                self.out(shift, "wait_send")

            self.block(1, self.me, shift, "head", self.far, "wait_send")
            self.block(2, self.me, shift, "head", self.near, "wait_send")
            self.block(3, self.far, shift, "head", self.near, "wait_send")


def return_gather_sems(count):
    return [
        pltpu.SemaphoreType.DMA((8 * count,)), pltpu.SemaphoreType.DMA((8 * count,)),
        pltpu.SemaphoreType.DMA((2,)),
    ]


def greet_all(heads, dp_count):
    barrier = pltpu.get_barrier_semaphore()
    place = lax.axis_index("dp")
    for other in heads:
        pl.semaphore_signal(barrier, inc=1, device_id={"head": other}, device_id_type=MESH)

    @pl.loop(1, dp_count)
    def _(shift):
        other = lax.rem(place + shift, dp_count)
        pl.semaphore_signal(barrier, inc=1, device_id={"dp": other}, device_id_type=MESH)

    pl.semaphore_wait(barrier, len(heads) + dp_count - 1)


ANYWHERE = pl.BlockSpec(memory_space=pl.ANY)
INSIDE = pl.BlockSpec(memory_space=pltpu.VMEM)


def digits(values):
    high = lax.div(values, 64)
    return high.astype(FULL), (values - high * 64).astype(FULL)


def turned_column(columns):
    count = columns[0].shape[0]
    lanes = lax.broadcasted_iota(jnp.int32, (count, 128), 1)
    spread = jnp.zeros((count, 128), FULL)
    for index, column in enumerate(columns):
        for at, digit in enumerate(digits(column)):
            spread = spread + jnp.where(lanes == 2 * index + at, digit, 0.0)
    shape = (8, 128)
    eye = lax.broadcasted_iota(jnp.int32, shape, 0) == lax.broadcasted_iota(jnp.int32, shape, 1)
    rows = nt(one_hot(eye), spread.astype(LOW)).astype(jnp.int32)
    return [rows[2 * at:2 * at + 1] * 64 + rows[2 * at + 1:2 * at + 2] for at in range(len(columns))]


def prepare_kernel(
    slots, slot_count, capacity,
    tile_ref, norm_ref, owner_ref, ids_ref, pos_ref, up_ref, x_in, g_in,
    w_ref, src_ref, col_ref, col_back_ref, col_out_ref, xn_out, hat_out, sent_out, up_out,
    x_ref, g_ref, xn_ref, hat_ref, up_full, up_low, held, sent_sum, sent_ref,
    load_sems, save_sems, *sems,
):
    images = x_ref.shape[0]
    gather = LineGather(held, *sems[:6])
    spread = ImageGather(up_out, *sems[6:8], own=up_low, local_sem=sems[8])
    load_up = pltpu.make_async_copy(up_ref, up_full, load_sems.at[2, 0])
    load_up.start()

    def load(image):
        return (
            pltpu.make_async_copy(x_in.at[image], x_ref.at[image], load_sems.at[0, image]),
            pltpu.make_async_copy(g_in.at[image], g_ref.at[image], load_sems.at[1, image]),
        )

    def save(image):
        return (
            pltpu.make_async_copy(xn_ref.at[image], xn_out.at[image], save_sems.at[0, image]),
            pltpu.make_async_copy(hat_ref.at[image], hat_out.at[image], save_sems.at[1, image]),
        )

    for image in range(images):
        for copy in load(image):
            copy.start()
    me, head = lax.axis_index("dp"), lax.axis_index("head")
    held[me] = tile_ref[...].astype(LOW)
    greet(*gather.neighbours(), ("head", spread.near), ("head", spread.far))
    gather.start()
    load_up.wait()
    up_low[...] = up_full[...].astype(LOW)
    spread.start()
    shape = (sent_ref.shape[0], PATCH)
    sent_sum[...] = jnp.zeros_like(sent_sum)
    steps = gather.length - 1

    def image_step(image):
        for copy in load(image):
            copy.wait()
        normal, _ = normalise(x_ref[image].astype(FULL))
        hat_ref[image] = normal.astype(LOW)
        xn_ref[image] = (normal * norm_ref[0:1, :] + norm_ref[1:2, :]).astype(LOW)
        for copy in save(image):
            copy.start()

        ids, pos = ids_ref[image], pos_ref[image]
        kept = pos < capacity
        holder, within = slots.holder(me, jnp.minimum(pos, capacity - 1))
        sent_at = ids * slots.size(me, head) + within
        sent_at = jnp.where(kept & (holder == head), sent_at, slots.count * slots.big)
        shift = me - ids
        shift = jnp.where(shift < 0, shift + slots.count, shift)
        col_back_ref[image] = jnp.where(kept, slots.row(me, holder, shift) + within, -1)
        other_pair = jnp.where(lax.div(holder, 2) == lax.div(head, 2), 0, 2)
        apart = other_pair + jnp.where(lax.rem(holder, 2) == lax.rem(head, 2), 0, 1)
        out_at = apart * (slots.count * slots.big) + shift * slots.size(me, holder) + within
        col_out_ref[image] = jnp.where(kept, out_at, -1)
        first, second = turned_column([sent_at[:, 0:1], sent_at[:, 1:2]])
        col_ref[image] = jnp.concatenate([first, second], axis=0)
        sent_slots = lax.broadcasted_iota(jnp.int32, shape, 0)
        pick = one_hot((sent_slots == first) | (sent_slots == second))
        sent_sum[...] += nn(pick, g_ref[image])

    @pl.loop(0, max(steps, (images + 1) // 2))
    def _(turn):
        @pl.loop(2 * turn, jnp.minimum(2 * turn + 2, images))
        def _(image):
            image_step(image)

        @pl.when(turn < steps)
        def _():
            gather.step(turn + 1)

        @pl.when(turn == 1)
        def _():
            spread.wait_far(0, 1)

    sent_ref[...] = sent_sum[...].astype(LOW)
    save_sent = pltpu.make_async_copy(sent_ref, sent_out, load_sems.at[2, 1])
    save_sent.start()

    rows = w_ref.shape[0]
    tiles = owner_ref.shape[1]
    row_tile = lax.div(lax.broadcasted_iota(jnp.int32, (rows, tiles), 0), TILE)
    lane_tile = lax.broadcasted_iota(jnp.int32, (rows, tiles), 1)
    owner_rows = jnp.broadcast_to(owner_ref[...].astype(FULL), (8, tiles)).astype(LOW)
    owner = nt(one_hot(lane_tile == row_tile), owner_rows)[:, 0:1].astype(jnp.int32)
    before = (owner_ref[...] == owner) & (lane_tile < row_tile)
    rank = jnp.sum(jnp.where(before, 1.0, 0.0), axis=1, keepdims=True).astype(jnp.int32)
    within = lax.rem(lax.broadcasted_iota(jnp.int32, (rows, 1), 0), TILE)
    src = (owner * slot_count + rank) * TILE + within
    src_ref[...] = turned_column([src])[0]
    spread.wait_far(1, 3)
    gather.finish()
    blocks, depth, width = held.shape
    cut = rows // 4
    for part in range(4):
        lanes = lax.broadcasted_iota(jnp.int32, (cut, blocks * depth), 1)
        pick = one_hot(lanes == src[part * cut:(part + 1) * cut])
        block = nn(pick, held[...].reshape(blocks * depth, width))
        w_ref[pl.ds(part * cut, cut), :] = block.astype(LOW)
    spread.wait_far(3)
    spread.wait_near()
    spread.wait_corner()
    spread.finish()
    save_sent.wait()

    @pl.loop(0, images)
    def _(image):
        for copy in save(image):
            copy.wait()


def prepare(slots, tiles, patches, cotangent, norm_params, owners, ids, pos, up, weight_rows):
    images, _, width = patches.shape
    slot_count = tiles.shape[0] // TILE
    line = slots.count // 2
    most = slots.count * slots.big
    capacity = images * PATCH // slots.count
    wide = jax.ShapeDtypeStruct(patches.shape, LOW)
    pairs = jax.ShapeDtypeStruct((images, PATCH, 2), jnp.int32)
    return pl.pallas_call(
        functools.partial(prepare_kernel, slots, slot_count, capacity),
        in_specs=[INSIDE] * 5 + [ANYWHERE] * 3,
        out_specs=[INSIDE] * 5 + [ANYWHERE] * 4,
        out_shape=[
            jax.ShapeDtypeStruct((weight_rows, width), LOW),
            jax.ShapeDtypeStruct((1, weight_rows), jnp.int32),
            jax.ShapeDtypeStruct((images, 2, PATCH), jnp.int32), pairs, pairs, wide, wide,
            jax.ShapeDtypeStruct((most, width), LOW), jax.ShapeDtypeStruct((4,) + up.shape, LOW),
        ],
        scratch_shapes=[pltpu.VMEM(patches.shape, LOW)] * 4
        + [
            pltpu.VMEM(up.shape, FULL), pltpu.VMEM(up.shape, LOW),
            pltpu.VMEM((slots.count,) + tiles.shape, LOW), pltpu.VMEM((most, width), FULL),
            pltpu.VMEM((most, width), LOW),
            pltpu.SemaphoreType.DMA((3, images)), pltpu.SemaphoreType.DMA((2, images)),
        ]
        + [pltpu.SemaphoreType.DMA((line,))] * 6 + image_gather_sems() + [pltpu.SemaphoreType.DMA],
        compiler_params=params(collective_id=0, has_side_effects=True),
        name="prepare",
    )(tiles, norm_params, owners, ids, pos, up, patches, cotangent)


def head_mask(shape, axis, head):
    return lax.broadcasted_iota(jnp.int32, shape, axis) // HD == head


def forward_kernel(
    slots,
    w_ref, norm_ref, col_ref, xn_in, x_ref, g_sent_ref, down_ref,
    lse_ref, q_out, qt_out, k_out, kt_out, v_out, ot_out, x1_out, rows_out, g_rows_out, down_out,
    q_ref, qt_ref, k_ref, kt_ref, v_ref, ot_ref, x1_ref, xn_ref, own_ref, sent_ref, sent_sum,
    down_full, down_low, save_sems, own_sem, *exchange,
):
    images = xn_ref.shape[0]
    rows = w_ref.shape[0] // 4
    heads = rows // HD
    total_of = ImageSum(*exchange[:8])
    spread = ImageGather(x1_ref, *exchange[8:10])
    spread_down = ImageGather(down_out, *exchange[10:12], own=down_low, local_sem=exchange[12])
    send_g = SlotExchange(slots, g_sent_ref, g_rows_out, *exchange[13:16])
    send_rows = SlotExchange(slots, sent_ref, rows_out, *exchange[16:])
    me, near, far, corner = partners()

    def load(turn):
        image = total_of.image(turn)
        return pltpu.make_async_copy(xn_in.at[image], xn_ref.at[image], save_sems.at[6, turn])

    for turn in range(images):
        load(turn).start()
    load_down = pltpu.make_async_copy(down_ref, down_full, own_sem.at[1])
    load_down.start()
    own = pltpu.make_async_copy(x_ref.at[me], own_ref, own_sem.at[0])
    own.start()
    greet_all((near, far), slots.count)
    load_down.wait()
    down_low[...] = down_full[...].astype(LOW)
    spread_down.start_far(0, 1)
    spread_down.start_near()
    send_g.start()
    kept = ((q_ref, q_out), (qt_ref, qt_out), (k_ref, k_out), (kt_ref, kt_out), (v_ref, v_out), (ot_ref, ot_out))
    shrink = HD ** (-0.5)

    def save(image):
        return [
            pltpu.make_async_copy(ref.at[image], out.at[image], save_sems.at[index, image])
            for index, (ref, out) in enumerate(kept)
        ]

    @pl.loop(0, images)
    def _(turn):
        image = total_of.image(turn)
        load(turn).wait()
        xn = xn_ref[image]
        wq, wk, wv, wo = (w_ref[pl.ds(part * rows, rows), :] for part in range(4))
        q_ref[image] = (nt(xn, wq) * shrink).astype(LOW)
        qt = (nt(wq, xn) * shrink).astype(LOW)
        qt_ref[image] = qt
        k = nt(xn, wk).astype(LOW)
        k_ref[image] = k
        kt_ref[image] = nt(wk, xn).astype(LOW)
        v_ref[image] = nt(xn, wv).astype(LOW)
        vt = nt(wv, xn).astype(LOW)
        mixed = []
        for head in range(heads):
            span = slice(head * HD, (head + 1) * HD)
            only = jnp.where(head_mask(qt.shape, 0, head), qt, jnp.zeros_like(qt))
            scores = nn(k, only)
            top = jnp.max(scores, axis=0, keepdims=True)
            weights = jnp.exp(scores - top)
            total = jnp.sum(weights, axis=0, keepdims=True)
            mixed.append(nn(vt[span], weights.astype(LOW)) / total)
            lse_ref[image, head:head + 1, :] = top + jnp.log(total)
        ot = jnp.concatenate(mixed, axis=0).astype(LOW)
        ot_ref[image] = ot
        total_of.give(turn, tn(ot, wo))
        for copy in save(image):
            copy.start()

    own.wait()
    x1_ref[me] = (own_ref[...].astype(FULL) + total_of.result()).astype(LOW)
    spread.start()
    sent_sum[...] = jnp.zeros_like(sent_sum)

    def place(image):
        normal, _ = normalise(x1_ref[image].astype(FULL))
        low = (normal * norm_ref[2:3, :] + norm_ref[3:4, :]).astype(LOW)
        slots = lax.broadcasted_iota(jnp.int32, (sent_ref.shape[0], PATCH), 0)
        col = col_ref[image]
        pick = one_hot((slots == col[0:1, :]) | (slots == col[1:2, :]))
        sent_sum[...] += nn(pick, low)

    place(me)
    spread.wait_near()
    place(near)
    spread.wait_far()
    place(far)
    spread.wait_corner()
    keep = pltpu.make_async_copy(x1_ref, x1_out, own_sem.at[0])
    keep.start()
    spread_down.start_far(1)
    place(corner)
    sent_ref[...] = sent_sum[...].astype(LOW)
    send_rows.start()
    spread.finish()
    total_of.finish()
    keep.wait()
    send_g.finish()
    spread_down.wait_far()
    spread_down.wait_near()
    spread_down.wait_corner()
    spread_down.finish()
    send_rows.finish()

    @pl.loop(0, images)
    def _(image):
        for copy in save(image):
            copy.wait()


def attention_forward(slots, xn, w, norm_params, col_rows, patches, g_sent, down):
    images, _, width = patches.shape
    rows = w.shape[0] // 4
    flat, turned = (images, PATCH, rows), (images, rows, PATCH)
    saved = [flat, turned, flat, turned, flat, turned, patches.shape]
    outs = saved + [(slots.rows, width), (slots.rows, width), (4,) + down.shape]
    most = slots.count * slots.big
    return pl.pallas_call(
        functools.partial(forward_kernel, slots),
        in_specs=[INSIDE] * 3 + [ANYWHERE] * 4,
        out_specs=[INSIDE] + [ANYWHERE] * 10,
        out_shape=[jax.ShapeDtypeStruct((images, 8, PATCH), FULL)]
        + [jax.ShapeDtypeStruct(shape, LOW) for shape in outs],
        scratch_shapes=[pltpu.VMEM(shape, LOW) for shape in saved]
        + [
            pltpu.VMEM(patches.shape, LOW),
            pltpu.VMEM((PATCH, width), LOW), pltpu.VMEM((most, width), LOW),
            pltpu.VMEM((most, width), FULL),
            pltpu.VMEM(down.shape, FULL), pltpu.VMEM(down.shape, LOW),
            pltpu.SemaphoreType.DMA((7, images)), pltpu.SemaphoreType.DMA((2,)),
        ]
        + image_sum_scratch(PATCH, width) + image_gather_sems() + image_gather_sems()
        + [pltpu.SemaphoreType.DMA]
        + slot_exchange_sems(slots.count) + slot_exchange_sems(slots.count),
        compiler_params=params(collective_id=1, has_side_effects=True),
        name="attention_forward",
    )(w, norm_params, col_rows, xn, patches, g_sent, down)


def backward_kernel(
    experts, slots,
    w_ref, lse_ref, src_ref, norm_ref, small_ref,
    x1g_in, xn_in, hat_in, q_in, qt_in, k_in, kt_in, v_in, ot_in, x_ref, out_rows_ref, down_part,
    owned_ref, small_out, down_grad_ref, input_out, out_back,
    x1g_ref, xn_ref, hat_ref, q_ref, qt_ref, k_ref, kt_ref, v_ref, ot_ref, late_ref,
    grad_ref, own_ref, input_ref, padded_ref, load_sems, own_sem, *exchange,
):
    images = x1g_ref.shape[0]
    rows = w_ref.shape[0] // 4
    heads = rows // HD
    total_of = ImageSum(*exchange[:8])
    spread = ImageGather(input_ref, *exchange[8:10])
    back_out = SlotReturn(slots, out_rows_ref, out_back, *exchange[10:14])
    weights_sum = LineScatter(padded_ref, owned_ref, *exchange[14:24])
    down_sum = BlockSum(down_part, *exchange[24:32])
    small_sum = SmallSum(*exchange[32:40])
    late_sum = LateSum(*exchange[40:])
    me, near, far, corner = partners()
    dp_count = slots.count
    streamed = (
        (xn_in, xn_ref), (hat_in, hat_ref), (q_in, q_ref), (qt_in, qt_ref), (k_in, k_ref), (kt_in, kt_ref),
        (v_in, v_ref), (ot_in, ot_ref),
    )

    def load(turn):
        image, slot = total_of.image(turn), lax.rem(turn, 2)
        copies = [
            pltpu.make_async_copy(source.at[image], target.at[slot], load_sems.at[index, slot])
            for index, (source, target) in enumerate(streamed)
        ]
        copies.append(
            pltpu.make_async_copy(x1g_in.at[image], x1g_ref.at[image], load_sems.at[8, slot])
        )
        return copies

    for turn in range(2):
        for copy in load(turn):
            copy.start()
    own = pltpu.make_async_copy(x_ref.at[me], own_ref, own_sem.at[0])
    own.start()
    greet_all((near, far, corner), dp_count)
    small_sum.start(small_ref[...])
    down_sum.start()
    back_out.start()
    down_sum.across()
    late_ref[...] = jnp.zeros_like(late_ref)
    shrink = HD ** (-0.5)
    grad_ref[...] = jnp.zeros_like(grad_ref)

    @pl.loop(0, images)
    def _(turn):
        image, slot = total_of.image(turn), lax.rem(turn, 2)
        for copy in load(turn):
            copy.wait()
        wq, wk, wv, wo = (w_ref[pl.ds(part * rows, rows), :] for part in range(4))
        x1g, xn = x1g_ref[image], xn_ref[slot]
        q, qt, k, kt = q_ref[slot], qt_ref[slot], k_ref[slot], kt_ref[slot]
        v, ot = v_ref[slot], ot_ref[slot]
        do = nt(x1g, wo).astype(LOW)
        dot = nt(wo, x1g).astype(LOW)
        product = dot.astype(FULL) * ot.astype(FULL)
        dqt, dk, dv = [], None, None
        for head in range(heads):
            span = slice(head * HD, (head + 1) * HD)
            zero_t = jnp.zeros_like(qt)
            mask_t = head_mask(qt.shape, 0, head)
            mask = head_mask(q.shape, 1, head)
            scores = nn(k, jnp.where(mask_t, qt, zero_t))
            weights = jnp.exp(scores - lse_ref[image, head:head + 1, :])
            back = nn(v, jnp.where(mask_t, dot, zero_t))
            delta = jnp.sum(product[span], axis=0, keepdims=True)
            score_grad = (weights * (back - delta)).astype(LOW)
            dqt.append(nn(kt[span], score_grad) * shrink)
            dk_one = nn(score_grad, jnp.where(mask, q, jnp.zeros_like(q)))
            dv_one = nn(weights.astype(LOW), jnp.where(mask, do, jnp.zeros_like(do)))
            dk = dk_one if dk is None else dk + dk_one
            dv = dv_one if dv is None else dv + dv_one
        dqt = jnp.concatenate(dqt, axis=0).astype(LOW)
        dk, dv = dk.astype(LOW), dv.astype(LOW)
        part = tn(dqt, wq) + nn(dk, wk) + nn(dv, wv)
        total_of.give(turn, part)
        late_ref[0:1, :] += jnp.sum(part * hat_ref[slot].astype(FULL), axis=0, keepdims=True)
        late_ref[1:2, :] += jnp.sum(part, axis=0, keepdims=True)
        pieces = (nn(dqt, xn), tn(dk, xn), tn(dv, xn), nn(ot, x1g))
        for part, piece in enumerate(pieces):
            grad_ref[pl.ds(part * rows, rows), :] += piece

        @pl.when(turn + 2 < images)
        def _():
            for copy in load(turn + 2):
                copy.start()

        @pl.when(turn == 1)
        def _():
            small_sum.across()

    late_sum.start([late_ref[0:1, :], late_ref[1:2, :]])
    low = grad_ref[...].astype(LOW)
    depth = padded_ref.shape[1]
    parts = min(dp_count, 8)
    cut = dp_count // parts * depth
    for part in range(parts):
        row = lax.broadcasted_iota(jnp.int32, (cut, low.shape[0]), 0) + part * cut
        pick = one_hot(row == src_ref[...])
        block = nn(pick, low).astype(LOW)
        padded_ref[pl.ds(part * (dp_count // parts), dp_count // parts)] = block.reshape(
            dp_count // parts, depth, block.shape[1]
        )
    weights_sum.start()
    small_sum.back()
    own.wait()
    normal, scale = normalise(own_ref[...].astype(FULL))
    back = norm_back(normal, scale, norm_ref[0:1, :], total_of.result())[0]
    input_ref[me] = (x1g_ref[me].astype(FULL) + back).astype(LOW)
    spread.start()
    late_sum.across()
    steps = weights_sum.length

    @pl.loop(0, steps - 1)
    def _(turn):
        weights_sum.step(steps - 1 - turn)

        @pl.when(turn == steps - 2)
        def _():
            spread.wait_far()

    weights_sum.result()
    small_sum.result(small_out)
    late_sum.result(small_out, experts)
    down_grad_ref[...] = down_sum.result()
    spread.wait_near()
    spread.wait_corner()
    keep = pltpu.make_async_copy(input_ref, input_out, own_sem.at[0])
    keep.start()
    back_out.finish()
    spread.finish()
    total_of.finish()
    weights_sum.finish()
    small_sum.finish()
    late_sum.finish()
    down_sum.finish()
    keep.wait()


def attention_backward(
    experts, slots, depth,
    x1_grad, w, xn, hat, saved, lse, src_row, norm_params, small, patches, out_rows, down_part,
):
    images, _, width = patches.shape
    rows = w.shape[0] // 4
    dp_count = slots.count
    flat, turned = (2, PATCH, rows), (2, rows, PATCH)
    units = down_part.shape[1]
    return pl.pallas_call(
        functools.partial(backward_kernel, experts, slots),
        in_specs=[INSIDE] * 5 + [ANYWHERE] * 12,
        out_specs=[INSIDE] * 3 + [ANYWHERE] * 2,
        out_shape=[
            jax.ShapeDtypeStruct((depth, width), FULL), jax.ShapeDtypeStruct(small.shape, FULL),
            jax.ShapeDtypeStruct((units, width), FULL),
            jax.ShapeDtypeStruct(patches.shape, LOW),
            jax.ShapeDtypeStruct((dp_count * slots.big, width), LOW),
        ],
        scratch_shapes=[pltpu.VMEM(patches.shape, LOW)]
        + [pltpu.VMEM((2, PATCH, width), LOW)] * 2
        + [pltpu.VMEM(shape, LOW) for shape in (flat, turned, flat, turned, flat, turned)]
        + [
            pltpu.VMEM((8, width), FULL), pltpu.VMEM(w.shape, FULL), pltpu.VMEM((PATCH, width), LOW),
            pltpu.VMEM(patches.shape, LOW), pltpu.VMEM((dp_count, depth, width), LOW),
            pltpu.SemaphoreType.DMA((9, 2)), pltpu.SemaphoreType.DMA((2,)),
        ]
        + image_sum_scratch(PATCH, width) + image_gather_sems()
        + slot_return_scratch(slots, width)
        + line_scatter_scratch(dp_count, depth, width)
        + block_sum_scratch(units, width)
        + small_sum_scratch(small.shape[0], width, dp_count)
        + late_sum_scratch(width, dp_count),
        compiler_params=params(collective_id=2, has_side_effects=True),
        name="attention_backward",
    )(
        w, lse, src_row, norm_params, small, x1_grad, xn, hat, *saved, patches, out_rows, down_part,
    )


def picked_rows(col, held_ref, start, count):
    lanes = lax.broadcasted_iota(jnp.int32, (col.shape[0], count), 1) + start
    pick = one_hot((lanes == col[:, 0:1]) | (lanes == col[:, 1:2]))
    return nn(pick, held_ref[pl.ds(start, count), :])


def combine_kernel(col_ref, x1_ref, *refs):
    *held, out_ref = refs
    total = x1_ref[0].astype(FULL)
    col = col_ref[0]
    count = 2 * held[0].shape[0]
    for part in range(2):
        lanes = lax.broadcasted_iota(jnp.int32, (col.shape[0], count), 1) + part * count
        pick = one_hot((lanes == col[:, 0:1]) | (lanes == col[:, 1:2]))
        rows = jnp.concatenate([held[2 * part][...], held[2 * part + 1][...]], axis=0)
        total = total + nn(pick, rows)
    out_ref[0] = total.astype(LOW)


def combine_forward(col, x1, held):
    images, _, width = x1.shape
    wide = lead((1, PATCH, width))
    return pl.pallas_call(
        combine_kernel,
        grid=(images,),
        in_specs=[lead((1, PATCH, 2)), wide] + [whole(rows.shape) for rows in held],
        out_specs=wide,
        out_shape=jax.ShapeDtypeStruct(x1.shape, LOW),
        compiler_params=params(),
        cost_estimate=pl.CostEstimate(
            flops=2 * images * PATCH * sum(rows.size for rows in held),
            bytes_accessed=4 * x1.size + 2 * sum(rows.size for rows in held), transcendentals=0,
        ),
        name="combine_forward",
    )(col, x1, *held)


def expert_kernel(
    slots,
    rows_ref, g_ref, router_in, col_ref, norm_ref,
    up_in, down_in, x1_in, cot_in,
    up_grad_ref, small_ref, down_out, out_out, x1g_out,
    router_ref, up_ref, down_ref, og_ref, gate_ref, probs_ref, down_stage, out_ref, back_ref,
    held, total, x1_ref, cot_ref, x1g_ref,
    load_sems, save_sems, image_sems, out_sem, *exchange,
):
    images, count = x1_in.shape[0], rows_ref.shape[0]
    out_sum, back_sum = total.at[pl.ds(0, count)], total.at[pl.ds(count, count)]
    up_sum = ImageSum(*exchange[:8])
    back = ReturnGather(slots, back_ref, held, *exchange[8:])
    parts = up_in.shape[0]

    def load(turn):
        part, slot = up_sum.image(turn), lax.rem(turn, 2)
        return (
            pltpu.make_async_copy(up_in.at[part], up_ref.at[slot], load_sems.at[0, slot]),
            pltpu.make_async_copy(down_in.at[part], down_ref.at[slot], load_sems.at[1, slot]),
        )

    def save(turn):
        slot = lax.rem(turn, 2)
        return pltpu.make_async_copy(
            down_stage.at[slot], down_out.at[up_sum.image(turn)], save_sems.at[slot]
        )

    for turn in range(2):
        for copy in load(turn):
            copy.start()
    rows = rows_ref[...]
    experts = router_in.shape[0]
    router_ref[...] = jnp.zeros_like(router_ref)
    router_ref[0:experts, :] = router_in[...]
    lane = lax.broadcasted_iota(jnp.int32, (1, router_ref.shape[0]), 1)
    mine = jnp.where(lane == lax.axis_index("dp"), 1.0, 0.0)
    logits = nt(rows, router_ref[...].astype(LOW)) + jnp.where(lane < experts, 0.0, -1e30)
    top = jnp.max(logits, axis=-1, keepdims=True)
    weights = jnp.exp(logits - top)
    probs = weights / jnp.sum(weights, axis=-1, keepdims=True)
    gate = jnp.sum(probs * mine, axis=-1, keepdims=True)
    probs_ref[...] = probs
    gate_ref[...] = gate
    og_ref[...] = (gate * g_ref[...].astype(FULL)).astype(LOW)
    out_sum[...] = jnp.zeros_like(out_sum)
    back_sum[...] = jnp.zeros_like(back_sum)
    greet_all((back.near, back.far), slots.count)

    @pl.loop(0, parts)
    def _(turn):
        slot = lax.rem(turn, 2)
        for copy in load(turn):
            copy.wait()
        rows, og = rows_ref[...], og_ref[...]
        up, down = up_ref[slot], down_ref[slot]
        hidden = nn(rows, up)
        slope = (2.0 / jnp.pi) ** 0.5
        square = hidden * hidden
        bend = jnp.tanh(slope * (hidden + 0.044715 * (square * hidden)))
        act = (0.5 * hidden * (1.0 + bend)).astype(LOW)
        out_sum[...] += nn(act, down)
        act_grad = nt(og, down)
        inner = slope * (1.0 + (3.0 * 0.044715) * square)
        curve = 0.5 * (1.0 + bend) + 0.5 * hidden * (1.0 - bend * bend) * inner
        hidden_grad = (curve * act_grad).astype(LOW)
        back_sum[...] += nt(hidden_grad, up)
        up_sum.give(turn, tn(rows, hidden_grad))

        @pl.when(turn >= 2)
        def _():
            save(turn - 2).wait()

        down_stage[lax.rem(turn, 2)] = tn(act, og).astype(LOW)
        save(turn).start()

        @pl.when(turn + 2 < parts)
        def _():
            for copy in load(turn + 2):
                copy.start()

    out = out_sum[...].astype(LOW).astype(FULL)
    gate, probs = gate_ref[...], probs_ref[...]
    gate_grad = jnp.sum(g_ref[...].astype(FULL) * out, axis=-1, keepdims=True)
    logit_grad = (gate_grad * (probs * (mine - gate))).astype(LOW)
    plain = back_sum[...].astype(LOW).astype(FULL)
    back_ref[...] = (plain + nn(logit_grad, router_ref[...].astype(LOW))).astype(LOW)
    back.start()
    out_ref[...] = (gate * out).astype(LOW)
    save_out = pltpu.make_async_copy(out_ref, out_out, out_sem)
    save_out.start()
    small_ref[...] = jnp.zeros_like(small_ref)
    small_ref[0:experts, :] = tn(logit_grad, rows_ref[...])[0:experts]

    def image_load(image):
        slot = lax.rem(image, 2)
        return (
            pltpu.make_async_copy(x1_in.at[image], x1_ref.at[slot], image_sems.at[0, slot]),
            pltpu.make_async_copy(cot_in.at[image], cot_ref.at[slot], image_sems.at[1, slot]),
        )

    def image_save(image):
        slot = lax.rem(image, 2)
        return pltpu.make_async_copy(x1g_ref.at[slot], x1g_out.at[image], image_sems.at[2, slot])

    for image in range(2):
        for copy in image_load(image):
            copy.start()
    back.of_phase(0, back.relay)
    total_rows = held.shape[0]
    piece = 3 * 256
    if total_rows % piece:
        piece = slots.phase_rows
    done = 0
    for phase in range(4):
        back.of_phase(phase, back.forward)
        if phase < 3:
            back.of_phase(phase + 1, back.relay)
        back.of_phase(phase, back.rest)
        ready = (phase + 1) * slots.phase_rows
        while done + piece <= ready:
            @pl.loop(0, images)
            def _(image, start=done):
                part = picked_rows(col_ref[image], held, start, piece)
                span = pl.ds(image * PATCH, PATCH)
                if start == 0:
                    total[span] = part
                else:
                    total[span] += part

            done += piece

    back_scale = 1.0 / 4.0

    @pl.loop(0, images)
    def _(image):
        slot = lax.rem(image, 2)
        for copy in image_load(image):
            copy.wait()

        @pl.when(image >= 2)
        def _():
            image_save(image - 2).wait()

        normal, scale = normalise(x1_ref[slot].astype(FULL))
        upstream = total[pl.ds(image * PATCH, PATCH)]
        result, gain_sum, shift_sum = norm_back(normal, scale, norm_ref[2:3, :], upstream)
        x1g_ref[slot] = (cot_ref[slot].astype(FULL) + result).astype(LOW)
        small_ref[experts + 2:experts + 3, :] += gain_sum * back_scale
        small_ref[experts + 3:experts + 4, :] += shift_sum * back_scale
        image_save(image).start()

        @pl.when(image + 2 < images)
        def _():
            for copy in image_load(image + 2):
                copy.start()

    up_grad_ref[...] = up_sum.result()
    back.finish()
    up_sum.finish()
    save_out.wait()
    for turn in range(parts - 2, parts):
        save(turn).wait()
    for image in range(images - 2, images):
        image_save(image).wait()


def expert_stage(slots, rows, g_rows, up, down, router, col, x1, cotangent, norm_params):
    count, width = rows.shape
    parts, _, units = up.shape
    images = x1.shape[0]
    small_rows = -(-(router.shape[0] + 4) // 16) * 16
    lanes = 128
    flat = pltpu.VMEM((count, width), LOW)
    pair = pltpu.VMEM((2, PATCH, width), LOW)
    return pl.pallas_call(
        functools.partial(expert_kernel, slots),
        in_specs=[INSIDE] * 5 + [ANYWHERE] * 4,
        out_specs=[INSIDE] * 2 + [ANYWHERE] * 3,
        out_shape=[
            jax.ShapeDtypeStruct((width, units), FULL),
            jax.ShapeDtypeStruct((small_rows, width), FULL),
            jax.ShapeDtypeStruct(down.shape, LOW),
            jax.ShapeDtypeStruct((count, width), LOW),
            jax.ShapeDtypeStruct(x1.shape, LOW),
        ],
        scratch_shapes=[
            pltpu.VMEM((lanes, width), FULL),
            pltpu.VMEM((2,) + up.shape[1:], LOW), pltpu.VMEM((2,) + down.shape[1:], LOW), flat,
            pltpu.VMEM((count, 1), FULL), pltpu.VMEM((count, lanes), FULL),
            pltpu.VMEM((2, units, width), LOW), flat, flat,
            pltpu.VMEM((4 * slots.phase_rows, width), LOW),
            pltpu.VMEM((max(images * PATCH, 2 * count), width), FULL), pair, pair, pair,
            pltpu.SemaphoreType.DMA((2, 2)), pltpu.SemaphoreType.DMA((2,)),
            pltpu.SemaphoreType.DMA((3, 2)), pltpu.SemaphoreType.DMA,
        ]
        + image_sum_scratch(width, units) + return_gather_sems(slots.count),
        compiler_params=params(collective_id=3, has_side_effects=True),
        name="expert_stage",
    )(
        rows, g_rows, router, col, norm_params, up, down, x1, cotangent,
    )


def body(
    patches, cotangent, expert_ids, slot_pos, owners,
    tile_master, tile_first, tile_second,
    expert_up, up_first, up_second,
    expert_down, down_first, down_second,
    router, router_first, router_second,
    norm_params, norm_first, norm_second,
):
    tok_rows, width = patches.shape
    experts = router.shape[0]
    capacity = tok_rows // experts
    dp_count = lax.axis_size("dp")
    head_count = lax.axis_size("head")
    images = tok_rows // PATCH
    slots = Slots(dp_count, capacity // head_count)
    slot_count = tile_master.shape[0]

    by_image = (images, PATCH, width)
    x_images, g_images = patches.reshape(by_image), cotangent.reshape(by_image)
    pairs = (images, PATCH, 2)
    w, src, col_rows, col, col_out, xn, hat, g_sent, up_all = prepare(
        slots, tile_master.reshape(slot_count * TILE, width), x_images, g_images, norm_params,
        owners, expert_ids.reshape(pairs), slot_pos.reshape(pairs), expert_up[0],
        owners.shape[1] * TILE,
    )
    lse, *saved, x1, rows, g_rows, down_all = attention_forward(
        slots, xn, w, norm_params, col_rows, x_images, g_sent, expert_down[0]
    )
    up_grad, small, down_part, out, x1_grad = expert_stage(
        slots, rows, g_rows, up_all, down_all, router, col, x1, g_images, norm_params
    )
    owned_grad, small, down_grad, input_low, out_back = attention_backward(
        experts, slots, slot_count * TILE,
        x1_grad, w, xn, hat, saved, lse, src, norm_params, small, x_images, out, down_part,
    )
    owned_grad = owned_grad.reshape(slot_count, TILE, width)
    input_grad = input_low.reshape(tok_rows, width).astype(FULL)

    def from_head(rows, apart):
        return lax.ppermute(rows, "head", [(at, at ^ apart) for at in range(head_count)])

    out_far = from_head(out_back, 2)
    held = [out_back, from_head(out_back, 1), out_far, from_head(out_far, 1)]
    block_out = combine_forward(col_out, x1, held).reshape(tok_rows, width)

    router_total, norm_total = small[:experts], small[experts:experts + 4]

    tile_new, tile_first_new, tile_second_new = adam_update(
        tile_master, tile_first, tile_second, owned_grad, rate_attention, decay_factor
    )
    up_new, up_first_new, up_second_new = adam_update(
        expert_up, up_first, up_second, up_grad[None], rate_up, decay_factor
    )
    down_new, down_first_new, down_second_new = adam_update(
        expert_down, down_first, down_second, down_grad[None], rate_down, decay_factor
    )
    router_new, router_first_new, router_second_new = adam_update(
        router, router_first, router_second, router_total, rate_router, decay_factor
    )
    norm_new, norm_first_new, norm_second_all = adam_update(
        norm_params, norm_first, norm_second, norm_total, rate_norm, 0.0
    )
    return (
        block_out,
        input_grad,
        tile_new,
        tile_first_new,
        tile_second_new,
        tile_new.astype(LOW),
        up_new,
        up_first_new,
        up_second_new,
        up_new.astype(LOW),
        down_new,
        down_first_new,
        down_second_new,
        down_new.astype(LOW),
        router_new,
        router_first_new,
        router_second_new,
        norm_new,
        norm_first_new,
        norm_second_all[:2],
        norm_second_all[2:],
    )


def solution(mesh):
    row = P("dp", None)
    tiles = P(("dp", "head"), None, None)
    up = P("dp", None, "head")
    down = P("dp", "head", None)
    in_specs = (
        row, row, row, row, P("head", None), tiles, tiles, tiles,
        up, up, up, down, down, down, P(), P(), P(), P(), P(), P(),
    )
    out_specs = (
        row, row, tiles, tiles, tiles, tiles, up, up, up, up, down, down, down, down,
        P(), P(), P(), P(), P(), P(), P(),
    )
    return jax.shard_map(body, mesh=mesh, in_specs=in_specs, out_specs=out_specs, check_vma=False)
```

```python
import functools

import jax
import jax.numpy as jnp
from jax import lax
from jax.experimental import pallas as pl
from jax.experimental.pallas import tpu as pltpu
from jax.sharding import PartitionSpec as P

HD = 64
PATCH = 576
TILE = 8
STEP = 10

eps_norm = 1e-06
beta_one = 0.9
beta_two = 0.999
adam_eps = 1e-08
rate_attention = 0.12
rate_up = 0.08
rate_down = 0.3
rate_router = 0.05
rate_norm = 0.4
decay_factor = 0.1

LOW = jnp.bfloat16
FULL = jnp.float32
MESH = pl.DeviceIdType.MESH
VMEM_BYTES = 61 * 1024 * 1024


def adam_update(weight, moment_one, moment_two, gradient, step_rate, weight_decay):
    moment_one = beta_one * moment_one + (1.0 - beta_one) * gradient
    moment_two = beta_two * moment_two + (1.0 - beta_two) * gradient * gradient
    fixed_one = moment_one / (1.0 - beta_one**STEP)
    fixed_two = moment_two / (1.0 - beta_two**STEP)
    weight = weight - step_rate * (
        fixed_one / (jnp.sqrt(fixed_two) + adam_eps) + weight_decay * weight
    )
    return (weight, moment_one, moment_two)


def nn(left, right):
    return lax.dot_general(left, right, (((1,), (0,)), ((), ())), preferred_element_type=FULL)


def nt(left, right):
    return lax.dot_general(left, right, (((1,), (1,)), ((), ())), preferred_element_type=FULL)


def tn(left, right):
    return lax.dot_general(left, right, (((0,), (0,)), ((), ())), preferred_element_type=FULL)


def params(**more):
    return pltpu.CompilerParams(vmem_limit_bytes=VMEM_BYTES, **more)


def whole(shape):
    return pl.BlockSpec(shape, lambda *_: (0,) * len(shape))


def lead(shape):
    return pl.BlockSpec(shape, lambda i: (i,) + (0,) * (len(shape) - 1))


def normalise(values):
    average = jnp.mean(values, axis=-1, keepdims=True)
    centred = values - average
    variance = jnp.mean(centred * centred, axis=-1, keepdims=True)
    scale = lax.rsqrt(variance + eps_norm)
    return centred * scale, scale


def norm_back(normal, scale, gain, upstream):
    inner = upstream * gain
    mean_inner = jnp.mean(inner, axis=-1, keepdims=True)
    mean_cross = jnp.mean(inner * normal, axis=-1, keepdims=True)
    result = scale * (inner - mean_inner - normal * mean_cross)
    gain_sum = jnp.sum(upstream * normal, axis=0, keepdims=True)
    shift_sum = jnp.sum(upstream, axis=0, keepdims=True)
    return result, gain_sum, shift_sum


def one_hot(condition):
    return jnp.where(condition, 1.0, 0.0).astype(LOW)


def remote(src, dst, sends, recvs, index, axis, other):
    return pltpu.make_async_remote_copy(
        src_ref=src, dst_ref=dst, send_sem=sends.at[index], recv_sem=recvs.at[index],
        device_id={axis: other}, device_id_type=MESH,
    )


def greet(*others):
    barrier = pltpu.get_barrier_semaphore()
    for axis, other in others:
        pl.semaphore_signal(barrier, inc=1, device_id={axis: other}, device_id_type=MESH)
    pl.semaphore_wait(barrier, len(others))


def partners():
    me = lax.axis_index("head")
    near = me + 1 - 2 * lax.rem(me, 2)
    far = lax.rem(me + 2, 4)
    corner = lax.rem(near + 2, 4)
    return me, near, far, corner


class LineGather:
    def __init__(self, held, up_send, up_recv, down_send, down_recv, pair_send, pair_recv):
        self.held = held
        self.length = held.shape[0] // 2
        self.sems = ((up_send, up_recv), (down_send, down_recv), (pair_send, pair_recv))
        me = lax.axis_index("dp")
        self.place, self.side = me // 2, lax.rem(me, 2)
        self.above = lax.rem(self.place + 1, self.length) * 2 + self.side
        self.below = lax.rem(self.place + self.length - 1, self.length) * 2 + self.side
        self.other = self.place * 2 + 1 - self.side

    def neighbours(self):
        return ("dp", self.above), ("dp", self.below), ("dp", self.other)

    def copy(self, way, origin, side=None):
        index = origin * 2 + (self.side if side is None else side)
        target = (self.above, self.below, self.other)[way]
        block = self.held.at[index]
        return remote(block, block, *self.sems[way], origin, "dp", target)

    def pass_on(self, origin, up, down):
        @pl.when(up & (self.place < self.length - 1))
        def _():
            self.copy(0, origin).start()

        @pl.when(down & (self.place > 0))
        def _():
            self.copy(1, origin).start()

        self.copy(2, origin).start()

    def start(self):
        self.pass_on(self.place, True, True)

    def step(self, k):
        low, high = self.place - k, self.place + k

        @pl.when(low >= 0)
        def _():
            self.copy(0, low).wait_recv()
            self.pass_on(low, True, False)

        @pl.when(high < self.length)
        def _():
            self.copy(1, high).wait_recv()
            self.pass_on(high, False, True)

    def finish(self):
        @pl.loop(0, self.length)
        def _(origin):
            self.copy(2, origin).wait_recv()
            self.copy(2, origin).wait_send()

            @pl.when((origin <= self.place) & (self.place < self.length - 1))
            def _():
                self.copy(0, origin).wait_send()

            @pl.when((origin >= self.place) & (self.place > 0))
            def _():
                self.copy(1, origin).wait_send()


class ImageSum:
    def __init__(self, stage, corner_in, near_in, passed, mine, far_in, sends, recvs):
        self.stage, self.corner_in, self.near_in = stage, corner_in, near_in
        self.passed, self.mine, self.far_in = passed, mine, far_in
        self.sends, self.recvs = sends, recvs
        self.me, self.near, self.far, self.corner = partners()
        self.core = lax.rem(self.me, 2)

    def image(self, turn):
        base = self.me - self.core
        other = lax.rem(base + 2, 4)
        return jnp.where(turn < 2, other, base - 2) + turn

    def to_corner(self):
        return remote(
            self.stage.at[0], self.corner_in, self.sends, self.recvs, 0, "head", self.near
        )

    def to_near(self):
        return remote(
            self.stage.at[1], self.near_in, self.sends, self.recvs, 1, "head", self.near
        )

    def to_far(self):
        return remote(self.passed, self.far_in, self.sends, self.recvs, 2, "head", self.far)

    def give(self, turn, part):
        theirs = lax.rem(turn, 2) != self.core

        @pl.when((turn < 2) & theirs)
        def _():
            self.stage[0] = part.astype(LOW)
            self.to_corner().start()

        @pl.when((turn >= 2) & theirs)
        def _():
            self.stage[1] = part.astype(LOW)
            self.to_near().start()

        @pl.when((turn < 2) & ~theirs)
        def _():
            self.to_corner().wait_recv()
            self.passed[...] = (part + self.corner_in[...].astype(FULL)).astype(LOW)
            self.to_far().start()

        @pl.when((turn >= 2) & ~theirs)
        def _():
            self.mine[...] = part

    def result(self):
        self.to_near().wait_recv()
        self.to_far().wait_recv()
        return self.mine[...] + self.near_in[...].astype(FULL) + self.far_in[...].astype(FULL)

    def finish(self):
        self.to_corner().wait_send()
        self.to_near().wait_send()
        self.to_far().wait_send()


def image_sum_scratch(rows, width):
    block = pltpu.VMEM((rows, width), LOW)
    return [
        pltpu.VMEM((2, rows, width), LOW), block, block, block,
        pltpu.VMEM((rows, width), FULL), block,
        pltpu.SemaphoreType.DMA((3,)), pltpu.SemaphoreType.DMA((3,)),
    ]


class LineScatter:
    def __init__(
        self, blocks, out, pair_in, up_in, down_in, total,
        up_send, up_recv, down_send, down_recv, pair_send, pair_recv,
    ):
        self.blocks, self.out, self.total = blocks, out, total
        self.arrived = (up_in, down_in, pair_in)
        self.sems = ((up_send, up_recv), (down_send, down_recv), (pair_send, pair_recv))
        self.length = blocks.shape[0] // 2
        me = lax.axis_index("dp")
        self.place, self.side = me // 2, lax.rem(me, 2)
        self.targets = (
            lax.rem(self.place + 1, self.length) * 2 + self.side,
            lax.rem(self.place + self.length - 1, self.length) * 2 + self.side,
            self.place * 2 + 1 - self.side,
        )

    def copy(self, way, block):
        source = (
            self.blocks.at[block * 2 + 1 - self.side] if way == 2 else self.total.at[block]
        )
        return remote(
            source, self.arrived[way].at[block], *self.sems[way], block, "dp", self.targets[way]
        )

    def start(self):
        @pl.loop(0, self.length)
        def _(turn):
            distance = self.length - 1 - turn

            @pl.when(self.place + distance < self.length)
            def _():
                self.copy(2, self.place + distance).start()

            @pl.when((self.place >= distance) & (distance > 0))
            def _():
                self.copy(2, self.place - distance).start()

    def pair_sum(self, block):
        self.copy(2, block).wait_recv()
        own = self.blocks[block * 2 + self.side].astype(FULL)
        return own + self.arrived[2][block].astype(FULL)

    def forward(self, way, block, first):
        both = self.pair_sum(block)

        @pl.when(first)
        def _():
            self.total[block] = both.astype(LOW)

        @pl.when(~first)
        def _():
            self.copy(way, block).wait_recv()
            self.total[block] = (both + self.arrived[way][block].astype(FULL)).astype(LOW)

        self.copy(way, block).start()

    def step(self, distance):
        @pl.when(self.place + distance < self.length)
        def _():
            self.forward(0, self.place + distance, self.place == 0)

        @pl.when(self.place >= distance)
        def _():
            self.forward(1, self.place - distance, self.place == self.length - 1)

    def result(self):
        self.out[...] = self.pair_sum(self.place)

        @pl.when(self.place > 0)
        def _():
            self.copy(0, self.place).wait_recv()
            self.out[...] += self.arrived[0][self.place].astype(FULL)

        @pl.when(self.place < self.length - 1)
        def _():
            self.copy(1, self.place).wait_recv()
            self.out[...] += self.arrived[1][self.place].astype(FULL)

    def finish(self):
        @pl.loop(0, self.length)
        def _(block):
            self.copy(2, block).wait_send()

            @pl.when(block > self.place)
            def _():
                self.copy(0, block).wait_send()

            @pl.when(block < self.place)
            def _():
                self.copy(1, block).wait_send()


def line_scatter_scratch(dp_count, rows, width):
    line = dp_count // 2
    return [pltpu.VMEM((line, rows, width), LOW)] * 4 + [pltpu.SemaphoreType.DMA((line,))] * 6


class SmallSum:
    def __init__(self, flat, head_in, dp_in, done, head_send, head_recv, dp_send, dp_recv):
        self.flat, self.head_in, self.dp_in, self.done = flat, head_in, dp_in, done
        self.head_sems, self.dp_sems = (head_send, head_recv), (dp_send, dp_recv)
        self.me, *self.others = partners()
        self.place, self.count = lax.axis_index("dp"), dp_in.shape[0]

    def to_head(self, lane):
        other = self.others[lane]
        return remote(
            self.flat.at[other], self.head_in.at[self.me], *self.head_sems, lane, "head", other
        )

    def back_head(self, lane):
        block = self.done.at[self.me]
        return remote(block, block, *self.head_sems, 3 + lane, "head", self.others[lane])

    def to_dp(self, shift):
        block = self.dp_in.at[self.place]
        other = lax.rem(self.place + shift, self.count)
        return remote(block, block, *self.dp_sems, shift, "dp", other)

    def start(self, value):
        groups, rows, lanes = self.flat.shape
        flat = jnp.concatenate(
            [value[:, at:at + lanes] for at in range(0, value.shape[1], lanes)], axis=0
        )
        for group in range(groups):
            self.flat[group] = flat[group * rows:(group + 1) * rows]
        for lane in range(3):
            self.to_head(lane).start()
        self.head_in[self.me] = self.flat[self.me]

    def across(self):
        for lane in range(3):
            self.to_head(lane).wait_recv()
        total = self.head_in[0]
        for head in range(1, self.head_in.shape[0]):
            total = total + self.head_in[head]
        self.dp_in[self.place] = total

        @pl.loop(1, self.count)
        def _(shift):
            self.to_dp(shift).start()

    def back(self):
        @pl.loop(1, self.count)
        def _(shift):
            self.to_dp(shift).wait_recv()

        total = lax.fori_loop(
            1, self.count, lambda at, so_far: so_far + self.dp_in[at], self.dp_in[0]
        )
        self.done[self.me] = total
        for lane in range(3):
            self.back_head(lane).start()

    def result(self, out):
        for lane in range(3):
            self.back_head(lane).wait_recv()
        flat = jnp.concatenate([self.done[group] for group in range(self.done.shape[0])], axis=0)
        rows, width = out.shape
        lanes = flat.shape[1]
        for at in range(width // lanes):
            out[:, at * lanes:(at + 1) * lanes] = flat[at * rows:(at + 1) * rows]

    def finish(self):
        for lane in range(3):
            self.to_head(lane).wait_send()
            self.back_head(lane).wait_send()

        @pl.loop(1, self.count)
        def _(shift):
            self.to_dp(shift).wait_send()


def small_sum_scratch(rows, width, dp_count):
    block = (rows * width // 128 // 4, 128)
    return [
        pltpu.VMEM((4,) + block, FULL), pltpu.VMEM((4,) + block, FULL),
        pltpu.VMEM((dp_count,) + block, FULL), pltpu.VMEM((4,) + block, FULL),
        pltpu.SemaphoreType.DMA((6,)), pltpu.SemaphoreType.DMA((6,)),
        pltpu.SemaphoreType.DMA((dp_count,)), pltpu.SemaphoreType.DMA((dp_count,)),
    ]


class LateSum:
    def __init__(self, dp_in, head_in, dp_send, dp_recv, head_send, head_recv):
        self.dp_in, self.head_in = dp_in, head_in
        self.dp_sems, self.head_sems = (dp_send, dp_recv), (head_send, head_recv)
        self.me, *self.others = partners()
        self.place, self.count = lax.axis_index("dp"), dp_in.shape[0]

    def to_dp(self, shift):
        block = self.dp_in.at[self.place]
        other = lax.rem(self.place + shift, self.count)
        return remote(block, block, *self.dp_sems, shift, "dp", other)

    def to_head(self, lane):
        block = self.head_in.at[self.me]
        return remote(block, block, *self.head_sems, lane, "head", self.others[lane])

    def start(self, rows):
        lanes = self.dp_in.shape[2]
        cuts = [
            row[:, at:at + lanes] for row in rows for at in range(0, row.shape[1], lanes)
        ]
        cuts += [jnp.zeros_like(cuts[0])] * (self.dp_in.shape[1] - len(cuts))
        self.dp_in[self.place] = jnp.concatenate(cuts, axis=0)

        @pl.loop(1, self.count)
        def _(shift):
            self.to_dp(shift).start()

    def across(self):
        @pl.loop(1, self.count)
        def _(shift):
            self.to_dp(shift).wait_recv()

        self.head_in[self.me] = lax.fori_loop(
            1, self.count, lambda at, so_far: so_far + self.dp_in[at], self.dp_in[0]
        )
        for lane in range(3):
            self.to_head(lane).start()

    def result(self, out, first):
        for lane in range(3):
            self.to_head(lane).wait_recv()
        total = self.head_in[0]
        for head in range(1, self.head_in.shape[0]):
            total = total + self.head_in[head]
        lanes = total.shape[1]
        cuts = out.shape[1] // lanes
        for row in range(2):
            for at in range(cuts):
                piece = total[row * cuts + at:row * cuts + at + 1]
                out[first + row:first + row + 1, at * lanes:(at + 1) * lanes] = piece

    def finish(self):
        for lane in range(3):
            self.to_head(lane).wait_send()

        @pl.loop(1, self.count)
        def _(shift):
            self.to_dp(shift).wait_send()


def late_sum_scratch(width, dp_count):
    block = (-(-2 * width // 128 // 8) * 8, 128)
    return [
        pltpu.VMEM((dp_count,) + block, FULL), pltpu.VMEM((4,) + block, FULL),
        pltpu.SemaphoreType.DMA((dp_count,)), pltpu.SemaphoreType.DMA((dp_count,)),
        pltpu.SemaphoreType.DMA((3,)), pltpu.SemaphoreType.DMA((3,)),
    ]


GATHER_CUTS = 4
COLUMN_CUTS = 3


class ImageGather:
    def __init__(self, held, sends, recvs, own=None, local_sem=None, columns=False):
        self.held, self.sends, self.recvs, self.columns = held, sends, recvs, columns
        self.me, self.near, self.far, self.corner = partners()
        self.own = held.at[self.me] if own is None else own
        self.local = None if own is None else pltpu.make_async_copy(own, held.at[self.me], local_sem)
        self.size = held.shape[1] // GATHER_CUTS
        self.wide = held.shape[2] // COLUMN_CUTS

    def piece(self, lane, cut):
        span = pl.ds(cut * self.size, self.size)
        image = self.far if lane == 2 else self.me
        if self.columns:
            block = self.held.at[image, :, pl.ds(cut * self.wide, self.wide)]
        else:
            block = self.held.at[image, span]
        source = block if self.columns or lane == 2 else self.own.at[span]
        other = self.far if lane == 0 else self.near
        index = lane * GATHER_CUTS + cut
        return remote(source, block, self.sends, self.recvs, index, "head", other)

    def start_far(self, first=0, last=GATHER_CUTS):
        for cut in range(first, last):
            self.piece(0, cut).start()

    def start_near(self, last=GATHER_CUTS):
        for cut in range(last):
            self.piece(1, cut).start()
        if self.local is not None:
            self.local.start()

    def start(self):
        self.start_far()
        self.start_near()

    def wait_near(self, first=0, last=GATHER_CUTS):
        for cut in range(first, last):
            self.piece(1, cut).wait_recv()

    def wait_far(self, first=0, last=GATHER_CUTS):
        for cut in range(first, last):
            self.piece(0, cut).wait_recv()
            self.piece(2, cut).start()

    def wait_corner(self, first=0, last=GATHER_CUTS):
        for cut in range(first, last):
            self.piece(2, cut).wait_recv()

    def finish(self, last=GATHER_CUTS):
        for cut in range(last):
            for lane in range(3):
                self.piece(lane, cut).wait_send()
        if self.local is not None:
            self.local.wait()


def image_gather_sems():
    return [pltpu.SemaphoreType.DMA((3 * GATHER_CUTS,)), pltpu.SemaphoreType.DMA((3 * GATHER_CUTS,))]


class BlockSum:
    def __init__(self, parts, first, mine, passed, corner_in, near_in, far_in, local_sems, sends, recvs):
        self.mine, self.passed, self.corner_in = mine, passed, corner_in
        self.near_in, self.far_in = near_in, far_in
        me, near, far, corner = partners()
        span = pl.ds(first, mine.shape[0])
        self.to_corner = remote(parts.at[corner, span], corner_in, sends, recvs, 0, "head", near)
        self.to_near = remote(parts.at[near, span], near_in, sends, recvs, 1, "head", near)
        self.to_far = remote(passed, far_in, sends, recvs, 2, "head", far)
        self.load_far = pltpu.make_async_copy(parts.at[far, span], passed, local_sems.at[0])
        self.load_mine = pltpu.make_async_copy(parts.at[me, span], mine, local_sems.at[1])

    def start(self):
        for copy in (self.to_corner, self.load_far, self.to_near, self.load_mine):
            copy.start()

    def across(self):
        self.load_far.wait()
        self.to_corner.wait_recv()
        both = self.passed[...].astype(FULL) + self.corner_in[...].astype(FULL)
        self.passed[...] = both.astype(LOW)
        self.to_far.start()

    def result(self):
        self.load_mine.wait()
        self.to_near.wait_recv()
        self.to_far.wait_recv()
        total = self.mine[...].astype(FULL) + self.near_in[...].astype(FULL)
        return total + self.far_in[...].astype(FULL)

    def finish(self):
        for copy in (self.to_corner, self.to_near, self.to_far):
            copy.wait_send()


def block_sum_scratch(rows, width):
    return [pltpu.VMEM((rows, width), LOW)] * 5 + [
        pltpu.SemaphoreType.DMA((2,)), pltpu.SemaphoreType.DMA((3,)), pltpu.SemaphoreType.DMA((3,)),
    ]


class Slots:
    def __init__(self, count, share):
        self.count, self.share = count, share
        self.big = -(-share // 16) * 16
        rest = 2 * share - self.big
        self.small = rest if rest > 0 and rest % 16 == 0 else self.big
        self.more = self.big - self.small
        self.both = self.big + self.small
        self.rows = count // 2 * self.both
        self.turns = count // 4
        self.phase_rows = self.turns * 2 * self.both

    def size(self, source, head):
        return self.small + self.more * ((head + source + 1) % 2)

    def packed(self, source, head):
        return (source // 2) * self.both + (source % 2) * self.size(0, head)

    def row(self, source, head, shift):
        first = self.size(source, 0) * (head % 2)
        group = (head // 2) * self.turns * self.both + self.turns * first
        return (
            (shift // self.turns) * self.phase_rows + group
            + (shift % self.turns) * self.size(source, head)
        )

    def holder(self, source, slot):
        pair, within = slot // self.both, slot % self.both
        first = self.size(source, 0)
        second = jnp.where(within >= first, 1, 0)
        return 2 * pair + second, within - second * first

    def span(self, start, extra):
        if extra:
            return pl.ds(pl.multiple_of(start + self.small, 16), self.more)
        return pl.ds(pl.multiple_of(start, 16), self.small)

    def each(self, is_big, make, action):
        getattr(make(False), action)()
        if self.more:
            @pl.when(is_big)
            def _():
                getattr(make(True), action)()


class SlotExchange:
    def __init__(self, slots, sent, rows, sends, recvs, local_sems, cut=None):
        self.slots, self.sent, self.rows = slots, sent, rows
        self.sems, self.local_sems = (sends, recvs), local_sems
        self.place, self.head = lax.axis_index("dp"), lax.axis_index("head")
        wide = sent.shape[1] // COLUMN_CUTS
        self.cut = 0 if cut is None else cut
        self.lanes = pl.ds(0, sent.shape[1]) if cut is None else pl.ds(cut * wide, wide)

    def index(self, shift, extra):
        return 2 * (self.cut * self.slots.count + shift) + int(extra)

    def out(self, shift, action):
        slots = self.slots
        expert = lax.rem(self.place + shift, slots.count)
        mine = slots.size(self.place, self.head)
        at, to = expert * mine, slots.packed(self.place, self.head)
        slots.each(mine > slots.small, lambda extra: remote(
            self.sent.at[slots.span(at, extra), self.lanes], self.rows.at[slots.span(to, extra), self.lanes],
            *self.sems, self.index(shift, extra), "dp", expert,
        ), action)

    def into(self, shift):
        slots = self.slots
        source = lax.rem(self.place + slots.count - shift, slots.count)
        size = slots.size(source, self.head)
        to = slots.packed(source, self.head)
        slots.each(size > slots.small, lambda extra: remote(
            self.sent.at[slots.span(0, extra), self.lanes], self.rows.at[slots.span(to, extra), self.lanes],
            *self.sems, self.index(shift, extra), "dp", source,
        ), "wait_recv")

    def own(self, action):
        slots = self.slots
        mine = slots.size(self.place, self.head)
        at, to = self.place * mine, slots.packed(self.place, self.head)
        slots.each(mine > slots.small, lambda extra: pltpu.make_async_copy(
            self.sent.at[slots.span(at, extra), self.lanes], self.rows.at[slots.span(to, extra), self.lanes],
            self.local_sems.at[2 * self.cut + int(extra)],
        ), action)

    def start(self):
        @pl.loop(1, self.slots.count)
        def _(shift):
            self.out(shift, "start")

        self.own("start")

    def finish(self):
        @pl.loop(1, self.slots.count)
        def _(shift):
            self.into(shift)
            self.out(shift, "wait_send")

        self.own("wait")


class SlotReturn:
    def __init__(self, slots, rows, back, zeros, sends, recvs, local_sems):
        self.slots, self.rows, self.back, self.zeros = slots, rows, back, zeros
        self.sems, self.local_sems = (sends, recvs), local_sems
        self.place, self.head = lax.axis_index("dp"), lax.axis_index("head")
        self.mine = slots.size(self.place, self.head)

    def out(self, shift, action):
        slots = self.slots
        source = lax.rem(self.place + shift, slots.count)
        size = slots.size(source, self.head)
        at, to = slots.packed(source, self.head), shift * size
        slots.each(size > slots.small, lambda extra: remote(
            self.rows.at[slots.span(at, extra)], self.back.at[slots.span(to, extra)],
            *self.sems, 2 * shift + int(extra), "dp", source,
        ), action)

    def into(self, shift):
        slots = self.slots
        expert = lax.rem(self.place + slots.count - shift, slots.count)
        slots.each(self.mine > slots.small, lambda extra: remote(
            self.rows.at[slots.span(0, extra)], self.back.at[slots.span(shift * self.mine, extra)],
            *self.sems, 2 * shift + int(extra), "dp", expert,
        ), "wait_recv")

    def own(self, action):
        slots = self.slots
        at = slots.packed(self.place, self.head)
        slots.each(self.mine > slots.small, lambda extra: pltpu.make_async_copy(
            self.rows.at[slots.span(at, extra)], self.back.at[slots.span(0, extra)],
            self.local_sems.at[int(extra)],
        ), action)

    def blank(self, action):
        slots = self.slots
        if slots.more:
            @pl.when(self.mine == slots.small)
            def _():
                tail = self.back.at[pl.ds(slots.count * slots.small, slots.count * slots.more)]
                copy = pltpu.make_async_copy(self.zeros, tail, self.local_sems.at[2])
                getattr(copy, action)()

    def start(self):
        if self.slots.more:
            self.zeros[...] = jnp.zeros_like(self.zeros)
        self.blank("start")

        @pl.loop(1, self.slots.count)
        def _(shift):
            self.out(shift, "start")

        self.own("start")

    def finish(self):
        @pl.loop(1, self.slots.count)
        def _(shift):
            self.into(shift)
            self.out(shift, "wait_send")

        self.own("wait")
        self.blank("wait")


def slot_return_scratch(slots, width):
    return [pltpu.VMEM((max(slots.count * slots.more, 16), width), LOW)] + [
        pltpu.SemaphoreType.DMA((2 * slots.count,)), pltpu.SemaphoreType.DMA((2 * slots.count,)),
        pltpu.SemaphoreType.DMA((3,)),
    ]


def slot_exchange_sems(count, cuts=1):
    return [
        pltpu.SemaphoreType.DMA((2 * count * cuts,)), pltpu.SemaphoreType.DMA((2 * count * cuts,)),
        pltpu.SemaphoreType.DMA((2 * cuts,)),
    ]


class ReturnGather:
    def __init__(self, slots, rows, held, sends, recvs, local_sems):
        self.slots, self.rows, self.held = slots, rows, held
        self.sems, self.local_sems = (sends, recvs), local_sems
        self.place = lax.axis_index("dp")
        self.me, self.near, self.far, self.corner = partners()

    def out(self, shift, action):
        slots = self.slots
        source = lax.rem(self.place + shift, slots.count)
        size = slots.size(source, self.me)
        at, to = slots.packed(source, self.me), slots.row(source, self.me, shift)
        slots.each(size > slots.small, lambda extra: remote(
            self.rows.at[slots.span(at, extra)], self.held.at[slots.span(to, extra)],
            *self.sems, 2 * shift + int(extra), "dp", source,
        ), action)

    def own(self, action):
        slots = self.slots
        size = slots.size(self.place, self.me)
        at, to = slots.packed(self.place, self.me), slots.row(self.place, self.me, 0)
        slots.each(size > slots.small, lambda extra: pltpu.make_async_copy(
            self.rows.at[slots.span(at, extra)], self.held.at[slots.span(to, extra)],
            self.local_sems.at[int(extra)],
        ), action)

    def block(self, lane, head, shift, axis, other, action):
        slots = self.slots
        size = slots.size(self.place, head)
        to = slots.row(self.place, head, shift)

        def make(extra):
            block = self.held.at[slots.span(to, extra)]
            index = 2 * (lane * slots.count + shift) + int(extra)
            return remote(block, block, *self.sems, index, axis, other)

        slots.each(size > slots.small, make, action)

    def start(self):
        @pl.loop(1, self.slots.count)
        def _(shift):
            self.out(shift, "start")

        self.own("start")

    def relay(self, shift):
        @pl.when(shift == 0)
        def _():
            self.own("wait")

        @pl.when(shift > 0)
        def _():
            expert = lax.rem(self.place + self.slots.count - shift, self.slots.count)
            self.block(0, self.me, shift, "dp", expert, "wait_recv")

        self.block(1, self.me, shift, "head", self.far, "start")
        self.block(2, self.me, shift, "head", self.near, "start")

    def forward(self, shift):
        self.block(1, self.far, shift, "head", self.far, "wait_recv")
        self.block(3, self.far, shift, "head", self.near, "start")

    def rest(self, shift):
        self.block(2, self.near, shift, "head", self.near, "wait_recv")
        self.block(3, self.corner, shift, "head", self.near, "wait_recv")

    def of_phase(self, phase, action):
        @pl.loop(0, self.slots.turns)
        def _(turn):
            action(phase * self.slots.turns + turn)

    def finish(self):
        @pl.loop(0, self.slots.count)
        def _(shift):
            @pl.when(shift > 0)
            def _():
                self.out(shift, "wait_send")

            self.block(1, self.me, shift, "head", self.far, "wait_send")
            self.block(2, self.me, shift, "head", self.near, "wait_send")
            self.block(3, self.far, shift, "head", self.near, "wait_send")


def return_gather_sems(count):
    return [
        pltpu.SemaphoreType.DMA((8 * count,)), pltpu.SemaphoreType.DMA((8 * count,)),
        pltpu.SemaphoreType.DMA((2,)),
    ]


def greet_all(heads, dp_count):
    barrier = pltpu.get_barrier_semaphore()
    place = lax.axis_index("dp")
    for other in heads:
        pl.semaphore_signal(barrier, inc=1, device_id={"head": other}, device_id_type=MESH)

    @pl.loop(1, dp_count)
    def _(shift):
        other = lax.rem(place + shift, dp_count)
        pl.semaphore_signal(barrier, inc=1, device_id={"dp": other}, device_id_type=MESH)

    pl.semaphore_wait(barrier, len(heads) + dp_count - 1)


ANYWHERE = pl.BlockSpec(memory_space=pl.ANY)
INSIDE = pl.BlockSpec(memory_space=pltpu.VMEM)


def digits(values):
    high = lax.div(values, 64)
    return [high.astype(FULL), (values - high * 64).astype(FULL)]


def digit_weights(shape, digit_axis):
    digit = lax.broadcasted_iota(jnp.int32, shape, digit_axis)
    value = lax.broadcasted_iota(jnp.int32, shape, 1 - digit_axis)
    weight = jnp.where(lax.rem(digit, 2) == 0, 64.0, 1.0)
    return jnp.where(lax.div(digit, 2) == value, weight, 0.0).astype(LOW)


def turned_rows(rows):
    count = rows[0].shape[1]
    parts = [part for row in rows for part in digits(row)]
    parts += [jnp.zeros((1, count), FULL)] * (8 - len(parts))
    spread = jnp.concatenate(parts, axis=0).astype(LOW)
    return tn(spread, digit_weights((8, 128), 0)).astype(jnp.int32)


def turned_column(column):
    lanes = lax.broadcasted_iota(jnp.int32, (column.shape[0], 128), 1)
    high, low = digits(column)
    spread = jnp.where(lanes == 0, high, jnp.where(lanes == 1, low, 0.0)).astype(LOW)
    return nt(digit_weights((8, 128), 1), spread)[0:1].astype(jnp.int32)


def prepare_kernel(
    slots, slot_count, capacity,
    tile_ref, norm_ref, owner_ref, ids_ref, pos_ref, up_ref, x_in, g_in,
    w_ref, src_ref, col_ref, col_back_ref, xn_out, hat_out, sent_out, up_out,
    x_ref, g_ref, xn_ref, hat_ref, up_full, up_low, held, sent_sum, sent_ref,
    load_sems, save_sems, *sems,
):
    images = x_ref.shape[0]
    gather = LineGather(held, *sems[:6])
    spread = ImageGather(up_out, *sems[6:8], own=up_low, local_sem=sems[8])
    load_up = pltpu.make_async_copy(up_ref, up_full, load_sems.at[2, 0])
    load_up.start()

    def load(image):
        return (
            pltpu.make_async_copy(x_in.at[image], x_ref.at[image], load_sems.at[0, image]),
            pltpu.make_async_copy(g_in.at[image], g_ref.at[image], load_sems.at[1, image]),
        )

    def save(image):
        return (
            pltpu.make_async_copy(xn_ref.at[image], xn_out.at[image], save_sems.at[0, image]),
            pltpu.make_async_copy(hat_ref.at[image], hat_out.at[image], save_sems.at[1, image]),
        )

    for image in range(images):
        for copy in load(image):
            copy.start()
    me, head = lax.axis_index("dp"), lax.axis_index("head")
    held[me] = tile_ref[...].astype(LOW)
    greet(*gather.neighbours(), ("head", spread.near), ("head", spread.far))
    gather.start()
    load_up.wait()
    up_low[...] = up_full[...].astype(LOW)
    spread.start()
    shape = (sent_ref.shape[0], PATCH)
    sent_sum[...] = jnp.zeros_like(sent_sum)
    steps = gather.length - 1

    def image_step(image):
        for copy in load(image):
            copy.wait()
        normal, _ = normalise(x_ref[image].astype(FULL))
        hat_ref[image] = normal.astype(LOW)
        xn_ref[image] = (normal * norm_ref[0:1, :] + norm_ref[1:2, :]).astype(LOW)
        for copy in save(image):
            copy.start()

        ids, pos = ids_ref[image], pos_ref[image]
        kept = pos < capacity
        holder, within = slots.holder(me, jnp.minimum(pos, capacity - 1))
        sent_at = ids * slots.size(me, head) + within
        sent_at = jnp.where(kept & (holder == head), sent_at, slots.count * slots.big)
        shift = me - ids
        shift = jnp.where(shift < 0, shift + slots.count, shift)
        back_at = jnp.where(kept, slots.row(me, holder, shift) + within + 1, 0)
        other_pair = jnp.where(lax.div(holder, 2) == lax.div(head, 2), 0, 2)
        apart = other_pair + jnp.where(lax.rem(holder, 2) == lax.rem(head, 2), 0, 1)
        out_at = apart * (slots.count * slots.big) + shift * slots.size(me, holder) + within
        out_at = jnp.where(kept, out_at + 1, 0)
        turned = turned_rows([back_at[0:1], back_at[1:2], out_at[0:1], out_at[1:2]])
        col_back_ref[image] = turned[:, 0:4] - 1
        col_ref[image] = sent_at
        first, second = sent_at[0:1], sent_at[1:2]
        sent_slots = lax.broadcasted_iota(jnp.int32, shape, 0)
        pick = one_hot((sent_slots == first) | (sent_slots == second))
        sent_sum[...] += nn(pick, g_ref[image])

    @pl.loop(0, max(steps, (images + 1) // 2))
    def _(turn):
        @pl.loop(2 * turn, jnp.minimum(2 * turn + 2, images))
        def _(image):
            image_step(image)

        @pl.when(turn < steps)
        def _():
            gather.step(turn + 1)

        @pl.when(turn == 1)
        def _():
            spread.wait_far(0, 1)

    sent_ref[...] = sent_sum[...].astype(LOW)
    save_sent = pltpu.make_async_copy(sent_ref, sent_out, load_sems.at[2, 1])
    save_sent.start()

    rows = w_ref.shape[0]
    tiles = owner_ref.shape[1]
    row_tile = lax.div(lax.broadcasted_iota(jnp.int32, (rows, tiles), 0), TILE)
    lane_tile = lax.broadcasted_iota(jnp.int32, (rows, tiles), 1)
    owner_rows = jnp.broadcast_to(owner_ref[...].astype(FULL), (8, tiles)).astype(LOW)
    owner = nt(one_hot(lane_tile == row_tile), owner_rows)[:, 0:1].astype(jnp.int32)
    before = (owner_ref[...] == owner) & (lane_tile < row_tile)
    rank = jnp.sum(jnp.where(before, 1.0, 0.0), axis=1, keepdims=True).astype(jnp.int32)
    within = lax.rem(lax.broadcasted_iota(jnp.int32, (rows, 1), 0), TILE)
    src = (owner * slot_count + rank) * TILE + within
    src_ref[...] = turned_column(src)
    spread.wait_far(1, 3)
    gather.finish()
    blocks, depth, width = held.shape
    cut = rows // 4
    for part in range(4):
        lanes = lax.broadcasted_iota(jnp.int32, (cut, blocks * depth), 1)
        pick = one_hot(lanes == src[part * cut:(part + 1) * cut])
        block = nn(pick, held[...].reshape(blocks * depth, width))
        w_ref[pl.ds(part * cut, cut), :] = block.astype(LOW)
    spread.wait_far(3)
    spread.wait_near()
    spread.wait_corner()
    spread.finish()
    save_sent.wait()

    @pl.loop(0, images)
    def _(image):
        for copy in save(image):
            copy.wait()


def prepare(slots, tiles, patches, cotangent, norm_params, owners, ids, pos, up, weight_rows):
    images, _, width = patches.shape
    slot_count = tiles.shape[0] // TILE
    line = slots.count // 2
    most = slots.count * slots.big
    capacity = images * PATCH // slots.count
    wide = jax.ShapeDtypeStruct(patches.shape, LOW)
    return pl.pallas_call(
        functools.partial(prepare_kernel, slots, slot_count, capacity),
        in_specs=[INSIDE] * 5 + [ANYWHERE] * 3,
        out_specs=[INSIDE] * 4 + [ANYWHERE] * 4,
        out_shape=[
            jax.ShapeDtypeStruct((weight_rows, width), LOW),
            jax.ShapeDtypeStruct((1, weight_rows), jnp.int32),
            jax.ShapeDtypeStruct((images, 2, PATCH), jnp.int32),
            jax.ShapeDtypeStruct((images, PATCH, 4), jnp.int32), wide, wide,
            jax.ShapeDtypeStruct((most, width), LOW), jax.ShapeDtypeStruct((4,) + up.shape, LOW),
        ],
        scratch_shapes=[pltpu.VMEM(patches.shape, LOW)] * 4
        + [
            pltpu.VMEM(up.shape, FULL), pltpu.VMEM(up.shape, LOW),
            pltpu.VMEM((slots.count,) + tiles.shape, LOW), pltpu.VMEM((most, width), FULL),
            pltpu.VMEM((most, width), LOW),
            pltpu.SemaphoreType.DMA((3, images)), pltpu.SemaphoreType.DMA((2, images)),
        ]
        + [pltpu.SemaphoreType.DMA((line,))] * 6 + image_gather_sems() + [pltpu.SemaphoreType.DMA],
        compiler_params=params(collective_id=0, has_side_effects=True),
        name="prepare",
    )(tiles, norm_params, owners, ids, pos, up, patches, cotangent)


def head_mask(shape, axis, head):
    return lax.broadcasted_iota(jnp.int32, shape, axis) // HD == head


def forward_kernel(
    slots,
    w_ref, norm_ref, col_ref, xn_in, x_ref, g_sent_ref, down_ref,
    lse_ref, q_out, qt_out, k_out, kt_out, v_out, ot_out, x1_out, rows_out, g_rows_out, down_out,
    q_ref, qt_ref, k_ref, kt_ref, v_ref, ot_ref, x1_ref, xn_ref, own_ref, sent_ref,
    down_full, down_low, picks, stats, norms, save_sems, own_sem, stat_send, stat_recv, *exchange,
):
    images = xn_ref.shape[0]
    rows = w_ref.shape[0] // 4
    heads = rows // HD
    total_of = ImageSum(*exchange[:8])
    spread = ImageGather(x1_ref, *exchange[8:10], columns=True)
    spread_down = ImageGather(down_out, *exchange[10:12], own=down_low, local_sem=exchange[12])
    send_g = SlotExchange(slots, g_sent_ref, g_rows_out, *exchange[13:16])
    send_rows = [
        SlotExchange(slots, sent_ref, rows_out, *exchange[16:], cut=cut) for cut in range(COLUMN_CUTS)
    ]
    me, near, far, corner = partners()

    def load(turn):
        image = total_of.image(turn)
        return pltpu.make_async_copy(xn_in.at[image], xn_ref.at[image], save_sems.at[6, turn])

    for turn in range(images):
        load(turn).start()
    load_down = pltpu.make_async_copy(down_ref, down_full, own_sem.at[1])
    load_down.start()
    own = pltpu.make_async_copy(x_ref.at[me], own_ref, own_sem.at[0])
    own.start()
    greet_all((near, far, corner), slots.count)
    load_down.wait()
    down_low[...] = down_full[...].astype(LOW)
    spread_down.start_far(0, 1)
    spread_down.start_near()
    send_g.start()
    kept = ((q_ref, q_out), (qt_ref, qt_out), (k_ref, k_out), (kt_ref, kt_out), (v_ref, v_out), (ot_ref, ot_out))
    shrink = HD ** (-0.5)

    def save(image):
        return [
            pltpu.make_async_copy(ref.at[image], out.at[image], save_sems.at[index, image])
            for index, (ref, out) in enumerate(kept)
        ]

    @pl.loop(0, images)
    def _(turn):
        image = total_of.image(turn)
        load(turn).wait()
        xn = xn_ref[image]
        wq, wk, wv, wo = (w_ref[pl.ds(part * rows, rows), :] for part in range(4))
        q_ref[image] = (nt(xn, wq) * shrink).astype(LOW)
        qt = (nt(wq, xn) * shrink).astype(LOW)
        qt_ref[image] = qt
        k = nt(xn, wk).astype(LOW)
        k_ref[image] = k
        kt_ref[image] = nt(wk, xn).astype(LOW)
        v_ref[image] = nt(xn, wv).astype(LOW)
        vt = nt(wv, xn).astype(LOW)
        mixed = []
        for head in range(heads):
            span = slice(head * HD, (head + 1) * HD)
            only = jnp.where(head_mask(qt.shape, 0, head), qt, jnp.zeros_like(qt))
            scores = nn(k, only)
            top = jnp.max(scores, axis=0, keepdims=True)
            weights = jnp.exp(scores - top)
            total = jnp.sum(weights, axis=0, keepdims=True)
            mixed.append(nn(vt[span], weights.astype(LOW)) / total)
            lse_ref[image, head:head + 1, :] = top + jnp.log(total)
        ot = jnp.concatenate(mixed, axis=0).astype(LOW)
        ot_ref[image] = ot
        total_of.give(turn, tn(ot, wo))
        for copy in save(image):
            copy.start()

    own.wait()
    x1 = (own_ref[...].astype(FULL) + total_of.result()).astype(LOW)
    x1_ref[me] = x1
    values = x1.astype(FULL)
    average = jnp.mean(values, axis=-1, keepdims=True)
    centred = values - average
    scale = lax.rsqrt(jnp.mean(centred * centred, axis=-1, keepdims=True) + eps_norm)
    lanes = lax.broadcasted_iota(jnp.int32, (PATCH, 128), 1)
    pair = jnp.where(lanes == 0, average, jnp.where(lanes == 1, scale, 0.0))
    eye = (8, 128)
    eye = lax.broadcasted_iota(jnp.int32, eye, 0) == lax.broadcasted_iota(jnp.int32, eye, 1)
    eye = jnp.where(eye, 1.0, 0.0)
    stats[me] = lax.dot_general(
        eye, pair, (((1,), (1,)), ((), ())), precision=lax.Precision.HIGHEST,
        preferred_element_type=FULL,
    )
    tell = [
        remote(stats.at[me], stats.at[me], stat_send, stat_recv, lane, "head", other)
        for lane, other in enumerate((near, far, corner))
    ]
    for copy in tell:
        copy.start()
    spread.start_far(0, COLUMN_CUTS)
    spread.start_near(COLUMN_CUTS)
    spread_down.start_far(1)

    @pl.loop(0, images)
    def _(image):
        rows_of = lax.broadcasted_iota(jnp.int32, (sent_ref.shape[0], PATCH), 0)
        col = col_ref[image]
        picks[image] = one_hot((rows_of == col[0:1, :]) | (rows_of == col[1:2, :]))

    for copy in tell:
        copy.wait_recv()

    @pl.loop(0, images)
    def _(image):
        norms[image] = lax.dot_general(
            stats[image], eye, (((0,), (0,)), ((), ())), precision=lax.Precision.HIGHEST,
            preferred_element_type=FULL,
        )

    for cut in range(COLUMN_CUTS):
        wide = sent_ref.shape[1] // COLUMN_CUTS
        span = slice(cut * wide, (cut + 1) * wide)

        def place(image, span=span):
            normal = (x1_ref[image, :, span].astype(FULL) - norms[image, :, 0:1]) * norms[image, :, 1:2]
            low = (normal * norm_ref[2:3, span] + norm_ref[3:4, span]).astype(LOW)
            return nn(picks[image], low)

        total = place(me)
        spread.wait_near(cut, cut + 1)
        total = total + place(near)
        spread.wait_far(cut, cut + 1)
        total = total + place(far)
        spread.wait_corner(cut, cut + 1)
        sent_ref[:, span] = (total + place(corner)).astype(LOW)
        send_rows[cut].start()

    keep = pltpu.make_async_copy(x1_ref, x1_out, own_sem.at[0])
    keep.start()
    for copy in tell:
        copy.wait_send()
    spread.finish(COLUMN_CUTS)
    total_of.finish()
    send_g.finish()
    spread_down.wait_far()
    spread_down.wait_near()
    spread_down.wait_corner()
    spread_down.finish()
    for copy in send_rows:
        copy.finish()
    keep.wait()

    @pl.loop(0, images)
    def _(image):
        for copy in save(image):
            copy.wait()


def attention_forward(slots, xn, w, norm_params, col_rows, patches, g_sent, down):
    images, _, width = patches.shape
    rows = w.shape[0] // 4
    flat, turned = (images, PATCH, rows), (images, rows, PATCH)
    saved = [flat, turned, flat, turned, flat, turned, patches.shape]
    outs = saved + [(slots.rows, width), (slots.rows, width), (4,) + down.shape]
    most = slots.count * slots.big
    return pl.pallas_call(
        functools.partial(forward_kernel, slots),
        in_specs=[INSIDE] * 3 + [ANYWHERE] * 4,
        out_specs=[INSIDE] + [ANYWHERE] * 10,
        out_shape=[jax.ShapeDtypeStruct((images, 8, PATCH), FULL)]
        + [jax.ShapeDtypeStruct(shape, LOW) for shape in outs],
        scratch_shapes=[pltpu.VMEM(shape, LOW) for shape in saved]
        + [
            pltpu.VMEM(patches.shape, LOW),
            pltpu.VMEM((PATCH, width), LOW), pltpu.VMEM((most, width), LOW),
            pltpu.VMEM(down.shape, FULL), pltpu.VMEM(down.shape, LOW),
            pltpu.VMEM((images, most, PATCH), LOW), pltpu.VMEM((images, 8, PATCH), FULL),
            pltpu.VMEM((images, PATCH, 128), FULL),
            pltpu.SemaphoreType.DMA((7, images)), pltpu.SemaphoreType.DMA((2,)),
            pltpu.SemaphoreType.DMA((3,)), pltpu.SemaphoreType.DMA((3,)),
        ]
        + image_sum_scratch(PATCH, width) + image_gather_sems() + image_gather_sems()
        + [pltpu.SemaphoreType.DMA]
        + slot_exchange_sems(slots.count) + slot_exchange_sems(slots.count, COLUMN_CUTS),
        compiler_params=params(collective_id=1, has_side_effects=True),
        name="attention_forward",
    )(w, norm_params, col_rows, xn, patches, g_sent, down)


def backward_kernel(
    experts, slots,
    w_ref, lse_ref, src_ref, norm_ref, small_ref,
    x1g_in, xn_in, hat_in, q_in, qt_in, k_in, kt_in, v_in, ot_in, x_ref, out_rows_ref, down_part,
    owned_ref, small_out, down_grad_ref, input_out, out_back,
    x1g_ref, xn_ref, hat_ref, q_ref, qt_ref, k_ref, kt_ref, v_ref, ot_ref, late_ref,
    grad_ref, own_ref, input_ref, padded_ref, load_sems, own_sem, *exchange,
):
    images = x1g_ref.shape[0]
    rows = w_ref.shape[0] // 4
    heads = rows // HD
    total_of = ImageSum(*exchange[:8])
    spread = ImageGather(input_ref, *exchange[8:10])
    back_out = SlotReturn(slots, out_rows_ref, out_back, *exchange[10:14])
    weights_sum = LineScatter(padded_ref, owned_ref, *exchange[14:24])
    down_sum = BlockSum(down_part, down_part.shape[1] // 2, *exchange[24:32])
    small_sum = SmallSum(*exchange[32:40])
    late_sum = LateSum(*exchange[40:])
    me, near, far, corner = partners()
    dp_count = slots.count
    streamed = (
        (xn_in, xn_ref), (hat_in, hat_ref), (q_in, q_ref), (qt_in, qt_ref), (k_in, k_ref), (kt_in, kt_ref),
        (v_in, v_ref), (ot_in, ot_ref),
    )

    def load(turn):
        image, slot = total_of.image(turn), lax.rem(turn, 2)
        copies = [
            pltpu.make_async_copy(source.at[image], target.at[slot], load_sems.at[index, slot])
            for index, (source, target) in enumerate(streamed)
        ]
        copies.append(
            pltpu.make_async_copy(x1g_in.at[image], x1g_ref.at[image], load_sems.at[8, slot])
        )
        return copies

    for turn in range(2):
        for copy in load(turn):
            copy.start()
    own = pltpu.make_async_copy(x_ref.at[me], own_ref, own_sem.at[0])
    own.start()
    greet_all((near, far, corner), dp_count)
    small_sum.start(small_ref[...])
    down_sum.start()
    back_out.start()
    down_sum.across()
    late_ref[...] = jnp.zeros_like(late_ref)
    shrink = HD ** (-0.5)
    grad_ref[...] = jnp.zeros_like(grad_ref)

    @pl.loop(0, images)
    def _(turn):
        image, slot = total_of.image(turn), lax.rem(turn, 2)
        for copy in load(turn):
            copy.wait()
        wq, wk, wv, wo = (w_ref[pl.ds(part * rows, rows), :] for part in range(4))
        x1g, xn = x1g_ref[image], xn_ref[slot]
        q, qt, k, kt = q_ref[slot], qt_ref[slot], k_ref[slot], kt_ref[slot]
        v, ot = v_ref[slot], ot_ref[slot]
        do = nt(x1g, wo).astype(LOW)
        dot = nt(wo, x1g).astype(LOW)
        product = dot.astype(FULL) * ot.astype(FULL)
        dqt, dk, dv = [], None, None
        for head in range(heads):
            span = slice(head * HD, (head + 1) * HD)
            zero_t = jnp.zeros_like(qt)
            mask_t = head_mask(qt.shape, 0, head)
            mask = head_mask(q.shape, 1, head)
            scores = nn(k, jnp.where(mask_t, qt, zero_t))
            weights = jnp.exp(scores - lse_ref[image, head:head + 1, :])
            back = nn(v, jnp.where(mask_t, dot, zero_t))
            delta = jnp.sum(product[span], axis=0, keepdims=True)
            score_grad = (weights * (back - delta)).astype(LOW)
            dqt.append(nn(kt[span], score_grad) * shrink)
            dk_one = nn(score_grad, jnp.where(mask, q, jnp.zeros_like(q)))
            dv_one = nn(weights.astype(LOW), jnp.where(mask, do, jnp.zeros_like(do)))
            dk = dk_one if dk is None else dk + dk_one
            dv = dv_one if dv is None else dv + dv_one
        dqt = jnp.concatenate(dqt, axis=0).astype(LOW)
        dk, dv = dk.astype(LOW), dv.astype(LOW)
        part = tn(dqt, wq) + nn(dk, wk) + nn(dv, wv)
        total_of.give(turn, part)
        late_ref[0:1, :] += jnp.sum(part * hat_ref[slot].astype(FULL), axis=0, keepdims=True)
        late_ref[1:2, :] += jnp.sum(part, axis=0, keepdims=True)
        pieces = (nn(dqt, xn), tn(dk, xn), tn(dv, xn), nn(ot, x1g))
        for part, piece in enumerate(pieces):
            grad_ref[pl.ds(part * rows, rows), :] += piece

        @pl.when(turn + 2 < images)
        def _():
            for copy in load(turn + 2):
                copy.start()

        @pl.when(turn == 1)
        def _():
            small_sum.across()

    late_sum.start([late_ref[0:1, :], late_ref[1:2, :]])
    low = grad_ref[...].astype(LOW)
    depth = padded_ref.shape[1]
    parts = min(dp_count, 8)
    cut = dp_count // parts * depth
    for part in range(parts):
        row = lax.broadcasted_iota(jnp.int32, (cut, low.shape[0]), 0) + part * cut
        pick = one_hot(row == src_ref[...])
        block = nn(pick, low).astype(LOW)
        padded_ref[pl.ds(part * (dp_count // parts), dp_count // parts)] = block.reshape(
            dp_count // parts, depth, block.shape[1]
        )
    weights_sum.start()
    small_sum.back()
    own.wait()
    normal, scale = normalise(own_ref[...].astype(FULL))
    back = norm_back(normal, scale, norm_ref[0:1, :], total_of.result())[0]
    input_ref[me] = (x1g_ref[me].astype(FULL) + back).astype(LOW)
    spread.start()
    late_sum.across()
    steps = weights_sum.length

    @pl.loop(0, steps - 1)
    def _(turn):
        weights_sum.step(steps - 1 - turn)

        @pl.when(turn == steps - 2)
        def _():
            spread.wait_far()

    weights_sum.result()
    small_sum.result(small_out)
    late_sum.result(small_out, experts)
    down_grad_ref[...] = down_sum.result()
    spread.wait_near()
    spread.wait_corner()
    keep = pltpu.make_async_copy(input_ref, input_out, own_sem.at[0])
    keep.start()
    back_out.finish()
    spread.finish()
    total_of.finish()
    weights_sum.finish()
    small_sum.finish()
    late_sum.finish()
    down_sum.finish()
    keep.wait()


def attention_backward(
    experts, slots, depth,
    x1_grad, w, xn, hat, saved, lse, src_row, norm_params, small, patches, out_rows, down_part,
):
    images, _, width = patches.shape
    rows = w.shape[0] // 4
    dp_count = slots.count
    flat, turned = (2, PATCH, rows), (2, rows, PATCH)
    units = down_part.shape[1]
    return pl.pallas_call(
        functools.partial(backward_kernel, experts, slots),
        in_specs=[INSIDE] * 5 + [ANYWHERE] * 12,
        out_specs=[INSIDE] * 3 + [ANYWHERE] * 2,
        out_shape=[
            jax.ShapeDtypeStruct((depth, width), FULL), jax.ShapeDtypeStruct(small.shape, FULL),
            jax.ShapeDtypeStruct((units // 2, width), FULL),
            jax.ShapeDtypeStruct(patches.shape, LOW),
            jax.ShapeDtypeStruct((dp_count * slots.big, width), LOW),
        ],
        scratch_shapes=[pltpu.VMEM(patches.shape, LOW)]
        + [pltpu.VMEM((2, PATCH, width), LOW)] * 2
        + [pltpu.VMEM(shape, LOW) for shape in (flat, turned, flat, turned, flat, turned)]
        + [
            pltpu.VMEM((8, width), FULL), pltpu.VMEM(w.shape, FULL), pltpu.VMEM((PATCH, width), LOW),
            pltpu.VMEM(patches.shape, LOW), pltpu.VMEM((dp_count, depth, width), LOW),
            pltpu.SemaphoreType.DMA((9, 2)), pltpu.SemaphoreType.DMA((2,)),
        ]
        + image_sum_scratch(PATCH, width) + image_gather_sems()
        + slot_return_scratch(slots, width)
        + line_scatter_scratch(dp_count, depth, width)
        + block_sum_scratch(units // 2, width)
        + small_sum_scratch(small.shape[0], width, dp_count)
        + late_sum_scratch(width, dp_count),
        compiler_params=params(collective_id=2, has_side_effects=True),
        name="attention_backward",
    )(
        w, lse, src_row, norm_params, small, x1_grad, xn, hat, *saved, patches, out_rows, down_part,
    )


def picked_rows(col, held_ref, start, count):
    lanes = lax.broadcasted_iota(jnp.int32, (col.shape[0], count), 1) + start
    pick = one_hot((lanes == col[:, 0:1]) | (lanes == col[:, 1:2]))
    return nn(pick, held_ref[pl.ds(start, count), :])


def combine_kernel(col_ref, x1_ref, *refs):
    *held, out_ref = refs
    total = x1_ref[0].astype(FULL)
    col = col_ref[0]
    count = 2 * held[0].shape[0]
    for part in range(2):
        lanes = lax.broadcasted_iota(jnp.int32, (col.shape[0], count), 1) + part * count
        pick = one_hot((lanes == col[:, 2:3]) | (lanes == col[:, 3:4]))
        rows = jnp.concatenate([held[2 * part][...], held[2 * part + 1][...]], axis=0)
        total = total + nn(pick, rows)
    out_ref[0] = total.astype(LOW)


def combine_forward(col, x1, held):
    images, _, width = x1.shape
    wide = lead((1, PATCH, width))
    return pl.pallas_call(
        combine_kernel,
        grid=(images,),
        in_specs=[lead((1, PATCH, 4)), wide] + [whole(rows.shape) for rows in held],
        out_specs=wide,
        out_shape=jax.ShapeDtypeStruct(x1.shape, LOW),
        compiler_params=params(),
        cost_estimate=pl.CostEstimate(
            flops=2 * images * PATCH * sum(rows.size for rows in held),
            bytes_accessed=4 * x1.size + 2 * sum(rows.size for rows in held), transcendentals=0,
        ),
        name="combine_forward",
    )(col, x1, *held)


def expert_kernel(
    slots,
    rows_ref, g_ref, router_in, col_ref, norm_ref,
    up_in, down_in, x1_in, cot_in,
    up_grad_ref, down_grad_ref, small_ref, down_out, out_out, x1g_out,
    router_ref, up_ref, down_ref, og_ref, gate_ref, probs_ref, down_stage, back_ref,
    held, total, x1_ref, cot_ref, x1g_ref,
    load_sems, save_sems, image_sems, out_sem, *exchange,
):
    images, count = x1_in.shape[0], rows_ref.shape[0]
    out_sum, back_sum = total.at[pl.ds(0, count)], total.at[pl.ds(count, count)]
    up_sum = ImageSum(*exchange[:8])
    back = ReturnGather(slots, back_ref, held, *exchange[8:11])
    down_sum = BlockSum(down_out, 0, *exchange[11:])
    parts = up_in.shape[0]

    def load(turn):
        part, slot = up_sum.image(turn), lax.rem(turn, 2)
        return (
            pltpu.make_async_copy(up_in.at[part], up_ref.at[slot], load_sems.at[0, slot]),
            pltpu.make_async_copy(down_in.at[part], down_ref.at[slot], load_sems.at[1, slot]),
        )

    def save(turn):
        slot = lax.rem(turn, 2)
        return pltpu.make_async_copy(
            down_stage.at[slot], down_out.at[up_sum.image(turn)], save_sems.at[slot]
        )

    for turn in range(2):
        for copy in load(turn):
            copy.start()
    rows = rows_ref[...]
    experts = router_in.shape[0]
    router_ref[...] = jnp.zeros_like(router_ref)
    router_ref[0:experts, :] = router_in[...]
    lane = lax.broadcasted_iota(jnp.int32, (1, router_ref.shape[0]), 1)
    mine = jnp.where(lane == lax.axis_index("dp"), 1.0, 0.0)
    logits = nt(rows, router_ref[...].astype(LOW)) + jnp.where(lane < experts, 0.0, -1e30)
    top = jnp.max(logits, axis=-1, keepdims=True)
    weights = jnp.exp(logits - top)
    probs = weights / jnp.sum(weights, axis=-1, keepdims=True)
    gate = jnp.sum(probs * mine, axis=-1, keepdims=True)
    probs_ref[...] = probs
    gate_ref[...] = gate
    og_ref[...] = (gate * g_ref[...].astype(FULL)).astype(LOW)
    out_sum[...] = jnp.zeros_like(out_sum)
    back_sum[...] = jnp.zeros_like(back_sum)
    greet_all((back.near, back.far), slots.count)

    @pl.loop(0, parts)
    def _(turn):
        slot = lax.rem(turn, 2)
        for copy in load(turn):
            copy.wait()
        rows, og = rows_ref[...], og_ref[...]
        up, down = up_ref[slot], down_ref[slot]
        hidden = nn(rows, up)
        slope = (2.0 / jnp.pi) ** 0.5
        square = hidden * hidden
        bend = jnp.tanh(slope * (hidden + 0.044715 * (square * hidden)))
        act = (0.5 * hidden * (1.0 + bend)).astype(LOW)
        out_sum[...] += nn(act, down)
        act_grad = nt(og, down)
        inner = slope * (1.0 + (3.0 * 0.044715) * square)
        curve = 0.5 * (1.0 + bend) + 0.5 * hidden * (1.0 - bend * bend) * inner
        hidden_grad = (curve * act_grad).astype(LOW)
        back_sum[...] += nt(hidden_grad, up)
        up_sum.give(turn, tn(rows, hidden_grad))

        @pl.when(turn >= 2)
        def _():
            save(turn - 2).wait()

        down_stage[lax.rem(turn, 2)] = tn(act, og).astype(LOW)
        save(turn).start()

        @pl.when(turn + 2 < parts)
        def _():
            for copy in load(turn + 2):
                copy.start()

    out = out_sum[...].astype(LOW).astype(FULL)
    gate, probs = gate_ref[...], probs_ref[...]
    gate_grad = jnp.sum(g_ref[...].astype(FULL) * out, axis=-1, keepdims=True)
    logit_grad = (gate_grad * (probs * (mine - gate))).astype(LOW)
    plain = back_sum[...].astype(LOW).astype(FULL)
    back_ref[...] = (plain + nn(logit_grad, router_ref[...].astype(LOW))).astype(LOW)
    back.start()
    og_ref[...] = (gate * out).astype(LOW)
    save_out = pltpu.make_async_copy(og_ref, out_out, out_sem)
    save_out.start()
    small_ref[...] = jnp.zeros_like(small_ref)
    small_ref[0:experts, :] = tn(logit_grad, rows_ref[...])[0:experts]

    def image_load(image):
        slot = lax.rem(image, 2)
        return (
            pltpu.make_async_copy(x1_in.at[image], x1_ref.at[slot], image_sems.at[0, slot]),
            pltpu.make_async_copy(cot_in.at[image], cot_ref.at[slot], image_sems.at[1, slot]),
        )

    def image_save(image):
        slot = lax.rem(image, 2)
        return pltpu.make_async_copy(x1g_ref.at[slot], x1g_out.at[image], image_sems.at[2, slot])

    for image in range(2):
        for copy in image_load(image):
            copy.start()
    for turn in range(parts - 2, parts):
        save(turn).wait()
    down_sum.start()
    back.of_phase(0, back.relay)
    total_rows = held.shape[0]
    piece = 3 * 256
    if total_rows % piece:
        piece = slots.phase_rows
    done = 0
    for phase in range(4):
        back.of_phase(phase, back.forward)
        if phase < 3:
            back.of_phase(phase + 1, back.relay)
        if phase == 2:
            down_sum.across()
        back.of_phase(phase, back.rest)
        ready = (phase + 1) * slots.phase_rows
        while done + piece <= ready:
            @pl.loop(0, images)
            def _(image, start=done):
                part = picked_rows(col_ref[image], held, start, piece)
                span = pl.ds(image * PATCH, PATCH)
                if start == 0:
                    total[span] = part
                else:
                    total[span] += part

            done += piece

    back_scale = 1.0 / 4.0

    @pl.loop(0, images)
    def _(image):
        slot = lax.rem(image, 2)
        for copy in image_load(image):
            copy.wait()

        @pl.when(image >= 2)
        def _():
            image_save(image - 2).wait()

        normal, scale = normalise(x1_ref[slot].astype(FULL))
        upstream = total[pl.ds(image * PATCH, PATCH)]
        result, gain_sum, shift_sum = norm_back(normal, scale, norm_ref[2:3, :], upstream)
        x1g_ref[slot] = (cot_ref[slot].astype(FULL) + result).astype(LOW)
        small_ref[experts + 2:experts + 3, :] += gain_sum * back_scale
        small_ref[experts + 3:experts + 4, :] += shift_sum * back_scale
        image_save(image).start()

        @pl.when(image + 2 < images)
        def _():
            for copy in image_load(image + 2):
                copy.start()

    up_grad_ref[...] = up_sum.result()
    down_grad_ref[...] = down_sum.result()
    back.finish()
    up_sum.finish()
    down_sum.finish()
    save_out.wait()
    for image in range(images - 2, images):
        image_save(image).wait()


def expert_stage(slots, rows, g_rows, up, down, router, col, x1, cotangent, norm_params):
    count, width = rows.shape
    parts, _, units = up.shape
    images = x1.shape[0]
    small_rows = -(-(router.shape[0] + 4) // 16) * 16
    lanes = 128
    flat = pltpu.VMEM((count, width), LOW)
    pair = pltpu.VMEM((2, PATCH, width), LOW)
    return pl.pallas_call(
        functools.partial(expert_kernel, slots),
        in_specs=[INSIDE] * 5 + [ANYWHERE] * 4,
        out_specs=[INSIDE] * 3 + [ANYWHERE] * 3,
        out_shape=[
            jax.ShapeDtypeStruct((width, units), FULL),
            jax.ShapeDtypeStruct((units // 2, width), FULL),
            jax.ShapeDtypeStruct((small_rows, width), FULL),
            jax.ShapeDtypeStruct(down.shape, LOW),
            jax.ShapeDtypeStruct((count, width), LOW),
            jax.ShapeDtypeStruct(x1.shape, LOW),
        ],
        scratch_shapes=[
            pltpu.VMEM((lanes, width), FULL),
            pltpu.VMEM((2,) + up.shape[1:], LOW), pltpu.VMEM((2,) + down.shape[1:], LOW), flat,
            pltpu.VMEM((count, 1), FULL), pltpu.VMEM((count, lanes), FULL),
            pltpu.VMEM((2, units, width), LOW), flat,
            pltpu.VMEM((4 * slots.phase_rows, width), LOW),
            pltpu.VMEM((max(images * PATCH, 2 * count), width), FULL), pair, pair, pair,
            pltpu.SemaphoreType.DMA((2, 2)), pltpu.SemaphoreType.DMA((2,)),
            pltpu.SemaphoreType.DMA((3, 2)), pltpu.SemaphoreType.DMA,
        ]
        + image_sum_scratch(width, units) + return_gather_sems(slots.count)
        + block_sum_scratch(units // 2, width),
        compiler_params=params(collective_id=3, has_side_effects=True),
        name="expert_stage",
    )(
        rows, g_rows, router, col, norm_params, up, down, x1, cotangent,
    )


def body(
    patches, cotangent, expert_ids, slot_pos, owners,
    tile_master, tile_first, tile_second,
    expert_up, up_first, up_second,
    expert_down, down_first, down_second,
    router, router_first, router_second,
    norm_params, norm_first, norm_second,
):
    tok_rows, width = patches.shape
    experts = router.shape[0]
    capacity = tok_rows // experts
    dp_count = lax.axis_size("dp")
    head_count = lax.axis_size("head")
    images = tok_rows // PATCH
    slots = Slots(dp_count, capacity // head_count)
    slot_count = tile_master.shape[0]

    by_image = (images, PATCH, width)
    x_images, g_images = patches.reshape(by_image), cotangent.reshape(by_image)

    def pair_rows(pairs):
        return pairs.T.reshape(2, images, PATCH).transpose(1, 0, 2)

    w, src, col_rows, col, xn, hat, g_sent, up_all = prepare(
        slots, tile_master.reshape(slot_count * TILE, width), x_images, g_images, norm_params,
        owners, pair_rows(expert_ids), pair_rows(slot_pos), expert_up[0],
        owners.shape[1] * TILE,
    )
    lse, *saved, x1, rows, g_rows, down_all = attention_forward(
        slots, xn, w, norm_params, col_rows, x_images, g_sent, expert_down[0]
    )
    up_grad, down_first_half, small, down_part, out, x1_grad = expert_stage(
        slots, rows, g_rows, up_all, down_all, router, col, x1, g_images, norm_params
    )
    owned_grad, small, down_second_half, input_low, out_back = attention_backward(
        experts, slots, slot_count * TILE,
        x1_grad, w, xn, hat, saved, lse, src, norm_params, small, x_images, out, down_part,
    )
    down_grad = jnp.concatenate([down_first_half, down_second_half], axis=0)
    owned_grad = owned_grad.reshape(slot_count, TILE, width)
    input_grad = input_low.reshape(tok_rows, width).astype(FULL)

    def from_head(rows, apart):
        return lax.ppermute(rows, "head", [(at, at ^ apart) for at in range(head_count)])

    out_far = from_head(out_back, 2)
    held = [out_back, from_head(out_back, 1), out_far, from_head(out_far, 1)]
    block_out = combine_forward(col, x1, held).reshape(tok_rows, width)

    router_total, norm_total = small[:experts], small[experts:experts + 4]

    tile_new, tile_first_new, tile_second_new = adam_update(
        tile_master, tile_first, tile_second, owned_grad, rate_attention, decay_factor
    )
    up_new, up_first_new, up_second_new = adam_update(
        expert_up, up_first, up_second, up_grad[None], rate_up, decay_factor
    )
    down_new, down_first_new, down_second_new = adam_update(
        expert_down, down_first, down_second, down_grad[None], rate_down, decay_factor
    )
    router_new, router_first_new, router_second_new = adam_update(
        router, router_first, router_second, router_total, rate_router, decay_factor
    )
    norm_new, norm_first_new, norm_second_all = adam_update(
        norm_params, norm_first, norm_second, norm_total, rate_norm, 0.0
    )
    return (
        block_out,
        input_grad,
        tile_new,
        tile_first_new,
        tile_second_new,
        tile_new.astype(LOW),
        up_new,
        up_first_new,
        up_second_new,
        up_new.astype(LOW),
        down_new,
        down_first_new,
        down_second_new,
        down_new.astype(LOW),
        router_new,
        router_first_new,
        router_second_new,
        norm_new,
        norm_first_new,
        norm_second_all[:2],
        norm_second_all[2:],
    )


def solution(mesh):
    row = P("dp", None)
    tiles = P(("dp", "head"), None, None)
    up = P("dp", None, "head")
    down = P("dp", "head", None)
    in_specs = (
        row, row, row, row, P("head", None), tiles, tiles, tiles,
        up, up, up, down, down, down, P(), P(), P(), P(), P(), P(),
    )
    out_specs = (
        row, row, tiles, tiles, tiles, tiles, up, up, up, up, down, down, down, down,
        P(), P(), P(), P(), P(), P(), P(),
    )
    return jax.shard_map(body, mesh=mesh, in_specs=in_specs, out_specs=out_specs, check_vma=False)
```

```python
import functools

import jax
import jax.numpy as jnp
from jax import lax
from jax.experimental import pallas as pl
from jax.experimental.pallas import tpu as pltpu
from jax.sharding import PartitionSpec as P

HD = 64
PATCH = 576
TILE = 8
STEP = 10

eps_norm = 1e-06
beta_one = 0.9
beta_two = 0.999
adam_eps = 1e-08
rate_attention = 0.12
rate_up = 0.08
rate_down = 0.3
rate_router = 0.05
rate_norm = 0.4
decay_factor = 0.1

LOW = jnp.bfloat16
FULL = jnp.float32
MESH = pl.DeviceIdType.MESH
MOST_KEPT = 640
VMEM_BYTES = 61 * 1024 * 1024


def adam_update(weight, moment_one, moment_two, gradient, step_rate, weight_decay):
    moment_one = beta_one * moment_one + (1.0 - beta_one) * gradient
    moment_two = beta_two * moment_two + (1.0 - beta_two) * gradient * gradient
    fixed_one = moment_one / (1.0 - beta_one**STEP)
    fixed_two = moment_two / (1.0 - beta_two**STEP)
    weight = weight - step_rate * (
        fixed_one / (jnp.sqrt(fixed_two) + adam_eps) + weight_decay * weight
    )
    return (weight, moment_one, moment_two)


def nn(left, right):
    return lax.dot_general(left, right, (((1,), (0,)), ((), ())), preferred_element_type=FULL)


def nt(left, right):
    return lax.dot_general(left, right, (((1,), (1,)), ((), ())), preferred_element_type=FULL)


def tn(left, right):
    return lax.dot_general(left, right, (((0,), (0,)), ((), ())), preferred_element_type=FULL)


def params(**more):
    return pltpu.CompilerParams(vmem_limit_bytes=VMEM_BYTES, **more)


def whole(shape):
    return pl.BlockSpec(shape, lambda *_: (0,) * len(shape))


def lead(shape):
    return pl.BlockSpec(shape, lambda i: (i,) + (0,) * (len(shape) - 1))


def normalise(values):
    average = jnp.mean(values, axis=-1, keepdims=True)
    centred = values - average
    variance = jnp.mean(centred * centred, axis=-1, keepdims=True)
    scale = lax.rsqrt(variance + eps_norm)
    return centred * scale, scale


def norm_back(normal, scale, gain, upstream):
    inner = upstream * gain
    mean_inner = jnp.mean(inner, axis=-1, keepdims=True)
    mean_cross = jnp.mean(inner * normal, axis=-1, keepdims=True)
    result = scale * (inner - mean_inner - normal * mean_cross)
    gain_sum = jnp.sum(upstream * normal, axis=0, keepdims=True)
    shift_sum = jnp.sum(upstream, axis=0, keepdims=True)
    return result, gain_sum, shift_sum


def one_hot(condition):
    return jnp.where(condition, 1.0, 0.0).astype(LOW)


def remote(src, dst, sends, recvs, index, axis, other):
    return pltpu.make_async_remote_copy(
        src_ref=src, dst_ref=dst, send_sem=sends.at[index], recv_sem=recvs.at[index],
        device_id={axis: other}, device_id_type=MESH,
    )


def greet(*others):
    barrier = pltpu.get_barrier_semaphore()
    for axis, other in others:
        pl.semaphore_signal(barrier, inc=1, device_id={axis: other}, device_id_type=MESH)
    pl.semaphore_wait(barrier, len(others))


def partners():
    me = lax.axis_index("head")
    near = me + 1 - 2 * lax.rem(me, 2)
    far = lax.rem(me + 2, 4)
    corner = lax.rem(near + 2, 4)
    return me, near, far, corner


class LineGather:
    def __init__(self, held, up_send, up_recv, down_send, down_recv, pair_send, pair_recv):
        self.held = held
        self.length = held.shape[0] // 2
        self.sems = ((up_send, up_recv), (down_send, down_recv), (pair_send, pair_recv))
        me = lax.axis_index("dp")
        self.place, self.side = me // 2, lax.rem(me, 2)
        self.above = lax.rem(self.place + 1, self.length) * 2 + self.side
        self.below = lax.rem(self.place + self.length - 1, self.length) * 2 + self.side
        self.other = self.place * 2 + 1 - self.side

    def neighbours(self):
        return ("dp", self.above), ("dp", self.below), ("dp", self.other)

    def copy(self, way, origin, side=None):
        index = origin * 2 + (self.side if side is None else side)
        target = (self.above, self.below, self.other)[way]
        block = self.held.at[index]
        return remote(block, block, *self.sems[way], origin, "dp", target)

    def pass_on(self, origin, up, down):
        @pl.when(up & (self.place < self.length - 1))
        def _():
            self.copy(0, origin).start()

        @pl.when(down & (self.place > 0))
        def _():
            self.copy(1, origin).start()

        self.copy(2, origin).start()

    def start(self):
        self.pass_on(self.place, True, True)

    def step(self, k):
        low, high = self.place - k, self.place + k

        @pl.when(low >= 0)
        def _():
            self.copy(0, low).wait_recv()
            self.pass_on(low, True, False)

        @pl.when(high < self.length)
        def _():
            self.copy(1, high).wait_recv()
            self.pass_on(high, False, True)

    def finish(self):
        @pl.loop(0, self.length)
        def _(origin):
            self.copy(2, origin).wait_recv()
            self.copy(2, origin).wait_send()

            @pl.when((origin <= self.place) & (self.place < self.length - 1))
            def _():
                self.copy(0, origin).wait_send()

            @pl.when((origin >= self.place) & (self.place > 0))
            def _():
                self.copy(1, origin).wait_send()


class ImageSum:
    def __init__(self, stage, corner_in, near_in, passed, mine, far_in, sends, recvs):
        self.stage, self.corner_in, self.near_in = stage, corner_in, near_in
        self.passed, self.mine, self.far_in = passed, mine, far_in
        self.sends, self.recvs = sends, recvs
        self.me, self.near, self.far, self.corner = partners()
        self.core = lax.rem(self.me, 2)

    def image(self, turn):
        base = self.me - self.core
        other = lax.rem(base + 2, 4)
        return jnp.where(turn < 2, other, base - 2) + turn

    def to_corner(self):
        return remote(
            self.stage.at[0], self.corner_in, self.sends, self.recvs, 0, "head", self.near
        )

    def to_near(self):
        return remote(
            self.stage.at[1], self.near_in, self.sends, self.recvs, 1, "head", self.near
        )

    def to_far(self, half):
        rows = self.passed.shape[0] // 2
        span = pl.ds(half * rows, rows)
        return remote(
            self.passed.at[span], self.far_in.at[span], self.sends, self.recvs, 2 + half, "head",
            self.far,
        )

    def give(self, turn, part, hold=False):
        theirs = lax.rem(turn, 2) != self.core

        @pl.when((turn < 2) & theirs)
        def _():
            self.stage[0] = part.astype(LOW)
            self.to_corner().start()

        @pl.when((turn >= 2) & theirs)
        def _():
            self.stage[1] = part.astype(LOW)
            self.to_near().start()

        @pl.when((turn < 2) & ~theirs)
        def _():
            self.to_corner().wait_recv()
            self.passed[...] = (part + self.corner_in[...].astype(FULL)).astype(LOW)
            self.to_far(0).start()
            if not hold:
                self.to_far(1).start()

        @pl.when((turn >= 2) & ~theirs)
        def _():
            self.mine[...] = part

    def start_rest(self):
        self.to_far(1).start()

    def result(self):
        self.to_near().wait_recv()
        for half in range(2):
            self.to_far(half).wait_recv()
        return self.mine[...] + self.near_in[...].astype(FULL) + self.far_in[...].astype(FULL)

    def finish(self):
        self.to_corner().wait_send()
        self.to_near().wait_send()
        for half in range(2):
            self.to_far(half).wait_send()


def image_sum_scratch(rows, width):
    block = pltpu.VMEM((rows, width), LOW)
    return [
        pltpu.VMEM((2, rows, width), LOW), block, block, block,
        pltpu.VMEM((rows, width), FULL), block,
        pltpu.SemaphoreType.DMA((4,)), pltpu.SemaphoreType.DMA((4,)),
    ]


class LineScatter:
    def __init__(
        self, blocks, out, pair_in, up_in, down_in, total,
        up_send, up_recv, down_send, down_recv, pair_send, pair_recv,
    ):
        self.blocks, self.out, self.total = blocks, out, total
        self.arrived = (up_in, down_in, pair_in)
        self.sems = ((up_send, up_recv), (down_send, down_recv), (pair_send, pair_recv))
        self.length = blocks.shape[0] // 2
        me = lax.axis_index("dp")
        self.place, self.side = me // 2, lax.rem(me, 2)
        self.targets = (
            lax.rem(self.place + 1, self.length) * 2 + self.side,
            lax.rem(self.place + self.length - 1, self.length) * 2 + self.side,
            self.place * 2 + 1 - self.side,
        )

    def copy(self, way, block):
        source = (
            self.blocks.at[block * 2 + 1 - self.side] if way == 2 else self.total.at[block]
        )
        return remote(
            source, self.arrived[way].at[block], *self.sems[way], block, "dp", self.targets[way]
        )

    def start(self):
        @pl.loop(0, self.length)
        def _(turn):
            distance = self.length - 1 - turn

            @pl.when(self.place + distance < self.length)
            def _():
                self.copy(2, self.place + distance).start()

            @pl.when((self.place >= distance) & (distance > 0))
            def _():
                self.copy(2, self.place - distance).start()

    def pair_sum(self, block):
        self.copy(2, block).wait_recv()
        own = self.blocks[block * 2 + self.side].astype(FULL)
        return own + self.arrived[2][block].astype(FULL)

    def forward(self, way, block, first):
        both = self.pair_sum(block)

        @pl.when(first)
        def _():
            self.total[block] = both.astype(LOW)

        @pl.when(~first)
        def _():
            self.copy(way, block).wait_recv()
            self.total[block] = (both + self.arrived[way][block].astype(FULL)).astype(LOW)

        self.copy(way, block).start()

    def step(self, distance):
        @pl.when(self.place + distance < self.length)
        def _():
            self.forward(0, self.place + distance, self.place == 0)

        @pl.when(self.place >= distance)
        def _():
            self.forward(1, self.place - distance, self.place == self.length - 1)

    def result(self):
        self.out[...] = self.pair_sum(self.place)

        @pl.when(self.place > 0)
        def _():
            self.copy(0, self.place).wait_recv()
            self.out[...] += self.arrived[0][self.place].astype(FULL)

        @pl.when(self.place < self.length - 1)
        def _():
            self.copy(1, self.place).wait_recv()
            self.out[...] += self.arrived[1][self.place].astype(FULL)

    def finish(self):
        @pl.loop(0, self.length)
        def _(block):
            self.copy(2, block).wait_send()

            @pl.when(block > self.place)
            def _():
                self.copy(0, block).wait_send()

            @pl.when(block < self.place)
            def _():
                self.copy(1, block).wait_send()


def line_scatter_scratch(dp_count, rows, width):
    line = dp_count // 2
    return [pltpu.VMEM((line, rows, width), LOW)] * 4 + [pltpu.SemaphoreType.DMA((line,))] * 6


class SmallSum:
    def __init__(self, flat, head_in, dp_in, done, head_send, head_recv, dp_send, dp_recv):
        self.flat, self.head_in, self.dp_in, self.done = flat, head_in, dp_in, done
        self.head_sems, self.dp_sems = (head_send, head_recv), (dp_send, dp_recv)
        self.me, *self.others = partners()
        self.place, self.count = lax.axis_index("dp"), dp_in.shape[0]

    def to_head(self, lane):
        other = self.others[lane]
        return remote(
            self.flat.at[other], self.head_in.at[self.me], *self.head_sems, lane, "head", other
        )

    def back_head(self, lane):
        block = self.done.at[self.me]
        return remote(block, block, *self.head_sems, 3 + lane, "head", self.others[lane])

    def to_dp(self, shift):
        block = self.dp_in.at[self.place]
        other = lax.rem(self.place + shift, self.count)
        return remote(block, block, *self.dp_sems, shift, "dp", other)

    def start(self, value):
        groups, rows, lanes = self.flat.shape
        flat = jnp.concatenate(
            [value[:, at:at + lanes] for at in range(0, value.shape[1], lanes)], axis=0
        )
        for group in range(groups):
            self.flat[group] = flat[group * rows:(group + 1) * rows]
        for lane in range(3):
            self.to_head(lane).start()
        self.head_in[self.me] = self.flat[self.me]

    def across(self):
        for lane in range(3):
            self.to_head(lane).wait_recv()
        total = self.head_in[0]
        for head in range(1, self.head_in.shape[0]):
            total = total + self.head_in[head]
        self.dp_in[self.place] = total

        @pl.loop(1, self.count)
        def _(shift):
            self.to_dp(shift).start()

    def back(self):
        @pl.loop(1, self.count)
        def _(shift):
            self.to_dp(shift).wait_recv()

        total = lax.fori_loop(
            1, self.count, lambda at, so_far: so_far + self.dp_in[at], self.dp_in[0]
        )
        self.done[self.me] = total
        for lane in range(3):
            self.back_head(lane).start()

    def result(self, out):
        for lane in range(3):
            self.back_head(lane).wait_recv()
        flat = jnp.concatenate([self.done[group] for group in range(self.done.shape[0])], axis=0)
        rows, width = out.shape
        lanes = flat.shape[1]
        for at in range(width // lanes):
            out[:, at * lanes:(at + 1) * lanes] = flat[at * rows:(at + 1) * rows]

    def finish(self):
        for lane in range(3):
            self.to_head(lane).wait_send()
            self.back_head(lane).wait_send()

        @pl.loop(1, self.count)
        def _(shift):
            self.to_dp(shift).wait_send()


def small_sum_scratch(rows, width, dp_count):
    block = (rows * width // 128 // 4, 128)
    return [
        pltpu.VMEM((4,) + block, FULL), pltpu.VMEM((4,) + block, FULL),
        pltpu.VMEM((dp_count,) + block, FULL), pltpu.VMEM((4,) + block, FULL),
        pltpu.SemaphoreType.DMA((6,)), pltpu.SemaphoreType.DMA((6,)),
        pltpu.SemaphoreType.DMA((dp_count,)), pltpu.SemaphoreType.DMA((dp_count,)),
    ]


class LateSum:
    def __init__(self, dp_in, head_in, dp_send, dp_recv, head_send, head_recv):
        self.dp_in, self.head_in = dp_in, head_in
        self.dp_sems, self.head_sems = (dp_send, dp_recv), (head_send, head_recv)
        self.me, *self.others = partners()
        self.place, self.count = lax.axis_index("dp"), dp_in.shape[0]

    def to_dp(self, shift):
        block = self.dp_in.at[self.place]
        other = lax.rem(self.place + shift, self.count)
        return remote(block, block, *self.dp_sems, shift, "dp", other)

    def to_head(self, lane):
        block = self.head_in.at[self.me]
        return remote(block, block, *self.head_sems, lane, "head", self.others[lane])

    def start(self, rows):
        lanes = self.dp_in.shape[2]
        cuts = [
            row[:, at:at + lanes] for row in rows for at in range(0, row.shape[1], lanes)
        ]
        cuts += [jnp.zeros_like(cuts[0])] * (self.dp_in.shape[1] - len(cuts))
        self.dp_in[self.place] = jnp.concatenate(cuts, axis=0)

        @pl.loop(1, self.count)
        def _(shift):
            self.to_dp(shift).start()

    def across(self):
        @pl.loop(1, self.count)
        def _(shift):
            self.to_dp(shift).wait_recv()

        self.head_in[self.me] = lax.fori_loop(
            1, self.count, lambda at, so_far: so_far + self.dp_in[at], self.dp_in[0]
        )
        for lane in range(3):
            self.to_head(lane).start()

    def result(self, out, first):
        for lane in range(3):
            self.to_head(lane).wait_recv()
        total = self.head_in[0]
        for head in range(1, self.head_in.shape[0]):
            total = total + self.head_in[head]
        lanes = total.shape[1]
        cuts = out.shape[1] // lanes
        for row in range(2):
            for at in range(cuts):
                piece = total[row * cuts + at:row * cuts + at + 1]
                out[first + row:first + row + 1, at * lanes:(at + 1) * lanes] = piece

    def finish(self):
        for lane in range(3):
            self.to_head(lane).wait_send()

        @pl.loop(1, self.count)
        def _(shift):
            self.to_dp(shift).wait_send()


def late_sum_scratch(width, dp_count):
    block = (-(-2 * width // 128 // 8) * 8, 128)
    return [
        pltpu.VMEM((dp_count,) + block, FULL), pltpu.VMEM((4,) + block, FULL),
        pltpu.SemaphoreType.DMA((dp_count,)), pltpu.SemaphoreType.DMA((dp_count,)),
        pltpu.SemaphoreType.DMA((3,)), pltpu.SemaphoreType.DMA((3,)),
    ]


GATHER_CUTS = 4
COLUMN_CUTS = 3


class ImageGather:
    def __init__(self, held, sends, recvs, own=None, local_sem=None, columns=False):
        self.held, self.sends, self.recvs, self.columns = held, sends, recvs, columns
        self.me, self.near, self.far, self.corner = partners()
        self.own = held.at[self.me] if own is None else own
        self.local = None if own is None else pltpu.make_async_copy(own, held.at[self.me], local_sem)
        self.size = held.shape[1] // GATHER_CUTS
        self.wide = held.shape[2] // COLUMN_CUTS

    def piece(self, lane, cut):
        span = pl.ds(cut * self.size, self.size)
        image = self.far if lane == 2 else self.me
        if self.columns:
            block = self.held.at[image, :, pl.ds(cut * self.wide, self.wide)]
        else:
            block = self.held.at[image, span]
        source = block if self.columns or lane == 2 else self.own.at[span]
        other = self.far if lane == 0 else self.near
        index = lane * GATHER_CUTS + cut
        return remote(source, block, self.sends, self.recvs, index, "head", other)

    def start_far(self, first=0, last=GATHER_CUTS):
        for cut in range(first, last):
            self.piece(0, cut).start()

    def start_near(self, last=GATHER_CUTS):
        for cut in range(last):
            self.piece(1, cut).start()
        if self.local is not None:
            self.local.start()

    def start(self):
        self.start_far()
        self.start_near()

    def wait_near(self, first=0, last=GATHER_CUTS):
        for cut in range(first, last):
            self.piece(1, cut).wait_recv()

    def wait_far(self, first=0, last=GATHER_CUTS):
        for cut in range(first, last):
            self.piece(0, cut).wait_recv()
            self.piece(2, cut).start()

    def wait_corner(self, first=0, last=GATHER_CUTS):
        for cut in range(first, last):
            self.piece(2, cut).wait_recv()

    def finish(self, last=GATHER_CUTS):
        for cut in range(last):
            for lane in range(3):
                self.piece(lane, cut).wait_send()
        if self.local is not None:
            self.local.wait()


def image_gather_sems():
    return [pltpu.SemaphoreType.DMA((3 * GATHER_CUTS,)), pltpu.SemaphoreType.DMA((3 * GATHER_CUTS,))]


class BlockSum:
    def __init__(self, parts, mine, passed, corner_in, near_in, far_in, local_sems, sends, recvs):
        self.mine, self.passed, self.corner_in = mine, passed, corner_in
        self.near_in, self.far_in = near_in, far_in
        me, near, far, corner = partners()
        self.half = far_in.shape[0]
        self.to_corner = remote(parts.at[corner], corner_in, sends, recvs, 0, "head", near)
        self.to_near = remote(parts.at[near], near_in, sends, recvs, 1, "head", near)
        second = passed.at[pl.ds(self.half, self.half)]
        self.to_far = remote(second, far_in, sends, recvs, 2, "head", far)
        self.load_far = pltpu.make_async_copy(parts.at[far], passed, local_sems.at[0])
        self.load_mine = pltpu.make_async_copy(parts.at[me], mine, local_sems.at[1])

    def start(self):
        for copy in (self.to_corner, self.load_far, self.to_near, self.load_mine):
            copy.start()

    def across(self):
        self.load_far.wait()
        self.to_corner.wait_recv()
        both = self.passed[...].astype(FULL) + self.corner_in[...].astype(FULL)
        self.passed[...] = both.astype(LOW)
        self.to_far.start()

    def result(self, first_out, second_out):
        self.load_mine.wait()
        self.to_near.wait_recv()
        self.to_far.wait_recv()
        total = self.mine[...].astype(FULL) + self.near_in[...].astype(FULL)
        first_out[...] = total[:self.half]
        second_out[...] = total[self.half:] + self.far_in[...].astype(FULL)

    def finish(self):
        for copy in (self.to_corner, self.to_near, self.to_far):
            copy.wait_send()


def block_sum_scratch(rows, width):
    return [pltpu.VMEM((rows, width), LOW)] * 4 + [
        pltpu.VMEM((rows // 2, width), LOW),
        pltpu.SemaphoreType.DMA((2,)), pltpu.SemaphoreType.DMA((3,)), pltpu.SemaphoreType.DMA((3,)),
    ]


class Slots:
    def __init__(self, count, share):
        self.count, self.share = count, share
        self.big = -(-share // 16) * 16
        rest = 2 * share - self.big
        self.small = rest if rest > 0 and rest % 16 == 0 else self.big
        self.more = self.big - self.small
        self.both = self.big + self.small
        self.rows = count // 2 * self.both
        self.turns = count // 4
        self.phase_rows = self.turns * 2 * self.both

    def size(self, source, head):
        return self.small + self.more * ((head + source + 1) % 2)

    def packed(self, source, head):
        return (source // 2) * self.both + (source % 2) * self.size(0, head)

    def row(self, source, head, shift):
        first = self.size(source, 0) * (head % 2)
        group = (head // 2) * self.turns * self.both + self.turns * first
        return (
            (shift // self.turns) * self.phase_rows + group
            + (shift % self.turns) * self.size(source, head)
        )

    def holder(self, source, slot):
        pair, within = slot // self.both, slot % self.both
        first = self.size(source, 0)
        second = jnp.where(within >= first, 1, 0)
        return 2 * pair + second, within - second * first

    def span(self, start, extra):
        if extra:
            return pl.ds(pl.multiple_of(start + self.small, 16), self.more)
        return pl.ds(pl.multiple_of(start, 16), self.small)

    def each(self, is_big, make, action):
        getattr(make(False), action)()
        if self.more:
            @pl.when(is_big)
            def _():
                getattr(make(True), action)()


class SlotExchange:
    def __init__(self, slots, sent, rows, sends, recvs, local_sems, cut=None):
        self.slots, self.sent, self.rows = slots, sent, rows
        self.sems, self.local_sems = (sends, recvs), local_sems
        self.place, self.head = lax.axis_index("dp"), lax.axis_index("head")
        wide = sent.shape[1] // COLUMN_CUTS
        self.cut = 0 if cut is None else cut
        self.lanes = pl.ds(0, sent.shape[1]) if cut is None else pl.ds(cut * wide, wide)

    def index(self, shift, extra):
        return 2 * (self.cut * self.slots.count + shift) + int(extra)

    def out(self, shift, action):
        slots = self.slots
        expert = lax.rem(self.place + shift, slots.count)
        mine = slots.size(self.place, self.head)
        at, to = expert * mine, slots.packed(self.place, self.head)
        slots.each(mine > slots.small, lambda extra: remote(
            self.sent.at[slots.span(at, extra), self.lanes], self.rows.at[slots.span(to, extra), self.lanes],
            *self.sems, self.index(shift, extra), "dp", expert,
        ), action)

    def into(self, shift):
        slots = self.slots
        source = lax.rem(self.place + slots.count - shift, slots.count)
        size = slots.size(source, self.head)
        to = slots.packed(source, self.head)
        slots.each(size > slots.small, lambda extra: remote(
            self.sent.at[slots.span(0, extra), self.lanes], self.rows.at[slots.span(to, extra), self.lanes],
            *self.sems, self.index(shift, extra), "dp", source,
        ), "wait_recv")

    def own(self, action):
        slots = self.slots
        mine = slots.size(self.place, self.head)
        at, to = self.place * mine, slots.packed(self.place, self.head)
        slots.each(mine > slots.small, lambda extra: pltpu.make_async_copy(
            self.sent.at[slots.span(at, extra), self.lanes], self.rows.at[slots.span(to, extra), self.lanes],
            self.local_sems.at[2 * self.cut + int(extra)],
        ), action)

    def start(self):
        @pl.loop(1, self.slots.count)
        def _(shift):
            self.out(shift, "start")

        self.own("start")

    def finish(self):
        @pl.loop(1, self.slots.count)
        def _(shift):
            self.into(shift)
            self.out(shift, "wait_send")

        self.own("wait")


class SlotReturn:
    def __init__(self, slots, rows, back, zeros, sends, recvs, local_sems):
        self.slots, self.rows, self.back, self.zeros = slots, rows, back, zeros
        self.sems, self.local_sems = (sends, recvs), local_sems
        self.place, self.head = lax.axis_index("dp"), lax.axis_index("head")
        self.mine = slots.size(self.place, self.head)

    def out(self, shift, action):
        slots = self.slots
        source = lax.rem(self.place + shift, slots.count)
        size = slots.size(source, self.head)
        at, to = slots.packed(source, self.head), shift * size
        slots.each(size > slots.small, lambda extra: remote(
            self.rows.at[slots.span(at, extra)], self.back.at[slots.span(to, extra)],
            *self.sems, 2 * shift + int(extra), "dp", source,
        ), action)

    def into(self, shift):
        slots = self.slots
        expert = lax.rem(self.place + slots.count - shift, slots.count)
        slots.each(self.mine > slots.small, lambda extra: remote(
            self.rows.at[slots.span(0, extra)], self.back.at[slots.span(shift * self.mine, extra)],
            *self.sems, 2 * shift + int(extra), "dp", expert,
        ), "wait_recv")

    def own(self, action):
        slots = self.slots
        at = slots.packed(self.place, self.head)
        slots.each(self.mine > slots.small, lambda extra: pltpu.make_async_copy(
            self.rows.at[slots.span(at, extra)], self.back.at[slots.span(0, extra)],
            self.local_sems.at[int(extra)],
        ), action)

    def blank(self, action):
        slots = self.slots
        if slots.more:
            @pl.when(self.mine == slots.small)
            def _():
                tail = self.back.at[pl.ds(slots.count * slots.small, slots.count * slots.more)]
                copy = pltpu.make_async_copy(self.zeros, tail, self.local_sems.at[2])
                getattr(copy, action)()

    def start(self):
        if self.slots.more:
            self.zeros[...] = jnp.zeros_like(self.zeros)
        self.blank("start")

        @pl.loop(1, self.slots.count)
        def _(shift):
            self.out(shift, "start")

        self.own("start")

    def finish(self):
        @pl.loop(1, self.slots.count)
        def _(shift):
            self.into(shift)
            self.out(shift, "wait_send")

        self.own("wait")
        self.blank("wait")


def slot_return_scratch(slots, width):
    return [pltpu.VMEM((max(slots.count * slots.more, 16), width), LOW)] + [
        pltpu.SemaphoreType.DMA((2 * slots.count,)), pltpu.SemaphoreType.DMA((2 * slots.count,)),
        pltpu.SemaphoreType.DMA((3,)),
    ]


def slot_exchange_sems(count, cuts=1):
    return [
        pltpu.SemaphoreType.DMA((2 * count * cuts,)), pltpu.SemaphoreType.DMA((2 * count * cuts,)),
        pltpu.SemaphoreType.DMA((2 * cuts,)),
    ]


class ReturnGather:
    def __init__(self, slots, rows, held, sends, recvs, local_sems):
        self.slots, self.rows, self.held = slots, rows, held
        self.sems, self.local_sems = (sends, recvs), local_sems
        self.place = lax.axis_index("dp")
        self.me, self.near, self.far, self.corner = partners()

    def out(self, shift, action):
        slots = self.slots
        source = lax.rem(self.place + shift, slots.count)
        size = slots.size(source, self.me)
        at, to = slots.packed(source, self.me), slots.row(source, self.me, shift)
        slots.each(size > slots.small, lambda extra: remote(
            self.rows.at[slots.span(at, extra)], self.held.at[slots.span(to, extra)],
            *self.sems, 2 * shift + int(extra), "dp", source,
        ), action)

    def own(self, action):
        slots = self.slots
        size = slots.size(self.place, self.me)
        at, to = slots.packed(self.place, self.me), slots.row(self.place, self.me, 0)
        slots.each(size > slots.small, lambda extra: pltpu.make_async_copy(
            self.rows.at[slots.span(at, extra)], self.held.at[slots.span(to, extra)],
            self.local_sems.at[int(extra)],
        ), action)

    def block(self, lane, head, shift, axis, other, action):
        slots = self.slots
        size = slots.size(self.place, head)
        to = slots.row(self.place, head, shift)

        def make(extra):
            block = self.held.at[slots.span(to, extra)]
            index = 2 * (lane * slots.count + shift) + int(extra)
            return remote(block, block, *self.sems, index, axis, other)

        slots.each(size > slots.small, make, action)

    def send(self, phase):
        turns = self.slots.turns
        if phase == 0:
            self.own("start")

        @pl.loop(max(phase * turns, 1), (phase + 1) * turns)
        def _(shift):
            self.out(shift, "start")

    def relay(self, shift):
        @pl.when(shift == 0)
        def _():
            self.own("wait")

        @pl.when(shift > 0)
        def _():
            expert = lax.rem(self.place + self.slots.count - shift, self.slots.count)
            self.block(0, self.me, shift, "dp", expert, "wait_recv")

        self.block(1, self.me, shift, "head", self.far, "start")
        self.block(2, self.me, shift, "head", self.near, "start")

    def forward(self, shift):
        self.block(1, self.far, shift, "head", self.far, "wait_recv")
        self.block(3, self.far, shift, "head", self.near, "start")

    def rest(self, shift):
        self.block(2, self.near, shift, "head", self.near, "wait_recv")
        self.block(3, self.corner, shift, "head", self.near, "wait_recv")

    def of_phase(self, phase, action):
        @pl.loop(0, self.slots.turns)
        def _(turn):
            action(phase * self.slots.turns + turn)

    def finish(self):
        @pl.loop(0, self.slots.count)
        def _(shift):
            @pl.when(shift > 0)
            def _():
                self.out(shift, "wait_send")

            self.block(1, self.me, shift, "head", self.far, "wait_send")
            self.block(2, self.me, shift, "head", self.near, "wait_send")
            self.block(3, self.far, shift, "head", self.near, "wait_send")


def return_gather_sems(count):
    return [
        pltpu.SemaphoreType.DMA((8 * count,)), pltpu.SemaphoreType.DMA((8 * count,)),
        pltpu.SemaphoreType.DMA((2,)),
    ]


def greet_all(heads, dp_count):
    barrier = pltpu.get_barrier_semaphore()
    place = lax.axis_index("dp")
    for other in heads:
        pl.semaphore_signal(barrier, inc=1, device_id={"head": other}, device_id_type=MESH)

    @pl.loop(1, dp_count)
    def _(shift):
        other = lax.rem(place + shift, dp_count)
        pl.semaphore_signal(barrier, inc=1, device_id={"dp": other}, device_id_type=MESH)

    pl.semaphore_wait(barrier, len(heads) + dp_count - 1)


ANYWHERE = pl.BlockSpec(memory_space=pl.ANY)
INSIDE = pl.BlockSpec(memory_space=pltpu.VMEM)


def digits(values):
    high = lax.div(values, 64)
    return [high.astype(FULL), (values - high * 64).astype(FULL)]


def digit_weights(shape, digit_axis):
    digit = lax.broadcasted_iota(jnp.int32, shape, digit_axis)
    value = lax.broadcasted_iota(jnp.int32, shape, 1 - digit_axis)
    weight = jnp.where(lax.rem(digit, 2) == 0, 64.0, 1.0)
    return jnp.where(lax.div(digit, 2) == value, weight, 0.0).astype(LOW)


def turned_rows(rows):
    count = rows[0].shape[1]
    parts = [part for row in rows for part in digits(row)]
    parts += [jnp.zeros((1, count), FULL)] * (8 - len(parts))
    spread = jnp.concatenate(parts, axis=0).astype(LOW)
    return tn(spread, digit_weights((8, 128), 0)).astype(jnp.int32)


def turned_column(column):
    lanes = lax.broadcasted_iota(jnp.int32, (column.shape[0], 128), 1)
    high, low = digits(column)
    spread = jnp.where(lanes == 0, high, jnp.where(lanes == 1, low, 0.0)).astype(LOW)
    return nt(digit_weights((8, 128), 1), spread)[0:1].astype(jnp.int32)


def prepare_kernel(
    slots, slot_count, capacity,
    tile_ref, norm_ref, owner_ref, ids_ref, pos_ref, up_ref, x_in, g_in,
    w_ref, src_ref, col_ref, col_back_ref, xn_out, hat_out, sent_out, up_out,
    x_ref, g_ref, xn_ref, hat_ref, up_full, up_low, held, sent_sum, sent_ref,
    load_sems, save_sems, *sems,
):
    images = x_ref.shape[0]
    gather = LineGather(held, *sems[:6])
    spread = ImageGather(up_out, *sems[6:8], own=up_low, local_sem=sems[8])
    load_up = pltpu.make_async_copy(up_ref, up_full, load_sems.at[2, 0])
    load_up.start()

    def load(image):
        return (
            pltpu.make_async_copy(x_in.at[image], x_ref.at[image], load_sems.at[0, image]),
            pltpu.make_async_copy(g_in.at[image], g_ref.at[image], load_sems.at[1, image]),
        )

    def save(image):
        return (
            pltpu.make_async_copy(xn_ref.at[image], xn_out.at[image], save_sems.at[0, image]),
            pltpu.make_async_copy(hat_ref.at[image], hat_out.at[image], save_sems.at[1, image]),
        )

    for image in range(images):
        for copy in load(image):
            copy.start()
    me, head = lax.axis_index("dp"), lax.axis_index("head")
    held[me] = tile_ref[...].astype(LOW)
    greet(*gather.neighbours(), ("head", spread.near), ("head", spread.far))
    gather.start()
    load_up.wait()
    up_low[...] = up_full[...].astype(LOW)
    spread.start()
    shape = (sent_ref.shape[0], PATCH)
    sent_sum[...] = jnp.zeros_like(sent_sum)
    steps = gather.length - 1

    def image_step(image):
        for copy in load(image):
            copy.wait()
        normal, _ = normalise(x_ref[image].astype(FULL))
        hat_ref[image] = normal.astype(LOW)
        xn_ref[image] = (normal * norm_ref[0:1, :] + norm_ref[1:2, :]).astype(LOW)
        for copy in save(image):
            copy.start()

        ids, pos = ids_ref[image], pos_ref[image]
        kept = pos < capacity
        holder, within = slots.holder(me, jnp.minimum(pos, capacity - 1))
        sent_at = ids * slots.size(me, head) + within
        sent_at = jnp.where(kept & (holder == head), sent_at, slots.count * slots.big)
        shift = me - ids
        shift = jnp.where(shift < 0, shift + slots.count, shift)
        back_at = jnp.where(kept, slots.row(me, holder, shift) + within + 1, 0)
        other_pair = jnp.where(lax.div(holder, 2) == lax.div(head, 2), 0, 2)
        apart = other_pair + jnp.where(lax.rem(holder, 2) == lax.rem(head, 2), 0, 1)
        out_at = apart * (slots.count * slots.big) + shift * slots.size(me, holder) + within
        out_at = jnp.where(kept, out_at + 1, 0)
        turned = turned_rows([back_at[0:1], back_at[1:2], out_at[0:1], out_at[1:2]])
        col_back_ref[image] = turned[:, 0:4] - 1
        col_ref[image] = sent_at
        first, second = sent_at[0:1], sent_at[1:2]
        sent_slots = lax.broadcasted_iota(jnp.int32, shape, 0)
        pick = one_hot((sent_slots == first) | (sent_slots == second))
        sent_sum[...] += nn(pick, g_ref[image])

    @pl.loop(0, max(steps, (images + 1) // 2))
    def _(turn):
        @pl.loop(2 * turn, jnp.minimum(2 * turn + 2, images))
        def _(image):
            image_step(image)

        @pl.when(turn < steps)
        def _():
            gather.step(turn + 1)

        @pl.when(turn == 1)
        def _():
            spread.wait_far(0, 1)

    sent_ref[...] = sent_sum[...].astype(LOW)
    save_sent = pltpu.make_async_copy(sent_ref, sent_out, load_sems.at[2, 1])
    save_sent.start()

    rows = w_ref.shape[0]
    tiles = owner_ref.shape[1]
    row_tile = lax.div(lax.broadcasted_iota(jnp.int32, (rows, tiles), 0), TILE)
    lane_tile = lax.broadcasted_iota(jnp.int32, (rows, tiles), 1)
    owner_rows = jnp.broadcast_to(owner_ref[...].astype(FULL), (8, tiles)).astype(LOW)
    owner = nt(one_hot(lane_tile == row_tile), owner_rows)[:, 0:1].astype(jnp.int32)
    before = (owner_ref[...] == owner) & (lane_tile < row_tile)
    rank = jnp.sum(jnp.where(before, 1.0, 0.0), axis=1, keepdims=True).astype(jnp.int32)
    within = lax.rem(lax.broadcasted_iota(jnp.int32, (rows, 1), 0), TILE)
    src = (owner * slot_count + rank) * TILE + within
    src_ref[...] = turned_column(src)
    spread.wait_far(1, 3)
    gather.finish()
    blocks, depth, width = held.shape
    cut = rows // 4
    for part in range(4):
        lanes = lax.broadcasted_iota(jnp.int32, (cut, blocks * depth), 1)
        pick = one_hot(lanes == src[part * cut:(part + 1) * cut])
        block = nn(pick, held[...].reshape(blocks * depth, width))
        w_ref[pl.ds(part * cut, cut), :] = block.astype(LOW)
    spread.wait_far(3)
    spread.wait_near()
    spread.wait_corner()
    spread.finish()
    save_sent.wait()

    @pl.loop(0, images)
    def _(image):
        for copy in save(image):
            copy.wait()


def prepare(slots, tiles, patches, cotangent, norm_params, owners, ids, pos, up, weight_rows):
    images, _, width = patches.shape
    slot_count = tiles.shape[0] // TILE
    line = slots.count // 2
    most = slots.count * slots.big
    capacity = images * PATCH // slots.count
    wide = jax.ShapeDtypeStruct(patches.shape, LOW)
    return pl.pallas_call(
        functools.partial(prepare_kernel, slots, slot_count, capacity),
        in_specs=[INSIDE] * 5 + [ANYWHERE] * 3,
        out_specs=[INSIDE] * 4 + [ANYWHERE] * 4,
        out_shape=[
            jax.ShapeDtypeStruct((weight_rows, width), LOW),
            jax.ShapeDtypeStruct((1, weight_rows), jnp.int32),
            jax.ShapeDtypeStruct((images, 2, PATCH), jnp.int32),
            jax.ShapeDtypeStruct((images, PATCH, 4), jnp.int32), wide, wide,
            jax.ShapeDtypeStruct((most, width), LOW), jax.ShapeDtypeStruct((4,) + up.shape, LOW),
        ],
        scratch_shapes=[pltpu.VMEM(patches.shape, LOW)] * 4
        + [
            pltpu.VMEM(up.shape, FULL), pltpu.VMEM(up.shape, LOW),
            pltpu.VMEM((slots.count,) + tiles.shape, LOW), pltpu.VMEM((most, width), FULL),
            pltpu.VMEM((most, width), LOW),
            pltpu.SemaphoreType.DMA((3, images)), pltpu.SemaphoreType.DMA((2, images)),
        ]
        + [pltpu.SemaphoreType.DMA((line,))] * 6 + image_gather_sems() + [pltpu.SemaphoreType.DMA],
        compiler_params=params(collective_id=0, has_side_effects=True),
        name="prepare",
    )(tiles, norm_params, owners, ids, pos, up, patches, cotangent)


def head_mask(shape, axis, head):
    return lax.broadcasted_iota(jnp.int32, shape, axis) // HD == head


def forward_kernel(
    slots,
    w_ref, norm_ref, col_ref, xn_in, x_ref, g_sent_ref, down_ref,
    lse_ref, q_out, qt_out, k_out, kt_out, v_out, ot_out, x1_out, rows_out, g_rows_out, down_out,
    q_ref, qt_ref, k_ref, kt_ref, v_ref, ot_ref, x1_ref, xn_ref, own_ref, sent_ref,
    down_full, down_low, picks, stats, norms, save_sems, own_sem, stat_send, stat_recv, *exchange,
):
    images = xn_ref.shape[0]
    rows = w_ref.shape[0] // 4
    heads = rows // HD
    total_of = ImageSum(*exchange[:8])
    spread = ImageGather(x1_ref, *exchange[8:10], columns=True)
    spread_down = ImageGather(down_out, *exchange[10:12], own=down_low, local_sem=exchange[12])
    send_g = SlotExchange(slots, g_sent_ref, g_rows_out, *exchange[13:16])
    send_rows = [
        SlotExchange(slots, sent_ref, rows_out, *exchange[16:], cut=cut) for cut in range(COLUMN_CUTS)
    ]
    me, near, far, corner = partners()

    def load(turn):
        image = total_of.image(turn)
        return pltpu.make_async_copy(xn_in.at[image], xn_ref.at[image], save_sems.at[6, turn])

    for turn in range(images):
        load(turn).start()
    load_down = pltpu.make_async_copy(down_ref, down_full, own_sem.at[1])
    load_down.start()
    own = pltpu.make_async_copy(x_ref.at[me], own_ref, own_sem.at[0])
    own.start()
    greet_all((near, far, corner), slots.count)
    load_down.wait()
    down_low[...] = down_full[...].astype(LOW)
    spread_down.start_far(0, 1)
    spread_down.start_near()
    send_g.start()
    kept = ((q_ref, q_out), (qt_ref, qt_out), (k_ref, k_out), (kt_ref, kt_out), (v_ref, v_out), (ot_ref, ot_out))
    shrink = HD ** (-0.5)

    def save(image):
        return [
            pltpu.make_async_copy(ref.at[image], out.at[image], save_sems.at[index, image])
            for index, (ref, out) in enumerate(kept)
        ]

    @pl.loop(0, images)
    def _(turn):
        image = total_of.image(turn)
        load(turn).wait()
        xn = xn_ref[image]
        wq, wk, wv, wo = (w_ref[pl.ds(part * rows, rows), :] for part in range(4))
        q_ref[image] = (nt(xn, wq) * shrink).astype(LOW)
        qt = (nt(wq, xn) * shrink).astype(LOW)
        qt_ref[image] = qt
        k = nt(xn, wk).astype(LOW)
        k_ref[image] = k
        kt_ref[image] = nt(wk, xn).astype(LOW)
        v_ref[image] = nt(xn, wv).astype(LOW)
        vt = nt(wv, xn).astype(LOW)
        mixed = []
        for head in range(heads):
            span = slice(head * HD, (head + 1) * HD)
            only = jnp.where(head_mask(qt.shape, 0, head), qt, jnp.zeros_like(qt))
            scores = nn(k, only)
            top = jnp.max(scores, axis=0, keepdims=True)
            weights = jnp.exp(scores - top)
            total = jnp.sum(weights, axis=0, keepdims=True)
            mixed.append(nn(vt[span], weights.astype(LOW)) / total)
            lse_ref[image, head:head + 1, :] = top + jnp.log(total)
        ot = jnp.concatenate(mixed, axis=0).astype(LOW)
        ot_ref[image] = ot
        total_of.give(turn, tn(ot, wo))
        for copy in save(image):
            copy.start()

    own.wait()
    x1 = (own_ref[...].astype(FULL) + total_of.result()).astype(LOW)
    x1_ref[me] = x1
    values = x1.astype(FULL)
    average = jnp.mean(values, axis=-1, keepdims=True)
    centred = values - average
    scale = lax.rsqrt(jnp.mean(centred * centred, axis=-1, keepdims=True) + eps_norm)
    lanes = lax.broadcasted_iota(jnp.int32, (PATCH, 128), 1)
    pair = jnp.where(lanes == 0, average, jnp.where(lanes == 1, scale, 0.0))
    eye = (8, 128)
    eye = lax.broadcasted_iota(jnp.int32, eye, 0) == lax.broadcasted_iota(jnp.int32, eye, 1)
    eye = jnp.where(eye, 1.0, 0.0)
    stats[me] = lax.dot_general(
        eye, pair, (((1,), (1,)), ((), ())), precision=lax.Precision.HIGHEST,
        preferred_element_type=FULL,
    )
    tell = [
        remote(stats.at[me], stats.at[me], stat_send, stat_recv, lane, "head", other)
        for lane, other in enumerate((near, far, corner))
    ]
    for copy in tell:
        copy.start()
    spread.start_far(0, COLUMN_CUTS)
    spread.start_near(COLUMN_CUTS)
    spread_down.start_far(1)

    @pl.loop(0, images)
    def _(image):
        rows_of = lax.broadcasted_iota(jnp.int32, (sent_ref.shape[0], PATCH), 0)
        col = col_ref[image]
        picks[image] = one_hot((rows_of == col[0:1, :]) | (rows_of == col[1:2, :]))

    for copy in tell:
        copy.wait_recv()

    @pl.loop(0, images)
    def _(image):
        norms[image] = lax.dot_general(
            stats[image], eye, (((0,), (0,)), ((), ())), precision=lax.Precision.HIGHEST,
            preferred_element_type=FULL,
        )

    for cut in range(COLUMN_CUTS):
        wide = sent_ref.shape[1] // COLUMN_CUTS
        span = slice(cut * wide, (cut + 1) * wide)

        def place(image, span=span):
            normal = (x1_ref[image, :, span].astype(FULL) - norms[image, :, 0:1]) * norms[image, :, 1:2]
            low = (normal * norm_ref[2:3, span] + norm_ref[3:4, span]).astype(LOW)
            return nn(picks[image], low)

        total = place(me)
        spread.wait_near(cut, cut + 1)
        total = total + place(near)
        spread.wait_far(cut, cut + 1)
        total = total + place(far)
        spread.wait_corner(cut, cut + 1)
        sent_ref[:, span] = (total + place(corner)).astype(LOW)
        send_rows[cut].start()

    keep = pltpu.make_async_copy(x1_ref, x1_out, own_sem.at[0])
    keep.start()
    for copy in tell:
        copy.wait_send()
    spread.finish(COLUMN_CUTS)
    total_of.finish()
    send_g.finish()
    spread_down.wait_far()
    spread_down.wait_near()
    spread_down.wait_corner()
    spread_down.finish()
    for copy in send_rows:
        copy.finish()
    keep.wait()

    @pl.loop(0, images)
    def _(image):
        for copy in save(image):
            copy.wait()


def attention_forward(slots, xn, w, norm_params, col_rows, patches, g_sent, down):
    images, _, width = patches.shape
    rows = w.shape[0] // 4
    flat, turned = (images, PATCH, rows), (images, rows, PATCH)
    saved = [flat, turned, flat, turned, flat, turned, patches.shape]
    outs = saved + [(slots.rows, width), (slots.rows, width), (4,) + down.shape]
    most = slots.count * slots.big
    return pl.pallas_call(
        functools.partial(forward_kernel, slots),
        in_specs=[INSIDE] * 3 + [ANYWHERE] * 4,
        out_specs=[INSIDE] + [ANYWHERE] * 10,
        out_shape=[jax.ShapeDtypeStruct((images, 8, PATCH), FULL)]
        + [jax.ShapeDtypeStruct(shape, LOW) for shape in outs],
        scratch_shapes=[pltpu.VMEM(shape, LOW) for shape in saved]
        + [
            pltpu.VMEM(patches.shape, LOW),
            pltpu.VMEM((PATCH, width), LOW), pltpu.VMEM((most, width), LOW),
            pltpu.VMEM(down.shape, FULL), pltpu.VMEM(down.shape, LOW),
            pltpu.VMEM((images, most, PATCH), LOW), pltpu.VMEM((images, 8, PATCH), FULL),
            pltpu.VMEM((images, PATCH, 128), FULL),
            pltpu.SemaphoreType.DMA((7, images)), pltpu.SemaphoreType.DMA((2,)),
            pltpu.SemaphoreType.DMA((3,)), pltpu.SemaphoreType.DMA((3,)),
        ]
        + image_sum_scratch(PATCH, width) + image_gather_sems() + image_gather_sems()
        + [pltpu.SemaphoreType.DMA]
        + slot_exchange_sems(slots.count) + slot_exchange_sems(slots.count, COLUMN_CUTS),
        compiler_params=params(collective_id=1, has_side_effects=True),
        name="attention_forward",
    )(w, norm_params, col_rows, xn, patches, g_sent, down)


def backward_kernel(
    experts, slots,
    w_ref, lse_ref, src_ref, norm_ref, small_ref,
    x1g_in, xn_in, hat_in, q_in, qt_in, k_in, kt_in, v_in, ot_in, x_ref, out_rows_ref, down_part,
    owned_ref, small_out, down_first_ref, down_second_ref, input_out, out_back, passed_out,
    x1g_ref, xn_ref, hat_ref, q_ref, qt_ref, k_ref, kt_ref, v_ref, ot_ref, late_ref,
    grad_ref, own_ref, input_ref, padded_ref, load_sems, own_sem, *exchange,
):
    images = x1g_ref.shape[0]
    rows = w_ref.shape[0] // 4
    heads = rows // HD
    total_of = ImageSum(*exchange[:8])
    spread = ImageGather(input_ref, *exchange[8:10])
    back_out = SlotReturn(slots, out_rows_ref, out_back, *exchange[10:14])
    weights_sum = LineScatter(padded_ref, owned_ref, *exchange[14:24])
    down_sum = BlockSum(down_part, *exchange[24:32])
    small_sum = SmallSum(*exchange[32:40])
    late_sum = LateSum(*exchange[40:])
    me, near, far, corner = partners()
    dp_count = slots.count
    streamed = (
        (xn_in, xn_ref), (hat_in, hat_ref), (q_in, q_ref), (qt_in, qt_ref), (k_in, k_ref), (kt_in, kt_ref),
        (v_in, v_ref), (ot_in, ot_ref),
    )

    def load(turn):
        image, slot = total_of.image(turn), lax.rem(turn, 2)
        copies = [
            pltpu.make_async_copy(source.at[image], target.at[slot], load_sems.at[index, slot])
            for index, (source, target) in enumerate(streamed)
        ]
        copies.append(
            pltpu.make_async_copy(x1g_in.at[image], x1g_ref.at[image], load_sems.at[8, slot])
        )
        return copies

    for turn in range(2):
        for copy in load(turn):
            copy.start()
    own = pltpu.make_async_copy(x_ref.at[me], own_ref, own_sem.at[0])
    own.start()
    greet_all((near, far, corner), dp_count)
    small_sum.start(small_ref[...])
    down_sum.start()
    back_out.start()
    down_sum.across()
    half = down_sum.half
    save_passed = pltpu.make_async_copy(
        down_sum.passed.at[pl.ds(0, half)], passed_out, own_sem.at[1]
    )
    save_passed.start()
    late_ref[...] = jnp.zeros_like(late_ref)
    shrink = HD ** (-0.5)
    grad_ref[...] = jnp.zeros_like(grad_ref)

    @pl.loop(0, images)
    def _(turn):
        image, slot = total_of.image(turn), lax.rem(turn, 2)
        for copy in load(turn):
            copy.wait()
        wq, wk, wv, wo = (w_ref[pl.ds(part * rows, rows), :] for part in range(4))
        x1g, xn = x1g_ref[image], xn_ref[slot]
        q, qt, k, kt = q_ref[slot], qt_ref[slot], k_ref[slot], kt_ref[slot]
        v, ot = v_ref[slot], ot_ref[slot]
        do = nt(x1g, wo).astype(LOW)
        dot = nt(wo, x1g).astype(LOW)
        product = dot.astype(FULL) * ot.astype(FULL)
        dqt, dk, dv = [], None, None
        for head in range(heads):
            span = slice(head * HD, (head + 1) * HD)
            zero_t = jnp.zeros_like(qt)
            mask_t = head_mask(qt.shape, 0, head)
            mask = head_mask(q.shape, 1, head)
            scores = nn(k, jnp.where(mask_t, qt, zero_t))
            weights = jnp.exp(scores - lse_ref[image, head:head + 1, :])
            back = nn(v, jnp.where(mask_t, dot, zero_t))
            delta = jnp.sum(product[span], axis=0, keepdims=True)
            score_grad = (weights * (back - delta)).astype(LOW)
            dqt.append(nn(kt[span], score_grad) * shrink)
            dk_one = nn(score_grad, jnp.where(mask, q, jnp.zeros_like(q)))
            dv_one = nn(weights.astype(LOW), jnp.where(mask, do, jnp.zeros_like(do)))
            dk = dk_one if dk is None else dk + dk_one
            dv = dv_one if dv is None else dv + dv_one
        dqt = jnp.concatenate(dqt, axis=0).astype(LOW)
        dk, dv = dk.astype(LOW), dv.astype(LOW)
        part = tn(dqt, wq) + nn(dk, wk) + nn(dv, wv)
        total_of.give(turn, part)
        late_ref[0:1, :] += jnp.sum(part * hat_ref[slot].astype(FULL), axis=0, keepdims=True)
        late_ref[1:2, :] += jnp.sum(part, axis=0, keepdims=True)
        pieces = (nn(dqt, xn), tn(dk, xn), tn(dv, xn), nn(ot, x1g))
        for part, piece in enumerate(pieces):
            grad_ref[pl.ds(part * rows, rows), :] += piece

        @pl.when(turn + 2 < images)
        def _():
            for copy in load(turn + 2):
                copy.start()

        @pl.when(turn == 1)
        def _():
            small_sum.across()

    late_sum.start([late_ref[0:1, :], late_ref[1:2, :]])
    low = grad_ref[...].astype(LOW)
    depth = padded_ref.shape[1]
    parts = min(dp_count, 8)
    cut = dp_count // parts * depth
    for part in range(parts):
        row = lax.broadcasted_iota(jnp.int32, (cut, low.shape[0]), 0) + part * cut
        pick = one_hot(row == src_ref[...])
        block = nn(pick, low).astype(LOW)
        padded_ref[pl.ds(part * (dp_count // parts), dp_count // parts)] = block.reshape(
            dp_count // parts, depth, block.shape[1]
        )
    weights_sum.start()
    small_sum.back()
    own.wait()
    normal, scale = normalise(own_ref[...].astype(FULL))
    back = norm_back(normal, scale, norm_ref[0:1, :], total_of.result())[0]
    input_ref[me] = (x1g_ref[me].astype(FULL) + back).astype(LOW)
    spread.start()
    late_sum.across()
    steps = weights_sum.length

    @pl.loop(0, steps - 1)
    def _(turn):
        weights_sum.step(steps - 1 - turn)

        @pl.when(turn == steps - 2)
        def _():
            spread.wait_far()

    weights_sum.result()
    small_sum.result(small_out)
    late_sum.result(small_out, experts)
    down_sum.result(down_first_ref, down_second_ref)
    spread.wait_near()
    spread.wait_corner()
    keep = pltpu.make_async_copy(input_ref, input_out, own_sem.at[0])
    keep.start()
    back_out.finish()
    spread.finish()
    total_of.finish()
    weights_sum.finish()
    small_sum.finish()
    late_sum.finish()
    down_sum.finish()
    save_passed.wait()
    keep.wait()


def attention_backward(
    experts, slots, depth,
    x1_grad, w, xn, hat, saved, lse, src_row, norm_params, small, patches, out_rows, down_part,
):
    images, _, width = patches.shape
    rows = w.shape[0] // 4
    dp_count = slots.count
    flat, turned = (2, PATCH, rows), (2, rows, PATCH)
    units = down_part.shape[1]
    return pl.pallas_call(
        functools.partial(backward_kernel, experts, slots),
        in_specs=[INSIDE] * 5 + [ANYWHERE] * 12,
        out_specs=[INSIDE] * 4 + [ANYWHERE] * 3,
        out_shape=[
            jax.ShapeDtypeStruct((depth, width), FULL), jax.ShapeDtypeStruct(small.shape, FULL),
            jax.ShapeDtypeStruct((units // 2, width), FULL),
            jax.ShapeDtypeStruct((units // 2, width), FULL),
            jax.ShapeDtypeStruct(patches.shape, LOW),
            jax.ShapeDtypeStruct((dp_count * slots.big, width), LOW),
            jax.ShapeDtypeStruct((units // 2, width), LOW),
        ],
        scratch_shapes=[pltpu.VMEM(patches.shape, LOW)]
        + [pltpu.VMEM((2, PATCH, width), LOW)] * 2
        + [pltpu.VMEM(shape, LOW) for shape in (flat, turned, flat, turned, flat, turned)]
        + [
            pltpu.VMEM((8, width), FULL), pltpu.VMEM(w.shape, FULL), pltpu.VMEM((PATCH, width), LOW),
            pltpu.VMEM(patches.shape, LOW), pltpu.VMEM((dp_count, depth, width), LOW),
            pltpu.SemaphoreType.DMA((9, 2)), pltpu.SemaphoreType.DMA((2,)),
        ]
        + image_sum_scratch(PATCH, width) + image_gather_sems()
        + slot_return_scratch(slots, width)
        + line_scatter_scratch(dp_count, depth, width)
        + block_sum_scratch(units, width)
        + small_sum_scratch(small.shape[0], width, dp_count)
        + late_sum_scratch(width, dp_count),
        compiler_params=params(collective_id=2, has_side_effects=True),
        name="attention_backward",
    )(
        w, lse, src_row, norm_params, small, x1_grad, xn, hat, *saved, patches, out_rows, down_part,
    )


def picked_rows(col, held_ref, start, count):
    lanes = lax.broadcasted_iota(jnp.int32, (col.shape[0], count), 1) + start
    pick = one_hot((lanes == col[:, 0:1]) | (lanes == col[:, 1:2]))
    return nn(pick, held_ref[pl.ds(start, count), :])


def mixed_rows(col, first, second, start):
    count = first.shape[0] + second.shape[0]
    lanes = lax.broadcasted_iota(jnp.int32, (col.shape[0], count), 1) + start
    pick = one_hot((lanes == col[:, 2:3]) | (lanes == col[:, 3:4]))
    return nn(pick, jnp.concatenate([first[...], second[...]], axis=0))


def late_kernel(col_ref, sum_ref, first, second, block_ref):
    start = first.shape[0] + second.shape[0]
    block_ref[0] = (sum_ref[0] + mixed_rows(col_ref[0], first, second, start)).astype(LOW)


def late_stage(col, so_far, held):
    images, _, width = so_far.shape
    wide = lead((1, PATCH, width))
    return pl.pallas_call(
        late_kernel,
        grid=(images,),
        in_specs=[lead((1, PATCH, 4)), wide] + [whole(rows.shape) for rows in held],
        out_specs=wide,
        out_shape=jax.ShapeDtypeStruct(so_far.shape, LOW),
        compiler_params=params(),
        cost_estimate=pl.CostEstimate(
            flops=2 * images * PATCH * sum(rows.size for rows in held),
            bytes_accessed=6 * so_far.size + 2 * sum(rows.size for rows in held), transcendentals=0,
        ),
        name="late_stage",
    )(col, so_far, *held)


def early_kernel(
    col_ref, x1_ref, low_ref, held_own, held_near,
    tile_ref, tile_first, tile_second, tile_grad,
    router_ref, router_first, router_second, norm_ref, norm_first, norm_second, small_ref,
    sum_ref, input_ref, tile_new, tile_first_new, tile_second_new, tile_copy,
    router_new, router_first_new, router_second_new,
    norm_new, norm_first_new, norm_second_new, later_second_new,
):
    sum_ref[0] = x1_ref[0].astype(FULL) + mixed_rows(col_ref[0], held_own, held_near, 0)
    input_ref[0] = low_ref[0].astype(FULL)

    @pl.when(pl.program_id(0) == 0)
    def _():
        new, first, second = adam_update(
            tile_ref[...], tile_first[...], tile_second[...], tile_grad[...],
            rate_attention, decay_factor,
        )
        tile_new[...], tile_first_new[...], tile_second_new[...] = new, first, second
        tile_copy[...] = new.astype(LOW)
        experts = router_ref.shape[0]
        new, first, second = adam_update(
            router_ref[...], router_first[...], router_second[...], small_ref[0:experts, :],
            rate_router, decay_factor,
        )
        router_new[...], router_first_new[...], router_second_new[...] = new, first, second
        new, first, second = adam_update(
            norm_ref[...], norm_first[...], norm_second[...], small_ref[experts:experts + 4, :],
            rate_norm, 0.0,
        )
        norm_new[...], norm_first_new[...] = new, first
        norm_second_new[...], later_second_new[...] = second[0:2], second[2:4]


def early_stage(col, x1, input_low, held, tiles, routers, norms, small):
    images, _, width = x1.shape
    wide = lead((1, PATCH, width))
    tile, router, norm = tiles[0], routers[0], norms[0]
    fixed = [*held, *tiles, *routers, *norms, small]
    full = [tile.shape] * 3 + [tile.shape] + [router.shape] * 3 + [norm.shape] * 2 + [(2, width)] * 2
    kinds = [FULL] * 3 + [LOW] + [FULL] * 7
    return pl.pallas_call(
        early_kernel,
        grid=(images,),
        in_specs=[lead((1, PATCH, 4)), wide, wide] + [whole(array.shape) for array in fixed],
        out_specs=[wide, wide] + [whole(shape) for shape in full],
        out_shape=[jax.ShapeDtypeStruct(x1.shape, FULL), jax.ShapeDtypeStruct(x1.shape, FULL)]
        + [jax.ShapeDtypeStruct(shape, kind) for shape, kind in zip(full, kinds)],
        compiler_params=params(),
        cost_estimate=pl.CostEstimate(
            flops=2 * images * PATCH * sum(rows.size for rows in held),
            bytes_accessed=12 * x1.size + 2 * sum(rows.size for rows in held), transcendentals=0,
        ),
        name="early_stage",
    )(col, x1, input_low, *fixed)


def expert_kernel(
    slots,
    rows_ref, g_ref, router_in, col_ref, norm_ref,
    up_in, down_in, x1_in, cot_in,
    up_grad_ref, small_ref, down_out, out_out, x1g_out,
    router_ref, up_ref, down_ref, og_ref, gate_ref, probs_ref, down_stage, back_ref, act_all,
    held, total, x1_ref, cot_ref, x1g_ref,
    load_sems, save_sems, image_sems, out_sem, *exchange,
):
    images, count = x1_in.shape[0], rows_ref.shape[0]
    out_sum, back_sum = total.at[pl.ds(0, count)], total.at[pl.ds(count, count)]
    up_sum = ImageSum(*exchange[:8])
    back = ReturnGather(slots, back_ref, held, *exchange[8:])
    parts = up_in.shape[0]

    def load(turn):
        part, slot = up_sum.image(turn), lax.rem(turn, 2)
        return (
            pltpu.make_async_copy(up_in.at[part], up_ref.at[slot], load_sems.at[0, slot]),
            pltpu.make_async_copy(down_in.at[part], down_ref.at[slot], load_sems.at[1, slot]),
        )

    def save(turn):
        slot = lax.rem(turn, 2)
        return pltpu.make_async_copy(
            down_stage.at[slot], down_out.at[up_sum.image(turn)], save_sems.at[slot]
        )

    for turn in range(2):
        for copy in load(turn):
            copy.start()
    rows = rows_ref[...]
    experts = router_in.shape[0]
    router_ref[...] = jnp.zeros_like(router_ref)
    router_ref[0:experts, :] = router_in[...]
    lane = lax.broadcasted_iota(jnp.int32, (1, router_ref.shape[0]), 1)
    mine = jnp.where(lane == lax.axis_index("dp"), 1.0, 0.0)
    logits = nt(rows, router_ref[...].astype(LOW)) + jnp.where(lane < experts, 0.0, -1e30)
    top = jnp.max(logits, axis=-1, keepdims=True)
    weights = jnp.exp(logits - top)
    probs = weights / jnp.sum(weights, axis=-1, keepdims=True)
    gate = jnp.sum(probs * mine, axis=-1, keepdims=True)
    probs_ref[...] = probs
    gate_ref[...] = gate
    og_ref[...] = (gate * g_ref[...].astype(FULL)).astype(LOW)
    out_sum[...] = jnp.zeros_like(out_sum)
    back_sum[...] = jnp.zeros_like(back_sum)
    greet_all((back.near, back.far), slots.count)

    later = act_all.shape[0] > 1

    def down_grads(turn, act):
        @pl.when(turn >= 2)
        def _():
            save(turn - 2).wait()

        down_stage[lax.rem(turn, 2)] = tn(act, og_ref[...]).astype(LOW)
        save(turn).start()

    @pl.loop(0, parts)
    def _(turn):
        slot = lax.rem(turn, 2)
        for copy in load(turn):
            copy.wait()
        rows, og = rows_ref[...], og_ref[...]
        up, down = up_ref[slot], down_ref[slot]
        hidden = nn(rows, up)
        slope = (2.0 / jnp.pi) ** 0.5
        square = hidden * hidden
        bend = jnp.tanh(slope * (hidden + 0.044715 * (square * hidden)))
        act = (0.5 * hidden * (1.0 + bend)).astype(LOW)
        out_sum[...] += nn(act, down)
        act_grad = nt(og, down)
        inner = slope * (1.0 + (3.0 * 0.044715) * square)
        curve = 0.5 * (1.0 + bend) + 0.5 * hidden * (1.0 - bend * bend) * inner
        hidden_grad = (curve * act_grad).astype(LOW)
        back_sum[...] += nt(hidden_grad, up)
        up_sum.give(turn, tn(rows, hidden_grad), hold=True)
        if later:
            act_all[turn] = act
        else:
            down_grads(turn, act)

        @pl.when(turn + 2 < parts)
        def _():
            for copy in load(turn + 2):
                copy.start()

    out = out_sum[...].astype(LOW).astype(FULL)
    gate, probs = gate_ref[...], probs_ref[...]
    gate_grad = jnp.sum(g_ref[...].astype(FULL) * out, axis=-1, keepdims=True)
    logit_grad = (gate_grad * (probs * (mine - gate))).astype(LOW)
    plain = back_sum[...].astype(LOW).astype(FULL)
    back_ref[...] = (plain + nn(logit_grad, router_ref[...].astype(LOW))).astype(LOW)
    back.send(0)
    back.send(1)
    back.relay(0)
    small_ref[...] = jnp.zeros_like(small_ref)
    small_ref[0:experts, :] = tn(logit_grad, rows_ref[...])[0:experts]
    back_sum[...] = gate * out
    def image_load(image):
        slot = lax.rem(image, 2)
        return (
            pltpu.make_async_copy(x1_in.at[image], x1_ref.at[slot], image_sems.at[0, slot]),
            pltpu.make_async_copy(cot_in.at[image], cot_ref.at[slot], image_sems.at[1, slot]),
        )

    def image_save(image):
        slot = lax.rem(image, 2)
        return pltpu.make_async_copy(x1g_ref.at[slot], x1g_out.at[image], image_sems.at[2, slot])

    for image in range(2):
        for copy in image_load(image):
            copy.start()

    def relay(phase):
        @pl.loop(max(phase * slots.turns, 1), (phase + 1) * slots.turns)
        def _(shift):
            back.relay(shift)

    ahead = [
        lambda: (relay(0), back.send(2)),
        lambda: (relay(1), back.send(3)),
        lambda: (back.of_phase(0, back.forward), relay(2)),
        lambda: (back.of_phase(1, back.forward), relay(3)),
    ]
    if later:
        for turn in range(parts):
            down_grads(turn, act_all[turn])
            if turn < 3:
                ahead[turn]()
    else:
        for step in ahead[:3]:
            step()
    og_ref[...] = back_sum[...].astype(LOW)
    save_out = pltpu.make_async_copy(og_ref, out_out, out_sem)
    save_out.start()
    total_rows = held.shape[0]
    piece = 3 * 256
    if total_rows % piece:
        piece = slots.phase_rows
    done = 0
    back.of_phase(0, back.rest)
    for phase in range(1, 4):
        if phase == 1:
            ahead[3]()
            up_sum.start_rest()
        else:
            back.of_phase(phase, back.forward)
        back.of_phase(phase, back.rest)
        ready = (phase + 1) * slots.phase_rows
        while done + piece <= ready:
            @pl.loop(0, images)
            def _(image, start=done):
                part = picked_rows(col_ref[image], held, start, piece)
                span = pl.ds(image * PATCH, PATCH)
                if start == 0:
                    total[span] = part
                else:
                    total[span] += part

            done += piece

    back_scale = 1.0 / 4.0

    @pl.loop(0, images)
    def _(image):
        slot = lax.rem(image, 2)
        for copy in image_load(image):
            copy.wait()

        @pl.when(image >= 2)
        def _():
            image_save(image - 2).wait()

        normal, scale = normalise(x1_ref[slot].astype(FULL))
        upstream = total[pl.ds(image * PATCH, PATCH)]
        result, gain_sum, shift_sum = norm_back(normal, scale, norm_ref[2:3, :], upstream)
        x1g_ref[slot] = (cot_ref[slot].astype(FULL) + result).astype(LOW)
        small_ref[experts + 2:experts + 3, :] += gain_sum * back_scale
        small_ref[experts + 3:experts + 4, :] += shift_sum * back_scale
        image_save(image).start()

        @pl.when(image + 2 < images)
        def _():
            for copy in image_load(image + 2):
                copy.start()

    up_grad_ref[...] = up_sum.result()
    back.finish()
    up_sum.finish()
    save_out.wait()
    for turn in range(parts - 2, parts):
        save(turn).wait()
    for image in range(images - 2, images):
        image_save(image).wait()


def expert_stage(slots, rows, g_rows, up, down, router, col, x1, cotangent, norm_params):
    count, width = rows.shape
    parts, _, units = up.shape
    images = x1.shape[0]
    small_rows = -(-(router.shape[0] + 4) // 16) * 16
    lanes = 128
    flat = pltpu.VMEM((count, width), LOW)
    pair = pltpu.VMEM((2, PATCH, width), LOW)
    return pl.pallas_call(
        functools.partial(expert_kernel, slots),
        in_specs=[INSIDE] * 5 + [ANYWHERE] * 4,
        out_specs=[INSIDE] * 2 + [ANYWHERE] * 3,
        out_shape=[
            jax.ShapeDtypeStruct((width, units), FULL),
            jax.ShapeDtypeStruct((small_rows, width), FULL),
            jax.ShapeDtypeStruct(down.shape, LOW),
            jax.ShapeDtypeStruct((count, width), LOW),
            jax.ShapeDtypeStruct(x1.shape, LOW),
        ],
        scratch_shapes=[
            pltpu.VMEM((lanes, width), FULL),
            pltpu.VMEM((2,) + up.shape[1:], LOW), pltpu.VMEM((2,) + down.shape[1:], LOW), flat,
            pltpu.VMEM((count, 1), FULL), pltpu.VMEM((count, lanes), FULL),
            pltpu.VMEM((2, units, width), LOW), flat,
            pltpu.VMEM((parts, count, units) if count <= MOST_KEPT else (1, 16, 128), LOW),
            pltpu.VMEM((4 * slots.phase_rows, width), LOW),
            pltpu.VMEM((max(images * PATCH, 2 * count), width), FULL), pair, pair, pair,
            pltpu.SemaphoreType.DMA((2, 2)), pltpu.SemaphoreType.DMA((2,)),
            pltpu.SemaphoreType.DMA((3, 2)), pltpu.SemaphoreType.DMA,
        ]
        + image_sum_scratch(width, units) + return_gather_sems(slots.count),
        compiler_params=params(collective_id=3, has_side_effects=True),
        name="expert_stage",
    )(
        rows, g_rows, router, col, norm_params, up, down, x1, cotangent,
    )


def body(
    patches, cotangent, expert_ids, slot_pos, owners,
    tile_master, tile_first, tile_second,
    expert_up, up_first, up_second,
    expert_down, down_first, down_second,
    router, router_first, router_second,
    norm_params, norm_first, norm_second,
):
    tok_rows, width = patches.shape
    experts = router.shape[0]
    capacity = tok_rows // experts
    dp_count = lax.axis_size("dp")
    head_count = lax.axis_size("head")
    images = tok_rows // PATCH
    slots = Slots(dp_count, capacity // head_count)
    slot_count = tile_master.shape[0]

    by_image = (images, PATCH, width)
    x_images, g_images = patches.reshape(by_image), cotangent.reshape(by_image)

    def pair_rows(pairs):
        return pairs.T.reshape(2, images, PATCH).transpose(1, 0, 2)

    w, src, col_rows, col, xn, hat, g_sent, up_all = prepare(
        slots, tile_master.reshape(slot_count * TILE, width), x_images, g_images, norm_params,
        owners, pair_rows(expert_ids), pair_rows(slot_pos), expert_up[0],
        owners.shape[1] * TILE,
    )
    lse, *saved, x1, rows, g_rows, down_all = attention_forward(
        slots, xn, w, norm_params, col_rows, x_images, g_sent, expert_down[0]
    )
    up_grad, small, down_part, out, x1_grad = expert_stage(
        slots, rows, g_rows, up_all, down_all, router, col, x1, g_images, norm_params
    )
    owned_grad, small, down_half, down_rest, input_low, out_back, passed = attention_backward(
        experts, slots, slot_count * TILE,
        x1_grad, w, xn, hat, saved, lse, src, norm_params, small, x_images, out, down_part,
    )

    def from_head(rows, apart):
        return lax.ppermute(rows, "head", [(at, at ^ apart) for at in range(head_count)])

    out_far = from_head(out_back, 2)
    flat_tiles = (slot_count * TILE, width)
    (
        so_far, input_grad, tile_new, tile_first_new, tile_second_new, tile_copy,
        router_new, router_first_new, router_second_new,
        norm_new, norm_first_new, norm_second_new, later_second_new,
    ) = early_stage(
        col, x1, input_low, [out_back, from_head(out_back, 1)],
        [array.reshape(flat_tiles) for array in (tile_master, tile_first, tile_second)] + [owned_grad],
        [router, router_first, router_second], [norm_params, norm_first, norm_second], small,
    )
    up_new, up_first_new, up_second_new = adam_update(
        expert_up, up_first, up_second, up_grad[None], rate_up, decay_factor
    )
    out_far, so_far, _ = lax.optimization_barrier((out_far, so_far, up_new))
    block_out = late_stage(col, so_far, [out_far, from_head(out_far, 1)])
    passed, block_out = lax.optimization_barrier((from_head(passed, 2), block_out))
    down_half = down_half + passed.astype(FULL)
    down_grad = jnp.concatenate([down_half, down_rest], axis=0)
    tiles = [
        array.reshape(tile_master.shape)
        for array in (tile_new, tile_first_new, tile_second_new, tile_copy)
    ]
    down_new, down_first_new, down_second_new = adam_update(
        expert_down, down_first, down_second, down_grad[None], rate_down, decay_factor
    )
    return (
        block_out.reshape(tok_rows, width),
        input_grad.reshape(tok_rows, width),
        *tiles,
        up_new,
        up_first_new,
        up_second_new,
        up_new.astype(LOW),
        down_new,
        down_first_new,
        down_second_new,
        down_new.astype(LOW),
        router_new,
        router_first_new,
        router_second_new,
        norm_new,
        norm_first_new,
        norm_second_new,
        later_second_new,
    )


def solution(mesh):
    row = P("dp", None)
    tiles = P(("dp", "head"), None, None)
    up = P("dp", None, "head")
    down = P("dp", "head", None)
    in_specs = (
        row, row, row, row, P("head", None), tiles, tiles, tiles,
        up, up, up, down, down, down, P(), P(), P(), P(), P(), P(),
    )
    out_specs = (
        row, row, tiles, tiles, tiles, tiles, up, up, up, up, down, down, down, down,
        P(), P(), P(), P(), P(), P(), P(),
    )
    return jax.shard_map(body, mesh=mesh, in_specs=in_specs, out_specs=out_specs, check_vma=False)
```

```python
import functools

import jax
import jax.numpy as jnp
from jax import lax
from jax.experimental import pallas as pl
from jax.experimental.pallas import tpu as pltpu
from jax.sharding import PartitionSpec as P

HD = 64
PATCH = 576
TILE = 8
STEP = 10

eps_norm = 1e-06
beta_one = 0.9
beta_two = 0.999
adam_eps = 1e-08
rate_attention = 0.12
rate_up = 0.08
rate_down = 0.3
rate_router = 0.05
rate_norm = 0.4
decay_factor = 0.1

LOW = jnp.bfloat16
FULL = jnp.float32
MESH = pl.DeviceIdType.MESH
MOST_KEPT = 640
VMEM_BYTES = 61 * 1024 * 1024


def adam_update(weight, moment_one, moment_two, gradient, step_rate, weight_decay):
    moment_one = beta_one * moment_one + (1.0 - beta_one) * gradient
    moment_two = beta_two * moment_two + (1.0 - beta_two) * gradient * gradient
    fixed_one = moment_one / (1.0 - beta_one**STEP)
    fixed_two = moment_two / (1.0 - beta_two**STEP)
    weight = weight - step_rate * (
        fixed_one / (jnp.sqrt(fixed_two) + adam_eps) + weight_decay * weight
    )
    return (weight, moment_one, moment_two)


def nn(left, right):
    return lax.dot_general(left, right, (((1,), (0,)), ((), ())), preferred_element_type=FULL)


def nt(left, right):
    return lax.dot_general(left, right, (((1,), (1,)), ((), ())), preferred_element_type=FULL)


def tn(left, right):
    return lax.dot_general(left, right, (((0,), (0,)), ((), ())), preferred_element_type=FULL)


def params(**more):
    return pltpu.CompilerParams(vmem_limit_bytes=VMEM_BYTES, **more)


def whole(shape):
    return pl.BlockSpec(shape, lambda *_: (0,) * len(shape))


def lead(shape):
    return pl.BlockSpec(shape, lambda i: (i,) + (0,) * (len(shape) - 1))


def normalise(values):
    average = jnp.mean(values, axis=-1, keepdims=True)
    centred = values - average
    variance = jnp.mean(centred * centred, axis=-1, keepdims=True)
    scale = lax.rsqrt(variance + eps_norm)
    return centred * scale, scale


def norm_back(normal, scale, gain, upstream):
    inner = upstream * gain
    mean_inner = jnp.mean(inner, axis=-1, keepdims=True)
    mean_cross = jnp.mean(inner * normal, axis=-1, keepdims=True)
    result = scale * (inner - mean_inner - normal * mean_cross)
    gain_sum = jnp.sum(upstream * normal, axis=0, keepdims=True)
    shift_sum = jnp.sum(upstream, axis=0, keepdims=True)
    return result, gain_sum, shift_sum


def one_hot(condition):
    return jnp.where(condition, 1.0, 0.0).astype(LOW)


def remote(src, dst, sends, recvs, index, axis, other):
    return pltpu.make_async_remote_copy(
        src_ref=src, dst_ref=dst, send_sem=sends.at[index], recv_sem=recvs.at[index],
        device_id={axis: other}, device_id_type=MESH,
    )


def greet(*others):
    barrier = pltpu.get_barrier_semaphore()
    for axis, other in others:
        pl.semaphore_signal(barrier, inc=1, device_id={axis: other}, device_id_type=MESH)
    pl.semaphore_wait(barrier, len(others))


def partners():
    me = lax.axis_index("head")
    near = me + 1 - 2 * lax.rem(me, 2)
    far = lax.rem(me + 2, 4)
    corner = lax.rem(near + 2, 4)
    return me, near, far, corner


class LineGather:
    def __init__(self, held, up_send, up_recv, down_send, down_recv, pair_send, pair_recv):
        self.held = held
        self.length = held.shape[0] // 2
        self.sems = ((up_send, up_recv), (down_send, down_recv), (pair_send, pair_recv))
        me = lax.axis_index("dp")
        self.place, self.side = me // 2, lax.rem(me, 2)
        self.above = lax.rem(self.place + 1, self.length) * 2 + self.side
        self.below = lax.rem(self.place + self.length - 1, self.length) * 2 + self.side
        self.other = self.place * 2 + 1 - self.side

    def neighbours(self):
        return ("dp", self.above), ("dp", self.below), ("dp", self.other)

    def copy(self, way, origin, side=None):
        index = origin * 2 + (self.side if side is None else side)
        target = (self.above, self.below, self.other)[way]
        block = self.held.at[index]
        return remote(block, block, *self.sems[way], origin, "dp", target)

    def pass_on(self, origin, up, down):
        @pl.when(up & (self.place < self.length - 1))
        def _():
            self.copy(0, origin).start()

        @pl.when(down & (self.place > 0))
        def _():
            self.copy(1, origin).start()

        self.copy(2, origin).start()

    def start(self):
        self.pass_on(self.place, True, True)

    def step(self, k):
        low, high = self.place - k, self.place + k

        @pl.when(low >= 0)
        def _():
            self.copy(0, low).wait_recv()
            self.pass_on(low, True, False)

        @pl.when(high < self.length)
        def _():
            self.copy(1, high).wait_recv()
            self.pass_on(high, False, True)

    def finish(self):
        @pl.loop(0, self.length)
        def _(origin):
            self.copy(2, origin).wait_recv()
            self.copy(2, origin).wait_send()

            @pl.when((origin <= self.place) & (self.place < self.length - 1))
            def _():
                self.copy(0, origin).wait_send()

            @pl.when((origin >= self.place) & (self.place > 0))
            def _():
                self.copy(1, origin).wait_send()


class ImageSum:
    def __init__(self, stage, corner_in, near_in, passed, mine, far_in, sends, recvs):
        self.stage, self.corner_in, self.near_in = stage, corner_in, near_in
        self.passed, self.mine, self.far_in = passed, mine, far_in
        self.sends, self.recvs = sends, recvs
        self.me, self.near, self.far, self.corner = partners()
        self.core = lax.rem(self.me, 2)

    def image(self, turn):
        base = self.me - self.core
        other = lax.rem(base + 2, 4)
        return jnp.where(turn < 2, other, base - 2) + turn

    def to_corner(self):
        return remote(
            self.stage.at[0], self.corner_in, self.sends, self.recvs, 0, "head", self.near
        )

    def to_near(self):
        return remote(
            self.stage.at[1], self.near_in, self.sends, self.recvs, 1, "head", self.near
        )

    def to_far(self, half):
        rows = self.passed.shape[0] // 2
        span = pl.ds(half * rows, rows)
        return remote(
            self.passed.at[span], self.far_in.at[span], self.sends, self.recvs, 2 + half, "head",
            self.far,
        )

    def give(self, turn, part, hold=False):
        theirs = lax.rem(turn, 2) != self.core

        @pl.when((turn < 2) & theirs)
        def _():
            self.stage[0] = part.astype(LOW)
            self.to_corner().start()

        @pl.when((turn >= 2) & theirs)
        def _():
            self.stage[1] = part.astype(LOW)
            self.to_near().start()

        @pl.when((turn < 2) & ~theirs)
        def _():
            self.to_corner().wait_recv()
            self.passed[...] = (part + self.corner_in[...].astype(FULL)).astype(LOW)
            self.to_far(0).start()
            if not hold:
                self.to_far(1).start()

        @pl.when((turn >= 2) & ~theirs)
        def _():
            self.mine[...] = part

    def start_rest(self):
        self.to_far(1).start()

    def result(self):
        self.to_near().wait_recv()
        for half in range(2):
            self.to_far(half).wait_recv()
        return self.mine[...] + self.near_in[...].astype(FULL) + self.far_in[...].astype(FULL)

    def finish(self):
        self.to_corner().wait_send()
        self.to_near().wait_send()
        for half in range(2):
            self.to_far(half).wait_send()


def image_sum_scratch(rows, width):
    block = pltpu.VMEM((rows, width), LOW)
    return [
        pltpu.VMEM((2, rows, width), LOW), block, block, block,
        pltpu.VMEM((rows, width), FULL), block,
        pltpu.SemaphoreType.DMA((4,)), pltpu.SemaphoreType.DMA((4,)),
    ]


class LineScatter:
    def __init__(
        self, blocks, out, pair_in, up_in, down_in, total,
        up_send, up_recv, down_send, down_recv, pair_send, pair_recv,
    ):
        self.blocks, self.out, self.total = blocks, out, total
        self.arrived = (up_in, down_in, pair_in)
        self.sems = ((up_send, up_recv), (down_send, down_recv), (pair_send, pair_recv))
        self.length = blocks.shape[0] // 2
        me = lax.axis_index("dp")
        self.place, self.side = me // 2, lax.rem(me, 2)
        self.targets = (
            lax.rem(self.place + 1, self.length) * 2 + self.side,
            lax.rem(self.place + self.length - 1, self.length) * 2 + self.side,
            self.place * 2 + 1 - self.side,
        )

    def copy(self, way, block):
        source = (
            self.blocks.at[block * 2 + 1 - self.side] if way == 2 else self.total.at[block]
        )
        return remote(
            source, self.arrived[way].at[block], *self.sems[way], block, "dp", self.targets[way]
        )

    def start(self):
        @pl.loop(0, self.length)
        def _(turn):
            distance = self.length - 1 - turn

            @pl.when(self.place + distance < self.length)
            def _():
                self.copy(2, self.place + distance).start()

            @pl.when((self.place >= distance) & (distance > 0))
            def _():
                self.copy(2, self.place - distance).start()

    def pair_sum(self, block):
        self.copy(2, block).wait_recv()
        own = self.blocks[block * 2 + self.side].astype(FULL)
        return own + self.arrived[2][block].astype(FULL)

    def forward(self, way, block, first):
        both = self.pair_sum(block)

        @pl.when(first)
        def _():
            self.total[block] = both.astype(LOW)

        @pl.when(~first)
        def _():
            self.copy(way, block).wait_recv()
            self.total[block] = (both + self.arrived[way][block].astype(FULL)).astype(LOW)

        self.copy(way, block).start()

    def step(self, distance):
        @pl.when(self.place + distance < self.length)
        def _():
            self.forward(0, self.place + distance, self.place == 0)

        @pl.when(self.place >= distance)
        def _():
            self.forward(1, self.place - distance, self.place == self.length - 1)

    def result(self):
        self.out[...] = self.pair_sum(self.place)

        @pl.when(self.place > 0)
        def _():
            self.copy(0, self.place).wait_recv()
            self.out[...] += self.arrived[0][self.place].astype(FULL)

        @pl.when(self.place < self.length - 1)
        def _():
            self.copy(1, self.place).wait_recv()
            self.out[...] += self.arrived[1][self.place].astype(FULL)

    def finish(self):
        @pl.loop(0, self.length)
        def _(block):
            self.copy(2, block).wait_send()

            @pl.when(block > self.place)
            def _():
                self.copy(0, block).wait_send()

            @pl.when(block < self.place)
            def _():
                self.copy(1, block).wait_send()


def line_scatter_scratch(dp_count, rows, width):
    line = dp_count // 2
    return [pltpu.VMEM((line, rows, width), LOW)] * 4 + [pltpu.SemaphoreType.DMA((line,))] * 6


class SmallSum:
    def __init__(self, flat, head_in, dp_in, done, head_send, head_recv, dp_send, dp_recv):
        self.flat, self.head_in, self.dp_in, self.done = flat, head_in, dp_in, done
        self.head_sems, self.dp_sems = (head_send, head_recv), (dp_send, dp_recv)
        self.me, *self.others = partners()
        self.place, self.count = lax.axis_index("dp"), dp_in.shape[0]

    def to_head(self, lane):
        other = self.others[lane]
        return remote(
            self.flat.at[other], self.head_in.at[self.me], *self.head_sems, lane, "head", other
        )

    def back_head(self, lane):
        block = self.done.at[self.me]
        return remote(block, block, *self.head_sems, 3 + lane, "head", self.others[lane])

    def to_dp(self, shift):
        block = self.dp_in.at[self.place]
        other = lax.rem(self.place + shift, self.count)
        return remote(block, block, *self.dp_sems, shift, "dp", other)

    def start(self, value):
        groups, rows, lanes = self.flat.shape
        flat = jnp.concatenate(
            [value[:, at:at + lanes] for at in range(0, value.shape[1], lanes)], axis=0
        )
        for group in range(groups):
            self.flat[group] = flat[group * rows:(group + 1) * rows]
        for lane in range(3):
            self.to_head(lane).start()
        self.head_in[self.me] = self.flat[self.me]

    def across(self):
        for lane in range(3):
            self.to_head(lane).wait_recv()
        total = self.head_in[0]
        for head in range(1, self.head_in.shape[0]):
            total = total + self.head_in[head]
        self.dp_in[self.place] = total

        @pl.loop(1, self.count)
        def _(shift):
            self.to_dp(shift).start()

    def back(self):
        @pl.loop(1, self.count)
        def _(shift):
            self.to_dp(shift).wait_recv()

        total = lax.fori_loop(
            1, self.count, lambda at, so_far: so_far + self.dp_in[at], self.dp_in[0]
        )
        self.done[self.me] = total
        for lane in range(3):
            self.back_head(lane).start()

    def result(self, out):
        for lane in range(3):
            self.back_head(lane).wait_recv()
        flat = jnp.concatenate([self.done[group] for group in range(self.done.shape[0])], axis=0)
        rows, width = out.shape
        lanes = flat.shape[1]
        for at in range(width // lanes):
            out[:, at * lanes:(at + 1) * lanes] = flat[at * rows:(at + 1) * rows]

    def finish(self):
        for lane in range(3):
            self.to_head(lane).wait_send()
            self.back_head(lane).wait_send()

        @pl.loop(1, self.count)
        def _(shift):
            self.to_dp(shift).wait_send()


def small_sum_scratch(rows, width, dp_count):
    block = (rows * width // 128 // 4, 128)
    return [
        pltpu.VMEM((4,) + block, FULL), pltpu.VMEM((4,) + block, FULL),
        pltpu.VMEM((dp_count,) + block, FULL), pltpu.VMEM((4,) + block, FULL),
        pltpu.SemaphoreType.DMA((6,)), pltpu.SemaphoreType.DMA((6,)),
        pltpu.SemaphoreType.DMA((dp_count,)), pltpu.SemaphoreType.DMA((dp_count,)),
    ]


class LateSum:
    def __init__(self, dp_in, head_in, dp_send, dp_recv, head_send, head_recv):
        self.dp_in, self.head_in = dp_in, head_in
        self.dp_sems, self.head_sems = (dp_send, dp_recv), (head_send, head_recv)
        self.me, *self.others = partners()
        self.place, self.count = lax.axis_index("dp"), dp_in.shape[0]

    def to_dp(self, shift):
        block = self.dp_in.at[self.place]
        other = lax.rem(self.place + shift, self.count)
        return remote(block, block, *self.dp_sems, shift, "dp", other)

    def to_head(self, lane):
        block = self.head_in.at[self.me]
        return remote(block, block, *self.head_sems, lane, "head", self.others[lane])

    def start(self, rows):
        lanes = self.dp_in.shape[2]
        cuts = [
            row[:, at:at + lanes] for row in rows for at in range(0, row.shape[1], lanes)
        ]
        cuts += [jnp.zeros_like(cuts[0])] * (self.dp_in.shape[1] - len(cuts))
        self.dp_in[self.place] = jnp.concatenate(cuts, axis=0)

        @pl.loop(1, self.count)
        def _(shift):
            self.to_dp(shift).start()

    def across(self):
        @pl.loop(1, self.count)
        def _(shift):
            self.to_dp(shift).wait_recv()

        self.head_in[self.me] = lax.fori_loop(
            1, self.count, lambda at, so_far: so_far + self.dp_in[at], self.dp_in[0]
        )
        for lane in range(3):
            self.to_head(lane).start()

    def result(self, out, first):
        for lane in range(3):
            self.to_head(lane).wait_recv()
        total = self.head_in[0]
        for head in range(1, self.head_in.shape[0]):
            total = total + self.head_in[head]
        lanes = total.shape[1]
        cuts = out.shape[1] // lanes
        for row in range(2):
            for at in range(cuts):
                piece = total[row * cuts + at:row * cuts + at + 1]
                out[first + row:first + row + 1, at * lanes:(at + 1) * lanes] = piece

    def finish(self):
        for lane in range(3):
            self.to_head(lane).wait_send()

        @pl.loop(1, self.count)
        def _(shift):
            self.to_dp(shift).wait_send()


def late_sum_scratch(width, dp_count):
    block = (-(-2 * width // 128 // 8) * 8, 128)
    return [
        pltpu.VMEM((dp_count,) + block, FULL), pltpu.VMEM((4,) + block, FULL),
        pltpu.SemaphoreType.DMA((dp_count,)), pltpu.SemaphoreType.DMA((dp_count,)),
        pltpu.SemaphoreType.DMA((3,)), pltpu.SemaphoreType.DMA((3,)),
    ]


GATHER_CUTS = 4
COLUMN_CUTS = 3


class ImageGather:
    def __init__(self, held, sends, recvs, own=None, local_sem=None, columns=False):
        self.held, self.sends, self.recvs, self.columns = held, sends, recvs, columns
        self.me, self.near, self.far, self.corner = partners()
        self.own = held.at[self.me] if own is None else own
        self.local = None if own is None else pltpu.make_async_copy(own, held.at[self.me], local_sem)
        self.size = held.shape[1] // GATHER_CUTS
        self.wide = held.shape[2] // COLUMN_CUTS

    def piece(self, lane, cut):
        span = pl.ds(cut * self.size, self.size)
        image = self.far if lane == 2 else self.me
        if self.columns:
            block = self.held.at[image, :, pl.ds(cut * self.wide, self.wide)]
        else:
            block = self.held.at[image, span]
        source = block if self.columns or lane == 2 else self.own.at[span]
        other = self.far if lane == 0 else self.near
        index = lane * GATHER_CUTS + cut
        return remote(source, block, self.sends, self.recvs, index, "head", other)

    def start_far(self, first=0, last=GATHER_CUTS):
        for cut in range(first, last):
            self.piece(0, cut).start()

    def start_near(self, last=GATHER_CUTS):
        for cut in range(last):
            self.piece(1, cut).start()
        if self.local is not None:
            self.local.start()

    def start(self):
        self.start_far()
        self.start_near()

    def wait_near(self, first=0, last=GATHER_CUTS):
        for cut in range(first, last):
            self.piece(1, cut).wait_recv()

    def wait_far(self, first=0, last=GATHER_CUTS):
        for cut in range(first, last):
            self.piece(0, cut).wait_recv()
            self.piece(2, cut).start()

    def wait_corner(self, first=0, last=GATHER_CUTS):
        for cut in range(first, last):
            self.piece(2, cut).wait_recv()

    def finish(self, last=GATHER_CUTS):
        for cut in range(last):
            for lane in range(3):
                self.piece(lane, cut).wait_send()
        if self.local is not None:
            self.local.wait()


def image_gather_sems():
    return [pltpu.SemaphoreType.DMA((3 * GATHER_CUTS,)), pltpu.SemaphoreType.DMA((3 * GATHER_CUTS,))]


class BlockSum:
    def __init__(self, parts, mine, passed, corner_in, near_in, far_in, local_sems, sends, recvs):
        self.mine, self.passed, self.corner_in = mine, passed, corner_in
        self.near_in, self.far_in = near_in, far_in
        me, near, far, corner = partners()
        self.half = far_in.shape[0]
        self.to_corner = remote(parts.at[corner], corner_in, sends, recvs, 0, "head", near)
        self.to_near = remote(parts.at[near], near_in, sends, recvs, 1, "head", near)
        second = passed.at[pl.ds(self.half, self.half)]
        self.to_far = remote(second, far_in, sends, recvs, 2, "head", far)
        self.load_far = pltpu.make_async_copy(parts.at[far], passed, local_sems.at[0])
        self.load_mine = pltpu.make_async_copy(parts.at[me], mine, local_sems.at[1])

    def start(self):
        for copy in (self.to_corner, self.load_far, self.to_near, self.load_mine):
            copy.start()

    def across(self):
        self.load_far.wait()
        self.to_corner.wait_recv()
        both = self.passed[...].astype(FULL) + self.corner_in[...].astype(FULL)
        self.passed[...] = both.astype(LOW)
        self.to_far.start()

    def result(self, first_out, second_out):
        self.load_mine.wait()
        self.to_near.wait_recv()
        self.to_far.wait_recv()
        total = self.mine[...].astype(FULL) + self.near_in[...].astype(FULL)
        first_out[...] = total[:self.half]
        second_out[...] = total[self.half:] + self.far_in[...].astype(FULL)

    def finish(self):
        for copy in (self.to_corner, self.to_near, self.to_far):
            copy.wait_send()


def block_sum_scratch(rows, width):
    return [pltpu.VMEM((rows, width), LOW)] * 4 + [
        pltpu.VMEM((rows // 2, width), LOW),
        pltpu.SemaphoreType.DMA((2,)), pltpu.SemaphoreType.DMA((3,)), pltpu.SemaphoreType.DMA((3,)),
    ]


class Slots:
    def __init__(self, count, share):
        self.count, self.share = count, share
        self.big = -(-share // 16) * 16
        rest = 2 * share - self.big
        self.small = rest if rest > 0 and rest % 16 == 0 else self.big
        self.more = self.big - self.small
        self.both = self.big + self.small
        self.rows = count // 2 * self.both
        self.turns = count // 4
        self.phase_rows = self.turns * 2 * self.both

    def size(self, source, head):
        return self.small + self.more * ((head + source + 1) % 2)

    def packed(self, source, head):
        return (source // 2) * self.both + (source % 2) * self.size(0, head)

    def row(self, source, head, shift):
        first = self.size(source, 0) * (head % 2)
        group = (head // 2) * self.turns * self.both + self.turns * first
        return (
            (shift // self.turns) * self.phase_rows + group
            + (shift % self.turns) * self.size(source, head)
        )

    def holder(self, source, slot):
        pair, within = slot // self.both, slot % self.both
        first = self.size(source, 0)
        second = jnp.where(within >= first, 1, 0)
        return 2 * pair + second, within - second * first

    def span(self, start, extra):
        if extra:
            return pl.ds(pl.multiple_of(start + self.small, 16), self.more)
        return pl.ds(pl.multiple_of(start, 16), self.small)

    def each(self, is_big, make, action):
        getattr(make(False), action)()
        if self.more:
            @pl.when(is_big)
            def _():
                getattr(make(True), action)()


class SlotExchange:
    def __init__(self, slots, sent, rows, sends, recvs, local_sems, cut=None):
        self.slots, self.sent, self.rows = slots, sent, rows
        self.sems, self.local_sems = (sends, recvs), local_sems
        self.place, self.head = lax.axis_index("dp"), lax.axis_index("head")
        wide = sent.shape[1] // COLUMN_CUTS
        self.cut = 0 if cut is None else cut
        self.lanes = pl.ds(0, sent.shape[1]) if cut is None else pl.ds(cut * wide, wide)

    def index(self, shift, extra):
        return 2 * (self.cut * self.slots.count + shift) + int(extra)

    def out(self, shift, action):
        slots = self.slots
        expert = lax.rem(self.place + shift, slots.count)
        mine = slots.size(self.place, self.head)
        at, to = expert * mine, slots.packed(self.place, self.head)
        slots.each(mine > slots.small, lambda extra: remote(
            self.sent.at[slots.span(at, extra), self.lanes], self.rows.at[slots.span(to, extra), self.lanes],
            *self.sems, self.index(shift, extra), "dp", expert,
        ), action)

    def into(self, shift):
        slots = self.slots
        source = lax.rem(self.place + slots.count - shift, slots.count)
        size = slots.size(source, self.head)
        to = slots.packed(source, self.head)
        slots.each(size > slots.small, lambda extra: remote(
            self.sent.at[slots.span(0, extra), self.lanes], self.rows.at[slots.span(to, extra), self.lanes],
            *self.sems, self.index(shift, extra), "dp", source,
        ), "wait_recv")

    def own(self, action):
        slots = self.slots
        mine = slots.size(self.place, self.head)
        at, to = self.place * mine, slots.packed(self.place, self.head)
        slots.each(mine > slots.small, lambda extra: pltpu.make_async_copy(
            self.sent.at[slots.span(at, extra), self.lanes], self.rows.at[slots.span(to, extra), self.lanes],
            self.local_sems.at[2 * self.cut + int(extra)],
        ), action)

    def start(self):
        @pl.loop(1, self.slots.count)
        def _(shift):
            self.out(shift, "start")

        self.own("start")

    def finish(self):
        @pl.loop(1, self.slots.count)
        def _(shift):
            self.into(shift)
            self.out(shift, "wait_send")

        self.own("wait")


class SlotReturn:
    def __init__(self, slots, rows, back, zeros, sends, recvs, local_sems):
        self.slots, self.rows, self.back, self.zeros = slots, rows, back, zeros
        self.sems, self.local_sems = (sends, recvs), local_sems
        self.place, self.head = lax.axis_index("dp"), lax.axis_index("head")
        self.mine = slots.size(self.place, self.head)

    def out(self, shift, action):
        slots = self.slots
        source = lax.rem(self.place + shift, slots.count)
        size = slots.size(source, self.head)
        at, to = slots.packed(source, self.head), shift * size
        slots.each(size > slots.small, lambda extra: remote(
            self.rows.at[slots.span(at, extra)], self.back.at[slots.span(to, extra)],
            *self.sems, 2 * shift + int(extra), "dp", source,
        ), action)

    def into(self, shift):
        slots = self.slots
        expert = lax.rem(self.place + slots.count - shift, slots.count)
        slots.each(self.mine > slots.small, lambda extra: remote(
            self.rows.at[slots.span(0, extra)], self.back.at[slots.span(shift * self.mine, extra)],
            *self.sems, 2 * shift + int(extra), "dp", expert,
        ), "wait_recv")

    def own(self, action):
        slots = self.slots
        at = slots.packed(self.place, self.head)
        slots.each(self.mine > slots.small, lambda extra: pltpu.make_async_copy(
            self.rows.at[slots.span(at, extra)], self.back.at[slots.span(0, extra)],
            self.local_sems.at[int(extra)],
        ), action)

    def blank(self, action):
        slots = self.slots
        if slots.more:
            @pl.when(self.mine == slots.small)
            def _():
                tail = self.back.at[pl.ds(slots.count * slots.small, slots.count * slots.more)]
                copy = pltpu.make_async_copy(self.zeros, tail, self.local_sems.at[2])
                getattr(copy, action)()

    def start(self):
        if self.slots.more:
            self.zeros[...] = jnp.zeros_like(self.zeros)
        self.blank("start")

        @pl.loop(1, self.slots.count)
        def _(shift):
            self.out(shift, "start")

        self.own("start")

    def finish(self):
        @pl.loop(1, self.slots.count)
        def _(shift):
            self.into(shift)
            self.out(shift, "wait_send")

        self.own("wait")
        self.blank("wait")


def slot_return_scratch(slots, width):
    return [pltpu.VMEM((max(slots.count * slots.more, 16), width), LOW)] + [
        pltpu.SemaphoreType.DMA((2 * slots.count,)), pltpu.SemaphoreType.DMA((2 * slots.count,)),
        pltpu.SemaphoreType.DMA((3,)),
    ]


def slot_exchange_sems(count, cuts=1):
    return [
        pltpu.SemaphoreType.DMA((2 * count * cuts,)), pltpu.SemaphoreType.DMA((2 * count * cuts,)),
        pltpu.SemaphoreType.DMA((2 * cuts,)),
    ]


class ReturnGather:
    def __init__(self, slots, rows, held, sends, recvs, local_sems):
        self.slots, self.rows, self.held = slots, rows, held
        self.sems, self.local_sems = (sends, recvs), local_sems
        self.place = lax.axis_index("dp")
        self.me, self.near, self.far, self.corner = partners()

    def out(self, shift, action):
        slots = self.slots
        source = lax.rem(self.place + shift, slots.count)
        size = slots.size(source, self.me)
        at, to = slots.packed(source, self.me), slots.row(source, self.me, shift)
        slots.each(size > slots.small, lambda extra: remote(
            self.rows.at[slots.span(at, extra)], self.held.at[slots.span(to, extra)],
            *self.sems, 2 * shift + int(extra), "dp", source,
        ), action)

    def own(self, action):
        slots = self.slots
        size = slots.size(self.place, self.me)
        at, to = slots.packed(self.place, self.me), slots.row(self.place, self.me, 0)
        slots.each(size > slots.small, lambda extra: pltpu.make_async_copy(
            self.rows.at[slots.span(at, extra)], self.held.at[slots.span(to, extra)],
            self.local_sems.at[int(extra)],
        ), action)

    def block(self, lane, head, shift, axis, other, action):
        slots = self.slots
        size = slots.size(self.place, head)
        to = slots.row(self.place, head, shift)

        def make(extra):
            block = self.held.at[slots.span(to, extra)]
            index = 2 * (lane * slots.count + shift) + int(extra)
            return remote(block, block, *self.sems, index, axis, other)

        slots.each(size > slots.small, make, action)

    def send(self, phase):
        turns = self.slots.turns
        if phase == 0:
            self.own("start")

        @pl.loop(max(phase * turns, 1), (phase + 1) * turns)
        def _(shift):
            self.out(shift, "start")

    def relay(self, shift):
        @pl.when(shift == 0)
        def _():
            self.own("wait")

        @pl.when(shift > 0)
        def _():
            expert = lax.rem(self.place + self.slots.count - shift, self.slots.count)
            self.block(0, self.me, shift, "dp", expert, "wait_recv")

        self.block(1, self.me, shift, "head", self.far, "start")
        self.block(2, self.me, shift, "head", self.near, "start")

    def forward(self, shift):
        self.block(1, self.far, shift, "head", self.far, "wait_recv")
        self.block(3, self.far, shift, "head", self.near, "start")

    def rest(self, shift):
        self.block(2, self.near, shift, "head", self.near, "wait_recv")
        self.block(3, self.corner, shift, "head", self.near, "wait_recv")

    def of_phase(self, phase, action):
        @pl.loop(0, self.slots.turns)
        def _(turn):
            action(phase * self.slots.turns + turn)

    def finish(self):
        @pl.loop(0, self.slots.count)
        def _(shift):
            @pl.when(shift > 0)
            def _():
                self.out(shift, "wait_send")

            self.block(1, self.me, shift, "head", self.far, "wait_send")
            self.block(2, self.me, shift, "head", self.near, "wait_send")
            self.block(3, self.far, shift, "head", self.near, "wait_send")


def return_gather_sems(count):
    return [
        pltpu.SemaphoreType.DMA((8 * count,)), pltpu.SemaphoreType.DMA((8 * count,)),
        pltpu.SemaphoreType.DMA((2,)),
    ]


def greet_all(heads, dp_count):
    barrier = pltpu.get_barrier_semaphore()
    place = lax.axis_index("dp")
    for other in heads:
        pl.semaphore_signal(barrier, inc=1, device_id={"head": other}, device_id_type=MESH)

    @pl.loop(1, dp_count)
    def _(shift):
        other = lax.rem(place + shift, dp_count)
        pl.semaphore_signal(barrier, inc=1, device_id={"dp": other}, device_id_type=MESH)

    pl.semaphore_wait(barrier, len(heads) + dp_count - 1)


ANYWHERE = pl.BlockSpec(memory_space=pl.ANY)
INSIDE = pl.BlockSpec(memory_space=pltpu.VMEM)


def digits(values):
    high = lax.div(values, 64)
    return [high.astype(FULL), (values - high * 64).astype(FULL)]


def digit_weights(shape, digit_axis):
    digit = lax.broadcasted_iota(jnp.int32, shape, digit_axis)
    value = lax.broadcasted_iota(jnp.int32, shape, 1 - digit_axis)
    weight = jnp.where(lax.rem(digit, 2) == 0, 64.0, 1.0)
    return jnp.where(lax.div(digit, 2) == value, weight, 0.0).astype(LOW)


def turned_rows(rows):
    count = rows[0].shape[1]
    parts = [part for row in rows for part in digits(row)]
    parts += [jnp.zeros((1, count), FULL)] * (8 - len(parts))
    spread = jnp.concatenate(parts, axis=0).astype(LOW)
    return tn(spread, digit_weights((8, 128), 0)).astype(jnp.int32)


def turned_column(column):
    lanes = lax.broadcasted_iota(jnp.int32, (column.shape[0], 128), 1)
    high, low = digits(column)
    spread = jnp.where(lanes == 0, high, jnp.where(lanes == 1, low, 0.0)).astype(LOW)
    return nt(digit_weights((8, 128), 1), spread)[0:1].astype(jnp.int32)


def head_mask(shape, axis, head):
    return lax.broadcasted_iota(jnp.int32, shape, axis) // HD == head


def front_kernel(
    slots, slot_count, capacity,
    tile_ref, norm_ref, owner_ref, ids_ref, pos_ref, up_in, down_in, x_in, g_in,
    w_ref, src_ref, col_back_ref, lse_ref,
    xn_out, hat_out, up_out, down_out, q_out, qt_out, k_out, kt_out, v_out, ot_out, x1_out,
    rows_out, g_rows_out,
    x_ref, g_ref, xn_ref, hat_ref, full_ref, up_low, down_low, held, picks, sent_sum, sent_g, sent_ref,
    q_ref, qt_ref, k_ref, kt_ref, v_ref, ot_ref, stats, norms,
    load_sems, image_sems, save_sems, keep_sem, stat_send, stat_recv, *exchange,
):
    images = x_ref.shape[0]
    x1_ref = g_ref
    gather = LineGather(held, *exchange[:6])
    spread_up = ImageGather(up_out, *exchange[6:8], own=up_low, local_sem=exchange[8])
    spread_down = ImageGather(down_out, *exchange[9:11], own=down_low, local_sem=exchange[11])
    total_of = ImageSum(*exchange[12:20])
    spread = ImageGather(x1_ref, *exchange[20:22], columns=True)
    send_g = SlotExchange(slots, sent_g, g_rows_out, *exchange[22:25])
    send_rows = [
        SlotExchange(slots, sent_ref, rows_out, *exchange[25:], cut=cut) for cut in range(COLUMN_CUTS)
    ]
    head, near, far, corner = partners()
    load_up = pltpu.make_async_copy(up_in, full_ref, load_sems.at[2, 0])
    load_down = pltpu.make_async_copy(down_in, full_ref, load_sems.at[2, 1])
    load_up.start()

    def load_image(image):
        return (
            pltpu.make_async_copy(x_in.at[image], x_ref.at[image], load_sems.at[0, image]),
            pltpu.make_async_copy(g_in.at[image], g_ref.at[image], load_sems.at[1, image]),
        )

    def save_image(image):
        return [
            pltpu.make_async_copy(xn_ref.at[image], xn_out.at[image], image_sems.at[0, image]),
            pltpu.make_async_copy(hat_ref.at[image], hat_out.at[image], image_sems.at[1, image]),
        ]

    kept_refs = (
        (q_ref, q_out), (qt_ref, qt_out), (k_ref, k_out), (kt_ref, kt_out), (v_ref, v_out),
        (ot_ref, ot_out),
    )

    def save(image):
        return [
            pltpu.make_async_copy(ref.at[image], out.at[image], save_sems.at[index, image])
            for index, (ref, out) in enumerate(kept_refs)
        ]

    for image in range(images):
        for copy in load_image(image):
            copy.start()
    me = lax.axis_index("dp")
    held[me] = tile_ref[...].astype(LOW)
    greet_all((near, far, corner), slots.count)
    gather.start()
    load_up.wait()
    up_low[...] = full_ref[...].astype(LOW)
    spread_up.start()
    load_down.start()
    shape = (sent_ref.shape[0], PATCH)
    sent_sum[...] = jnp.zeros_like(sent_sum)
    steps = gather.length - 1

    def image_step(image):
        for copy in load_image(image):
            copy.wait()
        normal, _ = normalise(x_ref[image].astype(FULL))
        hat_ref[image] = normal.astype(LOW)
        xn_ref[image] = (normal * norm_ref[0:1, :] + norm_ref[1:2, :]).astype(LOW)
        for copy in save_image(image):
            copy.start()

        ids, pos = ids_ref[image], pos_ref[image]
        kept = pos < capacity
        holder, within = slots.holder(me, jnp.minimum(pos, capacity - 1))
        sent_at = ids * slots.size(me, head) + within
        sent_at = jnp.where(kept & (holder == head), sent_at, slots.count * slots.big)
        shift = me - ids
        shift = jnp.where(shift < 0, shift + slots.count, shift)
        back_at = jnp.where(kept, slots.row(me, holder, shift) + within + 1, 0)
        other_pair = jnp.where(lax.div(holder, 2) == lax.div(head, 2), 0, 2)
        apart = other_pair + jnp.where(lax.rem(holder, 2) == lax.rem(head, 2), 0, 1)
        out_at = apart * (slots.count * slots.big) + shift * slots.size(me, holder) + within
        out_at = jnp.where(kept, out_at + 1, 0)
        turned = turned_rows([back_at[0:1], back_at[1:2], out_at[0:1], out_at[1:2]])
        col_back_ref[image] = turned[:, 0:4] - 1
        first, second = sent_at[0:1], sent_at[1:2]
        sent_slots = lax.broadcasted_iota(jnp.int32, shape, 0)
        pick = one_hot((sent_slots == first) | (sent_slots == second))
        picks[image] = pick
        sent_sum[...] += nn(pick, g_ref[image])

    @pl.loop(0, max(steps, (images + 1) // 2))
    def _(turn):
        @pl.loop(2 * turn, jnp.minimum(2 * turn + 2, images))
        def _(image):
            image_step(image)

        @pl.when(turn < steps)
        def _():
            gather.step(turn + 1)

        @pl.when(turn == 1)
        def _():
            spread_up.wait_far(0, 1)

    sent_g[...] = sent_sum[...].astype(LOW)
    load_down.wait()
    down_low[...] = full_ref[...].astype(LOW)

    rows = w_ref.shape[0]
    tiles = owner_ref.shape[1]
    row_tile = lax.div(lax.broadcasted_iota(jnp.int32, (rows, tiles), 0), TILE)
    lane_tile = lax.broadcasted_iota(jnp.int32, (rows, tiles), 1)
    owner_rows = jnp.broadcast_to(owner_ref[...].astype(FULL), (8, tiles)).astype(LOW)
    owner = nt(one_hot(lane_tile == row_tile), owner_rows)[:, 0:1].astype(jnp.int32)
    before = (owner_ref[...] == owner) & (lane_tile < row_tile)
    rank = jnp.sum(jnp.where(before, 1.0, 0.0), axis=1, keepdims=True).astype(jnp.int32)
    within = lax.rem(lax.broadcasted_iota(jnp.int32, (rows, 1), 0), TILE)
    src = (owner * slot_count + rank) * TILE + within
    src_ref[...] = turned_column(src)
    spread_up.wait_far(1, 3)
    gather.finish()
    blocks, depth, width = held.shape
    cut = rows // 4
    for part in range(4):
        lanes = lax.broadcasted_iota(jnp.int32, (cut, blocks * depth), 1)
        pick = one_hot(lanes == src[part * cut:(part + 1) * cut])
        block = nn(pick, held[...].reshape(blocks * depth, width))
        w_ref[pl.ds(part * cut, cut), :] = block.astype(LOW)
    spread_down.start_far(0, 1)
    spread_down.start_near()
    send_g.start()
    me = head
    shrink = HD ** (-0.5)

    part_rows = w_ref.shape[0] // 4
    heads = part_rows // HD

    @pl.loop(0, images)
    def _(turn):
        image = total_of.image(turn)
        xn = xn_ref[image]
        wq, wk, wv, wo = (
            w_ref[pl.ds(part * part_rows, part_rows), :] for part in range(4)
        )
        q_ref[image] = (nt(xn, wq) * shrink).astype(LOW)
        qt = (nt(wq, xn) * shrink).astype(LOW)
        qt_ref[image] = qt
        k = nt(xn, wk).astype(LOW)
        k_ref[image] = k
        kt_ref[image] = nt(wk, xn).astype(LOW)
        v_ref[image] = nt(xn, wv).astype(LOW)
        vt = nt(wv, xn).astype(LOW)
        mixed = []
        for head in range(heads):
            span = slice(head * HD, (head + 1) * HD)
            only = jnp.where(head_mask(qt.shape, 0, head), qt, jnp.zeros_like(qt))
            scores = nn(k, only)
            top = jnp.max(scores, axis=0, keepdims=True)
            weights = jnp.exp(scores - top)
            total = jnp.sum(weights, axis=0, keepdims=True)
            mixed.append(nn(vt[span], weights.astype(LOW)) / total)
            lse_ref[image, head:head + 1, :] = top + jnp.log(total)
        ot = jnp.concatenate(mixed, axis=0).astype(LOW)
        ot_ref[image] = ot
        total_of.give(turn, tn(ot, wo))
        for copy in save(image):
            copy.start()

        @pl.when(turn == 0)
        def _():
            spread_up.wait_far(3)

    x1 = (x_ref[me].astype(FULL) + total_of.result()).astype(LOW)
    x1_ref[me] = x1
    values = x1.astype(FULL)
    average = jnp.mean(values, axis=-1, keepdims=True)
    centred = values - average
    scale = lax.rsqrt(jnp.mean(centred * centred, axis=-1, keepdims=True) + eps_norm)
    lanes = lax.broadcasted_iota(jnp.int32, (PATCH, 128), 1)
    pair = jnp.where(lanes == 0, average, jnp.where(lanes == 1, scale, 0.0))
    eye = (8, 128)
    eye = lax.broadcasted_iota(jnp.int32, eye, 0) == lax.broadcasted_iota(jnp.int32, eye, 1)
    eye = jnp.where(eye, 1.0, 0.0)
    stats[me] = lax.dot_general(
        eye, pair, (((1,), (1,)), ((), ())), precision=lax.Precision.HIGHEST,
        preferred_element_type=FULL,
    )
    tell = [
        remote(stats.at[me], stats.at[me], stat_send, stat_recv, lane, "head", other)
        for lane, other in enumerate((near, far, corner))
    ]
    for copy in tell:
        copy.start()
    spread.start_far(0, COLUMN_CUTS)
    spread.start_near(COLUMN_CUTS)
    spread_down.start_far(1)

    for copy in tell:
        copy.wait_recv()

    @pl.loop(0, images)
    def _(image):
        norms[image] = lax.dot_general(
            stats[image], eye, (((0,), (0,)), ((), ())), precision=lax.Precision.HIGHEST,
            preferred_element_type=FULL,
        )

    for cut in range(COLUMN_CUTS):
        wide = sent_ref.shape[1] // COLUMN_CUTS
        span = slice(cut * wide, (cut + 1) * wide)

        def place(image, span=span):
            normal = (x1_ref[image, :, span].astype(FULL) - norms[image, :, 0:1]) * norms[image, :, 1:2]
            low = (normal * norm_ref[2:3, span] + norm_ref[3:4, span]).astype(LOW)
            return nn(picks[image], low)

        total = place(me)
        spread.wait_near(cut, cut + 1)
        total = total + place(near)
        spread.wait_far(cut, cut + 1)
        total = total + place(far)
        spread.wait_corner(cut, cut + 1)
        sent_ref[:, span] = (total + place(corner)).astype(LOW)
        send_rows[cut].start()

    keep = pltpu.make_async_copy(x1_ref, x1_out, keep_sem)
    keep.start()
    for copy in tell:
        copy.wait_send()
    spread.finish(COLUMN_CUTS)
    total_of.finish()
    send_g.finish()
    spread_down.wait_far()
    spread_down.wait_near()
    spread_down.wait_corner()
    spread_down.finish()
    spread_up.wait_near()
    spread_up.wait_corner()
    spread_up.finish()
    for copy in send_rows:
        copy.finish()
    keep.wait()

    @pl.loop(0, images)
    def _(image):
        for copy in save(image) + save_image(image):
            copy.wait()


def front(slots, tiles, patches, cotangent, norm_params, owners, ids, pos, up, down, weight_rows):
    images, _, width = patches.shape
    slot_count = tiles.shape[0] // TILE
    line = slots.count // 2
    most = slots.count * slots.big
    capacity = images * PATCH // slots.count
    rows = weight_rows // 4
    flat, turned = (images, PATCH, rows), (images, rows, PATCH)
    saved = [flat, turned, flat, turned, flat, turned]
    outs = (
        [patches.shape] * 2 + [(4,) + up.shape, (4,) + down.shape] + saved
        + [patches.shape] + [(slots.rows, width)] * 2
    )
    return pl.pallas_call(
        functools.partial(front_kernel, slots, slot_count, capacity),
        in_specs=[INSIDE] * 5 + [ANYWHERE] * 4,
        out_specs=[INSIDE] * 4 + [ANYWHERE] * len(outs),
        out_shape=[
            jax.ShapeDtypeStruct((weight_rows, width), LOW),
            jax.ShapeDtypeStruct((1, weight_rows), jnp.int32),
            jax.ShapeDtypeStruct((images, PATCH, 4), jnp.int32),
            jax.ShapeDtypeStruct((images, 8, PATCH), FULL),
        ]
        + [jax.ShapeDtypeStruct(shape, LOW) for shape in outs],
        scratch_shapes=[pltpu.VMEM(patches.shape, LOW)] * 4
        + [
            pltpu.VMEM(up.shape, FULL), pltpu.VMEM(up.shape, LOW), pltpu.VMEM(down.shape, LOW),
            pltpu.VMEM((slots.count,) + tiles.shape, LOW), pltpu.VMEM((images, most, PATCH), LOW),
            pltpu.VMEM((most, width), FULL), pltpu.VMEM((most, width), LOW),
            pltpu.VMEM((most, width), LOW),
        ]
        + [pltpu.VMEM(shape, LOW) for shape in saved]
        + [
            pltpu.VMEM((images, 8, PATCH), FULL), pltpu.VMEM((images, PATCH, 128), FULL),
            pltpu.SemaphoreType.DMA((3, images)), pltpu.SemaphoreType.DMA((2, images)),
            pltpu.SemaphoreType.DMA((6, images)), pltpu.SemaphoreType.DMA,
            pltpu.SemaphoreType.DMA((3,)), pltpu.SemaphoreType.DMA((3,)),
        ]
        + [pltpu.SemaphoreType.DMA((line,))] * 6
        + image_gather_sems() + [pltpu.SemaphoreType.DMA]
        + image_gather_sems() + [pltpu.SemaphoreType.DMA]
        + image_sum_scratch(PATCH, width) + image_gather_sems()
        + slot_exchange_sems(slots.count) + slot_exchange_sems(slots.count, COLUMN_CUTS),
        compiler_params=params(collective_id=0, has_side_effects=True),
        name="front",
    )(tiles, norm_params, owners, ids, pos, up, down, patches, cotangent)


def backward_kernel(
    experts, slots,
    w_ref, lse_ref, src_ref, norm_ref, small_ref,
    x1g_in, xn_in, hat_in, q_in, qt_in, k_in, kt_in, v_in, ot_in, x_ref, out_rows_ref, down_part,
    owned_ref, small_out, down_first_ref, down_second_ref, input_out, out_back, passed_out,
    x1g_ref, xn_ref, hat_ref, q_ref, qt_ref, k_ref, kt_ref, v_ref, ot_ref, late_ref,
    grad_ref, own_ref, input_ref, padded_ref, load_sems, own_sem, *exchange,
):
    images = x1g_ref.shape[0]
    rows = w_ref.shape[0] // 4
    heads = rows // HD
    total_of = ImageSum(*exchange[:8])
    spread = ImageGather(input_ref, *exchange[8:10])
    back_out = SlotReturn(slots, out_rows_ref, out_back, *exchange[10:14])
    weights_sum = LineScatter(padded_ref, owned_ref, *exchange[14:24])
    down_sum = BlockSum(down_part, *exchange[24:32])
    small_sum = SmallSum(*exchange[32:40])
    late_sum = LateSum(*exchange[40:])
    me, near, far, corner = partners()
    dp_count = slots.count
    streamed = (
        (xn_in, xn_ref), (hat_in, hat_ref), (q_in, q_ref), (qt_in, qt_ref), (k_in, k_ref), (kt_in, kt_ref),
        (v_in, v_ref), (ot_in, ot_ref),
    )

    def load(turn):
        image, slot = total_of.image(turn), lax.rem(turn, 2)
        copies = [
            pltpu.make_async_copy(source.at[image], target.at[slot], load_sems.at[index, slot])
            for index, (source, target) in enumerate(streamed)
        ]
        copies.append(
            pltpu.make_async_copy(x1g_in.at[image], x1g_ref.at[image], load_sems.at[8, slot])
        )
        return copies

    for turn in range(2):
        for copy in load(turn):
            copy.start()
    own = pltpu.make_async_copy(x_ref.at[me], own_ref, own_sem.at[0])
    own.start()
    greet_all((near, far, corner), dp_count)
    small_sum.start(small_ref[...])
    down_sum.start()
    back_out.start()
    down_sum.across()
    half = down_sum.half
    save_passed = pltpu.make_async_copy(
        down_sum.passed.at[pl.ds(0, half)], passed_out, own_sem.at[1]
    )
    save_passed.start()
    late_ref[...] = jnp.zeros_like(late_ref)
    shrink = HD ** (-0.5)
    grad_ref[...] = jnp.zeros_like(grad_ref)

    @pl.loop(0, images)
    def _(turn):
        image, slot = total_of.image(turn), lax.rem(turn, 2)
        for copy in load(turn):
            copy.wait()
        wq, wk, wv, wo = (w_ref[pl.ds(part * rows, rows), :] for part in range(4))
        x1g, xn = x1g_ref[image], xn_ref[slot]
        q, qt, k, kt = q_ref[slot], qt_ref[slot], k_ref[slot], kt_ref[slot]
        v, ot = v_ref[slot], ot_ref[slot]
        do = nt(x1g, wo).astype(LOW)
        dot = nt(wo, x1g).astype(LOW)
        product = dot.astype(FULL) * ot.astype(FULL)
        dqt, dk, dv = [], None, None
        for head in range(heads):
            span = slice(head * HD, (head + 1) * HD)
            zero_t = jnp.zeros_like(qt)
            mask_t = head_mask(qt.shape, 0, head)
            mask = head_mask(q.shape, 1, head)
            scores = nn(k, jnp.where(mask_t, qt, zero_t))
            weights = jnp.exp(scores - lse_ref[image, head:head + 1, :])
            back = nn(v, jnp.where(mask_t, dot, zero_t))
            delta = jnp.sum(product[span], axis=0, keepdims=True)
            score_grad = (weights * (back - delta)).astype(LOW)
            dqt.append(nn(kt[span], score_grad) * shrink)
            dk_one = nn(score_grad, jnp.where(mask, q, jnp.zeros_like(q)))
            dv_one = nn(weights.astype(LOW), jnp.where(mask, do, jnp.zeros_like(do)))
            dk = dk_one if dk is None else dk + dk_one
            dv = dv_one if dv is None else dv + dv_one
        dqt = jnp.concatenate(dqt, axis=0).astype(LOW)
        dk, dv = dk.astype(LOW), dv.astype(LOW)
        part = tn(dqt, wq) + nn(dk, wk) + nn(dv, wv)
        total_of.give(turn, part)
        late_ref[0:1, :] += jnp.sum(part * hat_ref[slot].astype(FULL), axis=0, keepdims=True)
        late_ref[1:2, :] += jnp.sum(part, axis=0, keepdims=True)
        pieces = (nn(dqt, xn), tn(dk, xn), tn(dv, xn), nn(ot, x1g))
        for part, piece in enumerate(pieces):
            grad_ref[pl.ds(part * rows, rows), :] += piece

        @pl.when(turn + 2 < images)
        def _():
            for copy in load(turn + 2):
                copy.start()

        @pl.when(turn == 1)
        def _():
            small_sum.across()

    late_sum.start([late_ref[0:1, :], late_ref[1:2, :]])
    low = grad_ref[...].astype(LOW)
    depth = padded_ref.shape[1]
    parts = min(dp_count, 8)
    cut = dp_count // parts * depth
    for part in range(parts):
        row = lax.broadcasted_iota(jnp.int32, (cut, low.shape[0]), 0) + part * cut
        pick = one_hot(row == src_ref[...])
        block = nn(pick, low).astype(LOW)
        padded_ref[pl.ds(part * (dp_count // parts), dp_count // parts)] = block.reshape(
            dp_count // parts, depth, block.shape[1]
        )
    weights_sum.start()
    small_sum.back()
    own.wait()
    normal, scale = normalise(own_ref[...].astype(FULL))
    back = norm_back(normal, scale, norm_ref[0:1, :], total_of.result())[0]
    input_ref[me] = (x1g_ref[me].astype(FULL) + back).astype(LOW)
    spread.start()
    late_sum.across()
    steps = weights_sum.length

    @pl.loop(0, steps - 1)
    def _(turn):
        weights_sum.step(steps - 1 - turn)

        @pl.when(turn == steps - 2)
        def _():
            spread.wait_far()

    weights_sum.result()
    small_sum.result(small_out)
    late_sum.result(small_out, experts)
    down_sum.result(down_first_ref, down_second_ref)
    spread.wait_near()
    spread.wait_corner()
    keep = pltpu.make_async_copy(input_ref, input_out, own_sem.at[0])
    keep.start()
    back_out.finish()
    spread.finish()
    total_of.finish()
    weights_sum.finish()
    small_sum.finish()
    late_sum.finish()
    down_sum.finish()
    save_passed.wait()
    keep.wait()


def attention_backward(
    experts, slots, depth,
    x1_grad, w, xn, hat, saved, lse, src_row, norm_params, small, patches, out_rows, down_part,
):
    images, _, width = patches.shape
    rows = w.shape[0] // 4
    dp_count = slots.count
    flat, turned = (2, PATCH, rows), (2, rows, PATCH)
    units = down_part.shape[1]
    return pl.pallas_call(
        functools.partial(backward_kernel, experts, slots),
        in_specs=[INSIDE] * 5 + [ANYWHERE] * 12,
        out_specs=[INSIDE] * 4 + [ANYWHERE] * 3,
        out_shape=[
            jax.ShapeDtypeStruct((depth, width), FULL), jax.ShapeDtypeStruct(small.shape, FULL),
            jax.ShapeDtypeStruct((units // 2, width), FULL),
            jax.ShapeDtypeStruct((units // 2, width), FULL),
            jax.ShapeDtypeStruct(patches.shape, LOW),
            jax.ShapeDtypeStruct((dp_count * slots.big, width), LOW),
            jax.ShapeDtypeStruct((units // 2, width), LOW),
        ],
        scratch_shapes=[pltpu.VMEM(patches.shape, LOW)]
        + [pltpu.VMEM((2, PATCH, width), LOW)] * 2
        + [pltpu.VMEM(shape, LOW) for shape in (flat, turned, flat, turned, flat, turned)]
        + [
            pltpu.VMEM((8, width), FULL), pltpu.VMEM(w.shape, FULL), pltpu.VMEM((PATCH, width), LOW),
            pltpu.VMEM(patches.shape, LOW), pltpu.VMEM((dp_count, depth, width), LOW),
            pltpu.SemaphoreType.DMA((9, 2)), pltpu.SemaphoreType.DMA((2,)),
        ]
        + image_sum_scratch(PATCH, width) + image_gather_sems()
        + slot_return_scratch(slots, width)
        + line_scatter_scratch(dp_count, depth, width)
        + block_sum_scratch(units, width)
        + small_sum_scratch(small.shape[0], width, dp_count)
        + late_sum_scratch(width, dp_count),
        compiler_params=params(collective_id=2, has_side_effects=True),
        name="attention_backward",
    )(
        w, lse, src_row, norm_params, small, x1_grad, xn, hat, *saved, patches, out_rows, down_part,
    )


def picked_rows(col, held_ref, start, count):
    lanes = lax.broadcasted_iota(jnp.int32, (col.shape[0], count), 1) + start
    pick = one_hot((lanes == col[:, 0:1]) | (lanes == col[:, 1:2]))
    return nn(pick, held_ref[pl.ds(start, count), :])


def mixed_rows(col, first, second, start):
    count = first.shape[0] + second.shape[0]
    lanes = lax.broadcasted_iota(jnp.int32, (col.shape[0], count), 1) + start
    pick = one_hot((lanes == col[:, 2:3]) | (lanes == col[:, 3:4]))
    return nn(pick, jnp.concatenate([first[...], second[...]], axis=0))


def late_kernel(col_ref, sum_ref, first, second, block_ref):
    start = first.shape[0] + second.shape[0]
    block_ref[0] = (sum_ref[0] + mixed_rows(col_ref[0], first, second, start)).astype(LOW)


def late_stage(col, so_far, held):
    images, _, width = so_far.shape
    wide = lead((1, PATCH, width))
    return pl.pallas_call(
        late_kernel,
        grid=(images,),
        in_specs=[lead((1, PATCH, 4)), wide] + [whole(rows.shape) for rows in held],
        out_specs=wide,
        out_shape=jax.ShapeDtypeStruct(so_far.shape, LOW),
        compiler_params=params(),
        cost_estimate=pl.CostEstimate(
            flops=2 * images * PATCH * sum(rows.size for rows in held),
            bytes_accessed=6 * so_far.size + 2 * sum(rows.size for rows in held), transcendentals=0,
        ),
        name="late_stage",
    )(col, so_far, *held)


def early_kernel(
    col_ref, x1_ref, low_ref, held_own, held_near,
    tile_ref, tile_first, tile_second, tile_grad,
    router_ref, router_first, router_second, norm_ref, norm_first, norm_second, small_ref,
    sum_ref, input_ref, tile_new, tile_first_new, tile_second_new, tile_copy,
    router_new, router_first_new, router_second_new,
    norm_new, norm_first_new, norm_second_new, later_second_new,
):
    sum_ref[0] = x1_ref[0].astype(FULL) + mixed_rows(col_ref[0], held_own, held_near, 0)
    input_ref[0] = low_ref[0].astype(FULL)

    @pl.when(pl.program_id(0) == 0)
    def _():
        new, first, second = adam_update(
            tile_ref[...], tile_first[...], tile_second[...], tile_grad[...],
            rate_attention, decay_factor,
        )
        tile_new[...], tile_first_new[...], tile_second_new[...] = new, first, second
        tile_copy[...] = new.astype(LOW)
        experts = router_ref.shape[0]
        new, first, second = adam_update(
            router_ref[...], router_first[...], router_second[...], small_ref[0:experts, :],
            rate_router, decay_factor,
        )
        router_new[...], router_first_new[...], router_second_new[...] = new, first, second
        new, first, second = adam_update(
            norm_ref[...], norm_first[...], norm_second[...], small_ref[experts:experts + 4, :],
            rate_norm, 0.0,
        )
        norm_new[...], norm_first_new[...] = new, first
        norm_second_new[...], later_second_new[...] = second[0:2], second[2:4]


def early_stage(col, x1, input_low, held, tiles, routers, norms, small):
    images, _, width = x1.shape
    wide = lead((1, PATCH, width))
    tile, router, norm = tiles[0], routers[0], norms[0]
    fixed = [*held, *tiles, *routers, *norms, small]
    full = [tile.shape] * 3 + [tile.shape] + [router.shape] * 3 + [norm.shape] * 2 + [(2, width)] * 2
    kinds = [FULL] * 3 + [LOW] + [FULL] * 7
    return pl.pallas_call(
        early_kernel,
        grid=(images,),
        in_specs=[lead((1, PATCH, 4)), wide, wide] + [whole(array.shape) for array in fixed],
        out_specs=[wide, wide] + [whole(shape) for shape in full],
        out_shape=[jax.ShapeDtypeStruct(x1.shape, FULL), jax.ShapeDtypeStruct(x1.shape, FULL)]
        + [jax.ShapeDtypeStruct(shape, kind) for shape, kind in zip(full, kinds)],
        compiler_params=params(),
        cost_estimate=pl.CostEstimate(
            flops=2 * images * PATCH * sum(rows.size for rows in held),
            bytes_accessed=12 * x1.size + 2 * sum(rows.size for rows in held), transcendentals=0,
        ),
        name="early_stage",
    )(col, x1, input_low, *fixed)


def expert_kernel(
    slots,
    rows_ref, g_ref, router_in, col_ref, norm_ref,
    up_in, down_in, x1_in, cot_in,
    up_grad_ref, small_ref, down_out, out_out, x1g_out,
    router_ref, up_ref, down_ref, og_ref, gate_ref, probs_ref, down_stage, back_ref, act_all,
    held, total, x1_ref, cot_ref, x1g_ref,
    load_sems, save_sems, image_sems, out_sem, *exchange,
):
    images, count = x1_in.shape[0], rows_ref.shape[0]
    out_sum, back_sum = total.at[pl.ds(0, count)], total.at[pl.ds(count, count)]
    up_sum = ImageSum(*exchange[:8])
    back = ReturnGather(slots, back_ref, held, *exchange[8:])
    parts = up_in.shape[0]

    def load(turn):
        part, slot = up_sum.image(turn), lax.rem(turn, 2)
        return (
            pltpu.make_async_copy(up_in.at[part], up_ref.at[slot], load_sems.at[0, slot]),
            pltpu.make_async_copy(down_in.at[part], down_ref.at[slot], load_sems.at[1, slot]),
        )

    def save(turn):
        slot = lax.rem(turn, 2)
        return pltpu.make_async_copy(
            down_stage.at[slot], down_out.at[up_sum.image(turn)], save_sems.at[slot]
        )

    for turn in range(2):
        for copy in load(turn):
            copy.start()
    rows = rows_ref[...]
    experts = router_in.shape[0]
    router_ref[...] = jnp.zeros_like(router_ref)
    router_ref[0:experts, :] = router_in[...]
    lane = lax.broadcasted_iota(jnp.int32, (1, router_ref.shape[0]), 1)
    mine = jnp.where(lane == lax.axis_index("dp"), 1.0, 0.0)
    logits = nt(rows, router_ref[...].astype(LOW)) + jnp.where(lane < experts, 0.0, -1e30)
    top = jnp.max(logits, axis=-1, keepdims=True)
    weights = jnp.exp(logits - top)
    probs = weights / jnp.sum(weights, axis=-1, keepdims=True)
    gate = jnp.sum(probs * mine, axis=-1, keepdims=True)
    probs_ref[...] = probs
    gate_ref[...] = gate
    og_ref[...] = (gate * g_ref[...].astype(FULL)).astype(LOW)
    out_sum[...] = jnp.zeros_like(out_sum)
    back_sum[...] = jnp.zeros_like(back_sum)
    greet_all((back.near, back.far), slots.count)

    later = act_all.shape[0] > 1

    def down_grads(turn, act):
        @pl.when(turn >= 2)
        def _():
            save(turn - 2).wait()

        down_stage[lax.rem(turn, 2)] = tn(act, og_ref[...]).astype(LOW)
        save(turn).start()

    @pl.loop(0, parts)
    def _(turn):
        slot = lax.rem(turn, 2)
        for copy in load(turn):
            copy.wait()
        rows, og = rows_ref[...], og_ref[...]
        up, down = up_ref[slot], down_ref[slot]
        hidden = nn(rows, up)
        slope = (2.0 / jnp.pi) ** 0.5
        square = hidden * hidden
        bend = jnp.tanh(slope * (hidden + 0.044715 * (square * hidden)))
        act = (0.5 * hidden * (1.0 + bend)).astype(LOW)
        out_sum[...] += nn(act, down)
        act_grad = nt(og, down)
        inner = slope * (1.0 + (3.0 * 0.044715) * square)
        curve = 0.5 * (1.0 + bend) + 0.5 * hidden * (1.0 - bend * bend) * inner
        hidden_grad = (curve * act_grad).astype(LOW)
        back_sum[...] += nt(hidden_grad, up)
        up_sum.give(turn, tn(rows, hidden_grad), hold=True)
        if later:
            act_all[turn] = act
        else:
            down_grads(turn, act)

        @pl.when(turn + 2 < parts)
        def _():
            for copy in load(turn + 2):
                copy.start()

    out = out_sum[...].astype(LOW).astype(FULL)
    gate, probs = gate_ref[...], probs_ref[...]
    gate_grad = jnp.sum(g_ref[...].astype(FULL) * out, axis=-1, keepdims=True)
    logit_grad = (gate_grad * (probs * (mine - gate))).astype(LOW)
    plain = back_sum[...].astype(LOW).astype(FULL)
    back_ref[...] = (plain + nn(logit_grad, router_ref[...].astype(LOW))).astype(LOW)
    back.send(0)
    back.send(1)
    back.relay(0)
    small_ref[...] = jnp.zeros_like(small_ref)
    small_ref[0:experts, :] = tn(logit_grad, rows_ref[...])[0:experts]
    back_sum[...] = gate * out
    def image_load(image):
        slot = lax.rem(image, 2)
        return (
            pltpu.make_async_copy(x1_in.at[image], x1_ref.at[slot], image_sems.at[0, slot]),
            pltpu.make_async_copy(cot_in.at[image], cot_ref.at[slot], image_sems.at[1, slot]),
        )

    def image_save(image):
        slot = lax.rem(image, 2)
        return pltpu.make_async_copy(x1g_ref.at[slot], x1g_out.at[image], image_sems.at[2, slot])

    for image in range(2):
        for copy in image_load(image):
            copy.start()

    def relay(phase):
        @pl.loop(max(phase * slots.turns, 1), (phase + 1) * slots.turns)
        def _(shift):
            back.relay(shift)

    ahead = [
        lambda: (relay(0), back.send(2)),
        lambda: (relay(1), back.send(3)),
        lambda: (back.of_phase(0, back.forward), relay(2)),
        lambda: (back.of_phase(1, back.forward), relay(3)),
    ]
    if later:
        for turn in range(parts):
            down_grads(turn, act_all[turn])
            if turn < 3:
                ahead[turn]()
    else:
        for step in ahead[:3]:
            step()
    og_ref[...] = back_sum[...].astype(LOW)
    save_out = pltpu.make_async_copy(og_ref, out_out, out_sem)
    save_out.start()
    total_rows = held.shape[0]
    piece = 3 * 256
    if total_rows % piece:
        piece = slots.phase_rows
    done = 0
    back.of_phase(0, back.rest)
    for phase in range(1, 4):
        if phase == 1:
            ahead[3]()
            up_sum.start_rest()
        else:
            back.of_phase(phase, back.forward)
        back.of_phase(phase, back.rest)
        ready = (phase + 1) * slots.phase_rows
        while done + piece <= ready:
            @pl.loop(0, images)
            def _(image, start=done):
                part = picked_rows(col_ref[image], held, start, piece)
                span = pl.ds(image * PATCH, PATCH)
                if start == 0:
                    total[span] = part
                else:
                    total[span] += part

            done += piece

    back_scale = 1.0 / 4.0

    @pl.loop(0, images)
    def _(image):
        slot = lax.rem(image, 2)
        for copy in image_load(image):
            copy.wait()

        @pl.when(image >= 2)
        def _():
            image_save(image - 2).wait()

        normal, scale = normalise(x1_ref[slot].astype(FULL))
        upstream = total[pl.ds(image * PATCH, PATCH)]
        result, gain_sum, shift_sum = norm_back(normal, scale, norm_ref[2:3, :], upstream)
        x1g_ref[slot] = (cot_ref[slot].astype(FULL) + result).astype(LOW)
        small_ref[experts + 2:experts + 3, :] += gain_sum * back_scale
        small_ref[experts + 3:experts + 4, :] += shift_sum * back_scale
        image_save(image).start()

        @pl.when(image + 2 < images)
        def _():
            for copy in image_load(image + 2):
                copy.start()

    up_grad_ref[...] = up_sum.result()
    back.finish()
    up_sum.finish()
    save_out.wait()
    for turn in range(parts - 2, parts):
        save(turn).wait()
    for image in range(images - 2, images):
        image_save(image).wait()


def expert_stage(slots, rows, g_rows, up, down, router, col, x1, cotangent, norm_params):
    count, width = rows.shape
    parts, _, units = up.shape
    images = x1.shape[0]
    small_rows = -(-(router.shape[0] + 4) // 16) * 16
    lanes = 128
    flat = pltpu.VMEM((count, width), LOW)
    pair = pltpu.VMEM((2, PATCH, width), LOW)
    return pl.pallas_call(
        functools.partial(expert_kernel, slots),
        in_specs=[INSIDE] * 5 + [ANYWHERE] * 4,
        out_specs=[INSIDE] * 2 + [ANYWHERE] * 3,
        out_shape=[
            jax.ShapeDtypeStruct((width, units), FULL),
            jax.ShapeDtypeStruct((small_rows, width), FULL),
            jax.ShapeDtypeStruct(down.shape, LOW),
            jax.ShapeDtypeStruct((count, width), LOW),
            jax.ShapeDtypeStruct(x1.shape, LOW),
        ],
        scratch_shapes=[
            pltpu.VMEM((lanes, width), FULL),
            pltpu.VMEM((2,) + up.shape[1:], LOW), pltpu.VMEM((2,) + down.shape[1:], LOW), flat,
            pltpu.VMEM((count, 1), FULL), pltpu.VMEM((count, lanes), FULL),
            pltpu.VMEM((2, units, width), LOW), flat,
            pltpu.VMEM((parts, count, units) if count <= MOST_KEPT else (1, 16, 128), LOW),
            pltpu.VMEM((4 * slots.phase_rows, width), LOW),
            pltpu.VMEM((max(images * PATCH, 2 * count), width), FULL), pair, pair, pair,
            pltpu.SemaphoreType.DMA((2, 2)), pltpu.SemaphoreType.DMA((2,)),
            pltpu.SemaphoreType.DMA((3, 2)), pltpu.SemaphoreType.DMA,
        ]
        + image_sum_scratch(width, units) + return_gather_sems(slots.count),
        compiler_params=params(collective_id=3, has_side_effects=True),
        name="expert_stage",
    )(
        rows, g_rows, router, col, norm_params, up, down, x1, cotangent,
    )


def body(
    patches, cotangent, expert_ids, slot_pos, owners,
    tile_master, tile_first, tile_second,
    expert_up, up_first, up_second,
    expert_down, down_first, down_second,
    router, router_first, router_second,
    norm_params, norm_first, norm_second,
):
    tok_rows, width = patches.shape
    experts = router.shape[0]
    capacity = tok_rows // experts
    dp_count = lax.axis_size("dp")
    head_count = lax.axis_size("head")
    images = tok_rows // PATCH
    slots = Slots(dp_count, capacity // head_count)
    slot_count = tile_master.shape[0]

    by_image = (images, PATCH, width)
    x_images, g_images = patches.reshape(by_image), cotangent.reshape(by_image)

    def pair_rows(pairs):
        return pairs.T.reshape(2, images, PATCH).transpose(1, 0, 2)

    w, src, col, lse, xn, hat, up_all, down_all, *saved, x1, rows, g_rows = front(
        slots, tile_master.reshape(slot_count * TILE, width), x_images, g_images, norm_params,
        owners, pair_rows(expert_ids), pair_rows(slot_pos), expert_up[0], expert_down[0],
        owners.shape[1] * TILE,
    )
    up_grad, small, down_part, out, x1_grad = expert_stage(
        slots, rows, g_rows, up_all, down_all, router, col, x1, g_images, norm_params
    )
    owned_grad, small, down_half, down_rest, input_low, out_back, passed = attention_backward(
        experts, slots, slot_count * TILE,
        x1_grad, w, xn, hat, saved, lse, src, norm_params, small, x_images, out, down_part,
    )

    def from_head(rows, apart):
        return lax.ppermute(rows, "head", [(at, at ^ apart) for at in range(head_count)])

    out_far = from_head(out_back, 2)
    flat_tiles = (slot_count * TILE, width)
    (
        so_far, input_grad, tile_new, tile_first_new, tile_second_new, tile_copy,
        router_new, router_first_new, router_second_new,
        norm_new, norm_first_new, norm_second_new, later_second_new,
    ) = early_stage(
        col, x1, input_low, [out_back, from_head(out_back, 1)],
        [array.reshape(flat_tiles) for array in (tile_master, tile_first, tile_second)] + [owned_grad],
        [router, router_first, router_second], [norm_params, norm_first, norm_second], small,
    )
    up_new, up_first_new, up_second_new = adam_update(
        expert_up, up_first, up_second, up_grad[None], rate_up, decay_factor
    )
    out_far, so_far, _ = lax.optimization_barrier((out_far, so_far, up_new))
    block_out = late_stage(col, so_far, [out_far, from_head(out_far, 1)])
    passed, block_out = lax.optimization_barrier((from_head(passed, 2), block_out))
    down_half = down_half + passed.astype(FULL)
    down_grad = jnp.concatenate([down_half, down_rest], axis=0)
    tiles = [
        array.reshape(tile_master.shape)
        for array in (tile_new, tile_first_new, tile_second_new, tile_copy)
    ]
    down_new, down_first_new, down_second_new = adam_update(
        expert_down, down_first, down_second, down_grad[None], rate_down, decay_factor
    )
    return (
        block_out.reshape(tok_rows, width),
        input_grad.reshape(tok_rows, width),
        *tiles,
        up_new,
        up_first_new,
        up_second_new,
        up_new.astype(LOW),
        down_new,
        down_first_new,
        down_second_new,
        down_new.astype(LOW),
        router_new,
        router_first_new,
        router_second_new,
        norm_new,
        norm_first_new,
        norm_second_new,
        later_second_new,
    )


def solution(mesh):
    row = P("dp", None)
    tiles = P(("dp", "head"), None, None)
    up = P("dp", None, "head")
    down = P("dp", "head", None)
    in_specs = (
        row, row, row, row, P("head", None), tiles, tiles, tiles,
        up, up, up, down, down, down, P(), P(), P(), P(), P(), P(),
    )
    out_specs = (
        row, row, tiles, tiles, tiles, tiles, up, up, up, up, down, down, down, down,
        P(), P(), P(), P(), P(), P(), P(),
    )
    return jax.shard_map(body, mesh=mesh, in_specs=in_specs, out_specs=out_specs, check_vma=False)
```

```python
import functools

import jax
import jax.numpy as jnp
from jax import lax
from jax.experimental import pallas as pl
from jax.experimental.pallas import tpu as pltpu
from jax.sharding import PartitionSpec as P

HD = 64
PATCH = 576
TILE = 8
STEP = 10

eps_norm = 1e-06
beta_one = 0.9
beta_two = 0.999
adam_eps = 1e-08
rate_attention = 0.12
rate_up = 0.08
rate_down = 0.3
rate_router = 0.05
rate_norm = 0.4
decay_factor = 0.1

LOW = jnp.bfloat16
FULL = jnp.float32
MESH = pl.DeviceIdType.MESH
MOST_KEPT = 640
VMEM_BYTES = 61 * 1024 * 1024


def adam_update(weight, moment_one, moment_two, gradient, step_rate, weight_decay):
    moment_one = beta_one * moment_one + (1.0 - beta_one) * gradient
    moment_two = beta_two * moment_two + (1.0 - beta_two) * gradient * gradient
    fixed_one = moment_one / (1.0 - beta_one**STEP)
    fixed_two = moment_two / (1.0 - beta_two**STEP)
    weight = weight - step_rate * (
        fixed_one / (jnp.sqrt(fixed_two) + adam_eps) + weight_decay * weight
    )
    return (weight, moment_one, moment_two)


def nn(left, right):
    return lax.dot_general(left, right, (((1,), (0,)), ((), ())), preferred_element_type=FULL)


def nt(left, right):
    return lax.dot_general(left, right, (((1,), (1,)), ((), ())), preferred_element_type=FULL)


def tn(left, right):
    return lax.dot_general(left, right, (((0,), (0,)), ((), ())), preferred_element_type=FULL)


def params(**more):
    return pltpu.CompilerParams(vmem_limit_bytes=VMEM_BYTES, **more)


def whole(shape):
    return pl.BlockSpec(shape, lambda *_: (0,) * len(shape))


def lead(shape):
    return pl.BlockSpec(shape, lambda i: (i,) + (0,) * (len(shape) - 1))


def normalise(values):
    average = jnp.mean(values, axis=-1, keepdims=True)
    centred = values - average
    variance = jnp.mean(centred * centred, axis=-1, keepdims=True)
    scale = lax.rsqrt(variance + eps_norm)
    return centred * scale, scale


def norm_back(normal, scale, gain, upstream):
    inner = upstream * gain
    mean_inner = jnp.mean(inner, axis=-1, keepdims=True)
    mean_cross = jnp.mean(inner * normal, axis=-1, keepdims=True)
    result = scale * (inner - mean_inner - normal * mean_cross)
    gain_sum = jnp.sum(upstream * normal, axis=0, keepdims=True)
    shift_sum = jnp.sum(upstream, axis=0, keepdims=True)
    return result, gain_sum, shift_sum


def one_hot(condition):
    return jnp.where(condition, 1.0, 0.0).astype(LOW)


def remote(src, dst, sends, recvs, index, axis, other):
    return pltpu.make_async_remote_copy(
        src_ref=src, dst_ref=dst, send_sem=sends.at[index], recv_sem=recvs.at[index],
        device_id={axis: other}, device_id_type=MESH,
    )


def greet(*others):
    barrier = pltpu.get_barrier_semaphore()
    for axis, other in others:
        pl.semaphore_signal(barrier, inc=1, device_id={axis: other}, device_id_type=MESH)
    pl.semaphore_wait(barrier, len(others))


def partners():
    me = lax.axis_index("head")
    near = me + 1 - 2 * lax.rem(me, 2)
    far = lax.rem(me + 2, 4)
    corner = lax.rem(near + 2, 4)
    return me, near, far, corner


class LineGather:
    def __init__(self, held, up_send, up_recv, down_send, down_recv, pair_send, pair_recv):
        self.held = held
        self.length = held.shape[0] // 2
        self.sems = ((up_send, up_recv), (down_send, down_recv), (pair_send, pair_recv))
        me = lax.axis_index("dp")
        self.place, self.side = me // 2, lax.rem(me, 2)
        self.above = lax.rem(self.place + 1, self.length) * 2 + self.side
        self.below = lax.rem(self.place + self.length - 1, self.length) * 2 + self.side
        self.other = self.place * 2 + 1 - self.side

    def neighbours(self):
        return ("dp", self.above), ("dp", self.below), ("dp", self.other)

    def copy(self, way, origin, side=None):
        index = origin * 2 + (self.side if side is None else side)
        target = (self.above, self.below, self.other)[way]
        block = self.held.at[index]
        return remote(block, block, *self.sems[way], origin, "dp", target)

    def pass_on(self, origin, up, down):
        @pl.when(up & (self.place < self.length - 1))
        def _():
            self.copy(0, origin).start()

        @pl.when(down & (self.place > 0))
        def _():
            self.copy(1, origin).start()

        self.copy(2, origin).start()

    def start(self):
        self.pass_on(self.place, True, True)

    def step(self, k):
        low, high = self.place - k, self.place + k

        @pl.when(low >= 0)
        def _():
            self.copy(0, low).wait_recv()
            self.pass_on(low, True, False)

        @pl.when(high < self.length)
        def _():
            self.copy(1, high).wait_recv()
            self.pass_on(high, False, True)

    def finish(self):
        @pl.loop(0, self.length)
        def _(origin):
            self.copy(2, origin).wait_recv()
            self.copy(2, origin).wait_send()

            @pl.when((origin <= self.place) & (self.place < self.length - 1))
            def _():
                self.copy(0, origin).wait_send()

            @pl.when((origin >= self.place) & (self.place > 0))
            def _():
                self.copy(1, origin).wait_send()


class ImageSum:
    def __init__(self, stage, corner_in, near_in, passed, mine, far_in, sends, recvs):
        self.stage, self.corner_in, self.near_in = stage, corner_in, near_in
        self.passed, self.mine, self.far_in = passed, mine, far_in
        self.sends, self.recvs = sends, recvs
        self.me, self.near, self.far, self.corner = partners()
        self.core = lax.rem(self.me, 2)

    def image(self, turn):
        base = self.me - self.core
        other = lax.rem(base + 2, 4)
        return jnp.where(turn < 2, other, base - 2) + turn

    def to_corner(self):
        return remote(
            self.stage.at[0], self.corner_in, self.sends, self.recvs, 0, "head", self.near
        )

    def to_near(self):
        return remote(
            self.stage.at[1], self.near_in, self.sends, self.recvs, 1, "head", self.near
        )

    def to_far(self, half):
        rows = self.passed.shape[0] // 2
        span = pl.ds(half * rows, rows)
        return remote(
            self.passed.at[span], self.far_in.at[span], self.sends, self.recvs, 2 + half, "head",
            self.far,
        )

    def give(self, turn, part, hold=False):
        theirs = lax.rem(turn, 2) != self.core

        @pl.when((turn < 2) & theirs)
        def _():
            self.stage[0] = part.astype(LOW)
            self.to_corner().start()

        @pl.when((turn >= 2) & theirs)
        def _():
            self.stage[1] = part.astype(LOW)
            self.to_near().start()

        @pl.when((turn < 2) & ~theirs)
        def _():
            self.to_corner().wait_recv()
            self.passed[...] = (part + self.corner_in[...].astype(FULL)).astype(LOW)
            self.to_far(0).start()
            if not hold:
                self.to_far(1).start()

        @pl.when((turn >= 2) & ~theirs)
        def _():
            self.mine[...] = part

    def start_rest(self):
        self.to_far(1).start()

    def result(self):
        self.to_near().wait_recv()
        for half in range(2):
            self.to_far(half).wait_recv()
        return self.mine[...] + self.near_in[...].astype(FULL) + self.far_in[...].astype(FULL)

    def finish(self):
        self.to_corner().wait_send()
        self.to_near().wait_send()
        for half in range(2):
            self.to_far(half).wait_send()


def image_sum_scratch(rows, width):
    block = pltpu.VMEM((rows, width), LOW)
    return [
        pltpu.VMEM((2, rows, width), LOW), block, block, block,
        pltpu.VMEM((rows, width), FULL), block,
        pltpu.SemaphoreType.DMA((4,)), pltpu.SemaphoreType.DMA((4,)),
    ]


class LineScatter:
    def __init__(
        self, blocks, out, pair_in, up_in, down_in, total,
        up_send, up_recv, down_send, down_recv, pair_send, pair_recv,
    ):
        self.blocks, self.out, self.total = blocks, out, total
        self.arrived = (up_in, down_in, pair_in)
        self.sems = ((up_send, up_recv), (down_send, down_recv), (pair_send, pair_recv))
        self.length = blocks.shape[0] // 2
        me = lax.axis_index("dp")
        self.place, self.side = me // 2, lax.rem(me, 2)
        self.targets = (
            lax.rem(self.place + 1, self.length) * 2 + self.side,
            lax.rem(self.place + self.length - 1, self.length) * 2 + self.side,
            self.place * 2 + 1 - self.side,
        )

    def copy(self, way, block):
        source = (
            self.blocks.at[block * 2 + 1 - self.side] if way == 2 else self.total.at[block]
        )
        return remote(
            source, self.arrived[way].at[block], *self.sems[way], block, "dp", self.targets[way]
        )

    def start(self):
        @pl.loop(0, self.length)
        def _(turn):
            distance = self.length - 1 - turn

            @pl.when(self.place + distance < self.length)
            def _():
                self.copy(2, self.place + distance).start()

            @pl.when((self.place >= distance) & (distance > 0))
            def _():
                self.copy(2, self.place - distance).start()

    def pair_sum(self, block):
        self.copy(2, block).wait_recv()
        own = self.blocks[block * 2 + self.side].astype(FULL)
        return own + self.arrived[2][block].astype(FULL)

    def forward(self, way, block, first):
        both = self.pair_sum(block)

        @pl.when(first)
        def _():
            self.total[block] = both.astype(LOW)

        @pl.when(~first)
        def _():
            self.copy(way, block).wait_recv()
            self.total[block] = (both + self.arrived[way][block].astype(FULL)).astype(LOW)

        self.copy(way, block).start()

    def step(self, distance):
        @pl.when(self.place + distance < self.length)
        def _():
            self.forward(0, self.place + distance, self.place == 0)

        @pl.when(self.place >= distance)
        def _():
            self.forward(1, self.place - distance, self.place == self.length - 1)

    def result(self):
        self.out[...] = self.pair_sum(self.place)

        @pl.when(self.place > 0)
        def _():
            self.copy(0, self.place).wait_recv()
            self.out[...] += self.arrived[0][self.place].astype(FULL)

        @pl.when(self.place < self.length - 1)
        def _():
            self.copy(1, self.place).wait_recv()
            self.out[...] += self.arrived[1][self.place].astype(FULL)

    def finish(self):
        @pl.loop(0, self.length)
        def _(block):
            self.copy(2, block).wait_send()

            @pl.when(block > self.place)
            def _():
                self.copy(0, block).wait_send()

            @pl.when(block < self.place)
            def _():
                self.copy(1, block).wait_send()


def line_scatter_scratch(dp_count, rows, width):
    line = dp_count // 2
    return [pltpu.VMEM((line, rows, width), LOW)] * 4 + [pltpu.SemaphoreType.DMA((line,))] * 6


class SmallSum:
    def __init__(self, flat, head_in, dp_in, done, head_send, head_recv, dp_send, dp_recv):
        self.flat, self.head_in, self.dp_in, self.done = flat, head_in, dp_in, done
        self.head_sems, self.dp_sems = (head_send, head_recv), (dp_send, dp_recv)
        self.me, *self.others = partners()
        self.place, self.count = lax.axis_index("dp"), dp_in.shape[0]

    def to_head(self, lane):
        other = self.others[lane]
        return remote(
            self.flat.at[other], self.head_in.at[self.me], *self.head_sems, lane, "head", other
        )

    def back_head(self, lane):
        block = self.done.at[self.me]
        return remote(block, block, *self.head_sems, 3 + lane, "head", self.others[lane])

    def to_dp(self, shift):
        block = self.dp_in.at[self.place]
        other = lax.rem(self.place + shift, self.count)
        return remote(block, block, *self.dp_sems, shift, "dp", other)

    def start(self, value):
        groups, rows, lanes = self.flat.shape
        flat = jnp.concatenate(
            [value[:, at:at + lanes] for at in range(0, value.shape[1], lanes)], axis=0
        )
        for group in range(groups):
            self.flat[group] = flat[group * rows:(group + 1) * rows]
        for lane in range(3):
            self.to_head(lane).start()
        self.head_in[self.me] = self.flat[self.me]

    def across(self):
        for lane in range(3):
            self.to_head(lane).wait_recv()
        total = self.head_in[0]
        for head in range(1, self.head_in.shape[0]):
            total = total + self.head_in[head]
        self.dp_in[self.place] = total

        @pl.loop(1, self.count)
        def _(shift):
            self.to_dp(shift).start()

    def back(self):
        @pl.loop(1, self.count)
        def _(shift):
            self.to_dp(shift).wait_recv()

        total = lax.fori_loop(
            1, self.count, lambda at, so_far: so_far + self.dp_in[at], self.dp_in[0]
        )
        self.done[self.me] = total
        for lane in range(3):
            self.back_head(lane).start()

    def result(self, out):
        for lane in range(3):
            self.back_head(lane).wait_recv()
        flat = jnp.concatenate([self.done[group] for group in range(self.done.shape[0])], axis=0)
        rows, width = out.shape
        lanes = flat.shape[1]
        for at in range(width // lanes):
            out[:, at * lanes:(at + 1) * lanes] = flat[at * rows:(at + 1) * rows]

    def finish(self):
        for lane in range(3):
            self.to_head(lane).wait_send()
            self.back_head(lane).wait_send()

        @pl.loop(1, self.count)
        def _(shift):
            self.to_dp(shift).wait_send()


def small_sum_scratch(rows, width, dp_count):
    block = (rows * width // 128 // 4, 128)
    return [
        pltpu.VMEM((4,) + block, FULL), pltpu.VMEM((4,) + block, FULL),
        pltpu.VMEM((dp_count,) + block, FULL), pltpu.VMEM((4,) + block, FULL),
        pltpu.SemaphoreType.DMA((6,)), pltpu.SemaphoreType.DMA((6,)),
        pltpu.SemaphoreType.DMA((dp_count,)), pltpu.SemaphoreType.DMA((dp_count,)),
    ]


class LateSum:
    def __init__(self, dp_in, head_in, dp_send, dp_recv, head_send, head_recv):
        self.dp_in, self.head_in = dp_in, head_in
        self.dp_sems, self.head_sems = (dp_send, dp_recv), (head_send, head_recv)
        self.me, *self.others = partners()
        self.place, self.count = lax.axis_index("dp"), dp_in.shape[0]

    def to_dp(self, shift):
        block = self.dp_in.at[self.place]
        other = lax.rem(self.place + shift, self.count)
        return remote(block, block, *self.dp_sems, shift, "dp", other)

    def to_head(self, lane):
        block = self.head_in.at[self.me]
        return remote(block, block, *self.head_sems, lane, "head", self.others[lane])

    def start(self, rows):
        lanes = self.dp_in.shape[2]
        cuts = [
            row[:, at:at + lanes] for row in rows for at in range(0, row.shape[1], lanes)
        ]
        cuts += [jnp.zeros_like(cuts[0])] * (self.dp_in.shape[1] - len(cuts))
        self.dp_in[self.place] = jnp.concatenate(cuts, axis=0)

        @pl.loop(1, self.count)
        def _(shift):
            self.to_dp(shift).start()

    def across(self):
        @pl.loop(1, self.count)
        def _(shift):
            self.to_dp(shift).wait_recv()

        self.head_in[self.me] = lax.fori_loop(
            1, self.count, lambda at, so_far: so_far + self.dp_in[at], self.dp_in[0]
        )
        for lane in range(3):
            self.to_head(lane).start()

    def result(self, out, first):
        for lane in range(3):
            self.to_head(lane).wait_recv()
        total = self.head_in[0]
        for head in range(1, self.head_in.shape[0]):
            total = total + self.head_in[head]
        lanes = total.shape[1]
        cuts = out.shape[1] // lanes
        for row in range(2):
            for at in range(cuts):
                piece = total[row * cuts + at:row * cuts + at + 1]
                out[first + row:first + row + 1, at * lanes:(at + 1) * lanes] = piece

    def finish(self):
        for lane in range(3):
            self.to_head(lane).wait_send()

        @pl.loop(1, self.count)
        def _(shift):
            self.to_dp(shift).wait_send()


def late_sum_scratch(width, dp_count):
    block = (-(-2 * width // 128 // 8) * 8, 128)
    return [
        pltpu.VMEM((dp_count,) + block, FULL), pltpu.VMEM((4,) + block, FULL),
        pltpu.SemaphoreType.DMA((dp_count,)), pltpu.SemaphoreType.DMA((dp_count,)),
        pltpu.SemaphoreType.DMA((3,)), pltpu.SemaphoreType.DMA((3,)),
    ]


GATHER_CUTS = 4
COLUMN_CUTS = 3


class ImageGather:
    def __init__(self, held, sends, recvs, own=None, local_sem=None, columns=False):
        self.held, self.sends, self.recvs, self.columns = held, sends, recvs, columns
        self.me, self.near, self.far, self.corner = partners()
        self.own = held.at[self.me] if own is None else own
        self.local = None if own is None else pltpu.make_async_copy(own, held.at[self.me], local_sem)
        self.size = held.shape[1] // GATHER_CUTS
        self.wide = held.shape[2] // COLUMN_CUTS

    def piece(self, lane, cut):
        span = pl.ds(cut * self.size, self.size)
        image = self.far if lane == 2 else self.me
        if self.columns:
            block = self.held.at[image, :, pl.ds(cut * self.wide, self.wide)]
        else:
            block = self.held.at[image, span]
        source = block if self.columns or lane == 2 else self.own.at[span]
        other = self.far if lane == 0 else self.near
        index = lane * GATHER_CUTS + cut
        return remote(source, block, self.sends, self.recvs, index, "head", other)

    def start_far(self, first=0, last=GATHER_CUTS):
        for cut in range(first, last):
            self.piece(0, cut).start()

    def start_near(self, last=GATHER_CUTS):
        for cut in range(last):
            self.piece(1, cut).start()
        if self.local is not None:
            self.local.start()

    def start(self):
        self.start_far()
        self.start_near()

    def wait_near(self, first=0, last=GATHER_CUTS):
        for cut in range(first, last):
            self.piece(1, cut).wait_recv()

    def wait_far(self, first=0, last=GATHER_CUTS):
        for cut in range(first, last):
            self.piece(0, cut).wait_recv()
            self.piece(2, cut).start()

    def wait_corner(self, first=0, last=GATHER_CUTS):
        for cut in range(first, last):
            self.piece(2, cut).wait_recv()

    def finish(self, last=GATHER_CUTS):
        for cut in range(last):
            for lane in range(3):
                self.piece(lane, cut).wait_send()
        if self.local is not None:
            self.local.wait()


def image_gather_sems():
    return [pltpu.SemaphoreType.DMA((3 * GATHER_CUTS,)), pltpu.SemaphoreType.DMA((3 * GATHER_CUTS,))]


class BlockSum:
    def __init__(self, parts, mine, passed, corner_in, near_in, far_in, local_sems, sends, recvs):
        self.mine, self.passed, self.corner_in = mine, passed, corner_in
        self.near_in, self.far_in = near_in, far_in
        me, near, far, corner = partners()
        self.half = far_in.shape[0]
        self.to_corner = remote(parts.at[corner], corner_in, sends, recvs, 0, "head", near)
        self.to_near = remote(parts.at[near], near_in, sends, recvs, 1, "head", near)
        second = passed.at[pl.ds(self.half, self.half)]
        self.to_far = remote(second, far_in, sends, recvs, 2, "head", far)
        self.load_far = pltpu.make_async_copy(parts.at[far], passed, local_sems.at[0])
        self.load_mine = pltpu.make_async_copy(parts.at[me], mine, local_sems.at[1])

    def start(self):
        for copy in (self.to_corner, self.load_far, self.to_near, self.load_mine):
            copy.start()

    def across(self):
        self.load_far.wait()
        self.to_corner.wait_recv()
        both = self.passed[...].astype(FULL) + self.corner_in[...].astype(FULL)
        self.passed[...] = both.astype(LOW)
        self.to_far.start()

    def result(self, first_out, second_out):
        self.load_mine.wait()
        self.to_near.wait_recv()
        self.to_far.wait_recv()
        total = self.mine[...].astype(FULL) + self.near_in[...].astype(FULL)
        first_out[...] = total[:self.half]
        second_out[...] = total[self.half:] + self.far_in[...].astype(FULL)

    def finish(self):
        for copy in (self.to_corner, self.to_near, self.to_far):
            copy.wait_send()


def block_sum_scratch(rows, width):
    return [pltpu.VMEM((rows, width), LOW)] * 4 + [
        pltpu.VMEM((rows // 2, width), LOW),
        pltpu.SemaphoreType.DMA((2,)), pltpu.SemaphoreType.DMA((3,)), pltpu.SemaphoreType.DMA((3,)),
    ]


class Slots:
    def __init__(self, count, share):
        self.count, self.share = count, share
        self.big = -(-share // 16) * 16
        rest = 2 * share - self.big
        self.small = rest if rest > 0 and rest % 16 == 0 else self.big
        self.more = self.big - self.small
        self.both = self.big + self.small
        self.rows = count // 2 * self.both
        self.turns = count // 4
        self.phase_rows = self.turns * 2 * self.both

    def size(self, source, head):
        return self.small + self.more * ((head + source + 1) % 2)

    def packed(self, source, head):
        return (source // 2) * self.both + (source % 2) * self.size(0, head)

    def row(self, source, head, shift):
        first = self.size(source, 0) * (head % 2)
        group = (head // 2) * self.turns * self.both + self.turns * first
        return (
            (shift // self.turns) * self.phase_rows + group
            + (shift % self.turns) * self.size(source, head)
        )

    def holder(self, source, slot):
        pair, within = slot // self.both, slot % self.both
        first = self.size(source, 0)
        second = jnp.where(within >= first, 1, 0)
        return 2 * pair + second, within - second * first

    def span(self, start, extra):
        if extra:
            return pl.ds(pl.multiple_of(start + self.small, 16), self.more)
        return pl.ds(pl.multiple_of(start, 16), self.small)

    def each(self, is_big, make, action):
        getattr(make(False), action)()
        if self.more:
            @pl.when(is_big)
            def _():
                getattr(make(True), action)()


class SlotExchange:
    def __init__(self, slots, sent, rows, sends, recvs, local_sems, cut=None):
        self.slots, self.sent, self.rows = slots, sent, rows
        self.sems, self.local_sems = (sends, recvs), local_sems
        self.place, self.head = lax.axis_index("dp"), lax.axis_index("head")
        wide = sent.shape[1] // COLUMN_CUTS
        self.cut = 0 if cut is None else cut
        self.lanes = pl.ds(0, sent.shape[1]) if cut is None else pl.ds(cut * wide, wide)

    def index(self, shift, extra):
        return 2 * (self.cut * self.slots.count + shift) + int(extra)

    def out(self, shift, action):
        slots = self.slots
        expert = lax.rem(self.place + shift, slots.count)
        mine = slots.size(self.place, self.head)
        at, to = expert * mine, slots.packed(self.place, self.head)
        slots.each(mine > slots.small, lambda extra: remote(
            self.sent.at[slots.span(at, extra), self.lanes], self.rows.at[slots.span(to, extra), self.lanes],
            *self.sems, self.index(shift, extra), "dp", expert,
        ), action)

    def into(self, shift):
        slots = self.slots
        source = lax.rem(self.place + slots.count - shift, slots.count)
        size = slots.size(source, self.head)
        to = slots.packed(source, self.head)
        slots.each(size > slots.small, lambda extra: remote(
            self.sent.at[slots.span(0, extra), self.lanes], self.rows.at[slots.span(to, extra), self.lanes],
            *self.sems, self.index(shift, extra), "dp", source,
        ), "wait_recv")

    def own(self, action):
        slots = self.slots
        mine = slots.size(self.place, self.head)
        at, to = self.place * mine, slots.packed(self.place, self.head)
        slots.each(mine > slots.small, lambda extra: pltpu.make_async_copy(
            self.sent.at[slots.span(at, extra), self.lanes], self.rows.at[slots.span(to, extra), self.lanes],
            self.local_sems.at[2 * self.cut + int(extra)],
        ), action)

    def start(self):
        @pl.loop(1, self.slots.count)
        def _(shift):
            self.out(shift, "start")

        self.own("start")

    def finish(self):
        @pl.loop(1, self.slots.count)
        def _(shift):
            self.into(shift)
            self.out(shift, "wait_send")

        self.own("wait")


class SlotReturn:
    def __init__(self, slots, rows, back, zeros, sends, recvs, local_sems):
        self.slots, self.rows, self.back, self.zeros = slots, rows, back, zeros
        self.sems, self.local_sems = (sends, recvs), local_sems
        self.place, self.head = lax.axis_index("dp"), lax.axis_index("head")
        self.mine = slots.size(self.place, self.head)

    def out(self, shift, action):
        slots = self.slots
        source = lax.rem(self.place + shift, slots.count)
        size = slots.size(source, self.head)
        at, to = slots.packed(source, self.head), shift * size
        slots.each(size > slots.small, lambda extra: remote(
            self.rows.at[slots.span(at, extra)], self.back.at[slots.span(to, extra)],
            *self.sems, 2 * shift + int(extra), "dp", source,
        ), action)

    def into(self, shift):
        slots = self.slots
        expert = lax.rem(self.place + slots.count - shift, slots.count)
        slots.each(self.mine > slots.small, lambda extra: remote(
            self.rows.at[slots.span(0, extra)], self.back.at[slots.span(shift * self.mine, extra)],
            *self.sems, 2 * shift + int(extra), "dp", expert,
        ), "wait_recv")

    def own(self, action):
        slots = self.slots
        at = slots.packed(self.place, self.head)
        slots.each(self.mine > slots.small, lambda extra: pltpu.make_async_copy(
            self.rows.at[slots.span(at, extra)], self.back.at[slots.span(0, extra)],
            self.local_sems.at[int(extra)],
        ), action)

    def blank(self, action):
        slots = self.slots
        if slots.more:
            @pl.when(self.mine == slots.small)
            def _():
                tail = self.back.at[pl.ds(slots.count * slots.small, slots.count * slots.more)]
                copy = pltpu.make_async_copy(self.zeros, tail, self.local_sems.at[2])
                getattr(copy, action)()

    def start(self):
        if self.slots.more:
            self.zeros[...] = jnp.zeros_like(self.zeros)
        self.blank("start")

        @pl.loop(1, self.slots.count)
        def _(shift):
            self.out(shift, "start")

        self.own("start")

    def finish(self):
        @pl.loop(1, self.slots.count)
        def _(shift):
            self.into(shift)
            self.out(shift, "wait_send")

        self.own("wait")
        self.blank("wait")


def slot_return_scratch(slots, width):
    return [pltpu.VMEM((max(slots.count * slots.more, 16), width), LOW)] + [
        pltpu.SemaphoreType.DMA((2 * slots.count,)), pltpu.SemaphoreType.DMA((2 * slots.count,)),
        pltpu.SemaphoreType.DMA((3,)),
    ]


def slot_exchange_sems(count, cuts=1):
    return [
        pltpu.SemaphoreType.DMA((2 * count * cuts,)), pltpu.SemaphoreType.DMA((2 * count * cuts,)),
        pltpu.SemaphoreType.DMA((2 * cuts,)),
    ]


class ReturnGather:
    def __init__(self, slots, rows, held, sends, recvs, local_sems):
        self.slots, self.rows, self.held = slots, rows, held
        self.sems, self.local_sems = (sends, recvs), local_sems
        self.place = lax.axis_index("dp")
        self.me, self.near, self.far, self.corner = partners()

    def out(self, shift, action):
        slots = self.slots
        source = lax.rem(self.place + shift, slots.count)
        size = slots.size(source, self.me)
        at, to = slots.packed(source, self.me), slots.row(source, self.me, shift)
        slots.each(size > slots.small, lambda extra: remote(
            self.rows.at[slots.span(at, extra)], self.held.at[slots.span(to, extra)],
            *self.sems, 2 * shift + int(extra), "dp", source,
        ), action)

    def own(self, action):
        slots = self.slots
        size = slots.size(self.place, self.me)
        at, to = slots.packed(self.place, self.me), slots.row(self.place, self.me, 0)
        slots.each(size > slots.small, lambda extra: pltpu.make_async_copy(
            self.rows.at[slots.span(at, extra)], self.held.at[slots.span(to, extra)],
            self.local_sems.at[int(extra)],
        ), action)

    def block(self, lane, head, shift, axis, other, action):
        slots = self.slots
        size = slots.size(self.place, head)
        to = slots.row(self.place, head, shift)

        def make(extra):
            block = self.held.at[slots.span(to, extra)]
            index = 2 * (lane * slots.count + shift) + int(extra)
            return remote(block, block, *self.sems, index, axis, other)

        slots.each(size > slots.small, make, action)

    def send(self, phase):
        turns = self.slots.turns
        if phase == 0:
            self.own("start")

        @pl.loop(max(phase * turns, 1), (phase + 1) * turns)
        def _(shift):
            self.out(shift, "start")

    def relay(self, shift):
        @pl.when(shift == 0)
        def _():
            self.own("wait")

        @pl.when(shift > 0)
        def _():
            expert = lax.rem(self.place + self.slots.count - shift, self.slots.count)
            self.block(0, self.me, shift, "dp", expert, "wait_recv")

        self.block(1, self.me, shift, "head", self.far, "start")
        self.block(2, self.me, shift, "head", self.near, "start")

    def forward(self, shift):
        self.block(1, self.far, shift, "head", self.far, "wait_recv")
        self.block(3, self.far, shift, "head", self.near, "start")

    def rest(self, shift):
        self.block(2, self.near, shift, "head", self.near, "wait_recv")
        self.block(3, self.corner, shift, "head", self.near, "wait_recv")

    def of_phase(self, phase, action):
        @pl.loop(0, self.slots.turns)
        def _(turn):
            action(phase * self.slots.turns + turn)

    def finish(self):
        @pl.loop(0, self.slots.count)
        def _(shift):
            @pl.when(shift > 0)
            def _():
                self.out(shift, "wait_send")

            self.block(1, self.me, shift, "head", self.far, "wait_send")
            self.block(2, self.me, shift, "head", self.near, "wait_send")
            self.block(3, self.far, shift, "head", self.near, "wait_send")


def return_gather_sems(count):
    return [
        pltpu.SemaphoreType.DMA((8 * count,)), pltpu.SemaphoreType.DMA((8 * count,)),
        pltpu.SemaphoreType.DMA((2,)),
    ]


def greet_all(heads, dp_count):
    barrier = pltpu.get_barrier_semaphore()
    place = lax.axis_index("dp")
    for other in heads:
        pl.semaphore_signal(barrier, inc=1, device_id={"head": other}, device_id_type=MESH)

    @pl.loop(1, dp_count)
    def _(shift):
        other = lax.rem(place + shift, dp_count)
        pl.semaphore_signal(barrier, inc=1, device_id={"dp": other}, device_id_type=MESH)

    pl.semaphore_wait(barrier, len(heads) + dp_count - 1)


ANYWHERE = pl.BlockSpec(memory_space=pl.ANY)
INSIDE = pl.BlockSpec(memory_space=pltpu.VMEM)


def digits(values):
    high = lax.div(values, 64)
    return [high.astype(FULL), (values - high * 64).astype(FULL)]


def digit_weights(shape, digit_axis):
    digit = lax.broadcasted_iota(jnp.int32, shape, digit_axis)
    value = lax.broadcasted_iota(jnp.int32, shape, 1 - digit_axis)
    weight = jnp.where(lax.rem(digit, 2) == 0, 64.0, 1.0)
    return jnp.where(lax.div(digit, 2) == value, weight, 0.0).astype(LOW)


def turned_rows(rows):
    count = rows[0].shape[1]
    parts = [part for row in rows for part in digits(row)]
    parts += [jnp.zeros((1, count), FULL)] * (8 - len(parts))
    spread = jnp.concatenate(parts, axis=0).astype(LOW)
    return tn(spread, digit_weights((8, 128), 0)).astype(jnp.int32)


def turned_column(column):
    lanes = lax.broadcasted_iota(jnp.int32, (column.shape[0], 128), 1)
    high, low = digits(column)
    spread = jnp.where(lanes == 0, high, jnp.where(lanes == 1, low, 0.0)).astype(LOW)
    return nt(digit_weights((8, 128), 1), spread)[0:1].astype(jnp.int32)


def head_mask(shape, axis, head):
    return lax.broadcasted_iota(jnp.int32, shape, axis) // HD == head


def front_kernel(
    slots, slot_count, capacity,
    tile_ref, norm_ref, owner_ref, ids_in, pos_in, up_in, down_in, x_in, g_in,
    w_ref, src_ref, col_back_ref, lse_ref,
    xn_out, hat_out, up_out, down_out, q_out, qt_out, k_out, kt_out, v_out, ot_out, x1_out,
    rows_out, g_rows_out,
    x_ref, g_ref, xn_ref, hat_ref, full_ref, up_low, down_low, held, picks, sent_sum, sent_g, sent_ref,
    q_ref, qt_ref, k_ref, kt_ref, v_ref, ot_ref, stats, norms, ids_ref, pos_ref,
    load_sems, image_sems, save_sems, keep_sem, stat_send, stat_recv, *exchange,
):
    images = x_ref.shape[0]
    for image in range(images):
        lanes = slice(image * PATCH, (image + 1) * PATCH)
        ids_ref[image], pos_ref[image] = ids_in[:, lanes], pos_in[:, lanes]
    x1_ref = g_ref
    gather = LineGather(held, *exchange[:6])
    spread_up = ImageGather(up_out, *exchange[6:8], own=up_low, local_sem=exchange[8])
    spread_down = ImageGather(down_out, *exchange[9:11], own=down_low, local_sem=exchange[11])
    total_of = ImageSum(*exchange[12:20])
    spread = ImageGather(x1_ref, *exchange[20:22], columns=True)
    send_g = SlotExchange(slots, sent_g, g_rows_out, *exchange[22:25])
    send_rows = [
        SlotExchange(slots, sent_ref, rows_out, *exchange[25:], cut=cut) for cut in range(COLUMN_CUTS)
    ]
    head, near, far, corner = partners()
    load_up = pltpu.make_async_copy(up_in, full_ref, load_sems.at[2, 0])
    load_down = pltpu.make_async_copy(down_in, full_ref, load_sems.at[2, 1])
    load_up.start()

    def load_image(image):
        return (
            pltpu.make_async_copy(x_in.at[image], x_ref.at[image], load_sems.at[0, image]),
            pltpu.make_async_copy(g_in.at[image], g_ref.at[image], load_sems.at[1, image]),
        )

    def save_image(image):
        return [
            pltpu.make_async_copy(xn_ref.at[image], xn_out.at[image], image_sems.at[0, image]),
            pltpu.make_async_copy(hat_ref.at[image], hat_out.at[image], image_sems.at[1, image]),
        ]

    kept_refs = (
        (q_ref, q_out), (qt_ref, qt_out), (k_ref, k_out), (kt_ref, kt_out), (v_ref, v_out),
        (ot_ref, ot_out),
    )

    def save(image):
        return [
            pltpu.make_async_copy(ref.at[image], out.at[image], save_sems.at[index, image])
            for index, (ref, out) in enumerate(kept_refs)
        ]

    for image in range(images):
        for copy in load_image(image):
            copy.start()
    me = lax.axis_index("dp")
    held[me] = tile_ref[...].astype(LOW)
    greet_all((near, far, corner), slots.count)
    gather.start()
    load_up.wait()
    up_low[...] = full_ref[...].astype(LOW)
    spread_up.start()
    load_down.start()
    shape = (sent_ref.shape[0], PATCH)
    sent_sum[...] = jnp.zeros_like(sent_sum)
    steps = gather.length - 1

    def image_step(image):
        for copy in load_image(image):
            copy.wait()
        normal, _ = normalise(x_ref[image].astype(FULL))
        hat_ref[image] = normal.astype(LOW)
        xn_ref[image] = (normal * norm_ref[0:1, :] + norm_ref[1:2, :]).astype(LOW)
        for copy in save_image(image):
            copy.start()

        ids, pos = ids_ref[image], pos_ref[image]
        kept = pos < capacity
        holder, within = slots.holder(me, jnp.minimum(pos, capacity - 1))
        sent_at = ids * slots.size(me, head) + within
        sent_at = jnp.where(kept & (holder == head), sent_at, slots.count * slots.big)
        shift = me - ids
        shift = jnp.where(shift < 0, shift + slots.count, shift)
        back_at = jnp.where(kept, slots.row(me, holder, shift) + within + 1, 0)
        other_pair = jnp.where(lax.div(holder, 2) == lax.div(head, 2), 0, 2)
        apart = other_pair + jnp.where(lax.rem(holder, 2) == lax.rem(head, 2), 0, 1)
        out_at = apart * (slots.count * slots.big) + shift * slots.size(me, holder) + within
        out_at = jnp.where(kept, out_at + 1, 0)
        turned = turned_rows([back_at[0:1], back_at[1:2], out_at[0:1], out_at[1:2]])
        col_back_ref[image] = turned[:, 0:4] - 1
        first, second = sent_at[0:1], sent_at[1:2]
        sent_slots = lax.broadcasted_iota(jnp.int32, shape, 0)
        pick = one_hot((sent_slots == first) | (sent_slots == second))
        picks[image] = pick
        sent_sum[...] += nn(pick, g_ref[image])

    @pl.loop(0, max(steps, (images + 1) // 2))
    def _(turn):
        @pl.loop(2 * turn, jnp.minimum(2 * turn + 2, images))
        def _(image):
            image_step(image)

        @pl.when(turn < steps)
        def _():
            gather.step(turn + 1)

        @pl.when(turn == 1)
        def _():
            spread_up.wait_far(0, 1)

    sent_g[...] = sent_sum[...].astype(LOW)
    load_down.wait()
    down_low[...] = full_ref[...].astype(LOW)

    rows = w_ref.shape[0]
    tiles = owner_ref.shape[1]
    row_tile = lax.div(lax.broadcasted_iota(jnp.int32, (rows, tiles), 0), TILE)
    lane_tile = lax.broadcasted_iota(jnp.int32, (rows, tiles), 1)
    owner_rows = jnp.broadcast_to(owner_ref[...].astype(FULL), (8, tiles)).astype(LOW)
    owner = nt(one_hot(lane_tile == row_tile), owner_rows)[:, 0:1].astype(jnp.int32)
    before = (owner_ref[...] == owner) & (lane_tile < row_tile)
    rank = jnp.sum(jnp.where(before, 1.0, 0.0), axis=1, keepdims=True).astype(jnp.int32)
    within = lax.rem(lax.broadcasted_iota(jnp.int32, (rows, 1), 0), TILE)
    src = (owner * slot_count + rank) * TILE + within
    src_ref[...] = turned_column(src)
    spread_up.wait_far(1, 3)
    gather.finish()
    blocks, depth, width = held.shape
    cut = rows // 4
    for part in range(4):
        lanes = lax.broadcasted_iota(jnp.int32, (cut, blocks * depth), 1)
        pick = one_hot(lanes == src[part * cut:(part + 1) * cut])
        block = nn(pick, held[...].reshape(blocks * depth, width))
        w_ref[pl.ds(part * cut, cut), :] = block.astype(LOW)
    spread_down.start_far(0, 1)
    spread_down.start_near()
    send_g.start()
    me = head
    shrink = HD ** (-0.5)

    part_rows = w_ref.shape[0] // 4
    heads = part_rows // HD

    @pl.loop(0, images)
    def _(turn):
        image = total_of.image(turn)
        xn = xn_ref[image]
        wq, wk, wv, wo = (
            w_ref[pl.ds(part * part_rows, part_rows), :] for part in range(4)
        )
        q = (nt(xn, wq) * shrink).astype(LOW)
        q_ref[image] = q
        qt = q.T
        qt_ref[image] = qt
        k = nt(xn, wk).astype(LOW)
        k_ref[image] = k
        kt_ref[image] = k.T
        v = nt(xn, wv).astype(LOW)
        v_ref[image] = v
        vt = v.T
        mixed = []
        for head in range(heads):
            span = slice(head * HD, (head + 1) * HD)
            only = jnp.where(head_mask(qt.shape, 0, head), qt, jnp.zeros_like(qt))
            scores = nn(k, only)
            top = jnp.max(scores, axis=0, keepdims=True)
            weights = jnp.exp(scores - top)
            total = jnp.sum(weights, axis=0, keepdims=True)
            mixed.append(nn(vt[span], weights.astype(LOW)) / total)
            lse_ref[image, head:head + 1, :] = top + jnp.log(total)
        ot = jnp.concatenate(mixed, axis=0).astype(LOW)
        ot_ref[image] = ot
        total_of.give(turn, tn(ot, wo))
        for copy in save(image):
            copy.start()

        @pl.when(turn == 0)
        def _():
            spread_up.wait_far(3)

    x1 = (x_ref[me].astype(FULL) + total_of.result()).astype(LOW)
    x1_ref[me] = x1
    values = x1.astype(FULL)
    average = jnp.mean(values, axis=-1, keepdims=True)
    centred = values - average
    scale = lax.rsqrt(jnp.mean(centred * centred, axis=-1, keepdims=True) + eps_norm)
    lanes = lax.broadcasted_iota(jnp.int32, (PATCH, 128), 1)
    pair = jnp.where(lanes == 0, average, jnp.where(lanes == 1, scale, 0.0))
    eye = (8, 128)
    eye = lax.broadcasted_iota(jnp.int32, eye, 0) == lax.broadcasted_iota(jnp.int32, eye, 1)
    eye = jnp.where(eye, 1.0, 0.0)
    stats[me] = lax.dot_general(
        eye, pair, (((1,), (1,)), ((), ())), precision=lax.Precision.HIGHEST,
        preferred_element_type=FULL,
    )
    tell = [
        remote(stats.at[me], stats.at[me], stat_send, stat_recv, lane, "head", other)
        for lane, other in enumerate((near, far, corner))
    ]
    for copy in tell:
        copy.start()
    spread.start_far(0, COLUMN_CUTS)
    spread.start_near(COLUMN_CUTS)
    spread_down.start_far(1)

    for copy in tell:
        copy.wait_recv()

    @pl.loop(0, images)
    def _(image):
        norms[image] = lax.dot_general(
            stats[image], eye, (((0,), (0,)), ((), ())), precision=lax.Precision.HIGHEST,
            preferred_element_type=FULL,
        )

    for cut in range(COLUMN_CUTS):
        wide = sent_ref.shape[1] // COLUMN_CUTS
        span = slice(cut * wide, (cut + 1) * wide)

        def place(image, span=span):
            normal = (x1_ref[image, :, span].astype(FULL) - norms[image, :, 0:1]) * norms[image, :, 1:2]
            low = (normal * norm_ref[2:3, span] + norm_ref[3:4, span]).astype(LOW)
            return nn(picks[image], low)

        total = place(me)
        spread.wait_near(cut, cut + 1)
        total = total + place(near)
        spread.wait_far(cut, cut + 1)
        total = total + place(far)
        spread.wait_corner(cut, cut + 1)
        sent_ref[:, span] = (total + place(corner)).astype(LOW)
        send_rows[cut].start()

    keep = pltpu.make_async_copy(x1_ref, x1_out, keep_sem)
    keep.start()
    for copy in tell:
        copy.wait_send()
    spread.finish(COLUMN_CUTS)
    total_of.finish()
    send_g.finish()
    spread_down.wait_far()
    spread_down.wait_near()
    spread_down.wait_corner()
    spread_down.finish()
    spread_up.wait_near()
    spread_up.wait_corner()
    spread_up.finish()
    for copy in send_rows:
        copy.finish()
    keep.wait()

    @pl.loop(0, images)
    def _(image):
        for copy in save(image) + save_image(image):
            copy.wait()


def front(slots, tiles, patches, cotangent, norm_params, owners, ids, pos, up, down, weight_rows):
    images, _, width = patches.shape
    slot_count = tiles.shape[0] // TILE
    line = slots.count // 2
    most = slots.count * slots.big
    capacity = images * PATCH // slots.count
    rows = weight_rows // 4
    flat, turned = (images, PATCH, rows), (images, rows, PATCH)
    saved = [flat, turned, flat, turned, flat, turned]
    outs = (
        [patches.shape] * 2 + [(4,) + up.shape, (4,) + down.shape] + saved
        + [patches.shape] + [(slots.rows, width)] * 2
    )
    return pl.pallas_call(
        functools.partial(front_kernel, slots, slot_count, capacity),
        in_specs=[INSIDE] * 5 + [ANYWHERE] * 4,
        out_specs=[INSIDE] * 4 + [ANYWHERE] * len(outs),
        out_shape=[
            jax.ShapeDtypeStruct((weight_rows, width), LOW),
            jax.ShapeDtypeStruct((1, weight_rows), jnp.int32),
            jax.ShapeDtypeStruct((images, PATCH, 4), jnp.int32),
            jax.ShapeDtypeStruct((images, 8, PATCH), FULL),
        ]
        + [jax.ShapeDtypeStruct(shape, LOW) for shape in outs],
        scratch_shapes=[pltpu.VMEM(patches.shape, LOW)] * 4
        + [
            pltpu.VMEM(up.shape, FULL), pltpu.VMEM(up.shape, LOW), pltpu.VMEM(down.shape, LOW),
            pltpu.VMEM((slots.count,) + tiles.shape, LOW), pltpu.VMEM((images, most, PATCH), LOW),
            pltpu.VMEM((most, width), FULL), pltpu.VMEM((most, width), LOW),
            pltpu.VMEM((most, width), LOW),
        ]
        + [pltpu.VMEM(shape, LOW) for shape in saved]
        + [
            pltpu.VMEM((images, 8, PATCH), FULL), pltpu.VMEM((images, PATCH, 128), FULL),
            pltpu.VMEM((images, 2, PATCH), jnp.int32), pltpu.VMEM((images, 2, PATCH), jnp.int32),
            pltpu.SemaphoreType.DMA((3, images)), pltpu.SemaphoreType.DMA((2, images)),
            pltpu.SemaphoreType.DMA((6, images)), pltpu.SemaphoreType.DMA,
            pltpu.SemaphoreType.DMA((3,)), pltpu.SemaphoreType.DMA((3,)),
        ]
        + [pltpu.SemaphoreType.DMA((line,))] * 6
        + image_gather_sems() + [pltpu.SemaphoreType.DMA]
        + image_gather_sems() + [pltpu.SemaphoreType.DMA]
        + image_sum_scratch(PATCH, width) + image_gather_sems()
        + slot_exchange_sems(slots.count) + slot_exchange_sems(slots.count, COLUMN_CUTS),
        compiler_params=params(collective_id=0, has_side_effects=True),
        name="front",
    )(tiles, norm_params, owners, ids, pos, up, down, patches, cotangent)


def backward_kernel(
    experts, slots,
    w_ref, lse_ref, src_ref, norm_ref, small_ref,
    x1g_in, xn_in, hat_in, q_in, qt_in, k_in, kt_in, v_in, ot_in, x_ref, out_rows_ref, down_part,
    owned_ref, small_out, down_first_ref, down_second_ref, input_out, out_back, passed_out,
    x1g_ref, xn_ref, hat_ref, q_ref, qt_ref, k_ref, kt_ref, v_ref, ot_ref, late_ref,
    grad_ref, own_ref, input_ref, padded_ref, load_sems, own_sem, *exchange,
):
    images = x1g_ref.shape[0]
    rows = w_ref.shape[0] // 4
    heads = rows // HD
    total_of = ImageSum(*exchange[:8])
    spread = ImageGather(input_ref, *exchange[8:10])
    back_out = SlotReturn(slots, out_rows_ref, out_back, *exchange[10:14])
    weights_sum = LineScatter(padded_ref, owned_ref, *exchange[14:24])
    down_sum = BlockSum(down_part, *exchange[24:32])
    small_sum = SmallSum(*exchange[32:40])
    late_sum = LateSum(*exchange[40:])
    me, near, far, corner = partners()
    dp_count = slots.count
    streamed = (
        (xn_in, xn_ref), (hat_in, hat_ref), (q_in, q_ref), (qt_in, qt_ref), (k_in, k_ref), (kt_in, kt_ref),
        (v_in, v_ref), (ot_in, ot_ref),
    )

    def load(turn):
        image, slot = total_of.image(turn), lax.rem(turn, 2)
        copies = [
            pltpu.make_async_copy(source.at[image], target.at[slot], load_sems.at[index, slot])
            for index, (source, target) in enumerate(streamed)
        ]
        copies.append(
            pltpu.make_async_copy(x1g_in.at[image], x1g_ref.at[image], load_sems.at[8, slot])
        )
        return copies

    for turn in range(2):
        for copy in load(turn):
            copy.start()
    own = pltpu.make_async_copy(x_ref.at[me], own_ref, own_sem.at[0])
    own.start()
    greet_all((near, far, corner), dp_count)
    small_sum.start(small_ref[...])
    down_sum.start()
    back_out.start()
    half = down_sum.half
    save_passed = pltpu.make_async_copy(
        down_sum.passed.at[pl.ds(0, half)], passed_out, own_sem.at[1]
    )
    late_ref[...] = jnp.zeros_like(late_ref)
    shrink = HD ** (-0.5)
    grad_ref[...] = jnp.zeros_like(grad_ref)

    @pl.loop(0, images)
    def _(turn):
        image, slot = total_of.image(turn), lax.rem(turn, 2)
        for copy in load(turn):
            copy.wait()
        wq, wk, wv, wo = (w_ref[pl.ds(part * rows, rows), :] for part in range(4))
        x1g, xn = x1g_ref[image], xn_ref[slot]
        q, qt, k, kt = q_ref[slot], qt_ref[slot], k_ref[slot], kt_ref[slot]
        v, ot = v_ref[slot], ot_ref[slot]
        do = nt(x1g, wo).astype(LOW)
        dot = do.T
        product = dot.astype(FULL) * ot.astype(FULL)
        dqt, dk, dv = [], None, None
        for head in range(heads):
            span = slice(head * HD, (head + 1) * HD)
            zero_t = jnp.zeros_like(qt)
            mask_t = head_mask(qt.shape, 0, head)
            mask = head_mask(q.shape, 1, head)
            scores = nn(k, jnp.where(mask_t, qt, zero_t))
            weights = jnp.exp(scores - lse_ref[image, head:head + 1, :])
            back = nn(v, jnp.where(mask_t, dot, zero_t))
            delta = jnp.sum(product[span], axis=0, keepdims=True)
            score_grad = (weights * (back - delta)).astype(LOW)
            dqt.append(nn(kt[span], score_grad) * shrink)
            dk_one = nn(score_grad, jnp.where(mask, q, jnp.zeros_like(q)))
            dv_one = nn(weights.astype(LOW), jnp.where(mask, do, jnp.zeros_like(do)))
            dk = dk_one if dk is None else dk + dk_one
            dv = dv_one if dv is None else dv + dv_one
        dqt = jnp.concatenate(dqt, axis=0).astype(LOW)
        dk, dv = dk.astype(LOW), dv.astype(LOW)
        part = tn(dqt, wq) + nn(dk, wk) + nn(dv, wv)
        total_of.give(turn, part)
        late_ref[0:1, :] += jnp.sum(part * hat_ref[slot].astype(FULL), axis=0, keepdims=True)
        late_ref[1:2, :] += jnp.sum(part, axis=0, keepdims=True)
        three = jnp.concatenate([dqt, dk.T, dv.T], axis=0)
        grad_ref[pl.ds(0, 3 * rows), :] += nn(three, xn)
        grad_ref[pl.ds(3 * rows, rows), :] += nn(ot, x1g)

        @pl.when(turn + 2 < images)
        def _():
            for copy in load(turn + 2):
                copy.start()

        @pl.when(turn == 0)
        def _():
            down_sum.across()
            save_passed.start()

        @pl.when(turn == 1)
        def _():
            small_sum.across()

    late_sum.start([late_ref[0:1, :], late_ref[1:2, :]])
    low = grad_ref[...].astype(LOW)
    depth = padded_ref.shape[1]
    parts = min(dp_count, 8)
    cut = dp_count // parts * depth
    for part in range(parts):
        row = lax.broadcasted_iota(jnp.int32, (cut, low.shape[0]), 0) + part * cut
        pick = one_hot(row == src_ref[...])
        block = nn(pick, low).astype(LOW)
        padded_ref[pl.ds(part * (dp_count // parts), dp_count // parts)] = block.reshape(
            dp_count // parts, depth, block.shape[1]
        )
    weights_sum.start()
    small_sum.back()
    own.wait()
    normal, scale = normalise(own_ref[...].astype(FULL))
    back = norm_back(normal, scale, norm_ref[0:1, :], total_of.result())[0]
    input_ref[me] = (x1g_ref[me].astype(FULL) + back).astype(LOW)
    spread.start()
    late_sum.across()
    steps = weights_sum.length

    @pl.loop(0, steps - 1)
    def _(turn):
        weights_sum.step(steps - 1 - turn)

        @pl.when(turn == steps - 2)
        def _():
            spread.wait_far()

    weights_sum.result()
    small_sum.result(small_out)
    late_sum.result(small_out, experts)
    down_sum.result(down_first_ref, down_second_ref)
    spread.wait_near()
    spread.wait_corner()
    keep = pltpu.make_async_copy(input_ref, input_out, own_sem.at[0])
    keep.start()
    back_out.finish()
    spread.finish()
    total_of.finish()
    weights_sum.finish()
    small_sum.finish()
    late_sum.finish()
    down_sum.finish()
    save_passed.wait()
    keep.wait()


def attention_backward(
    experts, slots, depth,
    x1_grad, w, xn, hat, saved, lse, src_row, norm_params, small, patches, out_rows, down_part,
):
    images, _, width = patches.shape
    rows = w.shape[0] // 4
    dp_count = slots.count
    flat, turned = (2, PATCH, rows), (2, rows, PATCH)
    units = down_part.shape[1]
    return pl.pallas_call(
        functools.partial(backward_kernel, experts, slots),
        in_specs=[INSIDE] * 5 + [ANYWHERE] * 12,
        out_specs=[INSIDE] * 4 + [ANYWHERE] * 3,
        out_shape=[
            jax.ShapeDtypeStruct((depth, width), FULL), jax.ShapeDtypeStruct(small.shape, FULL),
            jax.ShapeDtypeStruct((units // 2, width), FULL),
            jax.ShapeDtypeStruct((units // 2, width), FULL),
            jax.ShapeDtypeStruct(patches.shape, LOW),
            jax.ShapeDtypeStruct((dp_count * slots.big, width), LOW),
            jax.ShapeDtypeStruct((units // 2, width), LOW),
        ],
        scratch_shapes=[pltpu.VMEM(patches.shape, LOW)]
        + [pltpu.VMEM((2, PATCH, width), LOW)] * 2
        + [pltpu.VMEM(shape, LOW) for shape in (flat, turned, flat, turned, flat, turned)]
        + [
            pltpu.VMEM((8, width), FULL), pltpu.VMEM(w.shape, FULL), pltpu.VMEM((PATCH, width), LOW),
            pltpu.VMEM(patches.shape, LOW), pltpu.VMEM((dp_count, depth, width), LOW),
            pltpu.SemaphoreType.DMA((9, 2)), pltpu.SemaphoreType.DMA((2,)),
        ]
        + image_sum_scratch(PATCH, width) + image_gather_sems()
        + slot_return_scratch(slots, width)
        + line_scatter_scratch(dp_count, depth, width)
        + block_sum_scratch(units, width)
        + small_sum_scratch(small.shape[0], width, dp_count)
        + late_sum_scratch(width, dp_count),
        compiler_params=params(collective_id=2, has_side_effects=True),
        name="attention_backward",
    )(
        w, lse, src_row, norm_params, small, x1_grad, xn, hat, *saved, patches, out_rows, down_part,
    )


def picked_rows(col, held_ref, start, count):
    lanes = lax.broadcasted_iota(jnp.int32, (col.shape[0], count), 1) + start
    pick = one_hot((lanes == col[:, 0:1]) | (lanes == col[:, 1:2]))
    return nn(pick, held_ref[pl.ds(start, count), :])


def mixed_rows(col, first, second, start):
    count = first.shape[0] + second.shape[0]
    lanes = lax.broadcasted_iota(jnp.int32, (col.shape[0], count), 1) + start
    pick = one_hot((lanes == col[:, 2:3]) | (lanes == col[:, 3:4]))
    return nn(pick, jnp.concatenate([first[...], second[...]], axis=0))


def late_kernel(col_ref, sum_ref, first, second, block_ref):
    start = first.shape[0] + second.shape[0]
    block_ref[0] = (sum_ref[0] + mixed_rows(col_ref[0], first, second, start)).astype(LOW)


def late_stage(col, so_far, held):
    images, _, width = so_far.shape
    wide = lead((1, PATCH, width))
    return pl.pallas_call(
        late_kernel,
        grid=(images,),
        in_specs=[lead((1, PATCH, 4)), wide] + [whole(rows.shape) for rows in held],
        out_specs=wide,
        out_shape=jax.ShapeDtypeStruct(so_far.shape, LOW),
        compiler_params=params(),
        cost_estimate=pl.CostEstimate(
            flops=2 * images * PATCH * sum(rows.size for rows in held),
            bytes_accessed=6 * so_far.size + 2 * sum(rows.size for rows in held), transcendentals=0,
        ),
        name="late_stage",
    )(col, so_far, *held)


def early_kernel(
    col_ref, x1_ref, low_ref, held_own, held_near,
    tile_ref, tile_first, tile_second, tile_grad,
    router_ref, router_first, router_second, norm_ref, norm_first, norm_second, small_ref,
    sum_ref, input_ref, tile_new, tile_first_new, tile_second_new, tile_copy,
    router_new, router_first_new, router_second_new,
    norm_new, norm_first_new, norm_second_new, later_second_new,
):
    sum_ref[0] = x1_ref[0].astype(FULL) + mixed_rows(col_ref[0], held_own, held_near, 0)
    input_ref[0] = low_ref[0].astype(FULL)

    @pl.when(pl.program_id(0) == 0)
    def _():
        new, first, second = adam_update(
            tile_ref[...], tile_first[...], tile_second[...], tile_grad[...],
            rate_attention, decay_factor,
        )
        tile_new[...], tile_first_new[...], tile_second_new[...] = new, first, second
        tile_copy[...] = new.astype(LOW)
        experts = router_ref.shape[0]
        new, first, second = adam_update(
            router_ref[...], router_first[...], router_second[...], small_ref[0:experts, :],
            rate_router, decay_factor,
        )
        router_new[...], router_first_new[...], router_second_new[...] = new, first, second
        new, first, second = adam_update(
            norm_ref[...], norm_first[...], norm_second[...], small_ref[experts:experts + 4, :],
            rate_norm, 0.0,
        )
        norm_new[...], norm_first_new[...] = new, first
        norm_second_new[...], later_second_new[...] = second[0:2], second[2:4]


def early_stage(col, x1, input_low, held, tiles, routers, norms, small):
    images, _, width = x1.shape
    wide = lead((1, PATCH, width))
    tile, router, norm = tiles[0], routers[0], norms[0]
    fixed = [*held, *tiles, *routers, *norms, small]
    full = [tile.shape] * 3 + [tile.shape] + [router.shape] * 3 + [norm.shape] * 2 + [(2, width)] * 2
    kinds = [FULL] * 3 + [LOW] + [FULL] * 7
    return pl.pallas_call(
        early_kernel,
        grid=(images,),
        in_specs=[lead((1, PATCH, 4)), wide, wide] + [whole(array.shape) for array in fixed],
        out_specs=[wide, wide] + [whole(shape) for shape in full],
        out_shape=[jax.ShapeDtypeStruct(x1.shape, FULL), jax.ShapeDtypeStruct(x1.shape, FULL)]
        + [jax.ShapeDtypeStruct(shape, kind) for shape, kind in zip(full, kinds)],
        compiler_params=params(),
        cost_estimate=pl.CostEstimate(
            flops=2 * images * PATCH * sum(rows.size for rows in held),
            bytes_accessed=12 * x1.size + 2 * sum(rows.size for rows in held), transcendentals=0,
        ),
        name="early_stage",
    )(col, x1, input_low, *fixed)


def expert_kernel(
    slots,
    rows_ref, g_ref, router_in, col_ref, norm_ref,
    up_in, down_in, x1_in, cot_in,
    up_grad_ref, small_ref, down_out, out_out, x1g_out,
    router_ref, up_ref, down_ref, og_ref, gate_ref, probs_ref, down_stage, back_ref, act_all,
    held, total, x1_ref, cot_ref, x1g_ref,
    load_sems, save_sems, image_sems, out_sem, *exchange,
):
    images, count = x1_in.shape[0], rows_ref.shape[0]
    out_sum, back_sum = total.at[pl.ds(0, count)], total.at[pl.ds(count, count)]
    up_sum = ImageSum(*exchange[:8])
    back = ReturnGather(slots, back_ref, held, *exchange[8:])
    parts = up_in.shape[0]

    def load(turn):
        part, slot = up_sum.image(turn), lax.rem(turn, 2)
        return (
            pltpu.make_async_copy(up_in.at[part], up_ref.at[slot], load_sems.at[0, slot]),
            pltpu.make_async_copy(down_in.at[part], down_ref.at[slot], load_sems.at[1, slot]),
        )

    def save(turn):
        slot = lax.rem(turn, 2)
        return pltpu.make_async_copy(
            down_stage.at[slot], down_out.at[up_sum.image(turn)], save_sems.at[slot]
        )

    for turn in range(2):
        for copy in load(turn):
            copy.start()
    rows = rows_ref[...]
    experts = router_in.shape[0]
    router_ref[...] = jnp.zeros_like(router_ref)
    router_ref[0:experts, :] = router_in[...]
    lane = lax.broadcasted_iota(jnp.int32, (1, router_ref.shape[0]), 1)
    mine = jnp.where(lane == lax.axis_index("dp"), 1.0, 0.0)
    logits = nt(rows, router_ref[...].astype(LOW)) + jnp.where(lane < experts, 0.0, -1e30)
    top = jnp.max(logits, axis=-1, keepdims=True)
    weights = jnp.exp(logits - top)
    probs = weights / jnp.sum(weights, axis=-1, keepdims=True)
    gate = jnp.sum(probs * mine, axis=-1, keepdims=True)
    probs_ref[...] = probs
    gate_ref[...] = gate
    og_ref[...] = (gate * g_ref[...].astype(FULL)).astype(LOW)
    out_sum[...] = jnp.zeros_like(out_sum)
    back_sum[...] = jnp.zeros_like(back_sum)
    greet_all((back.near, back.far), slots.count)

    later = act_all.shape[0] > 1

    def down_grads(turn, act):
        @pl.when(turn >= 2)
        def _():
            save(turn - 2).wait()

        down_stage[lax.rem(turn, 2)] = tn(act, og_ref[...]).astype(LOW)
        save(turn).start()

    @pl.loop(0, parts)
    def _(turn):
        slot = lax.rem(turn, 2)
        for copy in load(turn):
            copy.wait()
        rows, og = rows_ref[...], og_ref[...]
        up, down = up_ref[slot], down_ref[slot]
        hidden = nn(rows, up)
        slope = (2.0 / jnp.pi) ** 0.5
        square = hidden * hidden
        bend = jnp.tanh(slope * (hidden + 0.044715 * (square * hidden)))
        act = (0.5 * hidden * (1.0 + bend)).astype(LOW)
        out_sum[...] += nn(act, down)
        act_grad = nt(og, down)
        inner = slope * (1.0 + (3.0 * 0.044715) * square)
        curve = 0.5 * (1.0 + bend) + 0.5 * hidden * (1.0 - bend * bend) * inner
        hidden_grad = (curve * act_grad).astype(LOW)
        back_sum[...] += nt(hidden_grad, up)
        up_sum.give(turn, tn(rows, hidden_grad), hold=True)
        if later:
            act_all[turn] = act
        else:
            down_grads(turn, act)

        @pl.when(turn + 2 < parts)
        def _():
            for copy in load(turn + 2):
                copy.start()

    out = out_sum[...].astype(LOW).astype(FULL)
    gate, probs = gate_ref[...], probs_ref[...]
    gate_grad = jnp.sum(g_ref[...].astype(FULL) * out, axis=-1, keepdims=True)
    logit_grad = (gate_grad * (probs * (mine - gate))).astype(LOW)
    plain = back_sum[...].astype(LOW).astype(FULL)
    back_ref[...] = (plain + nn(logit_grad, router_ref[...].astype(LOW))).astype(LOW)
    back.send(0)
    back.send(1)
    back.relay(0)
    small_ref[...] = jnp.zeros_like(small_ref)
    small_ref[0:experts, :] = tn(logit_grad, rows_ref[...])[0:experts]
    back_sum[...] = gate * out
    def image_load(image):
        slot = lax.rem(image, 2)
        return (
            pltpu.make_async_copy(x1_in.at[image], x1_ref.at[slot], image_sems.at[0, slot]),
            pltpu.make_async_copy(cot_in.at[image], cot_ref.at[slot], image_sems.at[1, slot]),
        )

    def image_save(image):
        slot = lax.rem(image, 2)
        return pltpu.make_async_copy(x1g_ref.at[slot], x1g_out.at[image], image_sems.at[2, slot])

    for image in range(2):
        for copy in image_load(image):
            copy.start()

    def relay(phase):
        @pl.loop(max(phase * slots.turns, 1), (phase + 1) * slots.turns)
        def _(shift):
            back.relay(shift)

    ahead = [
        lambda: (relay(0), back.send(2)),
        lambda: (relay(1), back.send(3)),
        lambda: (back.of_phase(0, back.forward), relay(2)),
        lambda: (back.of_phase(1, back.forward), relay(3)),
    ]
    if later:
        for turn in range(parts):
            down_grads(turn, act_all[turn])
            if turn < 3:
                ahead[turn]()
    else:
        for step in ahead[:3]:
            step()
    og_ref[...] = back_sum[...].astype(LOW)
    save_out = pltpu.make_async_copy(og_ref, out_out, out_sem)
    save_out.start()
    total_rows = held.shape[0]
    piece = 3 * 256
    if total_rows % piece:
        piece = slots.phase_rows
    done = 0
    back.of_phase(0, back.rest)
    for phase in range(1, 4):
        if phase == 1:
            ahead[3]()
            up_sum.start_rest()
        else:
            back.of_phase(phase, back.forward)
        back.of_phase(phase, back.rest)
        ready = (phase + 1) * slots.phase_rows
        while done + piece <= ready:
            @pl.loop(0, images)
            def _(image, start=done):
                part = picked_rows(col_ref[image], held, start, piece)
                span = pl.ds(image * PATCH, PATCH)
                if start == 0:
                    total[span] = part
                else:
                    total[span] += part

            done += piece

    back_scale = 1.0 / 4.0

    @pl.loop(0, images)
    def _(image):
        slot = lax.rem(image, 2)
        for copy in image_load(image):
            copy.wait()

        @pl.when(image >= 2)
        def _():
            image_save(image - 2).wait()

        normal, scale = normalise(x1_ref[slot].astype(FULL))
        upstream = total[pl.ds(image * PATCH, PATCH)]
        result, gain_sum, shift_sum = norm_back(normal, scale, norm_ref[2:3, :], upstream)
        x1g_ref[slot] = (cot_ref[slot].astype(FULL) + result).astype(LOW)
        small_ref[experts + 2:experts + 3, :] += gain_sum * back_scale
        small_ref[experts + 3:experts + 4, :] += shift_sum * back_scale
        image_save(image).start()

        @pl.when(image + 2 < images)
        def _():
            for copy in image_load(image + 2):
                copy.start()

    up_grad_ref[...] = up_sum.result()
    back.finish()
    up_sum.finish()
    save_out.wait()
    for turn in range(parts - 2, parts):
        save(turn).wait()
    for image in range(images - 2, images):
        image_save(image).wait()


def expert_stage(slots, rows, g_rows, up, down, router, col, x1, cotangent, norm_params):
    count, width = rows.shape
    parts, _, units = up.shape
    images = x1.shape[0]
    small_rows = -(-(router.shape[0] + 4) // 16) * 16
    lanes = 128
    flat = pltpu.VMEM((count, width), LOW)
    pair = pltpu.VMEM((2, PATCH, width), LOW)
    return pl.pallas_call(
        functools.partial(expert_kernel, slots),
        in_specs=[INSIDE] * 5 + [ANYWHERE] * 4,
        out_specs=[INSIDE] * 2 + [ANYWHERE] * 3,
        out_shape=[
            jax.ShapeDtypeStruct((width, units), FULL),
            jax.ShapeDtypeStruct((small_rows, width), FULL),
            jax.ShapeDtypeStruct(down.shape, LOW),
            jax.ShapeDtypeStruct((count, width), LOW),
            jax.ShapeDtypeStruct(x1.shape, LOW),
        ],
        scratch_shapes=[
            pltpu.VMEM((lanes, width), FULL),
            pltpu.VMEM((2,) + up.shape[1:], LOW), pltpu.VMEM((2,) + down.shape[1:], LOW), flat,
            pltpu.VMEM((count, 1), FULL), pltpu.VMEM((count, lanes), FULL),
            pltpu.VMEM((2, units, width), LOW), flat,
            pltpu.VMEM((parts, count, units) if count <= MOST_KEPT else (1, 16, 128), LOW),
            pltpu.VMEM((4 * slots.phase_rows, width), LOW),
            pltpu.VMEM((max(images * PATCH, 2 * count), width), FULL), pair, pair, pair,
            pltpu.SemaphoreType.DMA((2, 2)), pltpu.SemaphoreType.DMA((2,)),
            pltpu.SemaphoreType.DMA((3, 2)), pltpu.SemaphoreType.DMA,
        ]
        + image_sum_scratch(width, units) + return_gather_sems(slots.count),
        compiler_params=params(collective_id=3, has_side_effects=True),
        name="expert_stage",
    )(
        rows, g_rows, router, col, norm_params, up, down, x1, cotangent,
    )


def body(
    patches, cotangent, expert_ids, slot_pos, owners,
    tile_master, tile_first, tile_second,
    expert_up, up_first, up_second,
    expert_down, down_first, down_second,
    router, router_first, router_second,
    norm_params, norm_first, norm_second,
):
    tok_rows, width = patches.shape
    experts = router.shape[0]
    capacity = tok_rows // experts
    dp_count = lax.axis_size("dp")
    head_count = lax.axis_size("head")
    images = tok_rows // PATCH
    slots = Slots(dp_count, capacity // head_count)
    slot_count = tile_master.shape[0]

    by_image = (images, PATCH, width)
    x_images, g_images = patches.reshape(by_image), cotangent.reshape(by_image)
    w, src, col, lse, xn, hat, up_all, down_all, *saved, x1, rows, g_rows = front(
        slots, tile_master.reshape(slot_count * TILE, width), x_images, g_images, norm_params,
        owners, expert_ids.T, slot_pos.T, expert_up[0], expert_down[0],
        owners.shape[1] * TILE,
    )
    up_grad, small, down_part, out, x1_grad = expert_stage(
        slots, rows, g_rows, up_all, down_all, router, col, x1, g_images, norm_params
    )
    owned_grad, small, down_half, down_rest, input_low, out_back, passed = attention_backward(
        experts, slots, slot_count * TILE,
        x1_grad, w, xn, hat, saved, lse, src, norm_params, small, x_images, out, down_part,
    )

    def from_head(rows, apart):
        return lax.ppermute(rows, "head", [(at, at ^ apart) for at in range(head_count)])

    out_far = from_head(out_back, 2)
    flat_tiles = (slot_count * TILE, width)
    (
        so_far, input_grad, tile_new, tile_first_new, tile_second_new, tile_copy,
        router_new, router_first_new, router_second_new,
        norm_new, norm_first_new, norm_second_new, later_second_new,
    ) = early_stage(
        col, x1, input_low, [out_back, from_head(out_back, 1)],
        [array.reshape(flat_tiles) for array in (tile_master, tile_first, tile_second)] + [owned_grad],
        [router, router_first, router_second], [norm_params, norm_first, norm_second], small,
    )
    up_new, up_first_new, up_second_new = adam_update(
        expert_up, up_first, up_second, up_grad[None], rate_up, decay_factor
    )
    out_far, so_far, _ = lax.optimization_barrier((out_far, so_far, up_new))
    block_out = late_stage(col, so_far, [out_far, from_head(out_far, 1)])
    passed, block_out = lax.optimization_barrier((from_head(passed, 2), block_out))
    down_half = down_half + passed.astype(FULL)
    down_grad = jnp.concatenate([down_half, down_rest], axis=0)
    tiles = [
        array.reshape(tile_master.shape)
        for array in (tile_new, tile_first_new, tile_second_new, tile_copy)
    ]
    down_new, down_first_new, down_second_new = adam_update(
        expert_down, down_first, down_second, down_grad[None], rate_down, decay_factor
    )
    return (
        block_out.reshape(tok_rows, width),
        input_grad.reshape(tok_rows, width),
        *tiles,
        up_new,
        up_first_new,
        up_second_new,
        up_new.astype(LOW),
        down_new,
        down_first_new,
        down_second_new,
        down_new.astype(LOW),
        router_new,
        router_first_new,
        router_second_new,
        norm_new,
        norm_first_new,
        norm_second_new,
        later_second_new,
    )


def solution(mesh):
    row = P("dp", None)
    tiles = P(("dp", "head"), None, None)
    up = P("dp", None, "head")
    down = P("dp", "head", None)
    in_specs = (
        row, row, row, row, P("head", None), tiles, tiles, tiles,
        up, up, up, down, down, down, P(), P(), P(), P(), P(), P(),
    )
    out_specs = (
        row, row, tiles, tiles, tiles, tiles, up, up, up, up, down, down, down, down,
        P(), P(), P(), P(), P(), P(), P(),
    )
    return jax.shard_map(body, mesh=mesh, in_specs=in_specs, out_specs=out_specs, check_vma=False)
```

```python
import functools

import jax
import jax.numpy as jnp
from jax import lax
from jax.experimental import pallas as pl
from jax.experimental.pallas import tpu as pltpu
from jax.sharding import PartitionSpec as P

HD = 64
PATCH = 576
TILE = 8
STEP = 10

eps_norm = 1e-06
beta_one = 0.9
beta_two = 0.999
adam_eps = 1e-08
rate_attention = 0.12
rate_up = 0.08
rate_down = 0.3
rate_router = 0.05
rate_norm = 0.4
decay_factor = 0.1

LOW = jnp.bfloat16
FULL = jnp.float32
MESH = pl.DeviceIdType.MESH
MOST_KEPT = 640
VMEM_BYTES = 61 * 1024 * 1024


def adam_update(weight, moment_one, moment_two, gradient, step_rate, weight_decay):
    moment_one = beta_one * moment_one + (1.0 - beta_one) * gradient
    moment_two = beta_two * moment_two + (1.0 - beta_two) * gradient * gradient
    fixed_one = moment_one / (1.0 - beta_one**STEP)
    fixed_two = moment_two / (1.0 - beta_two**STEP)
    weight = weight - step_rate * (
        fixed_one / (jnp.sqrt(fixed_two) + adam_eps) + weight_decay * weight
    )
    return (weight, moment_one, moment_two)


def nn(left, right):
    return lax.dot_general(left, right, (((1,), (0,)), ((), ())), preferred_element_type=FULL)


def nt(left, right):
    return lax.dot_general(left, right, (((1,), (1,)), ((), ())), preferred_element_type=FULL)


def tn(left, right):
    return lax.dot_general(left, right, (((0,), (0,)), ((), ())), preferred_element_type=FULL)


def params(**more):
    return pltpu.CompilerParams(vmem_limit_bytes=VMEM_BYTES, **more)


def whole(shape):
    return pl.BlockSpec(shape, lambda *_: (0,) * len(shape))


def lead(shape):
    return pl.BlockSpec(shape, lambda i: (i,) + (0,) * (len(shape) - 1))


def normalise(values):
    average = jnp.mean(values, axis=-1, keepdims=True)
    centred = values - average
    variance = jnp.mean(centred * centred, axis=-1, keepdims=True)
    scale = lax.rsqrt(variance + eps_norm)
    return centred * scale, scale


def norm_back(normal, scale, gain, upstream):
    inner = upstream * gain
    mean_inner = jnp.mean(inner, axis=-1, keepdims=True)
    mean_cross = jnp.mean(inner * normal, axis=-1, keepdims=True)
    result = scale * (inner - mean_inner - normal * mean_cross)
    gain_sum = jnp.sum(upstream * normal, axis=0, keepdims=True)
    shift_sum = jnp.sum(upstream, axis=0, keepdims=True)
    return result, gain_sum, shift_sum


def one_hot(condition):
    return jnp.where(condition, 1.0, 0.0).astype(LOW)


def remote(src, dst, sends, recvs, index, axis, other):
    return pltpu.make_async_remote_copy(
        src_ref=src, dst_ref=dst, send_sem=sends.at[index], recv_sem=recvs.at[index],
        device_id={axis: other}, device_id_type=MESH,
    )


def greet(*others):
    barrier = pltpu.get_barrier_semaphore()
    for axis, other in others:
        pl.semaphore_signal(barrier, inc=1, device_id={axis: other}, device_id_type=MESH)
    pl.semaphore_wait(barrier, len(others))


def partners():
    me = lax.axis_index("head")
    near = me + 1 - 2 * lax.rem(me, 2)
    far = lax.rem(me + 2, 4)
    corner = lax.rem(near + 2, 4)
    return me, near, far, corner


class LineGather:
    def __init__(self, held, up_send, up_recv, down_send, down_recv, pair_send, pair_recv):
        self.held = held
        self.length = held.shape[0] // 2
        self.sems = ((up_send, up_recv), (down_send, down_recv), (pair_send, pair_recv))
        me = lax.axis_index("dp")
        self.place, self.side = me // 2, lax.rem(me, 2)
        self.above = lax.rem(self.place + 1, self.length) * 2 + self.side
        self.below = lax.rem(self.place + self.length - 1, self.length) * 2 + self.side
        self.other = self.place * 2 + 1 - self.side

    def neighbours(self):
        return ("dp", self.above), ("dp", self.below), ("dp", self.other)

    def copy(self, way, origin, side=None):
        index = origin * 2 + (self.side if side is None else side)
        target = (self.above, self.below, self.other)[way]
        block = self.held.at[index]
        return remote(block, block, *self.sems[way], origin, "dp", target)

    def pass_on(self, origin, up, down):
        @pl.when(up & (self.place < self.length - 1))
        def _():
            self.copy(0, origin).start()

        @pl.when(down & (self.place > 0))
        def _():
            self.copy(1, origin).start()

        self.copy(2, origin).start()

    def start(self):
        self.pass_on(self.place, True, True)

    def step(self, k):
        low, high = self.place - k, self.place + k

        @pl.when(low >= 0)
        def _():
            self.copy(0, low).wait_recv()
            self.pass_on(low, True, False)

        @pl.when(high < self.length)
        def _():
            self.copy(1, high).wait_recv()
            self.pass_on(high, False, True)

    def finish(self):
        @pl.loop(0, self.length)
        def _(origin):
            self.copy(2, origin).wait_recv()
            self.copy(2, origin).wait_send()

            @pl.when((origin <= self.place) & (self.place < self.length - 1))
            def _():
                self.copy(0, origin).wait_send()

            @pl.when((origin >= self.place) & (self.place > 0))
            def _():
                self.copy(1, origin).wait_send()


class ImageSum:
    def __init__(self, stage, corner_in, near_in, passed, mine, far_in, sends, recvs):
        self.stage, self.corner_in, self.near_in = stage, corner_in, near_in
        self.passed, self.mine, self.far_in = passed, mine, far_in
        self.sends, self.recvs = sends, recvs
        self.me, self.near, self.far, self.corner = partners()
        self.core = lax.rem(self.me, 2)

    def image(self, turn):
        base = self.me - self.core
        other = lax.rem(base + 2, 4)
        return jnp.where(turn < 2, other, base - 2) + turn

    def to_corner(self):
        return remote(
            self.stage.at[0], self.corner_in, self.sends, self.recvs, 0, "head", self.near
        )

    def to_near(self):
        return remote(
            self.stage.at[1], self.near_in, self.sends, self.recvs, 1, "head", self.near
        )

    def to_far(self, half):
        rows = self.passed.shape[0] // 2
        span = pl.ds(half * rows, rows)
        return remote(
            self.passed.at[span], self.far_in.at[span], self.sends, self.recvs, 2 + half, "head",
            self.far,
        )

    def give(self, turn, part, hold=False):
        theirs = lax.rem(turn, 2) != self.core

        @pl.when((turn < 2) & theirs)
        def _():
            self.stage[0] = part.astype(LOW)
            self.to_corner().start()

        @pl.when((turn >= 2) & theirs)
        def _():
            self.stage[1] = part.astype(LOW)
            self.to_near().start()

        @pl.when((turn < 2) & ~theirs)
        def _():
            self.to_corner().wait_recv()
            self.passed[...] = (part + self.corner_in[...].astype(FULL)).astype(LOW)
            self.to_far(0).start()
            if not hold:
                self.to_far(1).start()

        @pl.when((turn >= 2) & ~theirs)
        def _():
            self.mine[...] = part

    def start_rest(self):
        self.to_far(1).start()

    def result(self):
        self.to_near().wait_recv()
        for half in range(2):
            self.to_far(half).wait_recv()
        return self.mine[...] + self.near_in[...].astype(FULL) + self.far_in[...].astype(FULL)

    def finish(self):
        self.to_corner().wait_send()
        self.to_near().wait_send()
        for half in range(2):
            self.to_far(half).wait_send()


def image_sum_scratch(rows, width):
    block = pltpu.VMEM((rows, width), LOW)
    return [
        pltpu.VMEM((2, rows, width), LOW), block, block, block,
        pltpu.VMEM((rows, width), FULL), block,
        pltpu.SemaphoreType.DMA((4,)), pltpu.SemaphoreType.DMA((4,)),
    ]


class LineScatter:
    def __init__(
        self, blocks, out, pair_in, up_in, down_in, total,
        up_send, up_recv, down_send, down_recv, pair_send, pair_recv,
    ):
        self.blocks, self.out, self.total = blocks, out, total
        self.arrived = (up_in, down_in, pair_in)
        self.sems = ((up_send, up_recv), (down_send, down_recv), (pair_send, pair_recv))
        self.length = blocks.shape[0] // 2
        me = lax.axis_index("dp")
        self.place, self.side = me // 2, lax.rem(me, 2)
        self.targets = (
            lax.rem(self.place + 1, self.length) * 2 + self.side,
            lax.rem(self.place + self.length - 1, self.length) * 2 + self.side,
            self.place * 2 + 1 - self.side,
        )

    def copy(self, way, block):
        source = (
            self.blocks.at[block * 2 + 1 - self.side] if way == 2 else self.total.at[block]
        )
        return remote(
            source, self.arrived[way].at[block], *self.sems[way], block, "dp", self.targets[way]
        )

    def start(self):
        @pl.loop(0, self.length)
        def _(turn):
            distance = self.length - 1 - turn

            @pl.when(self.place + distance < self.length)
            def _():
                self.copy(2, self.place + distance).start()

            @pl.when((self.place >= distance) & (distance > 0))
            def _():
                self.copy(2, self.place - distance).start()

    def pair_sum(self, block):
        self.copy(2, block).wait_recv()
        own = self.blocks[block * 2 + self.side].astype(FULL)
        return own + self.arrived[2][block].astype(FULL)

    def forward(self, way, block, first):
        both = self.pair_sum(block)

        @pl.when(first)
        def _():
            self.total[block] = both.astype(LOW)

        @pl.when(~first)
        def _():
            self.copy(way, block).wait_recv()
            self.total[block] = (both + self.arrived[way][block].astype(FULL)).astype(LOW)

        self.copy(way, block).start()

    def step(self, distance):
        @pl.when(self.place + distance < self.length)
        def _():
            self.forward(0, self.place + distance, self.place == 0)

        @pl.when(self.place >= distance)
        def _():
            self.forward(1, self.place - distance, self.place == self.length - 1)

    def result(self):
        self.out[...] = self.pair_sum(self.place)

        @pl.when(self.place > 0)
        def _():
            self.copy(0, self.place).wait_recv()
            self.out[...] += self.arrived[0][self.place].astype(FULL)

        @pl.when(self.place < self.length - 1)
        def _():
            self.copy(1, self.place).wait_recv()
            self.out[...] += self.arrived[1][self.place].astype(FULL)

    def finish(self):
        @pl.loop(0, self.length)
        def _(block):
            self.copy(2, block).wait_send()

            @pl.when(block > self.place)
            def _():
                self.copy(0, block).wait_send()

            @pl.when(block < self.place)
            def _():
                self.copy(1, block).wait_send()


def line_scatter_scratch(dp_count, rows, width):
    line = dp_count // 2
    return [pltpu.VMEM((line, rows, width), LOW)] * 4 + [pltpu.SemaphoreType.DMA((line,))] * 6


class SmallSum:
    def __init__(self, flat, head_in, dp_in, done, head_send, head_recv, dp_send, dp_recv):
        self.flat, self.head_in, self.dp_in, self.done = flat, head_in, dp_in, done
        self.head_sems, self.dp_sems = (head_send, head_recv), (dp_send, dp_recv)
        self.me, *self.others = partners()
        self.place, self.count = lax.axis_index("dp"), dp_in.shape[0]

    def to_head(self, lane):
        other = self.others[lane]
        return remote(
            self.flat.at[other], self.head_in.at[self.me], *self.head_sems, lane, "head", other
        )

    def back_head(self, lane):
        block = self.done.at[self.me]
        return remote(block, block, *self.head_sems, 3 + lane, "head", self.others[lane])

    def to_dp(self, shift):
        block = self.dp_in.at[self.place]
        other = lax.rem(self.place + shift, self.count)
        return remote(block, block, *self.dp_sems, shift, "dp", other)

    def start(self, value):
        groups, rows, lanes = self.flat.shape
        flat = jnp.concatenate(
            [value[:, at:at + lanes] for at in range(0, value.shape[1], lanes)], axis=0
        )
        for group in range(groups):
            self.flat[group] = flat[group * rows:(group + 1) * rows]
        for lane in range(3):
            self.to_head(lane).start()
        self.head_in[self.me] = self.flat[self.me]

    def across(self):
        for lane in range(3):
            self.to_head(lane).wait_recv()
        total = self.head_in[0]
        for head in range(1, self.head_in.shape[0]):
            total = total + self.head_in[head]
        self.dp_in[self.place] = total

        @pl.loop(1, self.count)
        def _(shift):
            self.to_dp(shift).start()

    def back(self):
        @pl.loop(1, self.count)
        def _(shift):
            self.to_dp(shift).wait_recv()

        total = lax.fori_loop(
            1, self.count, lambda at, so_far: so_far + self.dp_in[at], self.dp_in[0]
        )
        self.done[self.me] = total
        for lane in range(3):
            self.back_head(lane).start()

    def result(self, out):
        for lane in range(3):
            self.back_head(lane).wait_recv()
        flat = jnp.concatenate([self.done[group] for group in range(self.done.shape[0])], axis=0)
        rows, width = out.shape
        lanes = flat.shape[1]
        for at in range(width // lanes):
            out[:, at * lanes:(at + 1) * lanes] = flat[at * rows:(at + 1) * rows]

    def finish(self):
        for lane in range(3):
            self.to_head(lane).wait_send()
            self.back_head(lane).wait_send()

        @pl.loop(1, self.count)
        def _(shift):
            self.to_dp(shift).wait_send()


def small_sum_scratch(rows, width, dp_count):
    block = (rows * width // 128 // 4, 128)
    return [
        pltpu.VMEM((4,) + block, FULL), pltpu.VMEM((4,) + block, FULL),
        pltpu.VMEM((dp_count,) + block, FULL), pltpu.VMEM((4,) + block, FULL),
        pltpu.SemaphoreType.DMA((6,)), pltpu.SemaphoreType.DMA((6,)),
        pltpu.SemaphoreType.DMA((dp_count,)), pltpu.SemaphoreType.DMA((dp_count,)),
    ]


class LateSum:
    def __init__(self, dp_in, head_in, dp_send, dp_recv, head_send, head_recv):
        self.dp_in, self.head_in = dp_in, head_in
        self.dp_sems, self.head_sems = (dp_send, dp_recv), (head_send, head_recv)
        self.me, *self.others = partners()
        self.place, self.count = lax.axis_index("dp"), dp_in.shape[0]

    def to_dp(self, shift):
        block = self.dp_in.at[self.place]
        other = lax.rem(self.place + shift, self.count)
        return remote(block, block, *self.dp_sems, shift, "dp", other)

    def to_head(self, lane):
        block = self.head_in.at[self.me]
        return remote(block, block, *self.head_sems, lane, "head", self.others[lane])

    def start(self, rows):
        lanes = self.dp_in.shape[2]
        cuts = [
            row[:, at:at + lanes] for row in rows for at in range(0, row.shape[1], lanes)
        ]
        cuts += [jnp.zeros_like(cuts[0])] * (self.dp_in.shape[1] - len(cuts))
        self.dp_in[self.place] = jnp.concatenate(cuts, axis=0)

        @pl.loop(1, self.count)
        def _(shift):
            self.to_dp(shift).start()

    def across(self):
        @pl.loop(1, self.count)
        def _(shift):
            self.to_dp(shift).wait_recv()

        self.head_in[self.me] = lax.fori_loop(
            1, self.count, lambda at, so_far: so_far + self.dp_in[at], self.dp_in[0]
        )
        for lane in range(3):
            self.to_head(lane).start()

    def result(self, out, first):
        for lane in range(3):
            self.to_head(lane).wait_recv()
        total = self.head_in[0]
        for head in range(1, self.head_in.shape[0]):
            total = total + self.head_in[head]
        lanes = total.shape[1]
        cuts = out.shape[1] // lanes
        for row in range(2):
            for at in range(cuts):
                piece = total[row * cuts + at:row * cuts + at + 1]
                out[first + row:first + row + 1, at * lanes:(at + 1) * lanes] = piece

    def finish(self):
        for lane in range(3):
            self.to_head(lane).wait_send()

        @pl.loop(1, self.count)
        def _(shift):
            self.to_dp(shift).wait_send()


def late_sum_scratch(width, dp_count):
    block = (-(-2 * width // 128 // 8) * 8, 128)
    return [
        pltpu.VMEM((dp_count,) + block, FULL), pltpu.VMEM((4,) + block, FULL),
        pltpu.SemaphoreType.DMA((dp_count,)), pltpu.SemaphoreType.DMA((dp_count,)),
        pltpu.SemaphoreType.DMA((3,)), pltpu.SemaphoreType.DMA((3,)),
    ]


GATHER_CUTS = 4
COLUMN_CUTS = 3


class ImageGather:
    def __init__(self, held, sends, recvs, own=None, local_sem=None, columns=False):
        self.held, self.sends, self.recvs, self.columns = held, sends, recvs, columns
        self.me, self.near, self.far, self.corner = partners()
        self.own = held.at[self.me] if own is None else own
        self.local = None if own is None else pltpu.make_async_copy(own, held.at[self.me], local_sem)
        self.size = held.shape[1] // GATHER_CUTS
        self.wide = held.shape[2] // COLUMN_CUTS

    def piece(self, lane, cut):
        span = pl.ds(cut * self.size, self.size)
        image = self.far if lane == 2 else self.me
        if self.columns:
            block = self.held.at[image, :, pl.ds(cut * self.wide, self.wide)]
        else:
            block = self.held.at[image, span]
        source = block if self.columns or lane == 2 else self.own.at[span]
        other = self.far if lane == 0 else self.near
        index = lane * GATHER_CUTS + cut
        return remote(source, block, self.sends, self.recvs, index, "head", other)

    def start_far(self, first=0, last=GATHER_CUTS):
        for cut in range(first, last):
            self.piece(0, cut).start()

    def start_near(self, last=GATHER_CUTS):
        for cut in range(last):
            self.piece(1, cut).start()
        if self.local is not None:
            self.local.start()

    def start(self):
        self.start_far()
        self.start_near()

    def wait_near(self, first=0, last=GATHER_CUTS):
        for cut in range(first, last):
            self.piece(1, cut).wait_recv()

    def wait_far(self, first=0, last=GATHER_CUTS):
        for cut in range(first, last):
            self.piece(0, cut).wait_recv()
            self.piece(2, cut).start()

    def wait_corner(self, first=0, last=GATHER_CUTS):
        for cut in range(first, last):
            self.piece(2, cut).wait_recv()

    def finish(self, last=GATHER_CUTS):
        for cut in range(last):
            for lane in range(3):
                self.piece(lane, cut).wait_send()
        if self.local is not None:
            self.local.wait()


def image_gather_sems():
    return [pltpu.SemaphoreType.DMA((3 * GATHER_CUTS,)), pltpu.SemaphoreType.DMA((3 * GATHER_CUTS,))]


class BlockSum:
    def __init__(
        self, parts, first, mine, passed, corner_in, near_in, far_in, local_sems, sends, recvs, far=True
    ):
        self.with_far = far
        self.mine, self.passed, self.corner_in = mine, passed, corner_in
        self.near_in, self.far_in = near_in, far_in
        me, near, opposite, corner = partners()
        span = pl.ds(first, mine.shape[0])
        self.to_corner = remote(parts.at[corner, span], corner_in, sends, recvs, 0, "head", near)
        self.to_near = remote(parts.at[near, span], near_in, sends, recvs, 1, "head", near)
        if far:
            self.to_far = remote(passed, far_in, sends, recvs, 2, "head", opposite)
        self.load_far = pltpu.make_async_copy(parts.at[opposite, span], passed, local_sems.at[0])
        self.load_mine = pltpu.make_async_copy(parts.at[me, span], mine, local_sems.at[1])

    def start(self):
        for copy in (self.to_corner, self.load_far, self.to_near, self.load_mine):
            copy.start()

    def across(self):
        self.load_far.wait()
        self.to_corner.wait_recv()
        both = self.passed[...].astype(FULL) + self.corner_in[...].astype(FULL)
        self.passed[...] = both.astype(LOW)
        if self.with_far:
            self.to_far.start()

    def result(self):
        self.load_mine.wait()
        self.to_near.wait_recv()
        total = self.mine[...].astype(FULL) + self.near_in[...].astype(FULL)
        if self.with_far:
            self.to_far.wait_recv()
            total = total + self.far_in[...].astype(FULL)
        return total

    def finish(self):
        self.to_corner.wait_send()
        self.to_near.wait_send()
        if self.with_far:
            self.to_far.wait_send()


def block_sum_scratch(rows, width):
    return [pltpu.VMEM((rows, width), LOW)] * 5 + [
        pltpu.SemaphoreType.DMA((2,)), pltpu.SemaphoreType.DMA((3,)), pltpu.SemaphoreType.DMA((3,)),
    ]


class Slots:
    def __init__(self, count, share):
        self.count, self.share = count, share
        self.big = -(-share // 16) * 16
        rest = 2 * share - self.big
        self.small = rest if rest > 0 and rest % 16 == 0 else self.big
        self.more = self.big - self.small
        self.both = self.big + self.small
        self.rows = count // 2 * self.both
        self.turns = count // 4
        self.phase_rows = self.turns * 2 * self.both

    def size(self, source, head):
        return self.small + self.more * ((head + source + 1) % 2)

    def packed(self, source, head):
        return (source // 2) * self.both + (source % 2) * self.size(0, head)

    def row(self, source, head, shift):
        first = self.size(source, 0) * (head % 2)
        group = (head // 2) * self.turns * self.both + self.turns * first
        return (
            (shift // self.turns) * self.phase_rows + group
            + (shift % self.turns) * self.size(source, head)
        )

    def holder(self, source, slot):
        pair, within = slot // self.both, slot % self.both
        first = self.size(source, 0)
        second = jnp.where(within >= first, 1, 0)
        return 2 * pair + second, within - second * first

    def span(self, start, extra):
        if extra:
            return pl.ds(pl.multiple_of(start + self.small, 16), self.more)
        return pl.ds(pl.multiple_of(start, 16), self.small)

    def each(self, is_big, make, action):
        getattr(make(False), action)()
        if self.more:
            @pl.when(is_big)
            def _():
                getattr(make(True), action)()


class SlotExchange:
    def __init__(self, slots, sent, rows, sends, recvs, local_sems, cut=None):
        self.slots, self.sent, self.rows = slots, sent, rows
        self.sems, self.local_sems = (sends, recvs), local_sems
        self.place, self.head = lax.axis_index("dp"), lax.axis_index("head")
        wide = sent.shape[1] // COLUMN_CUTS
        self.cut = 0 if cut is None else cut
        self.lanes = pl.ds(0, sent.shape[1]) if cut is None else pl.ds(cut * wide, wide)

    def index(self, shift, extra):
        return 2 * (self.cut * self.slots.count + shift) + int(extra)

    def out(self, shift, action):
        slots = self.slots
        expert = lax.rem(self.place + shift, slots.count)
        mine = slots.size(self.place, self.head)
        at, to = expert * mine, slots.packed(self.place, self.head)
        slots.each(mine > slots.small, lambda extra: remote(
            self.sent.at[slots.span(at, extra), self.lanes], self.rows.at[slots.span(to, extra), self.lanes],
            *self.sems, self.index(shift, extra), "dp", expert,
        ), action)

    def into(self, shift):
        slots = self.slots
        source = lax.rem(self.place + slots.count - shift, slots.count)
        size = slots.size(source, self.head)
        to = slots.packed(source, self.head)
        slots.each(size > slots.small, lambda extra: remote(
            self.sent.at[slots.span(0, extra), self.lanes], self.rows.at[slots.span(to, extra), self.lanes],
            *self.sems, self.index(shift, extra), "dp", source,
        ), "wait_recv")

    def own(self, action):
        slots = self.slots
        mine = slots.size(self.place, self.head)
        at, to = self.place * mine, slots.packed(self.place, self.head)
        slots.each(mine > slots.small, lambda extra: pltpu.make_async_copy(
            self.sent.at[slots.span(at, extra), self.lanes], self.rows.at[slots.span(to, extra), self.lanes],
            self.local_sems.at[2 * self.cut + int(extra)],
        ), action)

    def start(self):
        @pl.loop(1, self.slots.count)
        def _(shift):
            self.out(shift, "start")

        self.own("start")

    def finish(self):
        @pl.loop(1, self.slots.count)
        def _(shift):
            self.into(shift)
            self.out(shift, "wait_send")

        self.own("wait")


class SlotReturn:
    def __init__(self, slots, rows, back, zeros, sends, recvs, local_sems):
        self.slots, self.rows, self.back, self.zeros = slots, rows, back, zeros
        self.sems, self.local_sems = (sends, recvs), local_sems
        self.place, self.head = lax.axis_index("dp"), lax.axis_index("head")
        self.mine = slots.size(self.place, self.head)

    def out(self, shift, action):
        slots = self.slots
        source = lax.rem(self.place + shift, slots.count)
        size = slots.size(source, self.head)
        at, to = slots.packed(source, self.head), shift * size
        slots.each(size > slots.small, lambda extra: remote(
            self.rows.at[slots.span(at, extra)], self.back.at[slots.span(to, extra)],
            *self.sems, 2 * shift + int(extra), "dp", source,
        ), action)

    def into(self, shift):
        slots = self.slots
        expert = lax.rem(self.place + slots.count - shift, slots.count)
        slots.each(self.mine > slots.small, lambda extra: remote(
            self.rows.at[slots.span(0, extra)], self.back.at[slots.span(shift * self.mine, extra)],
            *self.sems, 2 * shift + int(extra), "dp", expert,
        ), "wait_recv")

    def own(self, action):
        slots = self.slots
        at = slots.packed(self.place, self.head)
        slots.each(self.mine > slots.small, lambda extra: pltpu.make_async_copy(
            self.rows.at[slots.span(at, extra)], self.back.at[slots.span(0, extra)],
            self.local_sems.at[int(extra)],
        ), action)

    def blank(self, action):
        slots = self.slots
        if slots.more:
            @pl.when(self.mine == slots.small)
            def _():
                tail = self.back.at[pl.ds(slots.count * slots.small, slots.count * slots.more)]
                copy = pltpu.make_async_copy(self.zeros, tail, self.local_sems.at[2])
                getattr(copy, action)()

    def start(self):
        if self.slots.more:
            self.zeros[...] = jnp.zeros_like(self.zeros)
        self.blank("start")

        @pl.loop(1, self.slots.count)
        def _(shift):
            self.out(shift, "start")

        self.own("start")

    def finish(self):
        @pl.loop(1, self.slots.count)
        def _(shift):
            self.into(shift)
            self.out(shift, "wait_send")

        self.own("wait")
        self.blank("wait")


def slot_return_scratch(slots, width):
    return [pltpu.VMEM((max(slots.count * slots.more, 16), width), LOW)] + [
        pltpu.SemaphoreType.DMA((2 * slots.count,)), pltpu.SemaphoreType.DMA((2 * slots.count,)),
        pltpu.SemaphoreType.DMA((3,)),
    ]


def slot_exchange_sems(count, cuts=1):
    return [
        pltpu.SemaphoreType.DMA((2 * count * cuts,)), pltpu.SemaphoreType.DMA((2 * count * cuts,)),
        pltpu.SemaphoreType.DMA((2 * cuts,)),
    ]


class ReturnGather:
    def __init__(self, slots, rows, held, sends, recvs, local_sems):
        self.slots, self.rows, self.held = slots, rows, held
        self.sems, self.local_sems = (sends, recvs), local_sems
        self.place = lax.axis_index("dp")
        self.me, self.near, self.far, self.corner = partners()

    def out(self, shift, action):
        slots = self.slots
        source = lax.rem(self.place + shift, slots.count)
        size = slots.size(source, self.me)
        at, to = slots.packed(source, self.me), slots.row(source, self.me, shift)
        slots.each(size > slots.small, lambda extra: remote(
            self.rows.at[slots.span(at, extra)], self.held.at[slots.span(to, extra)],
            *self.sems, 2 * shift + int(extra), "dp", source,
        ), action)

    def own(self, action):
        slots = self.slots
        size = slots.size(self.place, self.me)
        at, to = slots.packed(self.place, self.me), slots.row(self.place, self.me, 0)
        slots.each(size > slots.small, lambda extra: pltpu.make_async_copy(
            self.rows.at[slots.span(at, extra)], self.held.at[slots.span(to, extra)],
            self.local_sems.at[int(extra)],
        ), action)

    def block(self, lane, head, shift, axis, other, action):
        slots = self.slots
        size = slots.size(self.place, head)
        to = slots.row(self.place, head, shift)

        def make(extra):
            block = self.held.at[slots.span(to, extra)]
            index = 2 * (lane * slots.count + shift) + int(extra)
            return remote(block, block, *self.sems, index, axis, other)

        slots.each(size > slots.small, make, action)

    def send(self, phase):
        turns = self.slots.turns
        if phase == 0:
            self.own("start")

        @pl.loop(max(phase * turns, 1), (phase + 1) * turns)
        def _(shift):
            self.out(shift, "start")

    def relay(self, shift):
        @pl.when(shift == 0)
        def _():
            self.own("wait")

        @pl.when(shift > 0)
        def _():
            expert = lax.rem(self.place + self.slots.count - shift, self.slots.count)
            self.block(0, self.me, shift, "dp", expert, "wait_recv")

        self.block(1, self.me, shift, "head", self.far, "start")
        self.block(2, self.me, shift, "head", self.near, "start")

    def forward(self, shift):
        self.block(1, self.far, shift, "head", self.far, "wait_recv")
        self.block(3, self.far, shift, "head", self.near, "start")

    def rest(self, shift):
        self.block(2, self.near, shift, "head", self.near, "wait_recv")
        self.block(3, self.corner, shift, "head", self.near, "wait_recv")

    def of_phase(self, phase, action):
        @pl.loop(0, self.slots.turns)
        def _(turn):
            action(phase * self.slots.turns + turn)

    def finish(self):
        @pl.loop(0, self.slots.count)
        def _(shift):
            @pl.when(shift > 0)
            def _():
                self.out(shift, "wait_send")

            self.block(1, self.me, shift, "head", self.far, "wait_send")
            self.block(2, self.me, shift, "head", self.near, "wait_send")
            self.block(3, self.far, shift, "head", self.near, "wait_send")


def return_gather_sems(count):
    return [
        pltpu.SemaphoreType.DMA((8 * count,)), pltpu.SemaphoreType.DMA((8 * count,)),
        pltpu.SemaphoreType.DMA((2,)),
    ]


def greet_all(heads, dp_count):
    barrier = pltpu.get_barrier_semaphore()
    place = lax.axis_index("dp")
    for other in heads:
        pl.semaphore_signal(barrier, inc=1, device_id={"head": other}, device_id_type=MESH)

    @pl.loop(1, dp_count)
    def _(shift):
        other = lax.rem(place + shift, dp_count)
        pl.semaphore_signal(barrier, inc=1, device_id={"dp": other}, device_id_type=MESH)

    pl.semaphore_wait(barrier, len(heads) + dp_count - 1)


ANYWHERE = pl.BlockSpec(memory_space=pl.ANY)
INSIDE = pl.BlockSpec(memory_space=pltpu.VMEM)


def digits(values):
    high = lax.div(values, 64)
    return [high.astype(FULL), (values - high * 64).astype(FULL)]


def digit_weights(shape, digit_axis):
    digit = lax.broadcasted_iota(jnp.int32, shape, digit_axis)
    value = lax.broadcasted_iota(jnp.int32, shape, 1 - digit_axis)
    weight = jnp.where(lax.rem(digit, 2) == 0, 64.0, 1.0)
    return jnp.where(lax.div(digit, 2) == value, weight, 0.0).astype(LOW)


def turned_rows(rows):
    count = rows[0].shape[1]
    parts = [part for row in rows for part in digits(row)]
    parts += [jnp.zeros((1, count), FULL)] * (8 - len(parts))
    spread = jnp.concatenate(parts, axis=0).astype(LOW)
    return tn(spread, digit_weights((8, 128), 0)).astype(jnp.int32)


def turned_column(column):
    lanes = lax.broadcasted_iota(jnp.int32, (column.shape[0], 128), 1)
    high, low = digits(column)
    spread = jnp.where(lanes == 0, high, jnp.where(lanes == 1, low, 0.0)).astype(LOW)
    return nt(digit_weights((8, 128), 1), spread)[0:1].astype(jnp.int32)


def head_mask(shape, axis, head):
    return lax.broadcasted_iota(jnp.int32, shape, axis) // HD == head


def front_kernel(
    slots, slot_count, capacity,
    tile_ref, norm_ref, owner_ref, ids_in, pos_in, up_in, down_in, x_in, g_in,
    w_ref, src_ref, col_back_ref, lse_ref,
    xn_out, hat_out, up_out, down_out, q_out, qt_out, k_out, kt_out, v_out, ot_out, x1_out,
    rows_out, g_rows_out,
    x_ref, g_ref, xn_ref, hat_ref, full_ref, up_low, down_low, held, picks, sent_sum, sent_g, sent_ref,
    q_ref, qt_ref, k_ref, kt_ref, v_ref, ot_ref, stats, norms, ids_ref, pos_ref,
    load_sems, image_sems, save_sems, keep_sem, stat_send, stat_recv, *exchange,
):
    images = x_ref.shape[0]
    for image in range(images):
        lanes = slice(image * PATCH, (image + 1) * PATCH)
        ids_ref[image], pos_ref[image] = ids_in[:, lanes], pos_in[:, lanes]
    x1_ref = g_ref
    gather = LineGather(held, *exchange[:6])
    spread_up = ImageGather(up_out, *exchange[6:8], own=up_low, local_sem=exchange[8])
    spread_down = ImageGather(down_out, *exchange[9:11], own=down_low, local_sem=exchange[11])
    total_of = ImageSum(*exchange[12:20])
    spread = ImageGather(x1_ref, *exchange[20:22], columns=True)
    send_g = SlotExchange(slots, sent_g, g_rows_out, *exchange[22:25])
    send_rows = [
        SlotExchange(slots, sent_ref, rows_out, *exchange[25:], cut=cut) for cut in range(COLUMN_CUTS)
    ]
    head, near, far, corner = partners()
    load_up = pltpu.make_async_copy(up_in, full_ref, load_sems.at[2, 0])
    load_down = pltpu.make_async_copy(down_in, full_ref, load_sems.at[2, 1])
    load_up.start()

    def load_image(image):
        return (
            pltpu.make_async_copy(x_in.at[image], x_ref.at[image], load_sems.at[0, image]),
            pltpu.make_async_copy(g_in.at[image], g_ref.at[image], load_sems.at[1, image]),
        )

    def save_image(image):
        return [
            pltpu.make_async_copy(xn_ref.at[image], xn_out.at[image], image_sems.at[0, image]),
            pltpu.make_async_copy(hat_ref.at[image], hat_out.at[image], image_sems.at[1, image]),
        ]

    kept_refs = (
        (q_ref, q_out), (qt_ref, qt_out), (k_ref, k_out), (kt_ref, kt_out), (v_ref, v_out),
        (ot_ref, ot_out),
    )

    def save(image):
        return [
            pltpu.make_async_copy(ref.at[image], out.at[image], save_sems.at[index, image])
            for index, (ref, out) in enumerate(kept_refs)
        ]

    for image in range(images):
        for copy in load_image(image):
            copy.start()
    me = lax.axis_index("dp")
    held[me] = tile_ref[...].astype(LOW)
    greet_all((near, far, corner), slots.count)
    gather.start()
    load_up.wait()
    up_low[...] = full_ref[...].astype(LOW)
    spread_up.start()
    load_down.start()
    shape = (sent_ref.shape[0], PATCH)
    sent_sum[...] = jnp.zeros_like(sent_sum)
    steps = gather.length - 1

    def image_step(image):
        for copy in load_image(image):
            copy.wait()
        normal, _ = normalise(x_ref[image].astype(FULL))
        hat_ref[image] = normal.astype(LOW)
        xn_ref[image] = (normal * norm_ref[0:1, :] + norm_ref[1:2, :]).astype(LOW)
        for copy in save_image(image):
            copy.start()

        ids, pos = ids_ref[image], pos_ref[image]
        kept = pos < capacity
        holder, within = slots.holder(me, jnp.minimum(pos, capacity - 1))
        sent_at = ids * slots.size(me, head) + within
        sent_at = jnp.where(kept & (holder == head), sent_at, slots.count * slots.big)
        shift = me - ids
        shift = jnp.where(shift < 0, shift + slots.count, shift)
        back_at = jnp.where(kept, slots.row(me, holder, shift) + within + 1, 0)
        other_pair = jnp.where(lax.div(holder, 2) == lax.div(head, 2), 0, 2)
        apart = other_pair + jnp.where(lax.rem(holder, 2) == lax.rem(head, 2), 0, 1)
        out_at = apart * (slots.count * slots.big) + shift * slots.size(me, holder) + within
        out_at = jnp.where(kept, out_at + 1, 0)
        turned = turned_rows([back_at[0:1], back_at[1:2], out_at[0:1], out_at[1:2]])
        col_back_ref[image] = turned[:, 0:4] - 1
        first, second = sent_at[0:1], sent_at[1:2]
        sent_slots = lax.broadcasted_iota(jnp.int32, shape, 0)
        pick = one_hot((sent_slots == first) | (sent_slots == second))
        picks[image] = pick
        sent_sum[...] += nn(pick, g_ref[image])

    @pl.loop(0, max(steps, (images + 1) // 2))
    def _(turn):
        @pl.loop(2 * turn, jnp.minimum(2 * turn + 2, images))
        def _(image):
            image_step(image)

        @pl.when(turn < steps)
        def _():
            gather.step(turn + 1)

        @pl.when(turn == 1)
        def _():
            spread_up.wait_far(0, 1)

    sent_g[...] = sent_sum[...].astype(LOW)
    load_down.wait()
    down_low[...] = full_ref[...].astype(LOW)

    rows = w_ref.shape[0]
    tiles = owner_ref.shape[1]
    row_tile = lax.div(lax.broadcasted_iota(jnp.int32, (rows, tiles), 0), TILE)
    lane_tile = lax.broadcasted_iota(jnp.int32, (rows, tiles), 1)
    owner_rows = jnp.broadcast_to(owner_ref[...].astype(FULL), (8, tiles)).astype(LOW)
    owner = nt(one_hot(lane_tile == row_tile), owner_rows)[:, 0:1].astype(jnp.int32)
    before = (owner_ref[...] == owner) & (lane_tile < row_tile)
    rank = jnp.sum(jnp.where(before, 1.0, 0.0), axis=1, keepdims=True).astype(jnp.int32)
    within = lax.rem(lax.broadcasted_iota(jnp.int32, (rows, 1), 0), TILE)
    src = (owner * slot_count + rank) * TILE + within
    src_ref[...] = turned_column(src)
    spread_up.wait_far(1, 3)
    gather.finish()
    blocks, depth, width = held.shape
    cut = rows // 4
    for part in range(4):
        lanes = lax.broadcasted_iota(jnp.int32, (cut, blocks * depth), 1)
        pick = one_hot(lanes == src[part * cut:(part + 1) * cut])
        block = nn(pick, held[...].reshape(blocks * depth, width))
        w_ref[pl.ds(part * cut, cut), :] = block.astype(LOW)
    spread_down.start_far(0, 1)
    spread_down.start_near()
    send_g.start()
    me = head
    shrink = HD ** (-0.5)

    part_rows = w_ref.shape[0] // 4
    heads = part_rows // HD

    @pl.loop(0, images)
    def _(turn):
        image = total_of.image(turn)
        xn = xn_ref[image]
        wq, wk, wv, wo = (
            w_ref[pl.ds(part * part_rows, part_rows), :] for part in range(4)
        )
        q = (nt(xn, wq) * shrink).astype(LOW)
        q_ref[image] = q
        qt = q.T
        qt_ref[image] = qt
        k = nt(xn, wk).astype(LOW)
        k_ref[image] = k
        kt_ref[image] = k.T
        v = nt(xn, wv).astype(LOW)
        v_ref[image] = v
        vt = v.T
        mixed = []
        for head in range(heads):
            span = slice(head * HD, (head + 1) * HD)
            only = jnp.where(head_mask(qt.shape, 0, head), qt, jnp.zeros_like(qt))
            scores = nn(k, only)
            top = jnp.max(scores, axis=0, keepdims=True)
            weights = jnp.exp(scores - top)
            total = jnp.sum(weights, axis=0, keepdims=True)
            mixed.append(nn(vt[span], weights.astype(LOW)) / total)
            lse_ref[image, head:head + 1, :] = top + jnp.log(total)
        ot = jnp.concatenate(mixed, axis=0).astype(LOW)
        ot_ref[image] = ot
        total_of.give(turn, tn(ot, wo))
        for copy in save(image):
            copy.start()

        @pl.when(turn == 0)
        def _():
            spread_up.wait_far(3)

    x1 = (x_ref[me].astype(FULL) + total_of.result()).astype(LOW)
    x1_ref[me] = x1
    values = x1.astype(FULL)
    average = jnp.mean(values, axis=-1, keepdims=True)
    centred = values - average
    scale = lax.rsqrt(jnp.mean(centred * centred, axis=-1, keepdims=True) + eps_norm)
    lanes = lax.broadcasted_iota(jnp.int32, (PATCH, 128), 1)
    pair = jnp.where(lanes == 0, average, jnp.where(lanes == 1, scale, 0.0))
    eye = (8, 128)
    eye = lax.broadcasted_iota(jnp.int32, eye, 0) == lax.broadcasted_iota(jnp.int32, eye, 1)
    eye = jnp.where(eye, 1.0, 0.0)
    stats[me] = lax.dot_general(
        eye, pair, (((1,), (1,)), ((), ())), precision=lax.Precision.HIGHEST,
        preferred_element_type=FULL,
    )
    tell = [
        remote(stats.at[me], stats.at[me], stat_send, stat_recv, lane, "head", other)
        for lane, other in enumerate((near, far, corner))
    ]
    for copy in tell:
        copy.start()
    spread.start_far(0, COLUMN_CUTS)
    spread.start_near(COLUMN_CUTS)
    spread_down.start_far(1)

    for copy in tell:
        copy.wait_recv()

    @pl.loop(0, images)
    def _(image):
        norms[image] = lax.dot_general(
            stats[image], eye, (((0,), (0,)), ((), ())), precision=lax.Precision.HIGHEST,
            preferred_element_type=FULL,
        )

    for cut in range(COLUMN_CUTS):
        wide = sent_ref.shape[1] // COLUMN_CUTS
        span = slice(cut * wide, (cut + 1) * wide)

        def place(image, span=span):
            normal = (x1_ref[image, :, span].astype(FULL) - norms[image, :, 0:1]) * norms[image, :, 1:2]
            low = (normal * norm_ref[2:3, span] + norm_ref[3:4, span]).astype(LOW)
            return nn(picks[image], low)

        total = place(me)
        spread.wait_near(cut, cut + 1)
        total = total + place(near)
        spread.wait_far(cut, cut + 1)
        total = total + place(far)
        spread.wait_corner(cut, cut + 1)
        sent_ref[:, span] = (total + place(corner)).astype(LOW)
        send_rows[cut].start()

    keep = pltpu.make_async_copy(x1_ref, x1_out, keep_sem)
    keep.start()
    for copy in tell:
        copy.wait_send()
    spread.finish(COLUMN_CUTS)
    total_of.finish()
    send_g.finish()
    spread_down.wait_far()
    spread_down.wait_near()
    spread_down.wait_corner()
    spread_down.finish()
    spread_up.wait_near()
    spread_up.wait_corner()
    spread_up.finish()
    for copy in send_rows:
        copy.finish()
    keep.wait()

    @pl.loop(0, images)
    def _(image):
        for copy in save(image) + save_image(image):
            copy.wait()


def front(slots, tiles, patches, cotangent, norm_params, owners, ids, pos, up, down, weight_rows):
    images, _, width = patches.shape
    slot_count = tiles.shape[0] // TILE
    line = slots.count // 2
    most = slots.count * slots.big
    capacity = images * PATCH // slots.count
    rows = weight_rows // 4
    flat, turned = (images, PATCH, rows), (images, rows, PATCH)
    saved = [flat, turned, flat, turned, flat, turned]
    outs = (
        [patches.shape] * 2 + [(4,) + up.shape, (4,) + down.shape] + saved
        + [patches.shape] + [(slots.rows, width)] * 2
    )
    return pl.pallas_call(
        functools.partial(front_kernel, slots, slot_count, capacity),
        in_specs=[INSIDE] * 5 + [ANYWHERE] * 4,
        out_specs=[INSIDE] * 4 + [ANYWHERE] * len(outs),
        out_shape=[
            jax.ShapeDtypeStruct((weight_rows, width), LOW),
            jax.ShapeDtypeStruct((1, weight_rows), jnp.int32),
            jax.ShapeDtypeStruct((images, PATCH, 4), jnp.int32),
            jax.ShapeDtypeStruct((images, 8, PATCH), FULL),
        ]
        + [jax.ShapeDtypeStruct(shape, LOW) for shape in outs],
        scratch_shapes=[pltpu.VMEM(patches.shape, LOW)] * 4
        + [
            pltpu.VMEM(up.shape, FULL), pltpu.VMEM(up.shape, LOW), pltpu.VMEM(down.shape, LOW),
            pltpu.VMEM((slots.count,) + tiles.shape, LOW), pltpu.VMEM((images, most, PATCH), LOW),
            pltpu.VMEM((most, width), FULL), pltpu.VMEM((most, width), LOW),
            pltpu.VMEM((most, width), LOW),
        ]
        + [pltpu.VMEM(shape, LOW) for shape in saved]
        + [
            pltpu.VMEM((images, 8, PATCH), FULL), pltpu.VMEM((images, PATCH, 128), FULL),
            pltpu.VMEM((images, 2, PATCH), jnp.int32), pltpu.VMEM((images, 2, PATCH), jnp.int32),
            pltpu.SemaphoreType.DMA((3, images)), pltpu.SemaphoreType.DMA((2, images)),
            pltpu.SemaphoreType.DMA((6, images)), pltpu.SemaphoreType.DMA,
            pltpu.SemaphoreType.DMA((3,)), pltpu.SemaphoreType.DMA((3,)),
        ]
        + [pltpu.SemaphoreType.DMA((line,))] * 6
        + image_gather_sems() + [pltpu.SemaphoreType.DMA]
        + image_gather_sems() + [pltpu.SemaphoreType.DMA]
        + image_sum_scratch(PATCH, width) + image_gather_sems()
        + slot_exchange_sems(slots.count) + slot_exchange_sems(slots.count, COLUMN_CUTS),
        compiler_params=params(collective_id=0, has_side_effects=True),
        name="front",
    )(tiles, norm_params, owners, ids, pos, up, down, patches, cotangent)


def backward_kernel(
    experts, slots,
    w_ref, lse_ref, src_ref, norm_ref, small_ref,
    x1g_in, xn_in, hat_in, q_in, qt_in, k_in, kt_in, v_in, ot_in, x_ref, out_rows_ref, down_part,
    owned_ref, small_out, down_grad_ref, input_out, out_back,
    x1g_ref, xn_ref, hat_ref, q_ref, qt_ref, k_ref, kt_ref, v_ref, ot_ref, late_ref,
    grad_ref, own_ref, input_ref, padded_ref, load_sems, own_sem, *exchange,
):
    images = x1g_ref.shape[0]
    rows = w_ref.shape[0] // 4
    heads = rows // HD
    total_of = ImageSum(*exchange[:8])
    spread = ImageGather(input_ref, *exchange[8:10])
    back_out = SlotReturn(slots, out_rows_ref, out_back, *exchange[10:14])
    weights_sum = LineScatter(padded_ref, owned_ref, *exchange[14:24])
    down_sum = BlockSum(down_part, down_part.shape[1] // 2, *exchange[24:32])
    small_sum = SmallSum(*exchange[32:40])
    late_sum = LateSum(*exchange[40:])
    me, near, far, corner = partners()
    dp_count = slots.count
    streamed = (
        (xn_in, xn_ref), (hat_in, hat_ref), (q_in, q_ref), (qt_in, qt_ref), (k_in, k_ref), (kt_in, kt_ref),
        (v_in, v_ref), (ot_in, ot_ref),
    )

    def load(turn):
        image, slot = total_of.image(turn), lax.rem(turn, 2)
        copies = [
            pltpu.make_async_copy(source.at[image], target.at[slot], load_sems.at[index, slot])
            for index, (source, target) in enumerate(streamed)
        ]
        copies.append(
            pltpu.make_async_copy(x1g_in.at[image], x1g_ref.at[image], load_sems.at[8, slot])
        )
        return copies

    for turn in range(2):
        for copy in load(turn):
            copy.start()
    own = pltpu.make_async_copy(x_ref.at[me], own_ref, own_sem.at[0])
    own.start()
    greet_all((near, far, corner), dp_count)
    small_sum.start(small_ref[...])
    down_sum.start()
    back_out.start()
    late_ref[...] = jnp.zeros_like(late_ref)
    shrink = HD ** (-0.5)
    grad_ref[...] = jnp.zeros_like(grad_ref)

    @pl.loop(0, images)
    def _(turn):
        image, slot = total_of.image(turn), lax.rem(turn, 2)
        for copy in load(turn):
            copy.wait()
        wq, wk, wv, wo = (w_ref[pl.ds(part * rows, rows), :] for part in range(4))
        x1g, xn = x1g_ref[image], xn_ref[slot]
        q, qt, k, kt = q_ref[slot], qt_ref[slot], k_ref[slot], kt_ref[slot]
        v, ot = v_ref[slot], ot_ref[slot]
        do = nt(x1g, wo).astype(LOW)
        dot = do.T
        product = dot.astype(FULL) * ot.astype(FULL)
        dqt, dk, dv = [], None, None
        for head in range(heads):
            span = slice(head * HD, (head + 1) * HD)
            zero_t = jnp.zeros_like(qt)
            mask_t = head_mask(qt.shape, 0, head)
            mask = head_mask(q.shape, 1, head)
            scores = nn(k, jnp.where(mask_t, qt, zero_t))
            weights = jnp.exp(scores - lse_ref[image, head:head + 1, :])
            back = nn(v, jnp.where(mask_t, dot, zero_t))
            delta = jnp.sum(product[span], axis=0, keepdims=True)
            score_grad = (weights * (back - delta)).astype(LOW)
            dqt.append(nn(kt[span], score_grad) * shrink)
            dk_one = nn(score_grad, jnp.where(mask, q, jnp.zeros_like(q)))
            dv_one = nn(weights.astype(LOW), jnp.where(mask, do, jnp.zeros_like(do)))
            dk = dk_one if dk is None else dk + dk_one
            dv = dv_one if dv is None else dv + dv_one
        dqt = jnp.concatenate(dqt, axis=0).astype(LOW)
        dk, dv = dk.astype(LOW), dv.astype(LOW)
        part = tn(dqt, wq) + nn(dk, wk) + nn(dv, wv)
        total_of.give(turn, part)
        late_ref[0:1, :] += jnp.sum(part * hat_ref[slot].astype(FULL), axis=0, keepdims=True)
        late_ref[1:2, :] += jnp.sum(part, axis=0, keepdims=True)
        three = jnp.concatenate([dqt, dk.T, dv.T], axis=0)
        grad_ref[pl.ds(0, 3 * rows), :] += nn(three, xn)
        grad_ref[pl.ds(3 * rows, rows), :] += nn(ot, x1g)

        @pl.when(turn + 2 < images)
        def _():
            for copy in load(turn + 2):
                copy.start()

        @pl.when(turn == 0)
        def _():
            down_sum.across()

        @pl.when(turn == 1)
        def _():
            small_sum.across()

    late_sum.start([late_ref[0:1, :], late_ref[1:2, :]])
    low = grad_ref[...].astype(LOW)
    depth = padded_ref.shape[1]
    parts = min(dp_count, 8)
    cut = dp_count // parts * depth
    for part in range(parts):
        row = lax.broadcasted_iota(jnp.int32, (cut, low.shape[0]), 0) + part * cut
        pick = one_hot(row == src_ref[...])
        block = nn(pick, low).astype(LOW)
        padded_ref[pl.ds(part * (dp_count // parts), dp_count // parts)] = block.reshape(
            dp_count // parts, depth, block.shape[1]
        )
    weights_sum.start()
    small_sum.back()
    own.wait()
    normal, scale = normalise(own_ref[...].astype(FULL))
    back = norm_back(normal, scale, norm_ref[0:1, :], total_of.result())[0]
    input_ref[me] = (x1g_ref[me].astype(FULL) + back).astype(LOW)
    spread.start()
    late_sum.across()
    steps = weights_sum.length

    @pl.loop(0, steps - 1)
    def _(turn):
        weights_sum.step(steps - 1 - turn)

        @pl.when(turn == steps - 2)
        def _():
            spread.wait_far()

    weights_sum.result()
    small_sum.result(small_out)
    late_sum.result(small_out, experts)
    down_grad_ref[...] = down_sum.result()
    spread.wait_near()
    spread.wait_corner()
    keep = pltpu.make_async_copy(input_ref, input_out, own_sem.at[0])
    keep.start()
    back_out.finish()
    spread.finish()
    total_of.finish()
    weights_sum.finish()
    small_sum.finish()
    late_sum.finish()
    down_sum.finish()
    keep.wait()


def attention_backward(
    experts, slots, depth,
    x1_grad, w, xn, hat, saved, lse, src_row, norm_params, small, patches, out_rows, down_part,
):
    images, _, width = patches.shape
    rows = w.shape[0] // 4
    dp_count = slots.count
    flat, turned = (2, PATCH, rows), (2, rows, PATCH)
    units = down_part.shape[1]
    return pl.pallas_call(
        functools.partial(backward_kernel, experts, slots),
        in_specs=[INSIDE] * 5 + [ANYWHERE] * 12,
        out_specs=[INSIDE] * 3 + [ANYWHERE] * 2,
        out_shape=[
            jax.ShapeDtypeStruct((depth, width), FULL), jax.ShapeDtypeStruct(small.shape, FULL),
            jax.ShapeDtypeStruct((units // 2, width), FULL),
            jax.ShapeDtypeStruct(patches.shape, LOW),
            jax.ShapeDtypeStruct((dp_count * slots.big, width), LOW),
        ],
        scratch_shapes=[pltpu.VMEM(patches.shape, LOW)]
        + [pltpu.VMEM((2, PATCH, width), LOW)] * 2
        + [pltpu.VMEM(shape, LOW) for shape in (flat, turned, flat, turned, flat, turned)]
        + [
            pltpu.VMEM((8, width), FULL), pltpu.VMEM(w.shape, FULL), pltpu.VMEM((PATCH, width), LOW),
            pltpu.VMEM(patches.shape, LOW), pltpu.VMEM((dp_count, depth, width), LOW),
            pltpu.SemaphoreType.DMA((9, 2)), pltpu.SemaphoreType.DMA((2,)),
        ]
        + image_sum_scratch(PATCH, width) + image_gather_sems()
        + slot_return_scratch(slots, width)
        + line_scatter_scratch(dp_count, depth, width)
        + block_sum_scratch(units // 2, width)
        + small_sum_scratch(small.shape[0], width, dp_count)
        + late_sum_scratch(width, dp_count),
        compiler_params=params(collective_id=2, has_side_effects=True),
        cost_estimate=pl.CostEstimate(
            flops=60 * patches.size * width, bytes_accessed=60 * patches.size, transcendentals=0
        ),
        name="attention_backward",
    )(
        w, lse, src_row, norm_params, small, x1_grad, xn, hat, *saved, patches, out_rows, down_part,
    )


def picked_rows(col, held_ref, start, count):
    lanes = lax.broadcasted_iota(jnp.int32, (col.shape[0], count), 1) + start
    pick = one_hot((lanes == col[:, 0:1]) | (lanes == col[:, 1:2]))
    return nn(pick, held_ref[pl.ds(start, count), :])


def mixed_rows(col, first, second, start):
    count = first.shape[0] + second.shape[0]
    lanes = lax.broadcasted_iota(jnp.int32, (col.shape[0], count), 1) + start
    pick = one_hot((lanes == col[:, 2:3]) | (lanes == col[:, 3:4]))
    return nn(pick, jnp.concatenate([first[...], second[...]], axis=0))


def late_kernel(col_ref, sum_ref, first, second, block_ref):
    start = first.shape[0] + second.shape[0]
    block_ref[0] = (sum_ref[0] + mixed_rows(col_ref[0], first, second, start)).astype(LOW)


def late_stage(col, so_far, held):
    images, _, width = so_far.shape
    wide = lead((1, PATCH, width))
    return pl.pallas_call(
        late_kernel,
        grid=(images,),
        in_specs=[lead((1, PATCH, 4)), wide] + [whole(rows.shape) for rows in held],
        out_specs=wide,
        out_shape=jax.ShapeDtypeStruct(so_far.shape, LOW),
        compiler_params=params(),
        cost_estimate=pl.CostEstimate(
            flops=2 * images * PATCH * sum(rows.size for rows in held),
            bytes_accessed=6 * so_far.size + 2 * sum(rows.size for rows in held), transcendentals=0,
        ),
        name="late_stage",
    )(col, so_far, *held)


def early_kernel(
    col_ref, x1_ref, low_ref, held_own, held_near,
    tile_ref, tile_first, tile_second, tile_grad,
    router_ref, router_first, router_second, norm_ref, norm_first, norm_second, small_ref,
    sum_ref, input_ref, tile_new, tile_first_new, tile_second_new, tile_copy,
    router_new, router_first_new, router_second_new,
    norm_new, norm_first_new, norm_second_new, later_second_new,
):
    sum_ref[0] = x1_ref[0].astype(FULL) + mixed_rows(col_ref[0], held_own, held_near, 0)
    input_ref[0] = low_ref[0].astype(FULL)

    @pl.when(pl.program_id(0) == 0)
    def _():
        new, first, second = adam_update(
            tile_ref[...], tile_first[...], tile_second[...], tile_grad[...],
            rate_attention, decay_factor,
        )
        tile_new[...], tile_first_new[...], tile_second_new[...] = new, first, second
        tile_copy[...] = new.astype(LOW)
        experts = router_ref.shape[0]
        new, first, second = adam_update(
            router_ref[...], router_first[...], router_second[...], small_ref[0:experts, :],
            rate_router, decay_factor,
        )
        router_new[...], router_first_new[...], router_second_new[...] = new, first, second
        new, first, second = adam_update(
            norm_ref[...], norm_first[...], norm_second[...], small_ref[experts:experts + 4, :],
            rate_norm, 0.0,
        )
        norm_new[...], norm_first_new[...] = new, first
        norm_second_new[...], later_second_new[...] = second[0:2], second[2:4]


def early_stage(col, x1, input_low, held, tiles, routers, norms, small):
    images, _, width = x1.shape
    wide = lead((1, PATCH, width))
    tile, router, norm = tiles[0], routers[0], norms[0]
    fixed = [*held, *tiles, *routers, *norms, small]
    full = [tile.shape] * 3 + [tile.shape] + [router.shape] * 3 + [norm.shape] * 2 + [(2, width)] * 2
    kinds = [FULL] * 3 + [LOW] + [FULL] * 7
    return pl.pallas_call(
        early_kernel,
        grid=(images,),
        in_specs=[lead((1, PATCH, 4)), wide, wide] + [whole(array.shape) for array in fixed],
        out_specs=[wide, wide] + [whole(shape) for shape in full],
        out_shape=[jax.ShapeDtypeStruct(x1.shape, FULL), jax.ShapeDtypeStruct(x1.shape, FULL)]
        + [jax.ShapeDtypeStruct(shape, kind) for shape, kind in zip(full, kinds)],
        compiler_params=params(),
        cost_estimate=pl.CostEstimate(
            flops=2 * images * PATCH * sum(rows.size for rows in held),
            bytes_accessed=12 * x1.size + 2 * sum(rows.size for rows in held), transcendentals=0,
        ),
        name="early_stage",
    )(col, x1, input_low, *fixed)


def expert_kernel(
    slots,
    rows_ref, g_ref, router_in, col_ref, norm_ref,
    up_in, down_in, x1_in, cot_in,
    up_grad_ref, down_grad_ref, small_ref, down_out, out_out, x1g_out, passed_out,
    router_ref, up_ref, down_ref, og_ref, gate_ref, probs_ref, down_stage, back_ref, act_all,
    held, total, x1_ref, cot_ref, x1g_ref,
    load_sems, save_sems, image_sems, out_sem, pass_sem, *exchange,
):
    images, count = x1_in.shape[0], rows_ref.shape[0]
    out_sum, back_sum = total.at[pl.ds(0, count)], total.at[pl.ds(count, count)]
    up_sum = ImageSum(*exchange[:8])
    back = ReturnGather(slots, back_ref, held, *exchange[8:11])
    down_sum = BlockSum(down_out, 0, *exchange[11:], far=False)
    parts = up_in.shape[0]

    def load(turn):
        part, slot = up_sum.image(turn), lax.rem(turn, 2)
        return (
            pltpu.make_async_copy(up_in.at[part], up_ref.at[slot], load_sems.at[0, slot]),
            pltpu.make_async_copy(down_in.at[part], down_ref.at[slot], load_sems.at[1, slot]),
        )

    def save(turn):
        slot = lax.rem(turn, 2)
        return pltpu.make_async_copy(
            down_stage.at[slot], down_out.at[up_sum.image(turn)], save_sems.at[slot]
        )

    for turn in range(2):
        for copy in load(turn):
            copy.start()
    rows = rows_ref[...]
    experts = router_in.shape[0]
    router_ref[...] = jnp.zeros_like(router_ref)
    router_ref[0:experts, :] = router_in[...]
    lane = lax.broadcasted_iota(jnp.int32, (1, router_ref.shape[0]), 1)
    mine = jnp.where(lane == lax.axis_index("dp"), 1.0, 0.0)
    logits = nt(rows, router_ref[...].astype(LOW)) + jnp.where(lane < experts, 0.0, -1e30)
    top = jnp.max(logits, axis=-1, keepdims=True)
    weights = jnp.exp(logits - top)
    probs = weights / jnp.sum(weights, axis=-1, keepdims=True)
    gate = jnp.sum(probs * mine, axis=-1, keepdims=True)
    probs_ref[...] = probs
    gate_ref[...] = gate
    og_ref[...] = (gate * g_ref[...].astype(FULL)).astype(LOW)
    out_sum[...] = jnp.zeros_like(out_sum)
    back_sum[...] = jnp.zeros_like(back_sum)
    greet_all((back.near, back.far), slots.count)

    later = act_all.shape[0] > 1

    def down_grads(turn, act):
        @pl.when(turn >= 2)
        def _():
            save(turn - 2).wait()

        down_stage[lax.rem(turn, 2)] = tn(act, og_ref[...]).astype(LOW)
        save(turn).start()

    @pl.loop(0, parts)
    def _(turn):
        slot = lax.rem(turn, 2)
        for copy in load(turn):
            copy.wait()
        rows, og = rows_ref[...], og_ref[...]
        up, down = up_ref[slot], down_ref[slot]
        hidden = nn(rows, up)
        slope = (2.0 / jnp.pi) ** 0.5
        square = hidden * hidden
        bend = jnp.tanh(slope * (hidden + 0.044715 * (square * hidden)))
        act = (0.5 * hidden * (1.0 + bend)).astype(LOW)
        out_sum[...] += nn(act, down)
        act_grad = nt(og, down)
        inner = slope * (1.0 + (3.0 * 0.044715) * square)
        curve = 0.5 * (1.0 + bend) + 0.5 * hidden * (1.0 - bend * bend) * inner
        hidden_grad = (curve * act_grad).astype(LOW)
        back_sum[...] += nt(hidden_grad, up)
        up_sum.give(turn, tn(rows, hidden_grad), hold=True)
        if later:
            act_all[turn] = act
        else:
            down_grads(turn, act)

        @pl.when(turn + 2 < parts)
        def _():
            for copy in load(turn + 2):
                copy.start()

    out = out_sum[...].astype(LOW).astype(FULL)
    gate, probs = gate_ref[...], probs_ref[...]
    gate_grad = jnp.sum(g_ref[...].astype(FULL) * out, axis=-1, keepdims=True)
    logit_grad = (gate_grad * (probs * (mine - gate))).astype(LOW)
    plain = back_sum[...].astype(LOW).astype(FULL)
    back_ref[...] = (plain + nn(logit_grad, router_ref[...].astype(LOW))).astype(LOW)
    back.send(0)
    back.send(1)
    back.relay(0)
    small_ref[...] = jnp.zeros_like(small_ref)
    small_ref[0:experts, :] = tn(logit_grad, rows_ref[...])[0:experts]
    back_sum[...] = gate * out
    def image_load(image):
        slot = lax.rem(image, 2)
        return (
            pltpu.make_async_copy(x1_in.at[image], x1_ref.at[slot], image_sems.at[0, slot]),
            pltpu.make_async_copy(cot_in.at[image], cot_ref.at[slot], image_sems.at[1, slot]),
        )

    def image_save(image):
        slot = lax.rem(image, 2)
        return pltpu.make_async_copy(x1g_ref.at[slot], x1g_out.at[image], image_sems.at[2, slot])

    for image in range(2):
        for copy in image_load(image):
            copy.start()

    def relay(phase):
        @pl.loop(max(phase * slots.turns, 1), (phase + 1) * slots.turns)
        def _(shift):
            back.relay(shift)

    ahead = [
        lambda: (relay(0), back.send(2)),
        lambda: (relay(1), back.send(3)),
        lambda: (back.of_phase(0, back.forward), relay(2)),
        lambda: (back.of_phase(1, back.forward), relay(3)),
    ]
    if later:
        for turn in range(parts):
            down_grads(turn, act_all[turn])
            if turn < 3:
                ahead[turn]()
    else:
        for step in ahead[:3]:
            step()
    for turn in range(parts - 2, parts):
        save(turn).wait()
    down_sum.start()
    og_ref[...] = back_sum[...].astype(LOW)
    save_out = pltpu.make_async_copy(og_ref, out_out, out_sem)
    save_out.start()
    total_rows = held.shape[0]
    piece = 3 * 256
    if total_rows % piece:
        piece = slots.phase_rows
    done = 0
    back.of_phase(0, back.rest)
    for phase in range(1, 4):
        if phase == 1:
            ahead[3]()
            up_sum.start_rest()
        else:
            back.of_phase(phase, back.forward)
        back.of_phase(phase, back.rest)
        ready = (phase + 1) * slots.phase_rows
        while done + piece <= ready:
            @pl.loop(0, images)
            def _(image, start=done):
                part = picked_rows(col_ref[image], held, start, piece)
                span = pl.ds(image * PATCH, PATCH)
                if start == 0:
                    total[span] = part
                else:
                    total[span] += part

            done += piece

    back_scale = 1.0 / 4.0

    @pl.loop(0, images)
    def _(image):
        slot = lax.rem(image, 2)
        for copy in image_load(image):
            copy.wait()

        @pl.when(image >= 2)
        def _():
            image_save(image - 2).wait()

        normal, scale = normalise(x1_ref[slot].astype(FULL))
        upstream = total[pl.ds(image * PATCH, PATCH)]
        result, gain_sum, shift_sum = norm_back(normal, scale, norm_ref[2:3, :], upstream)
        x1g_ref[slot] = (cot_ref[slot].astype(FULL) + result).astype(LOW)
        small_ref[experts + 2:experts + 3, :] += gain_sum * back_scale
        small_ref[experts + 3:experts + 4, :] += shift_sum * back_scale
        image_save(image).start()

        @pl.when(image + 2 < images)
        def _():
            for copy in image_load(image + 2):
                copy.start()

    down_sum.across()
    save_passed = pltpu.make_async_copy(down_sum.passed, passed_out, pass_sem)
    save_passed.start()
    down_grad_ref[...] = down_sum.result()
    up_grad_ref[...] = up_sum.result()
    back.finish()
    up_sum.finish()
    down_sum.finish()
    save_passed.wait()
    save_out.wait()
    for image in range(images - 2, images):
        image_save(image).wait()


def expert_stage(slots, rows, g_rows, up, down, router, col, x1, cotangent, norm_params):
    count, width = rows.shape
    parts, _, units = up.shape
    images = x1.shape[0]
    small_rows = -(-(router.shape[0] + 4) // 16) * 16
    lanes = 128
    flat = pltpu.VMEM((count, width), LOW)
    pair = pltpu.VMEM((2, PATCH, width), LOW)
    return pl.pallas_call(
        functools.partial(expert_kernel, slots),
        in_specs=[INSIDE] * 5 + [ANYWHERE] * 4,
        out_specs=[INSIDE] * 3 + [ANYWHERE] * 4,
        out_shape=[
            jax.ShapeDtypeStruct((width, units), FULL),
            jax.ShapeDtypeStruct((units // 2, width), FULL),
            jax.ShapeDtypeStruct((small_rows, width), FULL),
            jax.ShapeDtypeStruct(down.shape, LOW),
            jax.ShapeDtypeStruct((count, width), LOW),
            jax.ShapeDtypeStruct(x1.shape, LOW),
            jax.ShapeDtypeStruct((units // 2, width), LOW),
        ],
        scratch_shapes=[
            pltpu.VMEM((lanes, width), FULL),
            pltpu.VMEM((2,) + up.shape[1:], LOW), pltpu.VMEM((2,) + down.shape[1:], LOW), flat,
            pltpu.VMEM((count, 1), FULL), pltpu.VMEM((count, lanes), FULL),
            pltpu.VMEM((2, units, width), LOW), flat,
            pltpu.VMEM((parts, count, units) if count <= MOST_KEPT else (1, 16, 128), LOW),
            pltpu.VMEM((4 * slots.phase_rows, width), LOW),
            pltpu.VMEM((max(images * PATCH, 2 * count), width), FULL), pair, pair, pair,
            pltpu.SemaphoreType.DMA((2, 2)), pltpu.SemaphoreType.DMA((2,)),
            pltpu.SemaphoreType.DMA((3, 2)), pltpu.SemaphoreType.DMA, pltpu.SemaphoreType.DMA,
        ]
        + image_sum_scratch(width, units) + return_gather_sems(slots.count)
        + block_sum_scratch(units // 2, width),
        compiler_params=params(collective_id=3, has_side_effects=True),
        name="expert_stage",
    )(
        rows, g_rows, router, col, norm_params, up, down, x1, cotangent,
    )


def body(
    patches, cotangent, expert_ids, slot_pos, owners,
    tile_master, tile_first, tile_second,
    expert_up, up_first, up_second,
    expert_down, down_first, down_second,
    router, router_first, router_second,
    norm_params, norm_first, norm_second,
):
    tok_rows, width = patches.shape
    experts = router.shape[0]
    capacity = tok_rows // experts
    dp_count = lax.axis_size("dp")
    head_count = lax.axis_size("head")
    images = tok_rows // PATCH
    slots = Slots(dp_count, capacity // head_count)
    slot_count = tile_master.shape[0]

    by_image = (images, PATCH, width)
    x_images, g_images = patches.reshape(by_image), cotangent.reshape(by_image)
    w, src, col, lse, xn, hat, up_all, down_all, *saved, x1, rows, g_rows = front(
        slots, tile_master.reshape(slot_count * TILE, width), x_images, g_images, norm_params,
        owners, expert_ids.T, slot_pos.T, expert_up[0], expert_down[0],
        owners.shape[1] * TILE,
    )
    up_grad, down_half, small, down_part, out, x1_grad, passed = expert_stage(
        slots, rows, g_rows, up_all, down_all, router, col, x1, g_images, norm_params
    )
    def from_head(rows, apart):
        return lax.ppermute(rows, "head", [(at, at ^ apart) for at in range(head_count)])

    passed = from_head(passed, 2)
    owned_grad, small, down_rest, input_low, out_back = attention_backward(
        experts, slots, slot_count * TILE,
        x1_grad, w, xn, hat, saved, lse, src, norm_params, small, x_images, out, down_part,
    )

    out_back, passed = lax.optimization_barrier((out_back, passed))
    out_far = from_head(out_back, 2)
    flat_tiles = (slot_count * TILE, width)
    (
        so_far, input_grad, tile_new, tile_first_new, tile_second_new, tile_copy,
        router_new, router_first_new, router_second_new,
        norm_new, norm_first_new, norm_second_new, later_second_new,
    ) = early_stage(
        col, x1, input_low, [out_back, from_head(out_back, 1)],
        [array.reshape(flat_tiles) for array in (tile_master, tile_first, tile_second)] + [owned_grad],
        [router, router_first, router_second], [norm_params, norm_first, norm_second], small,
    )
    up_new, up_first_new, up_second_new = adam_update(
        expert_up, up_first, up_second, up_grad[None], rate_up, decay_factor
    )
    out_far, so_far, _ = lax.optimization_barrier((out_far, so_far, up_new))
    block_out = late_stage(col, so_far, [out_far, from_head(out_far, 1)])
    down_half = down_half + passed.astype(FULL)
    down_grad = jnp.concatenate([down_half, down_rest], axis=0)
    tiles = [
        array.reshape(tile_master.shape)
        for array in (tile_new, tile_first_new, tile_second_new, tile_copy)
    ]
    down_new, down_first_new, down_second_new = adam_update(
        expert_down, down_first, down_second, down_grad[None], rate_down, decay_factor
    )
    return (
        block_out.reshape(tok_rows, width),
        input_grad.reshape(tok_rows, width),
        *tiles,
        up_new,
        up_first_new,
        up_second_new,
        up_new.astype(LOW),
        down_new,
        down_first_new,
        down_second_new,
        down_new.astype(LOW),
        router_new,
        router_first_new,
        router_second_new,
        norm_new,
        norm_first_new,
        norm_second_new,
        later_second_new,
    )


def solution(mesh):
    row = P("dp", None)
    tiles = P(("dp", "head"), None, None)
    up = P("dp", None, "head")
    down = P("dp", "head", None)
    in_specs = (
        row, row, row, row, P("head", None), tiles, tiles, tiles,
        up, up, up, down, down, down, P(), P(), P(), P(), P(), P(),
    )
    out_specs = (
        row, row, tiles, tiles, tiles, tiles, up, up, up, up, down, down, down, down,
        P(), P(), P(), P(), P(), P(), P(),
    )
    return jax.shard_map(body, mesh=mesh, in_specs=in_specs, out_specs=out_specs, check_vma=False)
```

```python
import functools

import jax
import jax.numpy as jnp
from jax import lax
from jax.experimental import pallas as pl
from jax.experimental.pallas import tpu as pltpu
from jax.sharding import PartitionSpec as P

HD = 64
PATCH = 576
TILE = 8
STEP = 10

eps_norm = 1e-06
beta_one = 0.9
beta_two = 0.999
adam_eps = 1e-08
rate_attention = 0.12
rate_up = 0.08
rate_down = 0.3
rate_router = 0.05
rate_norm = 0.4
decay_factor = 0.1

LOW = jnp.bfloat16
FULL = jnp.float32
MESH = pl.DeviceIdType.MESH
MOST_KEPT = 640
VMEM_BYTES = 61 * 1024 * 1024


def adam_update(weight, moment_one, moment_two, gradient, step_rate, weight_decay):
    moment_one = beta_one * moment_one + (1.0 - beta_one) * gradient
    moment_two = beta_two * moment_two + (1.0 - beta_two) * gradient * gradient
    fixed_one = moment_one / (1.0 - beta_one**STEP)
    fixed_two = moment_two / (1.0 - beta_two**STEP)
    weight = weight - step_rate * (
        fixed_one / (jnp.sqrt(fixed_two) + adam_eps) + weight_decay * weight
    )
    return (weight, moment_one, moment_two)


def nn(left, right):
    return lax.dot_general(left, right, (((1,), (0,)), ((), ())), preferred_element_type=FULL)


def nt(left, right):
    return lax.dot_general(left, right, (((1,), (1,)), ((), ())), preferred_element_type=FULL)


def tn(left, right):
    return lax.dot_general(left, right, (((0,), (0,)), ((), ())), preferred_element_type=FULL)


def params(**more):
    return pltpu.CompilerParams(vmem_limit_bytes=VMEM_BYTES, **more)


def whole(shape):
    return pl.BlockSpec(shape, lambda *_: (0,) * len(shape))


def lead(shape):
    return pl.BlockSpec(shape, lambda i: (i,) + (0,) * (len(shape) - 1))


def normalise(values):
    average = jnp.mean(values, axis=-1, keepdims=True)
    centred = values - average
    variance = jnp.mean(centred * centred, axis=-1, keepdims=True)
    scale = lax.rsqrt(variance + eps_norm)
    return centred * scale, scale


def norm_back(normal, scale, gain, upstream):
    inner = upstream * gain
    mean_inner = jnp.mean(inner, axis=-1, keepdims=True)
    mean_cross = jnp.mean(inner * normal, axis=-1, keepdims=True)
    result = scale * (inner - mean_inner - normal * mean_cross)
    gain_sum = jnp.sum(upstream * normal, axis=0, keepdims=True)
    shift_sum = jnp.sum(upstream, axis=0, keepdims=True)
    return result, gain_sum, shift_sum


def one_hot(condition):
    return jnp.where(condition, 1.0, 0.0).astype(LOW)


def remote(src, dst, sends, recvs, index, axis, other):
    return pltpu.make_async_remote_copy(
        src_ref=src, dst_ref=dst, send_sem=sends.at[index], recv_sem=recvs.at[index],
        device_id={axis: other}, device_id_type=MESH,
    )


def greet(*others):
    barrier = pltpu.get_barrier_semaphore()
    for axis, other in others:
        pl.semaphore_signal(barrier, inc=1, device_id={axis: other}, device_id_type=MESH)
    pl.semaphore_wait(barrier, len(others))


def partners():
    me = lax.axis_index("head")
    near = me + 1 - 2 * lax.rem(me, 2)
    far = lax.rem(me + 2, 4)
    corner = lax.rem(near + 2, 4)
    return me, near, far, corner


class LineGather:
    def __init__(self, held, up_send, up_recv, down_send, down_recv, pair_send, pair_recv):
        self.held = held
        self.length = held.shape[0] // 2
        self.sems = ((up_send, up_recv), (down_send, down_recv), (pair_send, pair_recv))
        me = lax.axis_index("dp")
        self.place, self.side = me // 2, lax.rem(me, 2)
        self.above = lax.rem(self.place + 1, self.length) * 2 + self.side
        self.below = lax.rem(self.place + self.length - 1, self.length) * 2 + self.side
        self.other = self.place * 2 + 1 - self.side

    def neighbours(self):
        return ("dp", self.above), ("dp", self.below), ("dp", self.other)

    def copy(self, way, origin, side=None):
        index = origin * 2 + (self.side if side is None else side)
        target = (self.above, self.below, self.other)[way]
        block = self.held.at[index]
        return remote(block, block, *self.sems[way], origin, "dp", target)

    def pass_on(self, origin, up, down):
        @pl.when(up & (self.place < self.length - 1))
        def _():
            self.copy(0, origin).start()

        @pl.when(down & (self.place > 0))
        def _():
            self.copy(1, origin).start()

        self.copy(2, origin).start()

    def start(self):
        self.pass_on(self.place, True, True)

    def step(self, k):
        low, high = self.place - k, self.place + k

        @pl.when(low >= 0)
        def _():
            self.copy(0, low).wait_recv()
            self.pass_on(low, True, False)

        @pl.when(high < self.length)
        def _():
            self.copy(1, high).wait_recv()
            self.pass_on(high, False, True)

    def finish(self):
        @pl.loop(0, self.length)
        def _(origin):
            self.copy(2, origin).wait_recv()
            self.copy(2, origin).wait_send()

            @pl.when((origin <= self.place) & (self.place < self.length - 1))
            def _():
                self.copy(0, origin).wait_send()

            @pl.when((origin >= self.place) & (self.place > 0))
            def _():
                self.copy(1, origin).wait_send()


class ImageSum:
    def __init__(self, stage, corner_in, near_in, passed, mine, far_in, sends, recvs):
        self.stage, self.corner_in, self.near_in = stage, corner_in, near_in
        self.passed, self.mine, self.far_in = passed, mine, far_in
        self.sends, self.recvs = sends, recvs
        self.me, self.near, self.far, self.corner = partners()
        self.core = lax.rem(self.me, 2)

    def image(self, turn):
        base = self.me - self.core
        other = lax.rem(base + 2, 4)
        return jnp.where(turn < 2, other, base - 2) + turn

    def to_corner(self):
        return remote(
            self.stage.at[0], self.corner_in, self.sends, self.recvs, 0, "head", self.near
        )

    def to_near(self):
        return remote(
            self.stage.at[1], self.near_in, self.sends, self.recvs, 1, "head", self.near
        )

    def to_far(self, half):
        rows = self.passed.shape[0] // 2
        span = pl.ds(half * rows, rows)
        return remote(
            self.passed.at[span], self.far_in.at[span], self.sends, self.recvs, 2 + half, "head",
            self.far,
        )

    def give(self, turn, part, hold=False):
        theirs = lax.rem(turn, 2) != self.core

        @pl.when((turn < 2) & theirs)
        def _():
            self.stage[0] = part.astype(LOW)
            self.to_corner().start()

        @pl.when((turn >= 2) & theirs)
        def _():
            self.stage[1] = part.astype(LOW)
            self.to_near().start()

        @pl.when((turn < 2) & ~theirs)
        def _():
            self.to_corner().wait_recv()
            self.passed[...] = (part + self.corner_in[...].astype(FULL)).astype(LOW)
            self.to_far(0).start()
            if not hold:
                self.to_far(1).start()

        @pl.when((turn >= 2) & ~theirs)
        def _():
            self.mine[...] = part

    def start_rest(self):
        self.to_far(1).start()

    def result(self):
        self.to_near().wait_recv()
        for half in range(2):
            self.to_far(half).wait_recv()
        return self.mine[...] + self.near_in[...].astype(FULL) + self.far_in[...].astype(FULL)

    def finish(self):
        self.to_corner().wait_send()
        self.to_near().wait_send()
        for half in range(2):
            self.to_far(half).wait_send()


def image_sum_scratch(rows, width):
    block = pltpu.VMEM((rows, width), LOW)
    return [
        pltpu.VMEM((2, rows, width), LOW), block, block, block,
        pltpu.VMEM((rows, width), FULL), block,
        pltpu.SemaphoreType.DMA((4,)), pltpu.SemaphoreType.DMA((4,)),
    ]


class LineScatter:
    def __init__(
        self, blocks, out, pair_in, up_in, down_in, total,
        up_send, up_recv, down_send, down_recv, pair_send, pair_recv,
    ):
        self.blocks, self.out, self.total = blocks, out, total
        self.arrived = (up_in, down_in, pair_in)
        self.sems = ((up_send, up_recv), (down_send, down_recv), (pair_send, pair_recv))
        self.length = blocks.shape[0] // 2
        me = lax.axis_index("dp")
        self.place, self.side = me // 2, lax.rem(me, 2)
        self.targets = (
            lax.rem(self.place + 1, self.length) * 2 + self.side,
            lax.rem(self.place + self.length - 1, self.length) * 2 + self.side,
            self.place * 2 + 1 - self.side,
        )

    def copy(self, way, block):
        source = (
            self.blocks.at[block * 2 + 1 - self.side] if way == 2 else self.total.at[block]
        )
        return remote(
            source, self.arrived[way].at[block], *self.sems[way], block, "dp", self.targets[way]
        )

    def start(self):
        @pl.loop(0, self.length)
        def _(turn):
            distance = self.length - 1 - turn

            @pl.when(self.place + distance < self.length)
            def _():
                self.copy(2, self.place + distance).start()

            @pl.when((self.place >= distance) & (distance > 0))
            def _():
                self.copy(2, self.place - distance).start()

    def pair_sum(self, block):
        self.copy(2, block).wait_recv()
        own = self.blocks[block * 2 + self.side].astype(FULL)
        return own + self.arrived[2][block].astype(FULL)

    def forward(self, way, block, first):
        both = self.pair_sum(block)

        @pl.when(first)
        def _():
            self.total[block] = both.astype(LOW)

        @pl.when(~first)
        def _():
            self.copy(way, block).wait_recv()
            self.total[block] = (both + self.arrived[way][block].astype(FULL)).astype(LOW)

        self.copy(way, block).start()

    def step(self, distance):
        @pl.when(self.place + distance < self.length)
        def _():
            self.forward(0, self.place + distance, self.place == 0)

        @pl.when(self.place >= distance)
        def _():
            self.forward(1, self.place - distance, self.place == self.length - 1)

    def result(self):
        self.out[...] = self.pair_sum(self.place)

        @pl.when(self.place > 0)
        def _():
            self.copy(0, self.place).wait_recv()
            self.out[...] += self.arrived[0][self.place].astype(FULL)

        @pl.when(self.place < self.length - 1)
        def _():
            self.copy(1, self.place).wait_recv()
            self.out[...] += self.arrived[1][self.place].astype(FULL)

    def finish(self):
        @pl.loop(0, self.length)
        def _(block):
            self.copy(2, block).wait_send()

            @pl.when(block > self.place)
            def _():
                self.copy(0, block).wait_send()

            @pl.when(block < self.place)
            def _():
                self.copy(1, block).wait_send()


def line_scatter_scratch(dp_count, rows, width):
    line = dp_count // 2
    return [pltpu.VMEM((line, rows, width), LOW)] * 4 + [pltpu.SemaphoreType.DMA((line,))] * 6


class SmallSum:
    def __init__(self, flat, head_in, dp_in, done, head_send, head_recv, dp_send, dp_recv):
        self.flat, self.head_in, self.dp_in, self.done = flat, head_in, dp_in, done
        self.head_sems, self.dp_sems = (head_send, head_recv), (dp_send, dp_recv)
        self.me, *self.others = partners()
        self.place, self.count = lax.axis_index("dp"), dp_in.shape[0]

    def to_head(self, lane):
        other = self.others[lane]
        return remote(
            self.flat.at[other], self.head_in.at[self.me], *self.head_sems, lane, "head", other
        )

    def back_head(self, lane):
        block = self.done.at[self.me]
        return remote(block, block, *self.head_sems, 3 + lane, "head", self.others[lane])

    def to_dp(self, shift):
        block = self.dp_in.at[self.place]
        other = lax.rem(self.place + shift, self.count)
        return remote(block, block, *self.dp_sems, shift, "dp", other)

    def start(self, value):
        groups, rows, lanes = self.flat.shape
        flat = jnp.concatenate(
            [value[:, at:at + lanes] for at in range(0, value.shape[1], lanes)], axis=0
        )
        for group in range(groups):
            self.flat[group] = flat[group * rows:(group + 1) * rows]
        for lane in range(3):
            self.to_head(lane).start()
        self.head_in[self.me] = self.flat[self.me]

    def across(self):
        for lane in range(3):
            self.to_head(lane).wait_recv()
        total = self.head_in[0]
        for head in range(1, self.head_in.shape[0]):
            total = total + self.head_in[head]
        self.dp_in[self.place] = total

        @pl.loop(1, self.count)
        def _(shift):
            self.to_dp(shift).start()

    def back(self):
        @pl.loop(1, self.count)
        def _(shift):
            self.to_dp(shift).wait_recv()

        total = lax.fori_loop(
            1, self.count, lambda at, so_far: so_far + self.dp_in[at], self.dp_in[0]
        )
        self.done[self.me] = total
        for lane in range(3):
            self.back_head(lane).start()

    def result(self, out):
        for lane in range(3):
            self.back_head(lane).wait_recv()
        flat = jnp.concatenate([self.done[group] for group in range(self.done.shape[0])], axis=0)
        rows, width = out.shape
        lanes = flat.shape[1]
        for at in range(width // lanes):
            out[:, at * lanes:(at + 1) * lanes] = flat[at * rows:(at + 1) * rows]

    def finish(self):
        for lane in range(3):
            self.to_head(lane).wait_send()
            self.back_head(lane).wait_send()

        @pl.loop(1, self.count)
        def _(shift):
            self.to_dp(shift).wait_send()


def small_sum_scratch(rows, width, dp_count):
    block = (rows * width // 128 // 4, 128)
    return [
        pltpu.VMEM((4,) + block, FULL), pltpu.VMEM((4,) + block, FULL),
        pltpu.VMEM((dp_count,) + block, FULL), pltpu.VMEM((4,) + block, FULL),
        pltpu.SemaphoreType.DMA((6,)), pltpu.SemaphoreType.DMA((6,)),
        pltpu.SemaphoreType.DMA((dp_count,)), pltpu.SemaphoreType.DMA((dp_count,)),
    ]


class LateSum:
    def __init__(self, dp_in, head_in, dp_send, dp_recv, head_send, head_recv):
        self.dp_in, self.head_in = dp_in, head_in
        self.dp_sems, self.head_sems = (dp_send, dp_recv), (head_send, head_recv)
        self.me, *self.others = partners()
        self.place, self.count = lax.axis_index("dp"), dp_in.shape[0]

    def to_dp(self, shift):
        block = self.dp_in.at[self.place]
        other = lax.rem(self.place + shift, self.count)
        return remote(block, block, *self.dp_sems, shift, "dp", other)

    def to_head(self, lane):
        block = self.head_in.at[self.me]
        return remote(block, block, *self.head_sems, lane, "head", self.others[lane])

    def start(self, rows):
        lanes = self.dp_in.shape[2]
        cuts = [
            row[:, at:at + lanes] for row in rows for at in range(0, row.shape[1], lanes)
        ]
        cuts += [jnp.zeros_like(cuts[0])] * (self.dp_in.shape[1] - len(cuts))
        self.dp_in[self.place] = jnp.concatenate(cuts, axis=0)

        @pl.loop(1, self.count)
        def _(shift):
            self.to_dp(shift).start()

    def across(self):
        @pl.loop(1, self.count)
        def _(shift):
            self.to_dp(shift).wait_recv()

        self.head_in[self.me] = lax.fori_loop(
            1, self.count, lambda at, so_far: so_far + self.dp_in[at], self.dp_in[0]
        )
        for lane in range(3):
            self.to_head(lane).start()

    def result(self, out, first):
        for lane in range(3):
            self.to_head(lane).wait_recv()
        total = self.head_in[0]
        for head in range(1, self.head_in.shape[0]):
            total = total + self.head_in[head]
        lanes = total.shape[1]
        cuts = out.shape[1] // lanes
        for row in range(2):
            for at in range(cuts):
                piece = total[row * cuts + at:row * cuts + at + 1]
                out[first + row:first + row + 1, at * lanes:(at + 1) * lanes] = piece

    def finish(self):
        for lane in range(3):
            self.to_head(lane).wait_send()

        @pl.loop(1, self.count)
        def _(shift):
            self.to_dp(shift).wait_send()


def late_sum_scratch(width, dp_count):
    block = (-(-2 * width // 128 // 8) * 8, 128)
    return [
        pltpu.VMEM((dp_count,) + block, FULL), pltpu.VMEM((4,) + block, FULL),
        pltpu.SemaphoreType.DMA((dp_count,)), pltpu.SemaphoreType.DMA((dp_count,)),
        pltpu.SemaphoreType.DMA((3,)), pltpu.SemaphoreType.DMA((3,)),
    ]


GATHER_CUTS = 4
COLUMN_CUTS = 3


class ImageGather:
    def __init__(self, held, sends, recvs, own=None, local_sem=None, columns=False):
        self.held, self.sends, self.recvs, self.columns = held, sends, recvs, columns
        self.me, self.near, self.far, self.corner = partners()
        self.own = held.at[self.me] if own is None else own
        self.local = None if own is None else pltpu.make_async_copy(own, held.at[self.me], local_sem)
        self.size = held.shape[1] // GATHER_CUTS
        self.wide = held.shape[2] // COLUMN_CUTS

    def piece(self, lane, cut):
        span = pl.ds(cut * self.size, self.size)
        image = self.far if lane == 2 else self.me
        if self.columns:
            block = self.held.at[image, :, pl.ds(cut * self.wide, self.wide)]
        else:
            block = self.held.at[image, span]
        source = block if self.columns or lane == 2 else self.own.at[span]
        other = self.far if lane == 0 else self.near
        index = lane * GATHER_CUTS + cut
        return remote(source, block, self.sends, self.recvs, index, "head", other)

    def start_far(self, first=0, last=GATHER_CUTS):
        for cut in range(first, last):
            self.piece(0, cut).start()

    def start_near(self, last=GATHER_CUTS):
        for cut in range(last):
            self.piece(1, cut).start()
        if self.local is not None:
            self.local.start()

    def start(self):
        self.start_far()
        self.start_near()

    def wait_near(self, first=0, last=GATHER_CUTS):
        for cut in range(first, last):
            self.piece(1, cut).wait_recv()

    def wait_far(self, first=0, last=GATHER_CUTS):
        for cut in range(first, last):
            self.piece(0, cut).wait_recv()
            self.piece(2, cut).start()

    def wait_corner(self, first=0, last=GATHER_CUTS):
        for cut in range(first, last):
            self.piece(2, cut).wait_recv()

    def finish(self, last=GATHER_CUTS):
        for cut in range(last):
            for lane in range(3):
                self.piece(lane, cut).wait_send()
        if self.local is not None:
            self.local.wait()


def image_gather_sems():
    return [pltpu.SemaphoreType.DMA((3 * GATHER_CUTS,)), pltpu.SemaphoreType.DMA((3 * GATHER_CUTS,))]


class BlockSum:
    def __init__(
        self, parts, first, mine, passed, corner_in, near_in, far_in, local_sems, sends, recvs, far=True
    ):
        self.with_far = far
        self.mine, self.passed, self.corner_in = mine, passed, corner_in
        self.near_in, self.far_in = near_in, far_in
        me, near, opposite, corner = partners()
        span = pl.ds(first, mine.shape[0])
        self.to_corner = remote(parts.at[corner, span], corner_in, sends, recvs, 0, "head", near)
        self.to_near = remote(parts.at[near, span], near_in, sends, recvs, 1, "head", near)
        if far:
            self.to_far = remote(passed, far_in, sends, recvs, 2, "head", opposite)
        self.load_far = pltpu.make_async_copy(parts.at[opposite, span], passed, local_sems.at[0])
        self.load_mine = pltpu.make_async_copy(parts.at[me, span], mine, local_sems.at[1])

    def start(self):
        for copy in (self.to_corner, self.load_far, self.to_near, self.load_mine):
            copy.start()

    def across(self):
        self.load_far.wait()
        self.to_corner.wait_recv()
        both = self.passed[...].astype(FULL) + self.corner_in[...].astype(FULL)
        self.passed[...] = both.astype(LOW)
        if self.with_far:
            self.to_far.start()

    def result(self):
        self.load_mine.wait()
        self.to_near.wait_recv()
        total = self.mine[...].astype(FULL) + self.near_in[...].astype(FULL)
        if self.with_far:
            self.to_far.wait_recv()
            total = total + self.far_in[...].astype(FULL)
        return total

    def finish(self):
        self.to_corner.wait_send()
        self.to_near.wait_send()
        if self.with_far:
            self.to_far.wait_send()


def block_sum_scratch(rows, width):
    return [pltpu.VMEM((rows, width), LOW)] * 5 + [
        pltpu.SemaphoreType.DMA((2,)), pltpu.SemaphoreType.DMA((3,)), pltpu.SemaphoreType.DMA((3,)),
    ]


class Slots:
    def __init__(self, count, share):
        self.count, self.share = count, share
        self.big = -(-share // 16) * 16
        rest = 2 * share - self.big
        self.small = rest if rest > 0 and rest % 16 == 0 else self.big
        self.more = self.big - self.small
        self.both = self.big + self.small
        self.rows = count // 2 * self.both
        self.turns = count // 4
        self.phase_rows = self.turns * 2 * self.both

    def size(self, source, head):
        return self.small + self.more * ((head + source + 1) % 2)

    def packed(self, source, head):
        return (source // 2) * self.both + (source % 2) * self.size(0, head)

    def row(self, source, head, shift):
        first = self.size(source, 0) * (head % 2)
        group = (head // 2) * self.turns * self.both + self.turns * first
        return (
            (shift // self.turns) * self.phase_rows + group
            + (shift % self.turns) * self.size(source, head)
        )

    def holder(self, source, slot):
        pair, within = slot // self.both, slot % self.both
        first = self.size(source, 0)
        second = jnp.where(within >= first, 1, 0)
        return 2 * pair + second, within - second * first

    def span(self, start, extra):
        if extra:
            return pl.ds(pl.multiple_of(start + self.small, 16), self.more)
        return pl.ds(pl.multiple_of(start, 16), self.small)

    def each(self, is_big, make, action):
        getattr(make(False), action)()
        if self.more:
            @pl.when(is_big)
            def _():
                getattr(make(True), action)()


class SlotExchange:
    def __init__(self, slots, sent, rows, sends, recvs, local_sems, cut=None):
        self.slots, self.sent, self.rows = slots, sent, rows
        self.sems, self.local_sems = (sends, recvs), local_sems
        self.place, self.head = lax.axis_index("dp"), lax.axis_index("head")
        wide = sent.shape[1] // COLUMN_CUTS
        self.cut = 0 if cut is None else cut
        self.lanes = pl.ds(0, sent.shape[1]) if cut is None else pl.ds(cut * wide, wide)

    def index(self, shift, extra):
        return 2 * (self.cut * self.slots.count + shift) + int(extra)

    def out(self, shift, action):
        slots = self.slots
        expert = lax.rem(self.place + shift, slots.count)
        mine = slots.size(self.place, self.head)
        at, to = expert * mine, slots.packed(self.place, self.head)
        slots.each(mine > slots.small, lambda extra: remote(
            self.sent.at[slots.span(at, extra), self.lanes], self.rows.at[slots.span(to, extra), self.lanes],
            *self.sems, self.index(shift, extra), "dp", expert,
        ), action)

    def into(self, shift):
        slots = self.slots
        source = lax.rem(self.place + slots.count - shift, slots.count)
        size = slots.size(source, self.head)
        to = slots.packed(source, self.head)
        slots.each(size > slots.small, lambda extra: remote(
            self.sent.at[slots.span(0, extra), self.lanes], self.rows.at[slots.span(to, extra), self.lanes],
            *self.sems, self.index(shift, extra), "dp", source,
        ), "wait_recv")

    def own(self, action):
        slots = self.slots
        mine = slots.size(self.place, self.head)
        at, to = self.place * mine, slots.packed(self.place, self.head)
        slots.each(mine > slots.small, lambda extra: pltpu.make_async_copy(
            self.sent.at[slots.span(at, extra), self.lanes], self.rows.at[slots.span(to, extra), self.lanes],
            self.local_sems.at[2 * self.cut + int(extra)],
        ), action)

    def start(self):
        @pl.loop(1, self.slots.count)
        def _(shift):
            self.out(shift, "start")

        self.own("start")

    def finish(self):
        @pl.loop(1, self.slots.count)
        def _(shift):
            self.into(shift)
            self.out(shift, "wait_send")

        self.own("wait")


class SlotReturn:
    def __init__(self, slots, rows, back, zeros, sends, recvs, local_sems):
        self.slots, self.rows, self.back, self.zeros = slots, rows, back, zeros
        self.sems, self.local_sems = (sends, recvs), local_sems
        self.place, self.head = lax.axis_index("dp"), lax.axis_index("head")
        self.mine = slots.size(self.place, self.head)

    def out(self, shift, action):
        slots = self.slots
        source = lax.rem(self.place + shift, slots.count)
        size = slots.size(source, self.head)
        at, to = slots.packed(source, self.head), shift * size
        slots.each(size > slots.small, lambda extra: remote(
            self.rows.at[slots.span(at, extra)], self.back.at[slots.span(to, extra)],
            *self.sems, 2 * shift + int(extra), "dp", source,
        ), action)

    def into(self, shift):
        slots = self.slots
        expert = lax.rem(self.place + slots.count - shift, slots.count)
        slots.each(self.mine > slots.small, lambda extra: remote(
            self.rows.at[slots.span(0, extra)], self.back.at[slots.span(shift * self.mine, extra)],
            *self.sems, 2 * shift + int(extra), "dp", expert,
        ), "wait_recv")

    def own(self, action):
        slots = self.slots
        at = slots.packed(self.place, self.head)
        slots.each(self.mine > slots.small, lambda extra: pltpu.make_async_copy(
            self.rows.at[slots.span(at, extra)], self.back.at[slots.span(0, extra)],
            self.local_sems.at[int(extra)],
        ), action)

    def blank(self, action):
        slots = self.slots
        if slots.more:
            @pl.when(self.mine == slots.small)
            def _():
                tail = self.back.at[pl.ds(slots.count * slots.small, slots.count * slots.more)]
                copy = pltpu.make_async_copy(self.zeros, tail, self.local_sems.at[2])
                getattr(copy, action)()

    def start(self):
        if self.slots.more:
            self.zeros[...] = jnp.zeros_like(self.zeros)
        self.blank("start")

        @pl.loop(1, self.slots.count)
        def _(shift):
            self.out(shift, "start")

        self.own("start")

    def finish(self):
        @pl.loop(1, self.slots.count)
        def _(shift):
            self.into(shift)
            self.out(shift, "wait_send")

        self.own("wait")
        self.blank("wait")


def slot_return_scratch(slots, width):
    return [pltpu.VMEM((max(slots.count * slots.more, 16), width), LOW)] + [
        pltpu.SemaphoreType.DMA((2 * slots.count,)), pltpu.SemaphoreType.DMA((2 * slots.count,)),
        pltpu.SemaphoreType.DMA((3,)),
    ]


def slot_exchange_sems(count, cuts=1):
    return [
        pltpu.SemaphoreType.DMA((2 * count * cuts,)), pltpu.SemaphoreType.DMA((2 * count * cuts,)),
        pltpu.SemaphoreType.DMA((2 * cuts,)),
    ]


class ReturnGather:
    def __init__(self, slots, rows, held, sends, recvs, local_sems):
        self.slots, self.rows, self.held = slots, rows, held
        self.sems, self.local_sems = (sends, recvs), local_sems
        self.place = lax.axis_index("dp")
        self.me, self.near, self.far, self.corner = partners()

    def out(self, shift, action):
        slots = self.slots
        source = lax.rem(self.place + shift, slots.count)
        size = slots.size(source, self.me)
        at, to = slots.packed(source, self.me), slots.row(source, self.me, shift)
        slots.each(size > slots.small, lambda extra: remote(
            self.rows.at[slots.span(at, extra)], self.held.at[slots.span(to, extra)],
            *self.sems, 2 * shift + int(extra), "dp", source,
        ), action)

    def own(self, action):
        slots = self.slots
        size = slots.size(self.place, self.me)
        at, to = slots.packed(self.place, self.me), slots.row(self.place, self.me, 0)
        slots.each(size > slots.small, lambda extra: pltpu.make_async_copy(
            self.rows.at[slots.span(at, extra)], self.held.at[slots.span(to, extra)],
            self.local_sems.at[int(extra)],
        ), action)

    def block(self, lane, head, shift, axis, other, action):
        slots = self.slots
        size = slots.size(self.place, head)
        to = slots.row(self.place, head, shift)

        def make(extra):
            block = self.held.at[slots.span(to, extra)]
            index = 2 * (lane * slots.count + shift) + int(extra)
            return remote(block, block, *self.sems, index, axis, other)

        slots.each(size > slots.small, make, action)

    def send(self, phase):
        turns = self.slots.turns
        if phase == 0:
            self.own("start")

        @pl.loop(max(phase * turns, 1), (phase + 1) * turns)
        def _(shift):
            self.out(shift, "start")

    def relay(self, shift):
        @pl.when(shift == 0)
        def _():
            self.own("wait")

        @pl.when(shift > 0)
        def _():
            expert = lax.rem(self.place + self.slots.count - shift, self.slots.count)
            self.block(0, self.me, shift, "dp", expert, "wait_recv")

        self.block(1, self.me, shift, "head", self.far, "start")
        self.block(2, self.me, shift, "head", self.near, "start")

    def forward(self, shift):
        self.block(1, self.far, shift, "head", self.far, "wait_recv")
        self.block(3, self.far, shift, "head", self.near, "start")

    def rest(self, shift):
        self.block(2, self.near, shift, "head", self.near, "wait_recv")
        self.block(3, self.corner, shift, "head", self.near, "wait_recv")

    def of_phase(self, phase, action):
        @pl.loop(0, self.slots.turns)
        def _(turn):
            action(phase * self.slots.turns + turn)

    def finish(self):
        @pl.loop(0, self.slots.count)
        def _(shift):
            @pl.when(shift > 0)
            def _():
                self.out(shift, "wait_send")

            self.block(1, self.me, shift, "head", self.far, "wait_send")
            self.block(2, self.me, shift, "head", self.near, "wait_send")
            self.block(3, self.far, shift, "head", self.near, "wait_send")


def return_gather_sems(count):
    return [
        pltpu.SemaphoreType.DMA((8 * count,)), pltpu.SemaphoreType.DMA((8 * count,)),
        pltpu.SemaphoreType.DMA((2,)),
    ]


def greet_all(heads, dp_count):
    barrier = pltpu.get_barrier_semaphore()
    place = lax.axis_index("dp")
    for other in heads:
        pl.semaphore_signal(barrier, inc=1, device_id={"head": other}, device_id_type=MESH)

    @pl.loop(1, dp_count)
    def _(shift):
        other = lax.rem(place + shift, dp_count)
        pl.semaphore_signal(barrier, inc=1, device_id={"dp": other}, device_id_type=MESH)

    pl.semaphore_wait(barrier, len(heads) + dp_count - 1)


ANYWHERE = pl.BlockSpec(memory_space=pl.ANY)
INSIDE = pl.BlockSpec(memory_space=pltpu.VMEM)


def digits(values):
    high = lax.div(values, 64)
    return [high.astype(FULL), (values - high * 64).astype(FULL)]


def digit_weights(shape, digit_axis):
    digit = lax.broadcasted_iota(jnp.int32, shape, digit_axis)
    value = lax.broadcasted_iota(jnp.int32, shape, 1 - digit_axis)
    weight = jnp.where(lax.rem(digit, 2) == 0, 64.0, 1.0)
    return jnp.where(lax.div(digit, 2) == value, weight, 0.0).astype(LOW)


def turned_rows(rows):
    count = rows[0].shape[1]
    parts = [part for row in rows for part in digits(row)]
    parts += [jnp.zeros((1, count), FULL)] * (8 - len(parts))
    spread = jnp.concatenate(parts, axis=0).astype(LOW)
    return tn(spread, digit_weights((8, 128), 0)).astype(jnp.int32)


def turned_column(column):
    lanes = lax.broadcasted_iota(jnp.int32, (column.shape[0], 128), 1)
    high, low = digits(column)
    spread = jnp.where(lanes == 0, high, jnp.where(lanes == 1, low, 0.0)).astype(LOW)
    return nt(digit_weights((8, 128), 1), spread)[0:1].astype(jnp.int32)


def head_mask(shape, axis, head):
    return lax.broadcasted_iota(jnp.int32, shape, axis) // HD == head


def front_kernel(
    slots, slot_count, capacity,
    tile_ref, norm_ref, owner_ref, ids_in, pos_in, up_in, down_in, x_in, g_in,
    w_ref, src_ref, col_back_ref, lse_ref,
    xn_out, hat_out, up_out, down_out, q_out, qt_out, k_out, kt_out, v_out, ot_out, x1_out,
    rows_out, g_rows_out,
    x_ref, g_ref, xn_ref, hat_ref, full_ref, up_low, down_low, held, picks, sent_sum, sent_g, sent_ref,
    q_ref, qt_ref, k_ref, kt_ref, v_ref, ot_ref, stats, norms, ids_ref, pos_ref,
    load_sems, image_sems, save_sems, keep_sem, stat_send, stat_recv, *exchange,
):
    images = x_ref.shape[0]
    for image in range(images):
        lanes = slice(image * PATCH, (image + 1) * PATCH)
        ids_ref[image], pos_ref[image] = ids_in[:, lanes], pos_in[:, lanes]
    x1_ref = g_ref
    gather = LineGather(held, *exchange[:6])
    spread_up = ImageGather(up_out, *exchange[6:8], own=up_low, local_sem=exchange[8])
    spread_down = ImageGather(down_out, *exchange[9:11], own=down_low, local_sem=exchange[11])
    total_of = ImageSum(*exchange[12:20])
    spread = ImageGather(x1_ref, *exchange[20:22], columns=True)
    send_g = SlotExchange(slots, sent_g, g_rows_out, *exchange[22:25])
    send_rows = [
        SlotExchange(slots, sent_ref, rows_out, *exchange[25:], cut=cut) for cut in range(COLUMN_CUTS)
    ]
    head, near, far, corner = partners()
    load_up = pltpu.make_async_copy(up_in, full_ref, load_sems.at[2, 0])
    load_down = pltpu.make_async_copy(down_in, full_ref, load_sems.at[2, 1])
    load_up.start()

    def load_image(image):
        return (
            pltpu.make_async_copy(x_in.at[image], x_ref.at[image], load_sems.at[0, image]),
            pltpu.make_async_copy(g_in.at[image], g_ref.at[image], load_sems.at[1, image]),
        )

    def save_image(image):
        return [
            pltpu.make_async_copy(xn_ref.at[image], xn_out.at[image], image_sems.at[0, image]),
            pltpu.make_async_copy(hat_ref.at[image], hat_out.at[image], image_sems.at[1, image]),
        ]

    kept_refs = (
        (q_ref, q_out), (qt_ref, qt_out), (k_ref, k_out), (kt_ref, kt_out), (v_ref, v_out),
        (ot_ref, ot_out),
    )

    def save(image):
        return [
            pltpu.make_async_copy(ref.at[image], out.at[image], save_sems.at[index, image])
            for index, (ref, out) in enumerate(kept_refs)
        ]

    for image in range(images):
        for copy in load_image(image):
            copy.start()
    me = lax.axis_index("dp")
    held[me] = tile_ref[...].astype(LOW)
    greet_all((near, far, corner), slots.count)
    gather.start()
    load_up.wait()
    up_low[...] = full_ref[...].astype(LOW)
    spread_up.start()
    load_down.start()
    shape = (sent_ref.shape[0], PATCH)
    sent_sum[...] = jnp.zeros_like(sent_sum)
    steps = gather.length - 1

    def image_step(image):
        for copy in load_image(image):
            copy.wait()
        normal, _ = normalise(x_ref[image].astype(FULL))
        hat_ref[image] = normal.astype(LOW)
        xn_ref[image] = (normal * norm_ref[0:1, :] + norm_ref[1:2, :]).astype(LOW)
        for copy in save_image(image):
            copy.start()

        ids, pos = ids_ref[image], pos_ref[image]
        kept = pos < capacity
        holder, within = slots.holder(me, jnp.minimum(pos, capacity - 1))
        sent_at = ids * slots.size(me, head) + within
        sent_at = jnp.where(kept & (holder == head), sent_at, slots.count * slots.big)
        shift = me - ids
        shift = jnp.where(shift < 0, shift + slots.count, shift)
        back_at = jnp.where(kept, slots.row(me, holder, shift) + within + 1, 0)
        other_pair = jnp.where(lax.div(holder, 2) == lax.div(head, 2), 0, 2)
        apart = other_pair + jnp.where(lax.rem(holder, 2) == lax.rem(head, 2), 0, 1)
        out_at = apart * (slots.count * slots.big) + shift * slots.size(me, holder) + within
        out_at = jnp.where(kept, out_at + 1, 0)
        turned = turned_rows([back_at[0:1], back_at[1:2], out_at[0:1], out_at[1:2]])
        col_back_ref[image] = turned[:, 0:4] - 1
        first, second = sent_at[0:1], sent_at[1:2]
        sent_slots = lax.broadcasted_iota(jnp.int32, shape, 0)
        pick = one_hot((sent_slots == first) | (sent_slots == second))
        picks[image] = pick
        sent_sum[...] += nn(pick, g_ref[image])

    @pl.loop(0, max(steps, (images + 1) // 2))
    def _(turn):
        @pl.loop(2 * turn, jnp.minimum(2 * turn + 2, images))
        def _(image):
            image_step(image)

        @pl.when(turn < steps)
        def _():
            gather.step(turn + 1)

        @pl.when(turn == 1)
        def _():
            spread_up.wait_far(0, 1)

    sent_g[...] = sent_sum[...].astype(LOW)
    load_down.wait()
    down_low[...] = full_ref[...].astype(LOW)

    rows = w_ref.shape[0]
    tiles = owner_ref.shape[1]
    row_tile = lax.div(lax.broadcasted_iota(jnp.int32, (rows, tiles), 0), TILE)
    lane_tile = lax.broadcasted_iota(jnp.int32, (rows, tiles), 1)
    owner_rows = jnp.broadcast_to(owner_ref[...].astype(FULL), (8, tiles)).astype(LOW)
    owner = nt(one_hot(lane_tile == row_tile), owner_rows)[:, 0:1].astype(jnp.int32)
    before = (owner_ref[...] == owner) & (lane_tile < row_tile)
    rank = jnp.sum(jnp.where(before, 1.0, 0.0), axis=1, keepdims=True).astype(jnp.int32)
    within = lax.rem(lax.broadcasted_iota(jnp.int32, (rows, 1), 0), TILE)
    src = (owner * slot_count + rank) * TILE + within
    src_ref[...] = turned_column(src)
    spread_up.wait_far(1, 3)
    gather.finish()
    blocks, depth, width = held.shape
    cut = rows // 4
    for part in range(4):
        lanes = lax.broadcasted_iota(jnp.int32, (cut, blocks * depth), 1)
        pick = one_hot(lanes == src[part * cut:(part + 1) * cut])
        block = nn(pick, held[...].reshape(blocks * depth, width))
        w_ref[pl.ds(part * cut, cut), :] = block.astype(LOW)
    spread_down.start_far(0, 1)
    spread_down.start_near()
    send_g.start()
    me = head
    shrink = HD ** (-0.5)

    part_rows = w_ref.shape[0] // 4
    heads = part_rows // HD

    @pl.loop(0, images)
    def _(turn):
        image = total_of.image(turn)
        xn = xn_ref[image]
        wq, wk, wv, wo = (
            w_ref[pl.ds(part * part_rows, part_rows), :] for part in range(4)
        )
        q = (nt(xn, wq) * shrink).astype(LOW)
        q_ref[image] = q
        qt = q.T
        qt_ref[image] = qt
        k = nt(xn, wk).astype(LOW)
        k_ref[image] = k
        kt_ref[image] = k.T
        v = nt(xn, wv).astype(LOW)
        v_ref[image] = v
        vt = v.T
        mixed = []
        for head in range(heads):
            span = slice(head * HD, (head + 1) * HD)
            only = jnp.where(head_mask(qt.shape, 0, head), qt, jnp.zeros_like(qt))
            scores = nn(k, only)
            top = jnp.max(scores, axis=0, keepdims=True)
            weights = jnp.exp(scores - top)
            total = jnp.sum(weights, axis=0, keepdims=True)
            mixed.append(nn(vt[span], weights.astype(LOW)) / total)
            lse_ref[image, head:head + 1, :] = top + jnp.log(total)
        ot = jnp.concatenate(mixed, axis=0).astype(LOW)
        ot_ref[image] = ot
        total_of.give(turn, tn(ot, wo))
        for copy in save(image):
            copy.start()

        @pl.when(turn == 0)
        def _():
            spread_up.wait_far(3)

    x1 = (x_ref[me].astype(FULL) + total_of.result()).astype(LOW)
    x1_ref[me] = x1
    values = x1.astype(FULL)
    average = jnp.mean(values, axis=-1, keepdims=True)
    centred = values - average
    scale = lax.rsqrt(jnp.mean(centred * centred, axis=-1, keepdims=True) + eps_norm)
    lanes = lax.broadcasted_iota(jnp.int32, (PATCH, 128), 1)
    pair = jnp.where(lanes == 0, average, jnp.where(lanes == 1, scale, 0.0))
    eye = (8, 128)
    eye = lax.broadcasted_iota(jnp.int32, eye, 0) == lax.broadcasted_iota(jnp.int32, eye, 1)
    eye = jnp.where(eye, 1.0, 0.0)
    stats[me] = lax.dot_general(
        eye, pair, (((1,), (1,)), ((), ())), precision=lax.Precision.HIGHEST,
        preferred_element_type=FULL,
    )
    tell = [
        remote(stats.at[me], stats.at[me], stat_send, stat_recv, lane, "head", other)
        for lane, other in enumerate((near, far, corner))
    ]
    for copy in tell:
        copy.start()
    spread.start_far(0, COLUMN_CUTS)
    spread.start_near(COLUMN_CUTS)
    spread_down.start_far(1)

    for copy in tell:
        copy.wait_recv()

    @pl.loop(0, images)
    def _(image):
        norms[image] = lax.dot_general(
            stats[image], eye, (((0,), (0,)), ((), ())), precision=lax.Precision.HIGHEST,
            preferred_element_type=FULL,
        )

    for cut in range(COLUMN_CUTS):
        wide = sent_ref.shape[1] // COLUMN_CUTS
        span = slice(cut * wide, (cut + 1) * wide)

        def place(image, span=span):
            normal = (x1_ref[image, :, span].astype(FULL) - norms[image, :, 0:1]) * norms[image, :, 1:2]
            low = (normal * norm_ref[2:3, span] + norm_ref[3:4, span]).astype(LOW)
            return nn(picks[image], low)

        total = place(me)
        spread.wait_near(cut, cut + 1)
        total = total + place(near)
        spread.wait_far(cut, cut + 1)
        total = total + place(far)
        spread.wait_corner(cut, cut + 1)
        sent_ref[:, span] = (total + place(corner)).astype(LOW)
        send_rows[cut].start()

    keep = pltpu.make_async_copy(x1_ref, x1_out, keep_sem)
    keep.start()
    for copy in tell:
        copy.wait_send()
    spread.finish(COLUMN_CUTS)
    total_of.finish()
    send_g.finish()
    spread_down.wait_far()
    spread_down.wait_near()
    spread_down.wait_corner()
    spread_down.finish()
    spread_up.wait_near()
    spread_up.wait_corner()
    spread_up.finish()
    for copy in send_rows:
        copy.finish()
    keep.wait()

    @pl.loop(0, images)
    def _(image):
        for copy in save(image) + save_image(image):
            copy.wait()


def front(slots, tiles, patches, cotangent, norm_params, owners, ids, pos, up, down, weight_rows):
    images, _, width = patches.shape
    slot_count = tiles.shape[0] // TILE
    line = slots.count // 2
    most = slots.count * slots.big
    capacity = images * PATCH // slots.count
    rows = weight_rows // 4
    flat, turned = (images, PATCH, rows), (images, rows, PATCH)
    saved = [flat, turned, flat, turned, flat, turned]
    outs = (
        [patches.shape] * 2 + [(4,) + up.shape, (4,) + down.shape] + saved
        + [patches.shape] + [(slots.rows, width)] * 2
    )
    return pl.pallas_call(
        functools.partial(front_kernel, slots, slot_count, capacity),
        in_specs=[INSIDE] * 5 + [ANYWHERE] * 4,
        out_specs=[INSIDE] * 4 + [ANYWHERE] * len(outs),
        out_shape=[
            jax.ShapeDtypeStruct((weight_rows, width), LOW),
            jax.ShapeDtypeStruct((1, weight_rows), jnp.int32),
            jax.ShapeDtypeStruct((images, PATCH, 4), jnp.int32),
            jax.ShapeDtypeStruct((images, 8, PATCH), FULL),
        ]
        + [jax.ShapeDtypeStruct(shape, LOW) for shape in outs],
        scratch_shapes=[pltpu.VMEM(patches.shape, LOW)] * 4
        + [
            pltpu.VMEM(up.shape, FULL), pltpu.VMEM(up.shape, LOW), pltpu.VMEM(down.shape, LOW),
            pltpu.VMEM((slots.count,) + tiles.shape, LOW), pltpu.VMEM((images, most, PATCH), LOW),
            pltpu.VMEM((most, width), FULL), pltpu.VMEM((most, width), LOW),
            pltpu.VMEM((most, width), LOW),
        ]
        + [pltpu.VMEM(shape, LOW) for shape in saved]
        + [
            pltpu.VMEM((images, 8, PATCH), FULL), pltpu.VMEM((images, PATCH, 128), FULL),
            pltpu.VMEM((images, 2, PATCH), jnp.int32), pltpu.VMEM((images, 2, PATCH), jnp.int32),
            pltpu.SemaphoreType.DMA((3, images)), pltpu.SemaphoreType.DMA((2, images)),
            pltpu.SemaphoreType.DMA((6, images)), pltpu.SemaphoreType.DMA,
            pltpu.SemaphoreType.DMA((3,)), pltpu.SemaphoreType.DMA((3,)),
        ]
        + [pltpu.SemaphoreType.DMA((line,))] * 6
        + image_gather_sems() + [pltpu.SemaphoreType.DMA]
        + image_gather_sems() + [pltpu.SemaphoreType.DMA]
        + image_sum_scratch(PATCH, width) + image_gather_sems()
        + slot_exchange_sems(slots.count) + slot_exchange_sems(slots.count, COLUMN_CUTS),
        compiler_params=params(collective_id=0, has_side_effects=True),
        name="front",
    )(tiles, norm_params, owners, ids, pos, up, down, patches, cotangent)


def backward_kernel(
    experts, slots,
    w_ref, lse_ref, src_ref, norm_ref, small_ref,
    x1g_in, xn_in, hat_in, q_in, qt_in, k_in, kt_in, v_in, ot_in, x_ref, out_rows_ref, down_part,
    owned_ref, small_out, down_grad_ref, input_out, out_back,
    x1g_ref, xn_ref, hat_ref, q_ref, qt_ref, k_ref, kt_ref, v_ref, ot_ref, late_ref,
    grad_ref, own_ref, input_ref, padded_ref, load_sems, own_sem, *exchange,
):
    images = x1g_ref.shape[0]
    rows = w_ref.shape[0] // 4
    heads = rows // HD
    total_of = ImageSum(*exchange[:8])
    spread = ImageGather(input_ref, *exchange[8:10])
    back_out = SlotReturn(slots, out_rows_ref, out_back, *exchange[10:14])
    weights_sum = LineScatter(padded_ref, owned_ref, *exchange[14:24])
    down_sum = BlockSum(down_part, down_part.shape[1] // 2, *exchange[24:32])
    small_sum = SmallSum(*exchange[32:40])
    late_sum = LateSum(*exchange[40:])
    me, near, far, corner = partners()
    dp_count = slots.count
    streamed = (
        (xn_in, xn_ref), (hat_in, hat_ref), (q_in, q_ref), (qt_in, qt_ref), (k_in, k_ref), (kt_in, kt_ref),
        (v_in, v_ref), (ot_in, ot_ref),
    )

    def load(turn):
        image, slot = total_of.image(turn), lax.rem(turn, 2)
        copies = [
            pltpu.make_async_copy(source.at[image], target.at[slot], load_sems.at[index, slot])
            for index, (source, target) in enumerate(streamed)
        ]
        copies.append(
            pltpu.make_async_copy(x1g_in.at[image], x1g_ref.at[image], load_sems.at[8, slot])
        )
        return copies

    for turn in range(2):
        for copy in load(turn):
            copy.start()
    own = pltpu.make_async_copy(x_ref.at[me], own_ref, own_sem.at[0])
    own.start()
    greet_all((near, far, corner), dp_count)
    small_sum.start(small_ref[...])
    down_sum.start()
    back_out.start()
    late_ref[...] = jnp.zeros_like(late_ref)
    shrink = HD ** (-0.5)
    grad_ref[...] = jnp.zeros_like(grad_ref)

    @pl.loop(0, images)
    def _(turn):
        image, slot = total_of.image(turn), lax.rem(turn, 2)
        for copy in load(turn):
            copy.wait()
        wq, wk, wv, wo = (w_ref[pl.ds(part * rows, rows), :] for part in range(4))
        x1g, xn = x1g_ref[image], xn_ref[slot]
        q, qt, k, kt = q_ref[slot], qt_ref[slot], k_ref[slot], kt_ref[slot]
        v, ot = v_ref[slot], ot_ref[slot]
        do = nt(x1g, wo).astype(LOW)
        dot = do.T
        product = dot.astype(FULL) * ot.astype(FULL)
        dqt, dk, dv = [], None, None
        for head in range(heads):
            span = slice(head * HD, (head + 1) * HD)
            zero_t = jnp.zeros_like(qt)
            mask_t = head_mask(qt.shape, 0, head)
            mask = head_mask(q.shape, 1, head)
            scores = nn(k, jnp.where(mask_t, qt, zero_t))
            weights = jnp.exp(scores - lse_ref[image, head:head + 1, :])
            back = nn(v, jnp.where(mask_t, dot, zero_t))
            delta = jnp.sum(product[span], axis=0, keepdims=True)
            score_grad = (weights * (back - delta)).astype(LOW)
            dqt.append(nn(kt[span], score_grad) * shrink)
            dk_one = nn(score_grad, jnp.where(mask, q, jnp.zeros_like(q)))
            dv_one = nn(weights.astype(LOW), jnp.where(mask, do, jnp.zeros_like(do)))
            dk = dk_one if dk is None else dk + dk_one
            dv = dv_one if dv is None else dv + dv_one
        dqt = jnp.concatenate(dqt, axis=0).astype(LOW)
        dk, dv = dk.astype(LOW), dv.astype(LOW)
        part = tn(dqt, wq) + nn(dk, wk) + nn(dv, wv)
        total_of.give(turn, part)
        late_ref[0:1, :] += jnp.sum(part * hat_ref[slot].astype(FULL), axis=0, keepdims=True)
        late_ref[1:2, :] += jnp.sum(part, axis=0, keepdims=True)
        three = jnp.concatenate([dqt, dk.T, dv.T], axis=0)
        grad_ref[pl.ds(0, 3 * rows), :] += nn(three, xn)
        grad_ref[pl.ds(3 * rows, rows), :] += nn(ot, x1g)

        @pl.when(turn + 2 < images)
        def _():
            for copy in load(turn + 2):
                copy.start()

        @pl.when(turn == 0)
        def _():
            down_sum.across()

        @pl.when(turn == 1)
        def _():
            small_sum.across()

    late_sum.start([late_ref[0:1, :], late_ref[1:2, :]])
    low = grad_ref[...].astype(LOW)
    depth = padded_ref.shape[1]
    parts = min(dp_count, 8)
    cut = dp_count // parts * depth
    for part in range(parts):
        row = lax.broadcasted_iota(jnp.int32, (cut, low.shape[0]), 0) + part * cut
        pick = one_hot(row == src_ref[...])
        block = nn(pick, low).astype(LOW)
        padded_ref[pl.ds(part * (dp_count // parts), dp_count // parts)] = block.reshape(
            dp_count // parts, depth, block.shape[1]
        )
    weights_sum.start()
    small_sum.back()
    own.wait()
    normal, scale = normalise(own_ref[...].astype(FULL))
    back = norm_back(normal, scale, norm_ref[0:1, :], total_of.result())[0]
    input_ref[me] = (x1g_ref[me].astype(FULL) + back).astype(LOW)
    spread.start()
    late_sum.across()
    steps = weights_sum.length

    @pl.loop(0, steps - 1)
    def _(turn):
        weights_sum.step(steps - 1 - turn)

        @pl.when(turn == steps - 2)
        def _():
            spread.wait_far()

    weights_sum.result()
    small_sum.result(small_out)
    late_sum.result(small_out, experts)
    down_grad_ref[...] = down_sum.result()
    spread.wait_near()
    spread.wait_corner()
    keep = pltpu.make_async_copy(input_ref, input_out, own_sem.at[0])
    keep.start()
    back_out.finish()
    spread.finish()
    total_of.finish()
    weights_sum.finish()
    small_sum.finish()
    late_sum.finish()
    down_sum.finish()
    keep.wait()


def attention_backward(
    experts, slots, depth,
    x1_grad, w, xn, hat, saved, lse, src_row, norm_params, small, patches, out_rows, down_part,
):
    images, _, width = patches.shape
    rows = w.shape[0] // 4
    dp_count = slots.count
    flat, turned = (2, PATCH, rows), (2, rows, PATCH)
    units = down_part.shape[1]
    return pl.pallas_call(
        functools.partial(backward_kernel, experts, slots),
        in_specs=[INSIDE] * 5 + [ANYWHERE] * 12,
        out_specs=[INSIDE] * 3 + [ANYWHERE] * 2,
        out_shape=[
            jax.ShapeDtypeStruct((depth, width), FULL), jax.ShapeDtypeStruct(small.shape, FULL),
            jax.ShapeDtypeStruct((units // 2, width), FULL),
            jax.ShapeDtypeStruct(patches.shape, LOW),
            jax.ShapeDtypeStruct((dp_count * slots.big, width), LOW),
        ],
        scratch_shapes=[pltpu.VMEM(patches.shape, LOW)]
        + [pltpu.VMEM((2, PATCH, width), LOW)] * 2
        + [pltpu.VMEM(shape, LOW) for shape in (flat, turned, flat, turned, flat, turned)]
        + [
            pltpu.VMEM((8, width), FULL), pltpu.VMEM(w.shape, FULL), pltpu.VMEM((PATCH, width), LOW),
            pltpu.VMEM(patches.shape, LOW), pltpu.VMEM((dp_count, depth, width), LOW),
            pltpu.SemaphoreType.DMA((9, 2)), pltpu.SemaphoreType.DMA((2,)),
        ]
        + image_sum_scratch(PATCH, width) + image_gather_sems()
        + slot_return_scratch(slots, width)
        + line_scatter_scratch(dp_count, depth, width)
        + block_sum_scratch(units // 2, width)
        + small_sum_scratch(small.shape[0], width, dp_count)
        + late_sum_scratch(width, dp_count),
        compiler_params=params(collective_id=2, has_side_effects=True),
        cost_estimate=pl.CostEstimate(
            flops=60 * patches.size * width, bytes_accessed=60 * patches.size, transcendentals=0
        ),
        name="attention_backward",
    )(
        w, lse, src_row, norm_params, small, x1_grad, xn, hat, *saved, patches, out_rows, down_part,
    )


def picked_rows(col, held_ref, start, count):
    lanes = lax.broadcasted_iota(jnp.int32, (col.shape[0], count), 1) + start
    pick = one_hot((lanes == col[:, 0:1]) | (lanes == col[:, 1:2]))
    return nn(pick, held_ref[pl.ds(start, count), :])


def mixed_rows(col, first, second, start):
    count = first.shape[0] + second.shape[0]
    lanes = lax.broadcasted_iota(jnp.int32, (col.shape[0], count), 1) + start
    pick = one_hot((lanes == col[:, 2:3]) | (lanes == col[:, 3:4]))
    return nn(pick, jnp.concatenate([first[...], second[...]], axis=0))


def late_kernel(col_ref, sum_ref, first, second, block_ref):
    start = first.shape[0] + second.shape[0]
    block_ref[0] = (sum_ref[0].astype(FULL) + mixed_rows(col_ref[0], first, second, start)).astype(LOW)


def late_stage(col, so_far, held):
    images, _, width = so_far.shape
    wide = lead((1, PATCH, width))
    return pl.pallas_call(
        late_kernel,
        grid=(images,),
        in_specs=[lead((1, PATCH, 4)), wide] + [whole(rows.shape) for rows in held],
        out_specs=wide,
        out_shape=jax.ShapeDtypeStruct(so_far.shape, LOW),
        compiler_params=params(),
        cost_estimate=pl.CostEstimate(
            flops=2 * images * PATCH * sum(rows.size for rows in held),
            bytes_accessed=6 * so_far.size + 2 * sum(rows.size for rows in held), transcendentals=0,
        ),
        name="late_stage",
    )(col, so_far, *held)


def early_kernel(
    col_ref, x1_ref, low_ref, held_own, held_near,
    tile_ref, tile_first, tile_second, tile_grad,
    router_ref, router_first, router_second, norm_ref, norm_first, norm_second, small_ref,
    sum_ref, input_ref, tile_new, tile_first_new, tile_second_new, tile_copy,
    router_new, router_first_new, router_second_new,
    norm_new, norm_first_new, norm_second_new, later_second_new,
):
    mix = mixed_rows(col_ref[0], held_own, held_near, 0)
    sum_ref[0] = (x1_ref[0].astype(FULL) + mix).astype(LOW)
    input_ref[0] = low_ref[0].astype(FULL)

    @pl.when(pl.program_id(0) == 0)
    def _():
        new, first, second = adam_update(
            tile_ref[...], tile_first[...], tile_second[...], tile_grad[...],
            rate_attention, decay_factor,
        )
        tile_new[...], tile_first_new[...], tile_second_new[...] = new, first, second
        tile_copy[...] = new.astype(LOW)
        experts = router_ref.shape[0]
        new, first, second = adam_update(
            router_ref[...], router_first[...], router_second[...], small_ref[0:experts, :],
            rate_router, decay_factor,
        )
        router_new[...], router_first_new[...], router_second_new[...] = new, first, second
        new, first, second = adam_update(
            norm_ref[...], norm_first[...], norm_second[...], small_ref[experts:experts + 4, :],
            rate_norm, 0.0,
        )
        norm_new[...], norm_first_new[...] = new, first
        norm_second_new[...], later_second_new[...] = second[0:2], second[2:4]


def early_stage(col, x1, input_low, held, tiles, routers, norms, small):
    images, _, width = x1.shape
    wide = lead((1, PATCH, width))
    tile, router, norm = tiles[0], routers[0], norms[0]
    fixed = [*held, *tiles, *routers, *norms, small]
    full = [tile.shape] * 3 + [tile.shape] + [router.shape] * 3 + [norm.shape] * 2 + [(2, width)] * 2
    kinds = [FULL] * 3 + [LOW] + [FULL] * 7
    return pl.pallas_call(
        early_kernel,
        grid=(images,),
        in_specs=[lead((1, PATCH, 4)), wide, wide] + [whole(array.shape) for array in fixed],
        out_specs=[wide, wide] + [whole(shape) for shape in full],
        out_shape=[jax.ShapeDtypeStruct(x1.shape, LOW), jax.ShapeDtypeStruct(x1.shape, FULL)]
        + [jax.ShapeDtypeStruct(shape, kind) for shape, kind in zip(full, kinds)],
        compiler_params=params(),
        cost_estimate=pl.CostEstimate(
            flops=2 * images * PATCH * sum(rows.size for rows in held),
            bytes_accessed=12 * x1.size + 2 * sum(rows.size for rows in held), transcendentals=0,
        ),
        name="early_stage",
    )(col, x1, input_low, *fixed)


def expert_kernel(
    slots,
    rows_ref, g_ref, router_in, col_ref, norm_ref,
    up_in, down_in, x1_in, cot_in,
    up_grad_ref, down_grad_ref, small_ref, down_out, out_out, x1g_out, passed_out,
    router_ref, up_ref, down_ref, og_ref, gate_ref, probs_ref, down_stage, back_ref, act_all,
    held, total, x1_ref, cot_ref, x1g_ref,
    load_sems, save_sems, image_sems, out_sem, pass_sem, *exchange,
):
    images, count = x1_in.shape[0], rows_ref.shape[0]
    out_sum, back_sum = total.at[pl.ds(0, count)], total.at[pl.ds(count, count)]
    up_sum = ImageSum(*exchange[:8])
    back = ReturnGather(slots, back_ref, held, *exchange[8:11])
    down_sum = BlockSum(down_out, 0, *exchange[11:], far=False)
    parts = up_in.shape[0]

    def load(turn):
        part, slot = up_sum.image(turn), lax.rem(turn, 2)
        return (
            pltpu.make_async_copy(up_in.at[part], up_ref.at[slot], load_sems.at[0, slot]),
            pltpu.make_async_copy(down_in.at[part], down_ref.at[slot], load_sems.at[1, slot]),
        )

    def save(turn):
        slot = lax.rem(turn, 2)
        return pltpu.make_async_copy(
            down_stage.at[slot], down_out.at[up_sum.image(turn)], save_sems.at[slot]
        )

    for turn in range(2):
        for copy in load(turn):
            copy.start()
    rows = rows_ref[...]
    experts = router_in.shape[0]
    router_ref[...] = jnp.zeros_like(router_ref)
    router_ref[0:experts, :] = router_in[...]
    lane = lax.broadcasted_iota(jnp.int32, (1, router_ref.shape[0]), 1)
    mine = jnp.where(lane == lax.axis_index("dp"), 1.0, 0.0)
    logits = nt(rows, router_ref[...].astype(LOW)) + jnp.where(lane < experts, 0.0, -1e30)
    top = jnp.max(logits, axis=-1, keepdims=True)
    weights = jnp.exp(logits - top)
    probs = weights / jnp.sum(weights, axis=-1, keepdims=True)
    gate = jnp.sum(probs * mine, axis=-1, keepdims=True)
    probs_ref[...] = probs
    gate_ref[...] = gate
    og_ref[...] = (gate * g_ref[...].astype(FULL)).astype(LOW)
    out_sum[...] = jnp.zeros_like(out_sum)
    back_sum[...] = jnp.zeros_like(back_sum)
    greet_all((back.near, back.far), slots.count)

    later = act_all.shape[0] > 1

    def down_grads(turn, act):
        @pl.when(turn >= 2)
        def _():
            save(turn - 2).wait()

        down_stage[lax.rem(turn, 2)] = tn(act, og_ref[...]).astype(LOW)
        save(turn).start()

    @pl.loop(0, parts)
    def _(turn):
        slot = lax.rem(turn, 2)
        for copy in load(turn):
            copy.wait()
        rows, og = rows_ref[...], og_ref[...]
        up, down = up_ref[slot], down_ref[slot]
        hidden = nn(rows, up)
        slope = (2.0 / jnp.pi) ** 0.5
        square = hidden * hidden
        bend = jnp.tanh(slope * (hidden + 0.044715 * (square * hidden)))
        act = (0.5 * hidden * (1.0 + bend)).astype(LOW)
        out_sum[...] += nn(act, down)
        act_grad = nt(og, down)
        inner = slope * (1.0 + (3.0 * 0.044715) * square)
        curve = 0.5 * (1.0 + bend) + 0.5 * hidden * (1.0 - bend * bend) * inner
        hidden_grad = (curve * act_grad).astype(LOW)
        back_sum[...] += nt(hidden_grad, up)
        up_sum.give(turn, tn(rows, hidden_grad), hold=True)
        if later:
            act_all[turn] = act
        else:
            down_grads(turn, act)

        @pl.when(turn + 2 < parts)
        def _():
            for copy in load(turn + 2):
                copy.start()

    out = out_sum[...].astype(LOW).astype(FULL)
    gate, probs = gate_ref[...], probs_ref[...]
    gate_grad = jnp.sum(g_ref[...].astype(FULL) * out, axis=-1, keepdims=True)
    logit_grad = (gate_grad * (probs * (mine - gate))).astype(LOW)
    plain = back_sum[...].astype(LOW).astype(FULL)
    back_ref[...] = (plain + nn(logit_grad, router_ref[...].astype(LOW))).astype(LOW)
    back.send(0)
    back.send(1)
    back.relay(0)
    small_ref[...] = jnp.zeros_like(small_ref)
    small_ref[0:experts, :] = tn(logit_grad, rows_ref[...])[0:experts]
    back_sum[...] = gate * out
    def image_load(image):
        slot = lax.rem(image, 2)
        return (
            pltpu.make_async_copy(x1_in.at[image], x1_ref.at[slot], image_sems.at[0, slot]),
            pltpu.make_async_copy(cot_in.at[image], cot_ref.at[slot], image_sems.at[1, slot]),
        )

    def image_save(image):
        slot = lax.rem(image, 2)
        return pltpu.make_async_copy(x1g_ref.at[slot], x1g_out.at[image], image_sems.at[2, slot])

    for image in range(2):
        for copy in image_load(image):
            copy.start()

    def relay(phase):
        @pl.loop(max(phase * slots.turns, 1), (phase + 1) * slots.turns)
        def _(shift):
            back.relay(shift)

    ahead = [
        lambda: (relay(0), back.send(2)),
        lambda: (relay(1), back.send(3)),
        lambda: (back.of_phase(0, back.forward), relay(2)),
        lambda: (back.of_phase(1, back.forward), relay(3)),
    ]
    if later:
        for turn in range(parts):
            down_grads(turn, act_all[turn])
            if turn < 3:
                ahead[turn]()
    else:
        for step in ahead[:3]:
            step()
    for turn in range(parts - 2, parts):
        save(turn).wait()
    down_sum.start()
    og_ref[...] = back_sum[...].astype(LOW)
    save_out = pltpu.make_async_copy(og_ref, out_out, out_sem)
    save_out.start()
    total_rows = held.shape[0]
    piece = 3 * 256
    if total_rows % piece:
        piece = slots.phase_rows
    done = 0
    back.of_phase(0, back.rest)
    for phase in range(1, 4):
        if phase == 1:
            ahead[3]()
            up_sum.start_rest()
        else:
            back.of_phase(phase, back.forward)
        back.of_phase(phase, back.rest)
        ready = (phase + 1) * slots.phase_rows
        while done + piece <= ready:
            @pl.loop(0, images)
            def _(image, start=done):
                part = picked_rows(col_ref[image], held, start, piece)
                span = pl.ds(image * PATCH, PATCH)
                if start == 0:
                    total[span] = part
                else:
                    total[span] += part

            done += piece

    back_scale = 1.0 / 4.0

    @pl.loop(0, images)
    def _(image):
        slot = lax.rem(image, 2)
        for copy in image_load(image):
            copy.wait()

        @pl.when(image >= 2)
        def _():
            image_save(image - 2).wait()

        normal, scale = normalise(x1_ref[slot].astype(FULL))
        upstream = total[pl.ds(image * PATCH, PATCH)]
        result, gain_sum, shift_sum = norm_back(normal, scale, norm_ref[2:3, :], upstream)
        x1g_ref[slot] = (cot_ref[slot].astype(FULL) + result).astype(LOW)
        small_ref[experts + 2:experts + 3, :] += gain_sum * back_scale
        small_ref[experts + 3:experts + 4, :] += shift_sum * back_scale
        image_save(image).start()

        @pl.when(image + 2 < images)
        def _():
            for copy in image_load(image + 2):
                copy.start()

    down_sum.across()
    save_passed = pltpu.make_async_copy(down_sum.passed, passed_out, pass_sem)
    save_passed.start()
    down_grad_ref[...] = down_sum.result()
    up_grad_ref[...] = up_sum.result()
    back.finish()
    up_sum.finish()
    down_sum.finish()
    save_passed.wait()
    save_out.wait()
    for image in range(images - 2, images):
        image_save(image).wait()


def expert_stage(slots, rows, g_rows, up, down, router, col, x1, cotangent, norm_params):
    count, width = rows.shape
    parts, _, units = up.shape
    images = x1.shape[0]
    small_rows = -(-(router.shape[0] + 4) // 16) * 16
    lanes = 128
    flat = pltpu.VMEM((count, width), LOW)
    pair = pltpu.VMEM((2, PATCH, width), LOW)
    return pl.pallas_call(
        functools.partial(expert_kernel, slots),
        in_specs=[INSIDE] * 5 + [ANYWHERE] * 4,
        out_specs=[INSIDE] * 3 + [ANYWHERE] * 4,
        out_shape=[
            jax.ShapeDtypeStruct((width, units), FULL),
            jax.ShapeDtypeStruct((units // 2, width), FULL),
            jax.ShapeDtypeStruct((small_rows, width), FULL),
            jax.ShapeDtypeStruct(down.shape, LOW),
            jax.ShapeDtypeStruct((count, width), LOW),
            jax.ShapeDtypeStruct(x1.shape, LOW),
            jax.ShapeDtypeStruct((units // 2, width), LOW),
        ],
        scratch_shapes=[
            pltpu.VMEM((lanes, width), FULL),
            pltpu.VMEM((2,) + up.shape[1:], LOW), pltpu.VMEM((2,) + down.shape[1:], LOW), flat,
            pltpu.VMEM((count, 1), FULL), pltpu.VMEM((count, lanes), FULL),
            pltpu.VMEM((2, units, width), LOW), flat,
            pltpu.VMEM((parts, count, units) if count <= MOST_KEPT else (1, 16, 128), LOW),
            pltpu.VMEM((4 * slots.phase_rows, width), LOW),
            pltpu.VMEM((max(images * PATCH, 2 * count), width), FULL), pair, pair, pair,
            pltpu.SemaphoreType.DMA((2, 2)), pltpu.SemaphoreType.DMA((2,)),
            pltpu.SemaphoreType.DMA((3, 2)), pltpu.SemaphoreType.DMA, pltpu.SemaphoreType.DMA,
        ]
        + image_sum_scratch(width, units) + return_gather_sems(slots.count)
        + block_sum_scratch(units // 2, width),
        compiler_params=params(collective_id=3, has_side_effects=True),
        name="expert_stage",
    )(
        rows, g_rows, router, col, norm_params, up, down, x1, cotangent,
    )


def body(
    patches, cotangent, expert_ids, slot_pos, owners,
    tile_master, tile_first, tile_second,
    expert_up, up_first, up_second,
    expert_down, down_first, down_second,
    router, router_first, router_second,
    norm_params, norm_first, norm_second,
):
    tok_rows, width = patches.shape
    experts = router.shape[0]
    capacity = tok_rows // experts
    dp_count = lax.axis_size("dp")
    head_count = lax.axis_size("head")
    images = tok_rows // PATCH
    slots = Slots(dp_count, capacity // head_count)
    slot_count = tile_master.shape[0]

    by_image = (images, PATCH, width)
    x_images, g_images = patches.reshape(by_image), cotangent.reshape(by_image)
    w, src, col, lse, xn, hat, up_all, down_all, *saved, x1, rows, g_rows = front(
        slots, tile_master.reshape(slot_count * TILE, width), x_images, g_images, norm_params,
        owners, expert_ids.T, slot_pos.T, expert_up[0], expert_down[0],
        owners.shape[1] * TILE,
    )
    up_grad, down_half, small, down_part, out, x1_grad, passed = expert_stage(
        slots, rows, g_rows, up_all, down_all, router, col, x1, g_images, norm_params
    )
    def from_head(rows, apart):
        return lax.ppermute(rows, "head", [(at, at ^ apart) for at in range(head_count)])

    passed = from_head(passed, 2)
    owned_grad, small, down_rest, input_low, out_back = attention_backward(
        experts, slots, slot_count * TILE,
        x1_grad, w, xn, hat, saved, lse, src, norm_params, small, x_images, out, down_part,
    )

    out_back, passed = lax.optimization_barrier((out_back, passed))
    out_far = from_head(out_back, 2)
    flat_tiles = (slot_count * TILE, width)
    (
        so_far, input_grad, tile_new, tile_first_new, tile_second_new, tile_copy,
        router_new, router_first_new, router_second_new,
        norm_new, norm_first_new, norm_second_new, later_second_new,
    ) = early_stage(
        col, x1, input_low, [out_back, from_head(out_back, 1)],
        [array.reshape(flat_tiles) for array in (tile_master, tile_first, tile_second)] + [owned_grad],
        [router, router_first, router_second], [norm_params, norm_first, norm_second], small,
    )
    up_new, up_first_new, up_second_new = adam_update(
        expert_up, up_first, up_second, up_grad[None], rate_up, decay_factor
    )
    out_far, so_far, _ = lax.optimization_barrier((out_far, so_far, up_new))
    block_out = late_stage(col, so_far, [out_far, from_head(out_far, 1)])
    down_half = down_half + passed.astype(FULL)
    down_grad = jnp.concatenate([down_half, down_rest], axis=0)
    tiles = [
        array.reshape(tile_master.shape)
        for array in (tile_new, tile_first_new, tile_second_new, tile_copy)
    ]
    down_new, down_first_new, down_second_new = adam_update(
        expert_down, down_first, down_second, down_grad[None], rate_down, decay_factor
    )
    return (
        block_out.reshape(tok_rows, width),
        input_grad.reshape(tok_rows, width),
        *tiles,
        up_new,
        up_first_new,
        up_second_new,
        up_new.astype(LOW),
        down_new,
        down_first_new,
        down_second_new,
        down_new.astype(LOW),
        router_new,
        router_first_new,
        router_second_new,
        norm_new,
        norm_first_new,
        norm_second_new,
        later_second_new,
    )


def solution(mesh):
    row = P("dp", None)
    tiles = P(("dp", "head"), None, None)
    up = P("dp", None, "head")
    down = P("dp", "head", None)
    in_specs = (
        row, row, row, row, P("head", None), tiles, tiles, tiles,
        up, up, up, down, down, down, P(), P(), P(), P(), P(), P(),
    )
    out_specs = (
        row, row, tiles, tiles, tiles, tiles, up, up, up, up, down, down, down, down,
        P(), P(), P(), P(), P(), P(), P(),
    )
    return jax.shard_map(body, mesh=mesh, in_specs=in_specs, out_specs=out_specs, check_vma=False)
```
